128 devices in a mesh: fsdp: 8 (over y, core), ctx: 8 (over z, x_lo), tp: 2 (over x_hi).
Axes of the slice: x: 4 (x_hi: 2, x_lo: 2; x = x_hi * 2 + x_lo), y: 4, z: 4, core: 2. Of those that a mesh axis runs over, the one named last changes fastest.
Arguments:
- x_prompt: bfloat16 [2, 8, 448, 2048], P(None, 'fsdp', 'ctx'), may hold values from -6 to 6
- x_cont: bfloat16 [2, 8, 512, 2048], P(None, 'fsdp', 'ctx'), may hold values from -6 to 6
- cot_prompt: bfloat16 [2, 8, 448, 2048], P(None, 'fsdp', 'ctx'), may hold values from -6 to 6
- cot_cont: bfloat16 [2, 8, 512, 2048], P(None, 'fsdp', 'ctx'), may hold values from -6 to 6
- ids_prompt: int32 [2, 8, 448, 8], P(None, 'fsdp', 'ctx'), may hold values from 0 to 63, all different within a row; in each aligned block of 56 rows (0 to 55, 56 to 111, ..., all dimensions but the last counted through in order) at most 7 rows name the same one
- ids_cont: int32 [2, 8, 512, 8], P(None, 'fsdp', 'ctx'), may hold values from 0 to 63, all different within a row; in each aligned block of 64 rows (0 to 63, 64 to 127, ..., all dimensions but the last counted through in order) at most 8 rows name the same one
- gates_prompt: float32 [2, 8, 448, 8], P(None, 'fsdp', 'ctx'), may hold values from 0 to 1, as said below
- gates_cont: float32 [2, 8, 512, 8], P(None, 'fsdp', 'ctx'), may hold values from 0 to 1, as said below
- norm_gain: bfloat16 [2048], P(('fsdp', 'ctx')), may hold values from 0.5 to 1.5
- query_weight: bfloat16 [2048, 4096], P(('fsdp', 'ctx'), 'tp'), may hold values from -0.125 to 0.125
- key_matrix: bfloat16 [2048, 512], P(('fsdp', 'ctx'), 'tp'), may hold values from -0.125 to 0.125
- value_matrix: bfloat16 [2048, 512], P(('fsdp', 'ctx'), 'tp'), may hold values from -0.125 to 0.125
- out_weight: bfloat16 [2048, 4096], P(('fsdp', 'ctx'), 'tp'), may hold values from -0.5 to 0.5
- query_gain: bfloat16 [128], P(('fsdp', 'ctx')), may hold values from 0.099609375 to 1.8984375
- key_gain: bfloat16 [128], P(('fsdp', 'ctx')), may hold values from 0.099609375 to 1.8984375
- moe_gain: bfloat16 [2048], P(('fsdp', 'ctx')), may hold values from 0.5 to 1.5
- expert_gate: bfloat16 [64, 2048, 768], P(('fsdp', 'ctx'), None, 'tp'), may hold values from -0.125 to 0.125
- expert_up: bfloat16 [64, 2048, 768], P(('fsdp', 'ctx'), None, 'tp'), may hold values from -0.125 to 0.125
- expert_down: bfloat16 [64, 768, 2048], P(('fsdp', 'ctx'), 'tp'), may hold values from -0.875 to 0.875
Outputs:
- output_prompt: bfloat16 [2, 8, 448, 2048], P(None, 'fsdp', 'ctx')
- output_cont: bfloat16 [2, 8, 512, 2048], P(None, 'fsdp', 'ctx')
- grad_prompt: bfloat16 [2, 8, 448, 2048], P(None, 'fsdp', 'ctx')
- grad_cont: bfloat16 [2, 8, 512, 2048], P(None, 'fsdp', 'ctx')
- grad_norm_gain: float32 [2048], P(('fsdp', 'ctx'))
- grad_query_weight: float32 [2048, 4096], P(('fsdp', 'ctx'), 'tp')
- grad_key_weight: float32 [2048, 512], P(('fsdp', 'ctx'), 'tp')
- grad_value_weight: float32 [2048, 512], P(('fsdp', 'ctx'), 'tp')
- grad_out_weight: float32 [2048, 4096], P(('fsdp', 'ctx'), 'tp')
- grad_query_gain: float32 [128], P(('fsdp', 'ctx'))
- grad_key_gain: float32 [128], P(('fsdp', 'ctx'))
- grad_moe_gain: float32 [2048], P(('fsdp', 'ctx'))
- grad_expert_gate: float32 [64, 2048, 768], P(('fsdp', 'ctx'), None, 'tp')
- grad_expert_up: float32 [64, 2048, 768], P(('fsdp', 'ctx'), None, 'tp')
- grad_expert_down: float32 [64, 768, 2048], P(('fsdp', 'ctx'), 'tp')
The draws below stay inside these ranges and needn't reach their ends.
Inputs may be any that keep to these rules, and one draw needn't show every extreme that they name: `ids_prompt`: each row names 8 different experts; in every aligned block of 56 rows (the prompt rows of one group and micro-batch on one index of ctx) every expert is named by exactly 7 rows. `ids_cont`: each row names 8 different experts; in every aligned block of 64 rows every expert is named by exactly 8 rows. `gates_prompt`: each row's 8 gates are positive and sum to one. `gates_cont`: each row's 8 gates are positive and sum to one.
All inputs are finite; a program needn't handle non-finite values.
Results may differ from the reference program's by a relative error of at most 0.035.
Values may be sent and summed in bfloat16 or wider, within the bound.
A program may use at most 256 MiB of HBM per device.

```python
import math
import jax
import jax.numpy as jnp
import numpy as np
from jax import lax

MODEL_WIDTH = 2048
QUERY_HEADS = 32
KEY_VALUE_HEADS = 4
HEAD_SIZE = 128
F = 768
TOPK = 8
PROMPT = 448
CL = 128
MB = 2
GROUPS = 8
CTOK = 512
PDEV = 56
CDEV = 64
E = 64
MP = 7
MC = 8


def draw_gates_prompt(key, part):
    key = jax.random.fold_in(key, 11)
    logits = 0.5 * jax.random.normal(key, (MB, GROUPS, PROMPT, TOPK), jnp.float32)
    return jax.nn.softmax(logits, axis=-1)


def draw_gates_cont(key, part):
    key = jax.random.fold_in(key, 23)
    logits = 0.5 * jax.random.normal(key, (MB, GROUPS, CTOK, TOPK), jnp.float32)
    return jax.nn.softmax(logits, axis=-1)


def level_of(stream_key, extent, split, smallest, largest):
    def one(axis_at, shards_of):
        draws = jax.random.uniform(jax.random.fold_in(jax.random.fold_in(stream_key, 6), axis_at), (shards_of,), jnp.float32, smallest / len(split), largest / len(split))
        return jnp.repeat(jnp.exp(draws), extent[axis_at] // shards_of).reshape((-1,) + (1,) * (len(extent) - axis_at - 1))

    level = one(*split[0])
    for cut in split[1:]:
        level = level * one(*cut)
    return level


def assign_block(stream_key, own, number, rows, number_of, top, bound, slope):
    sequence = jax.random.permutation(stream_key, number_of)
    packed, usual = shares(number_of, rows * top, bound, slope, True), shares(number_of, rows * top, bound, slope, False)
    places = jnp.arange(number_of)

    def named(sizes, rotation):
        used = int((sizes > 0).sum())
        fixed = max(1, used // 4)
        passed = fixed + (places - fixed + rotation * (used - fixed)) % max(1, number_of - fixed)
        return jnp.zeros((number_of,), jnp.int32).at[sequence[jnp.where(places < fixed, places, passed)]].set(jnp.asarray(sizes, jnp.int32))

    sizes = jnp.where(number % 4 == 0, named(packed, number // 4), named(usual, number - number // 4 - 1))
    mixed = jax.random.permutation(jax.random.fold_in(own, 3), number_of)
    giver, receiver = mixed[0:number_of // 2 * 2:2], mixed[1:number_of // 2 * 2:2]
    margin = jnp.minimum(sizes[giver] - 1, bound - sizes[receiver]) // 2
    margin = jnp.where((giver == sequence[0]) | (receiver == sequence[0]) | (sizes[receiver] == 0), 0, jnp.maximum(margin, 0))
    passed = jax.random.randint(jax.random.fold_in(own, 4), (number_of // 2,), 0, 1 << 20) % (margin + 1)
    sizes = sizes.at[giver].add(-passed).at[receiver].add(passed)
    labels = jnp.searchsorted(jnp.cumsum(sizes), jnp.arange(rows * top), side="right").astype(jnp.int32)
    listing = labels.reshape(top, rows).T
    listing = listing[jax.random.permutation(jax.random.fold_in(own, 1), rows)]
    rotation = jax.random.randint(jax.random.fold_in(own, 2), (rows, 1), 0, top)
    return jnp.take_along_axis(listing, (jnp.arange(top)[None, :] + rotation) % top, axis=1)


def shares(number_of, total, limit, slope, full):
    portions = [(1 << 20) // math.isqrt(grade ** slope) + 1 for grade in range(1, number_of + 1)]
    largest = limit if full else min(limit, max(-(-total // number_of), total * portions[0] // sum(portions)))
    least = 1 if total - largest >= number_of - 1 else 0
    given, surplus = [largest] + [least] * (number_of - 1), total - largest - least * (number_of - 1)
    while surplus > 0:
        free = [i for i in range(1, number_of) if given[i] < largest] or [i for i in range(1, number_of) if given[i] < limit]
        mass, budget = sum([portions[i] for i in free]), surplus
        for i in free:
            extra = min(limit - given[i], max(1, budget * portions[i] // mass), surplus)
            given[i] = given[i] + extra
            surplus = surplus - extra
    return np.array(given)


def gaussian(stream_key, extent, deviation, limit, pieces=(), kind=jnp.bfloat16):
    values = jax.random.normal(stream_key, extent, jnp.float32) * deviation
    if len(pieces) > 0:
        values = level_of(stream_key, extent, pieces, -0.22, 0.18) * values
    return jnp.clip(values, min=-limit, max=limit).astype(kind)


def setup_inputs(seed: int = 0) -> dict:
    key_list = jax.random.split(jax.random.key(seed), 20)
    x_prompt = gaussian(key_list[0], (MB, GROUPS, PROMPT, MODEL_WIDTH), 1.0, 6.0, ((1, 8), (2, 8)))
    x_cont = gaussian(key_list[1], (MB, GROUPS, CTOK, MODEL_WIDTH), 1.0, 6.0, ((1, 8), (2, 8)))
    cot_prompt = gaussian(key_list[2], (MB, GROUPS, PROMPT, MODEL_WIDTH), 1.0, 6.0, ((1, 8), (2, 8)))
    cot_cont = gaussian(key_list[3], (MB, GROUPS, CTOK, MODEL_WIDTH), 1.0, 6.0, ((1, 8), (2, 8)))
    ids_prompt_keys = jax.random.split(jax.random.fold_in(key_list[4], 1), MB * GROUPS * PROMPT // PDEV)
    ids_prompt_turns = jax.random.permutation(jax.random.fold_in(key_list[4], 3), MB * GROUPS * PROMPT // PDEV)
    ids_prompt = jax.vmap(lambda own, number: assign_block(jax.random.fold_in(key_list[4], 2), own, number, PDEV, E, TOPK, MP, 0))(ids_prompt_keys, ids_prompt_turns).reshape((MB, GROUPS, PROMPT, TOPK))
    ids_cont_keys = jax.random.split(jax.random.fold_in(key_list[5], 1), MB * GROUPS * CTOK // CDEV)
    ids_cont_turns = jax.random.permutation(jax.random.fold_in(key_list[5], 3), MB * GROUPS * CTOK // CDEV)
    ids_cont = jax.vmap(lambda own, number: assign_block(jax.random.fold_in(key_list[5], 2), own, number, CDEV, E, TOPK, MC, 0))(ids_cont_keys, ids_cont_turns).reshape((MB, GROUPS, CTOK, TOPK))
    gates_prompt = draw_gates_prompt(jax.random.fold_in(key_list[19], 71), 0)
    gates_cont = draw_gates_cont(jax.random.fold_in(key_list[19], 71), 0)
    norm_gain = jnp.clip(1.0 + 0.1 * jax.random.normal(key_list[8], (MODEL_WIDTH,), jnp.float32), 0.5, 1.5).astype(jnp.bfloat16)
    query_weight = gaussian(key_list[9], (MODEL_WIDTH, QUERY_HEADS * HEAD_SIZE), MODEL_WIDTH ** -0.5, 0.125, ((0, 64), (1, 2)))
    key_matrix = gaussian(key_list[10], (MODEL_WIDTH, KEY_VALUE_HEADS * HEAD_SIZE), MODEL_WIDTH ** -0.5, 0.125, ((0, 64), (1, 2)))
    value_matrix = gaussian(key_list[11], (MODEL_WIDTH, KEY_VALUE_HEADS * HEAD_SIZE), MODEL_WIDTH ** -0.5, 0.125, ((0, 64), (1, 2)))
    out_weight = gaussian(key_list[12], (MODEL_WIDTH, QUERY_HEADS * HEAD_SIZE), (QUERY_HEADS * HEAD_SIZE // 32) ** -0.5, 0.5, ((0, 64), (1, 2)))
    query_gain = jnp.clip(1.0 + 0.18 * jax.random.normal(key_list[13], (HEAD_SIZE,), jnp.float32), 0.099609375, 1.8984375).astype(jnp.bfloat16)
    key_gain = jnp.clip(1.0 + 0.18 * jax.random.normal(key_list[14], (HEAD_SIZE,), jnp.float32), 0.099609375, 1.8984375).astype(jnp.bfloat16)
    moe_gain = jnp.clip(1.0 + 0.1 * jax.random.normal(key_list[15], (MODEL_WIDTH,), jnp.float32), 0.5, 1.5).astype(jnp.bfloat16)
    expert_gate = gaussian(key_list[16], (E, MODEL_WIDTH, F), MODEL_WIDTH ** -0.5, 0.125, ((0, 64), (2, 2)))
    expert_up = gaussian(key_list[17], (E, MODEL_WIDTH, F), MODEL_WIDTH ** -0.5, 0.125, ((0, 64), (2, 2)))
    expert_down = gaussian(key_list[18], (E, F, MODEL_WIDTH), (F // 16) ** -0.5, 0.875, ((0, 64), (1, 2)))
    return dict(x_prompt=x_prompt, x_cont=x_cont, cot_prompt=cot_prompt, cot_cont=cot_cont, ids_prompt=ids_prompt, ids_cont=ids_cont, gates_prompt=gates_prompt, gates_cont=gates_cont, norm_gain=norm_gain, query_weight=query_weight, key_matrix=key_matrix, value_matrix=value_matrix, out_weight=out_weight, query_gain=query_gain, key_gain=key_gain, moe_gain=moe_gain, expert_gate=expert_gate, expert_up=expert_up, expert_down=expert_down)


EPS = 1e-06
THETA = 1000000.0
NEG = -1e+30
PRECISION_FULL = lax.Precision.HIGHEST

@jax.custom_vjp
def lower_precision(v):
    return lax.optimization_barrier(v.astype(jnp.bfloat16)).astype(jnp.float32)

@jax.custom_vjp
def lower_precision_back(v):
    return v

def low_keep(v):
    return (lower_precision(v), None)

def low_pass(kept, grad):
    return (grad,)

def back_keep(v):
    return (v, None)

def back_low(kept, grad):
    return (lower_precision(grad),)
lower_precision.defvjp(low_keep, low_pass)
lower_precision_back.defvjp(back_keep, back_low)

def normalize(value_rows, gain_vector):
    return value_rows * lax.rsqrt(lax.optimization_barrier(jnp.mean(value_rows * value_rows, axis=-1, keepdims=True)) + EPS) * gain_vector

def rotate(value_rows, cosine, sine):
    half_width = value_rows.shape[-1] // 2
    first_half = value_rows[..., :half_width]
    second_half = value_rows[..., half_width:]
    return jnp.concatenate([first_half * cosine - second_half * sine, second_half * cosine + first_half * sine], axis=-1)

def group_layer(tokens, expert_ids, expert_gates, params):
    norm_gain, query_weight, key_matrix, value_matrix, out_weight, query_gain, key_gain, moe_gain, expert_gate, expert_up, expert_down = params
    sequence_length = PROMPT + CTOK
    repeat_factor = QUERY_HEADS // KEY_VALUE_HEADS
    normed_input = lower_precision(normalize(tokens, norm_gain))
    query_rows = lower_precision_back(jnp.dot(normed_input, query_weight, precision=PRECISION_FULL)).reshape(sequence_length, QUERY_HEADS, HEAD_SIZE)
    keys_unnormed = lower_precision_back(jnp.dot(normed_input, key_matrix, precision=PRECISION_FULL)).reshape(sequence_length, KEY_VALUE_HEADS, HEAD_SIZE)
    value_rows = lower_precision_back(lower_precision(jnp.dot(normed_input, value_matrix, precision=PRECISION_FULL))).reshape(sequence_length, KEY_VALUE_HEADS, HEAD_SIZE)
    token_index = jnp.arange(sequence_length, dtype=jnp.int32)
    is_prompt = token_index < PROMPT
    cont_index = token_index - PROMPT
    rot_place = jnp.where(is_prompt, token_index, PROMPT + cont_index % CL).astype(jnp.float32)
    steps_freq = jnp.arange(HEAD_SIZE // 2, dtype=jnp.float32) * (2.0 / HEAD_SIZE)
    angles = rot_place[:, None] * jnp.power(THETA, -steps_freq)[None, :]
    cosine = jnp.cos(angles)[:, None, :]
    sine = jnp.sin(angles)[:, None, :]
    query_rows = lower_precision_back(lower_precision(rotate(normalize(query_rows, query_gain), cosine, sine)))
    keys_rot = lower_precision_back(lower_precision(rotate(normalize(keys_unnormed, key_gain), cosine, sine)))
    grouped_heads = query_rows.reshape(sequence_length, KEY_VALUE_HEADS, repeat_factor, HEAD_SIZE)
    scores = jnp.einsum('qhed,khd->heqk', grouped_heads, keys_rot, precision=PRECISION_FULL) * HEAD_SIZE ** (-0.5)
    scores = lower_precision_back(scores)
    earlier = token_index[None, :] <= token_index[:, None]
    same_cont = cont_index[None, :] // CL == cont_index[:, None] // CL
    visible = jnp.where(is_prompt[None, :], jnp.logical_or(jnp.logical_not(is_prompt[:, None]), earlier), jnp.logical_and(jnp.logical_not(is_prompt[:, None]), jnp.logical_and(same_cont, earlier)))
    scores = jnp.where(visible[None, None], scores, NEG)
    row_peak = lax.optimization_barrier(jnp.max(scores, axis=-1, keepdims=True))
    exp_scores = jnp.exp(scores - row_peak)
    probs = lower_precision(exp_scores / lax.optimization_barrier(jnp.sum(exp_scores, axis=-1, keepdims=True)))
    attended = jnp.einsum('heqk,khd->qhed', probs, value_rows, precision=PRECISION_FULL)
    attended = lower_precision_back(lower_precision(attended)).reshape(sequence_length, QUERY_HEADS * HEAD_SIZE)
    branch = lower_precision_back(jnp.einsum('qj,dj->qd', attended, out_weight, precision=PRECISION_FULL))
    middle = tokens + branch
    moe_in = lower_precision(normalize(middle, moe_gain))
    sort_order = jnp.argsort(expert_ids.reshape(-1), stable=True).astype(jnp.int32)
    slot_table = sort_order.reshape(E, sequence_length * TOPK // E)
    owner_rows = slot_table // TOPK
    expert_rows = lower_precision_back(moe_in[owner_rows])
    gate_pre = lower_precision_back(jnp.einsum('esd,edf->esf', expert_rows, expert_gate, precision=PRECISION_FULL))
    up_pre = lower_precision_back(jnp.einsum('esd,edf->esf', expert_rows, expert_up, precision=PRECISION_FULL))
    hidden = lower_precision(gate_pre * jax.nn.sigmoid(gate_pre) * up_pre)
    expert_out = lower_precision_back(lower_precision(jnp.einsum('esf,efd->esd', hidden, expert_down, precision=PRECISION_FULL)))
    slot_gate = expert_gates.reshape(-1)[slot_table]
    weighted = (expert_out * slot_gate[..., None]).reshape(-1, MODEL_WIDTH)
    moe_out = jax.ops.segment_sum(weighted, owner_rows.reshape(-1), num_segments=sequence_length)
    return middle + moe_out

def reference(x_prompt, x_cont, cot_prompt, cot_cont, ids_prompt, ids_cont, gates_prompt, gates_cont, norm_gain, query_weight, key_matrix, value_matrix, out_weight, query_gain, key_gain, moe_gain, expert_gate, expert_up, expert_down):
    sequence_length = PROMPT + CTOK
    routing = jnp.concatenate([ids_prompt, ids_cont], axis=2).reshape(MB * GROUPS, sequence_length, TOPK)
    mixing = jnp.concatenate([gates_prompt, gates_cont], axis=2).astype(jnp.float32).reshape(MB * GROUPS, sequence_length, TOPK)
    params = tuple((item.astype(jnp.float32) for item in (norm_gain, query_weight, key_matrix, value_matrix, out_weight, query_gain, key_gain, moe_gain, expert_gate, expert_up, expert_down)))

    def forward(first_part, second_part, weights_all):
        tokens = jnp.concatenate([first_part, second_part], axis=2).reshape(MB * GROUPS, sequence_length, MODEL_WIDTH)
        step_fn = jax.checkpoint(lambda item: group_layer(item[0], item[1], item[2], weights_all))
        result = lax.map(step_fn, (tokens, routing, mixing)).reshape(MB, GROUPS, sequence_length, MODEL_WIDTH)
        return (result[:, :, :PROMPT], result[:, :, PROMPT:])
    outputs, pullback = jax.vjp(forward, x_prompt.astype(jnp.float32), x_cont.astype(jnp.float32), params)
    grad_first, grad_second, grads = pullback((cot_prompt.astype(jnp.float32), cot_cont.astype(jnp.float32)))
    return (outputs[0].astype(jnp.bfloat16), outputs[1].astype(jnp.bfloat16), grad_first.astype(jnp.bfloat16), grad_second.astype(jnp.bfloat16), grads[0], grads[1], grads[2], grads[3], grads[4], grads[5], grads[6], grads[7], grads[8], grads[9], grads[10])
```

```python
import functools

import jax
import jax.numpy as jnp
from jax import lax
from jax.experimental import pallas as pl
from jax.experimental.pallas import tpu as pltpu
from jax.sharding import PartitionSpec as P

HEAD_SIZE = 128
TOPK = 8
PROMPT = 448
CL = 128
EPS = 1e-06
THETA = 1000000.0
NEG = -1e30
F32 = jnp.float32
BF16 = jnp.bfloat16
ALL = ("fsdp", "ctx")
MESH = pl.DeviceIdType.MESH
RING = 4
VMEM_LIMIT = 48 * 1024 * 1024


def place():
    f, c = lax.axis_index("fsdp"), lax.axis_index("ctx")
    return f // 2, f % 2, c // 2, c % 2


def device(y, core, z, x):
    return {"fsdp": y * 2 + core, "ctx": z * 2 + x}


def greet(partners):
    barrier = pltpu.get_barrier_semaphore()
    for partner in partners:
        pl.semaphore_signal(barrier, inc=1, device_id=partner, device_id_type=MESH)
    pl.semaphore_wait(barrier, len(partners))


def neighbours():
    y, core, z, x = place()
    up, down = (lambda v: lax.rem(v + 1, RING)), (lambda v: lax.rem(v + RING - 1, RING))
    return [
        device(y, core, z, 1 - x),
        device(y, 1 - core, z, x),
        device(up(y), core, z, x),
        device(down(y), core, z, x),
        device(y, core, up(z), x),
        device(y, core, down(z), x),
    ]


def other_tp():
    return {"tp": 1 - lax.axis_index("tp")}


def swap_halves(src, dst, send_sem, recv_sem):
    return pltpu.make_async_remote_copy(
        src_ref=src, dst_ref=dst, send_sem=send_sem, recv_sem=recv_sem, device_id=other_tp(),
        device_id_type=MESH,
    )


def gather_kernel(
    a_ref, b_ref, gate_ref, up_ref, a_all, b_all, wide_all,
    local_sem, send_sem, recv_sem, away_sem, home_sem, keep_sem, give_sem, take_sem,
):
    y, core, z, x = place()
    greet(neighbours() + [other_tp()])
    hidden = gate_ref.shape[1]
    wide = []
    for n, ref in enumerate((gate_ref, up_ref)):
        own_cols = wide_all.at[:, pl.ds(n * hidden, hidden)]
        far_cols = wide_all.at[:, pl.ds((2 + n) * hidden, hidden)]
        wide.append(pltpu.make_async_copy(ref, own_cols, keep_sem.at[n]))
        wide.append(swap_halves(ref, far_cols, give_sem.at[n], take_sem.at[n]))
    for copy in wide:
        copy.start()
    refs, own = (a_all, b_all), (a_ref, b_ref)
    started = []
    count = [0, 0]

    def chunk(n, i, j):
        return refs[n].at[j, core, i] if n == 0 else refs[n].at[i, core, j]

    def to(n, first, second):
        return device(second, core, first, x) if n == 0 else device(first, core, second, x)

    def send(n, ref, where, slot):
        copy = pltpu.make_async_remote_copy(
            src_ref=ref, dst_ref=ref, send_sem=send_sem.at[n, slot], recv_sem=recv_sem.at[n, slot],
            device_id=where, device_id_type=MESH,
        )
        copy.start()
        started.append(copy)

    def arrived(n, ref, slot):
        pltpu.make_async_remote_copy(
            src_ref=ref, dst_ref=ref, send_sem=send_sem.at[n, slot], recv_sem=recv_sem.at[n, slot],
            device_id=device(y, core, z, x), device_id_type=MESH,
        ).wait_recv()

    homes = []

    def across(n, i, j):
        slot = count[n]
        count[n] += 1
        ref = chunk(n, i, j)
        copy = pltpu.make_async_remote_copy(
            src_ref=ref, dst_ref=ref, send_sem=away_sem.at[n, slot], recv_sem=home_sem.at[n, slot],
            device_id=device(y, 1 - core, z, x), device_id_type=MESH,
        )
        copy.start()
        homes.append(copy)

    def second(n, i, j, k):
        base = 5 + 4 * k
        send(n, chunk(n, i, j), to(n, me[n][0], up(j)), base)
        send(n, chunk(n, i, j), to(n, me[n][0], down(j)), base + 1)
        across(n, i, j)

    up, down = (lambda v: lax.rem(v + 1, RING)), (lambda v: lax.rem(v + RING - 1, RING))
    me = ((z, y), (y, z))
    locals_ = []
    for n in (0, 1):
        i, j = me[n]
        keep = pltpu.make_async_copy(own[n], chunk(n, i, j).at[x], local_sem.at[n])
        keep.start()
        locals_.append(keep)
        copy = pltpu.make_async_remote_copy(
            src_ref=own[n], dst_ref=chunk(n, i, j).at[x], send_sem=send_sem.at[n, 0],
            recv_sem=recv_sem.at[n, 0], device_id=device(y, core, z, 1 - x), device_id_type=MESH,
        )
        copy.start()
        started.append(copy)
    for n in (0, 1):
        i, j = me[n]
        locals_[n].wait()
        arrived(n, chunk(n, i, j).at[1 - x], 0)
        send(n, chunk(n, i, j), to(n, up(i), j), 1)
        send(n, chunk(n, i, j), to(n, down(i), j), 2)
    for n in (0, 1):
        i, j = me[n]
        second(n, i, j, 0)
    for n in (0, 1):
        i, j = me[n]
        arrived(n, chunk(n, down(i), j), 1)
        send(n, chunk(n, down(i), j).at[0], to(n, up(i), j), 3)
        second(n, down(i), j, 1)
    for n in (0, 1):
        i, j = me[n]
        arrived(n, chunk(n, up(i), j), 2)
        send(n, chunk(n, up(i), j).at[1], to(n, down(i), j), 4)
        second(n, up(i), j, 2)
    for n in (0, 1):
        i, j = me[n]
        far = lax.rem(i + 2, RING)
        arrived(n, chunk(n, far, j).at[0], 3)
        arrived(n, chunk(n, far, j).at[1], 4)
        second(n, far, j, 3)
    for k in range(4):
        for n in (0, 1):
            i, j = me[n]
            it = (i, down(i), up(i), lax.rem(i + 2, RING))[k]
            base = 5 + 4 * k
            arrived(n, chunk(n, it, down(j)), base)
            send(n, chunk(n, it, down(j)).at[0], to(n, i, up(j)), base + 2)
            across(n, it, down(j))
            arrived(n, chunk(n, it, up(j)), base + 1)
            send(n, chunk(n, it, up(j)).at[1], to(n, i, down(j)), base + 3)
            across(n, it, up(j))
    for k in range(4):
        for n in (0, 1):
            i, j = me[n]
            it = (i, down(i), up(i), lax.rem(i + 2, RING))[k]
            base = 5 + 4 * k
            far = lax.rem(j + 2, RING)
            arrived(n, chunk(n, it, far).at[0], base + 2)
            arrived(n, chunk(n, it, far).at[1], base + 3)
            across(n, it, far)
    for copy in homes:
        copy.wait()
    for copy in started:
        copy.wait_send()
    for copy in wide:
        copy.wait()


def gather_weights(a, b, gate, up):
    rows = a.shape[0]
    shape = (RING, 2, RING, 2, rows)
    any_space = pl.BlockSpec(memory_space=pl.ANY)
    a_all, b_all, wide = pl.pallas_call(
        gather_kernel,
        in_specs=[any_space] * 4,
        out_specs=[any_space] * 3,
        out_shape=[jax.ShapeDtypeStruct(shape + (v.shape[1],), v.dtype) for v in (a, b)]
        + [jax.ShapeDtypeStruct((gate.shape[0], 4 * gate.shape[1]), gate.dtype)],
        scratch_shapes=[
            pltpu.SemaphoreType.DMA((2,)),
            pltpu.SemaphoreType.DMA((2, 21)),
            pltpu.SemaphoreType.DMA((2, 21)),
            pltpu.SemaphoreType.DMA((2, 16)),
            pltpu.SemaphoreType.DMA((2, 16)),
            pltpu.SemaphoreType.DMA((2,)),
            pltpu.SemaphoreType.DMA((2,)),
            pltpu.SemaphoreType.DMA((2,)),
        ],
        compiler_params=pltpu.CompilerParams(collective_id=0, has_side_effects=True),
        cost_estimate=pl.CostEstimate(flops=0, bytes_accessed=250_000_000, transcendentals=0),
        name="gather_weights",
    )(a, b, gate, up)
    return a_all.reshape(-1, a.shape[1]), b_all.reshape(-1, b.shape[1]), wide


ORDER = (2, 1, 3, 0)
SLICE = 16


def up(v):
    return lax.rem(v + 1, RING)


def down(v):
    return lax.rem(v + RING - 1, RING)


def add_into(target, *terms):
    flat = [target.shape[0]] if len(target.shape) == 3 else []
    for lead in range(flat[0]) if flat else (None,):
        for start in range(0, target.shape[-2], SLICE):
            at = (pl.ds(start, SLICE), slice(None))
            at = at if lead is None else (lead,) + at
            total = terms[0][at].astype(F32)
            for term in terms[1:]:
                total = total + term[at].astype(F32)
            target[at] = total.astype(target.dtype)


def scatter_kernel(
    a_ref, b_ref, extra_ref, wide_ref, a_out, b_out, wide_out, a_mine, b_mine, a_theirs, b_theirs, a_one, b_one, a_two, b_two,
    a_first, b_first, a_last, b_last, a_x, b_x, load_sem, send_sem, recv_sem,
    extra_load_sem, extra_send_sem, extra_recv_sem, give_sem, take_sem,
):
    y, core, z, x = place()
    greet(neighbours() + [other_tp()])
    wide = swap_halves(wide_ref, wide_out, give_sem, take_sem)
    wide.start()
    grads, outs = (a_ref, b_ref), (a_out, b_out)
    mine, theirs = (a_mine, b_mine), (a_theirs, b_theirs)
    one, two = (a_one, b_one), (a_two, b_two)
    first, last, side = (a_first, b_first), (a_last, b_last), (a_x, b_x)
    me = ((z, y), (y, z))
    sent = []

    def chunk(n, i, j, c):
        return grads[n].at[j, c, i] if n == 0 else grads[n].at[i, c, j]

    def to(n, i, j):
        return device(j, core, i, x) if n == 0 else device(i, core, j, x)

    def copy_of(n, src, dst, slot, where):
        return pltpu.make_async_remote_copy(
            src_ref=src, dst_ref=dst, send_sem=send_sem.at[n, slot], recv_sem=recv_sem.at[n, slot],
            device_id=where, device_id_type=MESH,
        )

    def send(n, src, dst, slot, where):
        copy = copy_of(n, src, dst, slot, where)
        copy.start()
        sent.append(copy)

    def arrived(n, dst, slot):
        copy_of(n, dst, dst, slot, device(y, core, z, x)).wait_recv()

    cols = b_ref.shape[-1]

    def columns(ref, start, count):
        return ref.at[:, :, pl.ds(start, count)]

    def extra_copy(slot):
        ref = columns(theirs[1].at[slot], cols, extra_ref.shape[-1])
        far = extra_ref.at[lax.rem(y + slot // RING, RING), 1 - core, lax.rem(z + slot % RING, RING)]
        return pltpu.make_async_remote_copy(
            src_ref=far, dst_ref=ref, send_sem=extra_send_sem.at[slot],
            recv_sem=extra_recv_sem.at[slot], device_id=device(y, 1 - core, z, x),
            device_id_type=MESH,
        )

    def extra_load(slot):
        near = extra_ref.at[lax.rem(y + slot // RING, RING), core, lax.rem(z + slot % RING, RING)]
        return pltpu.make_async_copy(
            near, columns(mine[1].at[slot], cols, extra_ref.shape[-1]), extra_load_sem.at[slot]
        )

    def load(n, di, dj):
        i, j = me[n]
        slot = di * RING + dj
        target = mine[n].at[slot] if n == 0 else columns(mine[n].at[slot], 0, cols)
        return pltpu.make_async_copy(
            chunk(n, lax.rem(i + di, RING), lax.rem(j + dj, RING), core), target,
            load_sem.at[n, slot],
        )

    for dj in ORDER:
        for di in ORDER:
            for n in (0, 1):
                i, j = me[n]
                slot = di * RING + dj
                there = chunk(n, lax.rem(i + di, RING), lax.rem(j + dj, RING), 1 - core)
                target = theirs[n].at[slot] if n == 0 else columns(theirs[n].at[slot], 0, cols)
                send(n, there, target, slot, device(y, 1 - core, z, x))
                load(n, di, dj).start()
                if n == 1:
                    extra_copy(slot).start()
                    extra_load(slot).start()

    def ready(n, di, dj):
        slot = di * RING + dj
        load(n, di, dj).wait()
        if n == 0:
            arrived(n, theirs[n].at[slot], slot)
        else:
            arrived(n, columns(theirs[n].at[slot], 0, cols), slot)
            extra_load(slot).wait()
            extra_copy(slot).wait_recv()
        return slot

    for di in ORDER:
        for n in (0, 1):
            i, j = me[n]
            slot = ready(n, di, 2)
            add_into(mine[n].at[slot], mine[n].at[slot], theirs[n].at[slot])
            for half in (0, 1):
                send(
                    n, mine[n].at[slot, half], one[n].at[di, half], 16 + di * 2 + half,
                    to(n, i, up(j) if half == 0 else down(j)),
                )
    for di in ORDER:
        for n in (0, 1):
            i, j = me[n]
            for half, dj in ((0, 1), (1, 3)):
                slot = ready(n, di, dj)
                arrived(n, one[n].at[di, half], 16 + di * 2 + half)
                add_into(
                    mine[n].at[slot, half], mine[n].at[slot, half], theirs[n].at[slot, half],
                    one[n].at[di, half],
                )
                add_into(
                    mine[n].at[slot, 1 - half], mine[n].at[slot, 1 - half],
                    theirs[n].at[slot, 1 - half],
                )
                send(
                    n, mine[n].at[slot], two[n].at[di, half], 24 + di * 2 + half,
                    to(n, i, up(j) if half == 0 else down(j)),
                )
    for di in ORDER:
        for n in (0, 1):
            i, j = me[n]
            slot = ready(n, di, 0)
            for half in (0, 1):
                arrived(n, two[n].at[di, half], 24 + di * 2 + half)
            add_into(
                mine[n].at[slot], mine[n].at[slot], theirs[n].at[slot], two[n].at[di, 0],
                two[n].at[di, 1],
            )
            if di == 2:
                for half in (0, 1):
                    send(
                        n, mine[n].at[slot, half], first[n].at[half], 32 + half,
                        to(n, up(i) if half == 0 else down(i), j),
                    )
            elif di != 0:
                half = 0 if di == 1 else 1
                arrived(n, first[n].at[half], 32 + half)
                add_into(mine[n].at[slot, half], mine[n].at[slot, half], first[n].at[half])
                send(
                    n, mine[n].at[slot], last[n].at[half], 34 + half,
                    to(n, up(i) if half == 0 else down(i), j),
                )
    for n in (0, 1):
        for half in (0, 1):
            arrived(n, last[n].at[half], 34 + half)
        add_into(mine[n].at[0], mine[n].at[0], last[n].at[0], last[n].at[1])
        send(n, mine[n].at[0, 1 - x], side[n], 36, device(y, core, z, 1 - x))
    for n in (0, 1):
        arrived(n, side[n], 36)
        add_into(outs[n], mine[n].at[0, x], side[n])
    for copy in sent:
        copy.wait_send()
    for slot in range(RING * RING):
        extra_copy(slot).wait_send()
    wide.wait()


def scatter_grads(a, b, extra, wide):
    peers = RING * RING * 4
    rows = a.shape[0] // peers
    shape = (RING, 2, RING, 2, rows)
    cols = (a.shape[1], b.shape[1] + extra.shape[1])
    buffers = []
    for lead in ((16, 2), (16, 2), (4, 2), (4, 2, 2), (2,), (2, 2), ()):
        buffers += [pltpu.VMEM(lead + (rows, c), a.dtype) for c in cols]
    any_space = pl.BlockSpec(memory_space=pl.ANY)
    return pl.pallas_call(
        scatter_kernel,
        in_specs=[any_space] * 4,
        out_specs=[pl.BlockSpec(memory_space=pltpu.VMEM)] * 2 + [any_space],
        out_shape=[jax.ShapeDtypeStruct((rows, c), F32) for c in cols]
        + [jax.ShapeDtypeStruct(wide.shape, wide.dtype)],
        scratch_shapes=buffers + [
            pltpu.SemaphoreType.DMA((2, 16)),
            pltpu.SemaphoreType.DMA((2, 37)),
            pltpu.SemaphoreType.DMA((2, 37)),
            pltpu.SemaphoreType.DMA((16,)),
            pltpu.SemaphoreType.DMA((16,)),
            pltpu.SemaphoreType.DMA((16,)),
            pltpu.SemaphoreType.DMA,
            pltpu.SemaphoreType.DMA,
        ],
        compiler_params=pltpu.CompilerParams(
            collective_id=1, has_side_effects=True, vmem_limit_bytes=44 * 1024 * 1024
        ),
        cost_estimate=pl.CostEstimate(flops=0, bytes_accessed=250_000_000, transcendentals=0),
        name="scatter_grads",
    )(*(v.reshape(shape + (v.shape[1],)) for v in (a, b, extra)), wide)


BLOCK = 64
CTX = 8


def dot(a, b, dims):
    return lax.dot_general(a, b, (dims, ((), ())), preferred_element_type=F32)


def rotated(u, gain, cosine, sine):
    scaling = lax.rsqrt(jnp.mean(u * u, axis=-1, keepdims=True) + EPS)
    normed = u * scaling
    n = normed * gain
    rot = n * cosine + pltpu.roll(n, HEAD_SIZE // 2, 1) * sine
    return rot.astype(BF16), normed, scaling


def rotated_back(e, normed, scaling, gain, cosine, sine):
    back = e * cosine + pltpu.roll(e * sine, HEAD_SIZE // 2, 1)
    scaled = back * gain
    inner = jnp.mean(scaled * normed, axis=-1, keepdims=True)
    return scaling * (scaled - normed * inner), jnp.sum(back * normed, axis=0, keepdims=True)


def ctx_peer(step):
    return {"ctx": lax.rem(lax.axis_index("ctx") + step, CTX)}


def beside():
    c = lax.axis_index("ctx")
    return {"ctx": c + 1 - 2 * lax.rem(c, 2)}


def remote(src, dst, send_sem, recv_sem, where):
    return pltpu.make_async_remote_copy(
        src_ref=src, dst_ref=dst, send_sem=send_sem, recv_sem=recv_sem, device_id=where,
        device_id_type=MESH,
    )


def softmax_parts(q_low, k, bias):
    s = dot(q_low, k, ((1,), (1,))) * (HEAD_SIZE ** -0.5) + bias
    e = jnp.exp(s - jnp.max(s, axis=-1, keepdims=True))
    return e / jnp.sum(e, axis=-1, keepdims=True)


def attention_kernel(
    kv, heads, qkv_ref, cos_ref, sin_ref, gq_ref, gk_ref, bias_ref, down_ref, o_ref, kv_ref, tall_ref,
    held, send_sem, recv_sem, keep_sem, give_sem, take_sem,
):
    c = lax.axis_index("ctx")
    greet([ctx_peer(step) for step in range(1, CTX)] + [other_tp()])
    half = down_ref.shape[0]
    keep = pltpu.make_async_copy(down_ref, tall_ref.at[pl.ds(0, half)], keep_sem)
    tall = swap_halves(down_ref, tall_ref.at[pl.ds(half, half)], give_sem, take_sem)
    micro, rows = held.shape[0], 2 * BLOCK
    q_cols = kv * heads * HEAD_SIZE
    cosine, sine, gq, gk = cos_ref[...], sin_ref[...], gq_ref[...], gk_ref[...]
    mine = pl.ds(pl.multiple_of(c * BLOCK, BLOCK), BLOCK)
    earlier, own = pl.ds(CTX * BLOCK, BLOCK), pl.ds((CTX + 1) * BLOCK, BLOCK)
    copies = []
    for m in range(micro):
        span = slice(m * rows, (m + 1) * rows)
        for h in range(2 * kv):
            cols = slice(h * HEAD_SIZE, (h + 1) * HEAD_SIZE)
            u = qkv_ref[span, q_cols + h * HEAD_SIZE : q_cols + (h + 1) * HEAD_SIZE]
            low = rotated(u, gk, cosine, sine)[0] if h < kv else u.astype(BF16)
            held[m, mine, cols] = low[:BLOCK]
            held[m, own, cols] = low[BLOCK:]
        for step in range(1, CTX):
            part = held.at[m, mine]
            copies.append(
                remote(part, part, send_sem.at[step, m], recv_sem.at[step, m], ctx_peer(step))
            )
        copies.append(
            remote(
                held.at[m, own], held.at[m, earlier], send_sem.at[0, m], recv_sem.at[0, m], beside()
            )
        )
        for copy in copies[-CTX:]:
            copy.start()
    keep.start()
    tall.start()

    def group(m, h, carry):
        span = slice(m * rows, (m + 1) * rows)
        k = held[m, :, pl.ds(pl.multiple_of(h * HEAD_SIZE, HEAD_SIZE), HEAD_SIZE)]
        v = held[m, :, pl.ds(pl.multiple_of((kv + h) * HEAD_SIZE, HEAD_SIZE), HEAD_SIZE)]
        for e in range(heads):
            cols = pl.ds(pl.multiple_of((h * heads + e) * HEAD_SIZE, HEAD_SIZE), HEAD_SIZE)
            q_low = rotated(qkv_ref[span, cols], gq, cosine, sine)[0]
            p = softmax_parts(q_low, k, bias_ref[...]).astype(BF16)
            o_ref[span, cols] = dot(p, v, ((1,), (0,))).astype(BF16)
        return carry

    for m in range(micro):
        for step in range(1, CTX):
            source = lax.rem(c + CTX - step, CTX)
            part = held.at[m, pl.ds(pl.multiple_of(source * BLOCK, BLOCK), BLOCK)]
            remote(
                part, part, send_sem.at[step, m], recv_sem.at[step, m], ctx_peer(step)
            ).wait_recv()
        copies[(m + 1) * CTX - 1].wait_recv()
        lax.fori_loop(0, kv, functools.partial(group, m), 0)
    kv_ref[...] = held[...]
    for copy in copies:
        copy.wait_send()
    keep.wait()
    tall.wait()


def attention_back_kernel(
    kv, heads, qkv_ref, cos_ref, sin_ref, gq_ref, gk_ref, bias_ref, kv_ref, do_ref, tall_ref,
    dqkv_ref, gains_ref, tall_out, grads, given, given_side, p_all, ds_all, q_all, do_all,
    send_sem, recv_sem, give_sem, take_sem,
):
    c = lax.axis_index("ctx")
    greet([ctx_peer(step) for step in range(1, CTX)] + [other_tp()])
    tall = swap_halves(tall_ref, tall_out, give_sem, take_sem)
    tall.start()
    micro, rows = grads.shape[0], 2 * BLOCK
    q_cols = kv * heads * HEAD_SIZE
    scale = HEAD_SIZE ** -0.5
    cosine, sine, gq, gk = cos_ref[...], sin_ref[...], gq_ref[...], gk_ref[...]
    mine = pl.ds(pl.multiple_of(c * BLOCK, BLOCK), BLOCK)
    earlier, own = pl.ds(CTX * BLOCK, BLOCK), pl.ds((CTX + 1) * BLOCK, BLOCK)

    def group(m, h, total):
        span = slice(m * rows, (m + 1) * rows)
        k_cols = pl.ds(pl.multiple_of(h * HEAD_SIZE, HEAD_SIZE), HEAD_SIZE)
        v_cols = pl.ds(pl.multiple_of((kv + h) * HEAD_SIZE, HEAD_SIZE), HEAD_SIZE)
        k, v = kv_ref[m, :, k_cols], kv_ref[m, :, v_cols]
        for e in range(heads):
            cols = pl.ds(pl.multiple_of((h * heads + e) * HEAD_SIZE, HEAD_SIZE), HEAD_SIZE)
            stack = slice(e * rows, (e + 1) * rows)
            q_low, normed, scaling = rotated(qkv_ref[span, cols], gq, cosine, sine)
            q_all[stack, :] = q_low
            p = softmax_parts(q_low, k, bias_ref[...])
            p_all[stack, :] = p.astype(BF16)
            do = do_ref[span, cols]
            do_all[stack, :] = do
            dp = dot(do, v, ((1,), (1,)))
            ds = (p * (dp - jnp.sum(dp * p, axis=-1, keepdims=True))).astype(BF16)
            ds_all[stack, :] = ds
            dqr = (dot(ds, k, ((1,), (0,))) * scale).astype(BF16).astype(F32)
            dq, part = rotated_back(dqr, normed, scaling, gq, cosine, sine)
            dqkv_ref[span, cols] = dq.astype(BF16)
            total = total + part
        grads[m, :, v_cols] = dot(p_all[...], do_all[...], ((0,), (0,))).astype(BF16)
        grads[m, :, k_cols] = (dot(ds_all[...], q_all[...], ((0,), (0,))) * scale).astype(BF16)
        return total

    total = jnp.zeros((1, HEAD_SIZE), F32)
    copies = []
    for m in range(micro):
        total = lax.fori_loop(0, kv, functools.partial(group, m), total)
        for step in range(1, CTX):
            peer = lax.rem(c + step, CTX)
            part = grads.at[m, pl.ds(pl.multiple_of(peer * BLOCK, BLOCK), BLOCK)]
            copies.append(
                remote(
                    part, given.at[step - 1, m], send_sem.at[step, m], recv_sem.at[step, m],
                    ctx_peer(step),
                )
            )
        copies.append(
            remote(
                grads.at[m, earlier], given_side.at[m], send_sem.at[0, m], recv_sem.at[0, m],
                beside(),
            )
        )
        for copy in copies[-CTX:]:
            copy.start()
    k_total = jnp.zeros((1, HEAD_SIZE), F32)
    for m in range(micro):
        for copy in copies[m * CTX : (m + 1) * CTX]:
            copy.wait_recv()
        for h in range(2 * kv):
            cols = slice(h * HEAD_SIZE, (h + 1) * HEAD_SIZE)
            at = slice(q_cols + h * HEAD_SIZE, q_cols + (h + 1) * HEAD_SIZE)
            prompt = grads[m, mine, cols].astype(F32)
            for step in range(CTX - 1):
                prompt = prompt + given[step, m, :, cols].astype(F32)
            cont = grads[m, own, cols].astype(F32) + given_side[m, :, cols].astype(F32)
            e = jnp.concatenate([prompt, cont], axis=0).astype(BF16)
            span = slice(m * rows, (m + 1) * rows)
            if h < kv:
                _, normed, scaling = rotated(qkv_ref[span, at], gk, cosine, sine)
                d, part = rotated_back(e.astype(F32), normed, scaling, gk, cosine, sine)
                k_total = k_total + part
                dqkv_ref[span, at] = d.astype(BF16)
            else:
                dqkv_ref[span, at] = e
    gains_ref[0:1, :] = total
    gains_ref[1:2, :] = k_total
    for copy in copies:
        copy.wait_send()
    tall.wait()


def attention(qkv, cosine, sine, gain_query, gain_key, bias, down, kv, micro):
    heads = qkv.shape[1] // HEAD_SIZE // kv - 2
    rows, keys = bias.shape
    vmem, any_space = (pl.BlockSpec(memory_space=space) for space in (pltpu.VMEM, pl.ANY))
    return pl.pallas_call(
        functools.partial(attention_kernel, kv, heads),
        in_specs=[vmem] * 6 + [any_space],
        out_specs=[vmem] * 2 + [any_space],
        out_shape=[
            jax.ShapeDtypeStruct((qkv.shape[0], kv * heads * HEAD_SIZE), BF16),
            jax.ShapeDtypeStruct((micro, keys, 2 * kv * HEAD_SIZE), BF16),
            jax.ShapeDtypeStruct((2 * down.shape[0], down.shape[1]), BF16),
        ],
        scratch_shapes=[
            pltpu.VMEM((micro, keys, 2 * kv * HEAD_SIZE), BF16),
            pltpu.SemaphoreType.DMA((CTX, micro)),
            pltpu.SemaphoreType.DMA((CTX, micro)),
            pltpu.SemaphoreType.DMA,
            pltpu.SemaphoreType.DMA,
            pltpu.SemaphoreType.DMA,
        ],
        compiler_params=pltpu.CompilerParams(
            collective_id=2, has_side_effects=True, vmem_limit_bytes=VMEM_LIMIT
        ),
        cost_estimate=pl.CostEstimate(flops=0, bytes_accessed=120_000_000, transcendentals=0),
        name="attention_forward",
    )(qkv, cosine, sine, gain_query, gain_key, bias, down)


def attention_back(qkv, cosine, sine, gain_query, gain_key, bias, kv_all, d_out, tall, kv):
    heads = qkv.shape[1] // HEAD_SIZE // kv - 2
    rows, keys = bias.shape
    micro, _, kv_cols = kv_all.shape
    vmem, any_space = (pl.BlockSpec(memory_space=space) for space in (pltpu.VMEM, pl.ANY))
    return pl.pallas_call(
        functools.partial(attention_back_kernel, kv, heads),
        in_specs=[vmem] * 8 + [any_space],
        out_specs=[vmem] * 2 + [any_space],
        out_shape=[
            jax.ShapeDtypeStruct(qkv.shape, BF16),
            jax.ShapeDtypeStruct((2, HEAD_SIZE), F32),
            jax.ShapeDtypeStruct(tall.shape, tall.dtype),
        ],
        scratch_shapes=[
            pltpu.VMEM((micro, keys, kv_cols), BF16),
            pltpu.VMEM((CTX - 1, micro, BLOCK, kv_cols), BF16),
            pltpu.VMEM((micro, BLOCK, kv_cols), BF16),
            pltpu.VMEM((heads * rows, keys), BF16),
            pltpu.VMEM((heads * rows, keys), BF16),
            pltpu.VMEM((heads * rows, HEAD_SIZE), BF16),
            pltpu.VMEM((heads * rows, HEAD_SIZE), BF16),
            pltpu.SemaphoreType.DMA((CTX, micro)),
            pltpu.SemaphoreType.DMA((CTX, micro)),
            pltpu.SemaphoreType.DMA,
            pltpu.SemaphoreType.DMA,
        ],
        compiler_params=pltpu.CompilerParams(
            collective_id=3, has_side_effects=True, vmem_limit_bytes=VMEM_LIMIT
        ),
        cost_estimate=pl.CostEstimate(flops=0, bytes_accessed=120_000_000, transcendentals=0),
        name="attention_backward",
    )(qkv, cosine, sine, gain_query, gain_key, bias, kv_all, d_out, tall)


def normalize(rows, gain):
    scaling = lax.rsqrt(jnp.mean(rows * rows, axis=-1, keepdims=True) + EPS)
    return rows * scaling * gain, scaling


def normalize_back(rows, scaling, gain, upstream):
    normed = rows * scaling
    gain_grad = jnp.sum((upstream * normed).reshape(-1, rows.shape[-1]), axis=0)
    scaled = upstream * gain
    inner = jnp.mean(scaled * normed, axis=-1, keepdims=True)
    return scaling * (scaled - normed * inner), gain_grad


def swap_tp(value):
    return lax.ppermute(value, "tp", [(0, 1), (1, 0)])


def local(
    x_prompt, x_cont, cot_prompt, cot_cont, ids_prompt, ids_cont, gates_prompt, gates_cont,
    norm_gain, query_weight, key_matrix, value_matrix, out_weight, query_gain, key_gain, moe_gain,
    expert_gate, expert_up, expert_down,
):
    micro = x_prompt.shape[0]
    prompt_rows, cont_rows, width = x_prompt.shape[2], x_cont.shape[2], x_prompt.shape[3]
    block = cont_rows
    rows = 2 * block
    s = lax.axis_index("ctx")
    ctx = lax.axis_size("ctx")
    first = lax.axis_index("tp") == 0
    peers = lax.axis_size(ALL)
    q_cols, kv_cols = query_weight.shape[1], key_matrix.shape[1]
    kv = kv_cols // HEAD_SIZE
    qkv_cols = q_cols + 2 * kv_cols
    shard_rows = query_weight.shape[0]
    hidden = expert_gate.shape[2]
    slots = cont_rows * TOPK // peers

    def exchange(rows_of):
        return lax.all_to_all(rows_of, ALL, split_axis=0, concat_axis=0, tiled=True)

    def pad(v):
        return jnp.pad(v[:, 0], ((0, 0), (0, block - prompt_rows), (0, 0)))

    x_first, x_second = pad(x_prompt), x_cont[:, 0]
    own_tokens = jnp.where(first, x_second, x_first).astype(F32)
    own_cot = jnp.where(first, cot_cont[:, 0], pad(cot_prompt)).astype(F32)
    ids_pad = jnp.pad(
        ids_prompt[:, 0], ((0, 0), (0, block - prompt_rows), (0, 0)), constant_values=-1
    )
    own_ids = jnp.where(first, ids_cont[:, 0], ids_pad)
    own_gates = jnp.where(first, gates_cont[:, 0], pad(gates_prompt))

    named = own_ids[:, :, :, None] == jnp.arange(peers, dtype=jnp.int32)
    chosen = jnp.any(named, axis=2)
    weight = jnp.sum(jnp.where(named, own_gates[:, :, :, None], 0.0), axis=2)
    lower = jnp.tril(jnp.ones((block, block), BF16), -1)
    rank = jnp.einsum("ts,mse->mte", lower, chosen.astype(BF16), preferred_element_type=F32)
    place = jnp.where(chosen, rank, -1.0)
    placed = place[:, :, :, None] == jnp.arange(slots, dtype=F32)
    flat = (micro, block, peers * slots)
    select = placed.astype(BF16).reshape(flat)
    mixing = jnp.where(placed, weight[:, :, :, None], 0.0).reshape(flat)
    mixing_high = mixing.astype(BF16)
    mixing_low = (mixing - mixing_high.astype(F32)).astype(BF16)
    slot_gate = jnp.sum(mixing, axis=1)

    extra = jnp.concatenate(
        [
            norm_gain[:, None],
            moe_gain[:, None],
            jnp.pad(query_gain, (0, shard_rows - query_gain.shape[0]))[:, None],
            jnp.pad(key_gain, (0, shard_rows - key_gain.shape[0]))[:, None],
            jnp.zeros((shard_rows, 124), BF16),
        ],
        axis=1,
    )
    w_qkv, w_out_extra, gu_all = gather_weights(
        jnp.concatenate([query_weight, key_matrix, value_matrix], axis=1),
        jnp.concatenate([out_weight, extra], axis=1),
        expert_gate[0],
        expert_up[0],
    )
    w_out = w_out_extra[:, :q_cols]
    gains = w_out_extra[:, q_cols:].astype(F32)
    gain_in, gain_moe = gains[:, 0], gains[:, 1]
    head_gains = gains[:, 2:4].reshape(peers, shard_rows, 2)[:, : query_gain.shape[0]]
    head_gains = head_gains.reshape(HEAD_SIZE, 2)
    gain_query, gain_key = head_gains[:, 0], head_gains[:, 1]

    cot_low, w_qkv = lax.optimization_barrier((own_cot.astype(BF16), w_qkv))
    spread = [
        (dot(select[m], cot_low[m], ((0,), (0,))) * slot_gate[m][:, None]).astype(BF16)
        for m in range(micro)
    ]
    d_eo_rows = exchange(jnp.stack(spread).reshape(micro, peers, slots, width).swapaxes(0, 1))

    offsets = jnp.arange(rows, dtype=jnp.int32)
    is_prompt = offsets < block
    prompt_pos = s * prompt_rows + offsets
    cont_pos = s * cont_rows + offsets - block
    rot_place = jnp.where(is_prompt, prompt_pos, PROMPT + cont_pos % CL).astype(F32)
    steps_freq = jnp.arange(HEAD_SIZE // 2, dtype=F32) * (2.0 / HEAD_SIZE)
    angles = rot_place[:, None] * jnp.power(THETA, -steps_freq)[None, :]
    cosine, sine = jnp.cos(angles), jnp.sin(angles)
    cosine = jnp.concatenate([cosine, cosine], axis=1)
    sine = jnp.concatenate([-sine, sine], axis=1)
    keys = (ctx + 2) * block
    key_index = jnp.arange(keys, dtype=jnp.int32)[None, :]
    key_off = key_index % block
    key_prompt_pos = key_index // block * prompt_rows + key_off
    key_cont = (s - 1) * cont_rows + key_index - ctx * block
    is_cont = jnp.logical_not(is_prompt)[:, None]
    visible = jnp.where(
        key_index < ctx * block,
        jnp.logical_and(
            key_off < prompt_rows,
            jnp.logical_or(is_cont, key_prompt_pos <= prompt_pos[:, None]),
        ),
        jnp.logical_and(
            is_cont,
            jnp.logical_and(
                key_cont // CL == cont_pos[:, None] // CL, key_cont <= cont_pos[:, None]
            ),
        ),
    )
    bias = jnp.where(visible, 0.0, NEG).astype(F32)

    def share_rows(own):
        other = swap_tp(own)
        return jnp.where(first, other, own), jnp.where(first, own, other)

    def sum_own(part):
        part = part.reshape(micro, rows, width)
        given = jnp.where(first, part[:, :block], part[:, block:]).astype(BF16)
        kept = jnp.where(first, part[:, block:], part[:, :block])
        return kept + swap_tp(given).astype(F32)

    tokens = jnp.concatenate([x_first, x_second], axis=1).astype(F32).reshape(-1, width)
    a = normalize(tokens, gain_in)[0].astype(BF16)
    qkv = dot(a, w_qkv, ((1,), (0,)))
    heads_in = (cosine, sine, gain_query[None], gain_key[None], bias)
    o, kv_all, down_all = attention(qkv, *heads_in, expert_down[0], kv, micro)
    middle = own_tokens + sum_own(dot(o, w_out, ((1,), (1,))))
    b_normed, b_scale = normalize(middle, gain_moe)
    b_low = b_normed.astype(BF16)

    got_rows, z_rows, d_gu_rows, backs = [], [], [], []
    for m in range(micro):
        got = exchange(dot(select[m], b_low[m], ((0,), (0,))).astype(BF16))
        d_eo = d_eo_rows[:, m].reshape(-1, width)
        pre = dot(got, gu_all, ((1,), (0,)))
        d_z = dot(d_eo, down_all, ((1,), (1,)))
        acts, d_gu = [], []
        for part in range(2):
            at = 2 * part * hidden
            g, u = pre[:, at : at + hidden], pre[:, at + hidden : at + 2 * hidden]
            dz = d_z[:, part * hidden : (part + 1) * hidden]
            sig = jax.nn.sigmoid(g)
            act = g * sig
            acts.append((act * u).astype(BF16))
            d_gu.append((dz * u * sig * (1.0 + g * (1.0 - sig))).astype(BF16))
            d_gu.append((dz * act).astype(BF16))
        d_gu = jnp.concatenate(d_gu, axis=1)
        backs.append(exchange(dot(d_gu, gu_all, ((1,), (1,))).astype(BF16)))
        got_rows.append(got)
        z_rows.append(jnp.concatenate(acts, axis=1))
        d_gu_rows.append(d_gu)

    rows_all = jnp.concatenate(got_rows, axis=0)
    d_eo_all = d_eo_rows.swapaxes(0, 1).reshape(-1, width)
    z_all = jnp.concatenate(z_rows, axis=0)
    d_gu_all = jnp.concatenate(d_gu_rows, axis=0)
    wide_other = dot(rows_all, d_gu_all[:, 2 * hidden :], ((0,), (0,))).astype(BF16)
    tall_other = dot(z_all[:, hidden:], d_eo_all, ((0,), (0,))).astype(BF16)
    grad_down = dot(z_all[:, :hidden], d_eo_all, ((0,), (0,)))

    d_b = jnp.stack([dot(select[m], backs[m], ((1,), (0,))) for m in range(micro)])
    middle_from, moe_total = normalize_back(middle, b_scale, gain_moe, d_b)
    d_h = own_cot + middle_from
    d_attn = jnp.concatenate(share_rows(d_h.astype(BF16)), axis=1).reshape(-1, width)

    z_late, d_attn = lax.optimization_barrier((z_all, d_attn))
    eo = dot(z_late, down_all, ((1,), (0,))).astype(BF16)
    eo_back = exchange(eo.reshape(micro, peers, slots, width).swapaxes(0, 1))
    moe_out = []
    for m in range(micro):
        term = eo_back[:, m].reshape(-1, width)
        moe_out.append(
            dot(mixing_high[m], term, ((1,), (0,))) + dot(mixing_low[m], term, ((1,), (0,)))
        )
    out_first, out_second = share_rows((middle + jnp.stack(moe_out)).astype(BF16))

    d_o = dot(d_attn, w_out, ((1,), (0,))).astype(BF16)
    grad_out = dot(d_attn, o, ((0,), (0,))).astype(BF16)
    d_qkv, head_totals, tall_there = attention_back(qkv, *heads_in, kv_all, d_o, tall_other, kv)
    input_grad = sum_own(dot(d_qkv, w_qkv, ((1,), (1,))))
    grad_qkv = dot(a, d_qkv, ((0,), (0,))).astype(BF16)
    scale_in = lax.rsqrt(jnp.mean(own_tokens * own_tokens, axis=-1, keepdims=True) + EPS)
    token_from, norm_total = normalize_back(own_tokens, scale_in, gain_in, input_grad)
    grad_first, grad_second = share_rows((d_h + token_from).astype(BF16))

    head_grads = head_totals.T.reshape(peers, -1, 2)
    head_grads = jnp.pad(head_grads, ((0, 0), (0, shard_rows - head_grads.shape[1]), (0, 0)))
    extra_grads = jnp.concatenate(
        [
            norm_total[:, None],
            moe_total[:, None],
            head_grads.reshape(-1, 2),
            jnp.zeros((peers * shard_rows, 124), F32),
        ],
        axis=1,
    ).astype(BF16)
    share, share_out, wide_there = scatter_grads(grad_qkv, grad_out, extra_grads, wide_other)
    late = lax.optimization_barrier((rows_all, d_gu_all, wide_there))
    grad_wide = [
        dot(late[0], late[1][:, n * hidden : (n + 1) * hidden], ((0,), (0,)))
        + late[2][:, n * hidden : (n + 1) * hidden].astype(F32)
        for n in range(2)
    ]
    gain_share = share_out[:, q_cols:]
    gain_share = gain_share + swap_tp(gain_share)
    head_rows = query_gain.shape[0]

    return (
        out_first[:, None, :prompt_rows],
        out_second[:, None],
        grad_first[:, None, :prompt_rows],
        grad_second[:, None],
        gain_share[:, 0],
        share[:, :q_cols],
        share[:, q_cols : q_cols + kv_cols],
        share[:, q_cols + kv_cols : qkv_cols],
        share_out[:, :q_cols],
        gain_share[:head_rows, 2],
        gain_share[:head_rows, 3],
        gain_share[:, 1],
        grad_wide[0][None],
        grad_wide[1][None],
        (grad_down + tall_there.astype(F32))[None],
    )


def solution(mesh):
    rows = P(None, "fsdp", "ctx", None)
    vector = P(("fsdp", "ctx"))
    matrix = P(("fsdp", "ctx"), "tp")
    wide = P(("fsdp", "ctx"), None, "tp")
    tall = P(("fsdp", "ctx"), "tp", None)
    in_specs = (rows,) * 8 + (vector,) + (matrix,) * 4 + (vector,) * 3 + (wide, wide, tall)
    out_specs = (rows,) * 4 + (vector,) + (matrix,) * 4 + (vector,) * 3 + (wide, wide, tall)
    return jax.shard_map(local, mesh=mesh, in_specs=in_specs, out_specs=out_specs, check_vma=False)
```

```python
import functools

import jax
import jax.numpy as jnp
from jax import lax
from jax.experimental import pallas as pl
from jax.experimental.pallas import tpu as pltpu
from jax.sharding import PartitionSpec as P

HEAD_SIZE = 128
TOPK = 8
PROMPT = 448
CL = 128
EPS = 1e-06
THETA = 1000000.0
NEG = -1e30
F32 = jnp.float32
BF16 = jnp.bfloat16
ALL = ("fsdp", "ctx")
MESH = pl.DeviceIdType.MESH
RING = 4
VMEM_LIMIT = 48 * 1024 * 1024


def place():
    f, c = lax.axis_index("fsdp"), lax.axis_index("ctx")
    return f // 2, f % 2, c // 2, c % 2


def device(y, core, z, x):
    return {"fsdp": y * 2 + core, "ctx": z * 2 + x}


def greet(partners):
    barrier = pltpu.get_barrier_semaphore()
    for partner in partners:
        pl.semaphore_signal(barrier, inc=1, device_id=partner, device_id_type=MESH)
    pl.semaphore_wait(barrier, len(partners))


def neighbours():
    y, core, z, x = place()
    up, down = (lambda v: lax.rem(v + 1, RING)), (lambda v: lax.rem(v + RING - 1, RING))
    return [
        device(y, core, z, 1 - x),
        device(y, 1 - core, z, x),
        device(up(y), core, z, x),
        device(down(y), core, z, x),
        device(y, core, up(z), x),
        device(y, core, down(z), x),
    ]


def other_tp():
    return {"tp": 1 - lax.axis_index("tp")}


def opposite():
    f = lax.axis_index("fsdp")
    return {"fsdp": f + 1 - 2 * (f % 2), "tp": 1 - lax.axis_index("tp")}


def native():
    return lax.axis_index("fsdp") % 2 == lax.axis_index("tp")


def swap_opposite(src, dst, send_sem, recv_sem):
    return pltpu.make_async_remote_copy(
        src_ref=src, dst_ref=dst, send_sem=send_sem, recv_sem=recv_sem, device_id=opposite(),
        device_id_type=MESH,
    )


def gather_kernel(
    a_ref, b_ref, gate_ref, up_ref, down_ref, a_all, b_all, wide_all, tall_all,
    local_sem, send_sem, recv_sem, away_sem, home_sem, keep_sem, give_sem, take_sem,
):
    y, core, z, x = place()
    greet(neighbours() + [opposite()])
    hidden = gate_ref.shape[1]
    shards = (
        (gate_ref, wide_all.at[:, pl.ds(0, hidden)]),
        (up_ref, wide_all.at[:, pl.ds(hidden, hidden)]),
        (down_ref, tall_all),
    )
    kept = [pltpu.make_async_copy(p, q, keep_sem.at[n]) for n, (p, q) in enumerate(shards)]
    moved = [
        swap_opposite(p, q, give_sem.at[n], take_sem.at[n]) for n, (p, q) in enumerate(shards)
    ]
    refs, own = (a_all, b_all), (a_ref, b_ref)
    started = []
    count = [0, 0]

    def chunk(n, i, j):
        return refs[n].at[j, core, i] if n == 0 else refs[n].at[i, core, j]

    def to(n, first, second):
        return device(second, core, first, x) if n == 0 else device(first, core, second, x)

    def send(n, ref, where, slot):
        copy = pltpu.make_async_remote_copy(
            src_ref=ref, dst_ref=ref, send_sem=send_sem.at[n, slot], recv_sem=recv_sem.at[n, slot],
            device_id=where, device_id_type=MESH,
        )
        copy.start()
        started.append(copy)

    def arrived(n, ref, slot):
        pltpu.make_async_remote_copy(
            src_ref=ref, dst_ref=ref, send_sem=send_sem.at[n, slot], recv_sem=recv_sem.at[n, slot],
            device_id=device(y, core, z, x), device_id_type=MESH,
        ).wait_recv()

    homes = []

    def across(n, i, j):
        slot = count[n]
        count[n] += 1
        ref = chunk(n, i, j)
        copy = pltpu.make_async_remote_copy(
            src_ref=ref, dst_ref=ref, send_sem=away_sem.at[n, slot], recv_sem=home_sem.at[n, slot],
            device_id=device(y, 1 - core, z, x), device_id_type=MESH,
        )
        copy.start()
        homes.append(copy)

    def second(n, i, j, k):
        base = 5 + 4 * k
        send(n, chunk(n, i, j), to(n, me[n][0], up(j)), base)
        send(n, chunk(n, i, j), to(n, me[n][0], down(j)), base + 1)
        across(n, i, j)

    up, down = (lambda v: lax.rem(v + 1, RING)), (lambda v: lax.rem(v + RING - 1, RING))
    me = ((z, y), (y, z))
    locals_ = []
    for n in (0, 1):
        i, j = me[n]
        keep = pltpu.make_async_copy(own[n], chunk(n, i, j).at[x], local_sem.at[n])
        keep.start()
        locals_.append(keep)
        copy = pltpu.make_async_remote_copy(
            src_ref=own[n], dst_ref=chunk(n, i, j).at[x], send_sem=send_sem.at[n, 0],
            recv_sem=recv_sem.at[n, 0], device_id=device(y, core, z, 1 - x), device_id_type=MESH,
        )
        copy.start()
        started.append(copy)
    for n in (0, 1):
        i, j = me[n]
        locals_[n].wait()
        arrived(n, chunk(n, i, j).at[1 - x], 0)
        send(n, chunk(n, i, j), to(n, up(i), j), 1)
        send(n, chunk(n, i, j), to(n, down(i), j), 2)
    for n in (0, 1):
        i, j = me[n]
        second(n, i, j, 0)

    @pl.when(native())
    def _():
        for copy in kept:
            copy.start()

    @pl.when(jnp.logical_not(native()))
    def _():
        for copy in moved:
            copy.start()

    for n in (0, 1):
        i, j = me[n]
        arrived(n, chunk(n, down(i), j), 1)
        send(n, chunk(n, down(i), j).at[0], to(n, up(i), j), 3)
        second(n, down(i), j, 1)
    for n in (0, 1):
        i, j = me[n]
        arrived(n, chunk(n, up(i), j), 2)
        send(n, chunk(n, up(i), j).at[1], to(n, down(i), j), 4)
        second(n, up(i), j, 2)
    for n in (0, 1):
        i, j = me[n]
        far = lax.rem(i + 2, RING)
        arrived(n, chunk(n, far, j).at[0], 3)
        arrived(n, chunk(n, far, j).at[1], 4)
        second(n, far, j, 3)
    for k in range(4):
        for n in (0, 1):
            i, j = me[n]
            it = (i, down(i), up(i), lax.rem(i + 2, RING))[k]
            base = 5 + 4 * k
            arrived(n, chunk(n, it, down(j)), base)
            send(n, chunk(n, it, down(j)).at[0], to(n, i, up(j)), base + 2)
            across(n, it, down(j))
            arrived(n, chunk(n, it, up(j)), base + 1)
            send(n, chunk(n, it, up(j)).at[1], to(n, i, down(j)), base + 3)
            across(n, it, up(j))
    for k in range(4):
        for n in (0, 1):
            i, j = me[n]
            it = (i, down(i), up(i), lax.rem(i + 2, RING))[k]
            base = 5 + 4 * k
            far = lax.rem(j + 2, RING)
            arrived(n, chunk(n, it, far).at[0], base + 2)
            arrived(n, chunk(n, it, far).at[1], base + 3)
            across(n, it, far)
    for copy in homes:
        copy.wait()
    for copy in started:
        copy.wait_send()

    @pl.when(native())
    def _():
        for copy in kept:
            copy.wait()

    @pl.when(jnp.logical_not(native()))
    def _():
        for copy in moved:
            copy.wait()


def gather_weights(a, b, gate, up, down):
    rows = a.shape[0]
    shape = (RING, 2, RING, 2, rows)
    any_space = pl.BlockSpec(memory_space=pl.ANY)
    a_all, b_all, wide, tall = pl.pallas_call(
        gather_kernel,
        in_specs=[any_space] * 5,
        out_specs=[any_space] * 4,
        out_shape=[jax.ShapeDtypeStruct(shape + (v.shape[1],), v.dtype) for v in (a, b)]
        + [
            jax.ShapeDtypeStruct((gate.shape[0], 2 * gate.shape[1]), gate.dtype),
            jax.ShapeDtypeStruct(down.shape, down.dtype),
        ],
        scratch_shapes=[
            pltpu.SemaphoreType.DMA((2,)),
            pltpu.SemaphoreType.DMA((2, 21)),
            pltpu.SemaphoreType.DMA((2, 21)),
            pltpu.SemaphoreType.DMA((2, 16)),
            pltpu.SemaphoreType.DMA((2, 16)),
            pltpu.SemaphoreType.DMA((3,)),
            pltpu.SemaphoreType.DMA((3,)),
            pltpu.SemaphoreType.DMA((3,)),
        ],
        compiler_params=pltpu.CompilerParams(collective_id=0, has_side_effects=True),
        cost_estimate=pl.CostEstimate(flops=0, bytes_accessed=250_000_000, transcendentals=0),
        name="gather_weights",
    )(a, b, gate, up, down)
    return a_all.reshape(-1, a.shape[1]), b_all.reshape(-1, b.shape[1]), wide, tall


ORDER = (2, 1, 3, 0)
SLICE = 16


def up(v):
    return lax.rem(v + 1, RING)


def down(v):
    return lax.rem(v + RING - 1, RING)


def add_into(target, *terms):
    flat = [target.shape[0]] if len(target.shape) == 3 else []
    for lead in range(flat[0]) if flat else (None,):
        for start in range(0, target.shape[-2], SLICE):
            at = (pl.ds(start, SLICE), slice(None))
            at = at if lead is None else (lead,) + at
            total = terms[0][at].astype(F32)
            for term in terms[1:]:
                total = total + term[at].astype(F32)
            target[at] = total.astype(target.dtype)


def scatter_kernel(
    a_ref, b_ref, extra_ref, wide_ref, tall_ref, a_out, b_out, wide_out, tall_out, a_mine, b_mine, a_theirs, b_theirs, a_one, b_one, a_two, b_two,
    a_first, b_first, a_last, b_last, a_x, b_x, load_sem, send_sem, recv_sem,
    gains_here, gains_there,
    extra_load_sem, extra_send_sem, extra_recv_sem, give_sem, take_sem, gains_sem,
):
    y, core, z, x = place()
    greet(neighbours() + [other_tp(), opposite()])
    moved = [
        swap_opposite(wide_ref, wide_out, give_sem.at[0], take_sem.at[0]),
        swap_opposite(tall_ref, tall_out, give_sem.at[1], take_sem.at[1]),
    ]

    @pl.when(jnp.logical_not(native()))
    def _():
        for copy in moved:
            copy.start()

    grads, outs = (a_ref, b_ref), (a_out, b_out)
    mine, theirs = (a_mine, b_mine), (a_theirs, b_theirs)
    one, two = (a_one, b_one), (a_two, b_two)
    first, last, side = (a_first, b_first), (a_last, b_last), (a_x, b_x)
    me = ((z, y), (y, z))
    sent = []

    def chunk(n, i, j, c):
        return grads[n].at[j, c, i] if n == 0 else grads[n].at[i, c, j]

    def to(n, i, j):
        return device(j, core, i, x) if n == 0 else device(i, core, j, x)

    def copy_of(n, src, dst, slot, where):
        return pltpu.make_async_remote_copy(
            src_ref=src, dst_ref=dst, send_sem=send_sem.at[n, slot], recv_sem=recv_sem.at[n, slot],
            device_id=where, device_id_type=MESH,
        )

    def send(n, src, dst, slot, where):
        copy = copy_of(n, src, dst, slot, where)
        copy.start()
        sent.append(copy)

    def arrived(n, dst, slot):
        copy_of(n, dst, dst, slot, device(y, core, z, x)).wait_recv()

    cols = b_ref.shape[-1]

    def columns(ref, start, count):
        return ref.at[:, :, pl.ds(start, count)]

    def extra_copy(slot):
        ref = columns(theirs[1].at[slot], cols, extra_ref.shape[-1])
        far = extra_ref.at[lax.rem(y + slot // RING, RING), 1 - core, lax.rem(z + slot % RING, RING)]
        return pltpu.make_async_remote_copy(
            src_ref=far, dst_ref=ref, send_sem=extra_send_sem.at[slot],
            recv_sem=extra_recv_sem.at[slot], device_id=device(y, 1 - core, z, x),
            device_id_type=MESH,
        )

    def extra_load(slot):
        near = extra_ref.at[lax.rem(y + slot // RING, RING), core, lax.rem(z + slot % RING, RING)]
        return pltpu.make_async_copy(
            near, columns(mine[1].at[slot], cols, extra_ref.shape[-1]), extra_load_sem.at[slot]
        )

    def load(n, di, dj):
        i, j = me[n]
        slot = di * RING + dj
        target = mine[n].at[slot] if n == 0 else columns(mine[n].at[slot], 0, cols)
        return pltpu.make_async_copy(
            chunk(n, lax.rem(i + di, RING), lax.rem(j + dj, RING), core), target,
            load_sem.at[n, slot],
        )

    for dj in ORDER:
        for di in ORDER:
            for n in (0, 1):
                i, j = me[n]
                slot = di * RING + dj
                there = chunk(n, lax.rem(i + di, RING), lax.rem(j + dj, RING), 1 - core)
                target = theirs[n].at[slot] if n == 0 else columns(theirs[n].at[slot], 0, cols)
                send(n, there, target, slot, device(y, 1 - core, z, x))
                load(n, di, dj).start()
                if n == 1:
                    extra_copy(slot).start()
                    extra_load(slot).start()

    def ready(n, di, dj):
        slot = di * RING + dj
        load(n, di, dj).wait()
        if n == 0:
            arrived(n, theirs[n].at[slot], slot)
        else:
            arrived(n, columns(theirs[n].at[slot], 0, cols), slot)
            extra_load(slot).wait()
            extra_copy(slot).wait_recv()
        return slot

    for di in ORDER:
        for n in (0, 1):
            i, j = me[n]
            slot = ready(n, di, 2)
            add_into(mine[n].at[slot], mine[n].at[slot], theirs[n].at[slot])
            for half in (0, 1):
                send(
                    n, mine[n].at[slot, half], one[n].at[di, half], 16 + di * 2 + half,
                    to(n, i, up(j) if half == 0 else down(j)),
                )
    for di in ORDER:
        for n in (0, 1):
            i, j = me[n]
            for half, dj in ((0, 1), (1, 3)):
                slot = ready(n, di, dj)
                arrived(n, one[n].at[di, half], 16 + di * 2 + half)
                add_into(
                    mine[n].at[slot, half], mine[n].at[slot, half], theirs[n].at[slot, half],
                    one[n].at[di, half],
                )
                add_into(
                    mine[n].at[slot, 1 - half], mine[n].at[slot, 1 - half],
                    theirs[n].at[slot, 1 - half],
                )
                send(
                    n, mine[n].at[slot], two[n].at[di, half], 24 + di * 2 + half,
                    to(n, i, up(j) if half == 0 else down(j)),
                )
    for di in ORDER:
        for n in (0, 1):
            i, j = me[n]
            slot = ready(n, di, 0)
            for half in (0, 1):
                arrived(n, two[n].at[di, half], 24 + di * 2 + half)
            add_into(
                mine[n].at[slot], mine[n].at[slot], theirs[n].at[slot], two[n].at[di, 0],
                two[n].at[di, 1],
            )
            if di == 2:
                for half in (0, 1):
                    send(
                        n, mine[n].at[slot, half], first[n].at[half], 32 + half,
                        to(n, up(i) if half == 0 else down(i), j),
                    )
            elif di != 0:
                half = 0 if di == 1 else 1
                arrived(n, first[n].at[half], 32 + half)
                add_into(mine[n].at[slot, half], mine[n].at[slot, half], first[n].at[half])
                send(
                    n, mine[n].at[slot], last[n].at[half], 34 + half,
                    to(n, up(i) if half == 0 else down(i), j),
                )
    for n in (0, 1):
        for half in (0, 1):
            arrived(n, last[n].at[half], 34 + half)
        add_into(mine[n].at[0], mine[n].at[0], last[n].at[0], last[n].at[1])
        send(n, mine[n].at[0, 1 - x], side[n], 36, device(y, core, z, 1 - x))
    for n in (0, 1):
        arrived(n, side[n], 36)
        add_into(outs[n], mine[n].at[0, x], side[n])
    gains_here[...] = b_out[:, cols:]
    gains = pltpu.make_async_remote_copy(
        src_ref=gains_here, dst_ref=gains_there, send_sem=gains_sem.at[0],
        recv_sem=gains_sem.at[1], device_id=other_tp(), device_id_type=MESH,
    )
    gains.start()
    for copy in sent:
        copy.wait_send()
    for slot in range(RING * RING):
        extra_copy(slot).wait_send()
    gains.wait()
    b_out[:, cols:] = gains_here[...] + gains_there[...]

    @pl.when(jnp.logical_not(native()))
    def _():
        for copy in moved:
            copy.wait()


def scatter_grads(a, b, extra, wide, tall):
    peers = RING * RING * 4
    rows = a.shape[0] // peers
    shape = (RING, 2, RING, 2, rows)
    cols = (a.shape[1], b.shape[1] + extra.shape[1])
    buffers = []
    for lead in ((16, 2), (16, 2), (4, 2), (4, 2, 2), (2,), (2, 2), ()):
        buffers += [pltpu.VMEM(lead + (rows, c), a.dtype) for c in cols]
    any_space = pl.BlockSpec(memory_space=pl.ANY)
    return pl.pallas_call(
        scatter_kernel,
        in_specs=[any_space] * 5,
        out_specs=[pl.BlockSpec(memory_space=pltpu.VMEM)] * 2 + [any_space] * 2,
        out_shape=[jax.ShapeDtypeStruct((rows, c), F32) for c in cols]
        + [jax.ShapeDtypeStruct(v.shape, v.dtype) for v in (wide, tall)],
        scratch_shapes=buffers + [
            pltpu.SemaphoreType.DMA((2, 16)),
            pltpu.SemaphoreType.DMA((2, 37)),
            pltpu.SemaphoreType.DMA((2, 37)),
            pltpu.VMEM((rows, extra.shape[1]), F32),
            pltpu.VMEM((rows, extra.shape[1]), F32),
            pltpu.SemaphoreType.DMA((16,)),
            pltpu.SemaphoreType.DMA((16,)),
            pltpu.SemaphoreType.DMA((16,)),
            pltpu.SemaphoreType.DMA((2,)),
            pltpu.SemaphoreType.DMA((2,)),
            pltpu.SemaphoreType.DMA((2,)),
        ],
        compiler_params=pltpu.CompilerParams(
            collective_id=1, has_side_effects=True, vmem_limit_bytes=44 * 1024 * 1024
        ),
        cost_estimate=pl.CostEstimate(flops=0, bytes_accessed=250_000_000, transcendentals=0),
        name="scatter_grads",
    )(*(v.reshape(shape + (v.shape[1],)) for v in (a, b, extra)), wide, tall)


BLOCK = 64
CTX = 8


def dot(a, b, dims):
    return lax.dot_general(a, b, (dims, ((), ())), preferred_element_type=F32)


def rotated(u, gain, cosine, sine):
    scaling = lax.rsqrt(jnp.mean(u * u, axis=-1, keepdims=True) + EPS)
    normed = u * scaling
    n = normed * gain
    rot = n * cosine + pltpu.roll(n, HEAD_SIZE // 2, 1) * sine
    return rot.astype(BF16), normed, scaling


def rotated_back(e, normed, scaling, gain, cosine, sine):
    back = e * cosine + pltpu.roll(e * sine, HEAD_SIZE // 2, 1)
    scaled = back * gain
    inner = jnp.mean(scaled * normed, axis=-1, keepdims=True)
    return scaling * (scaled - normed * inner), jnp.sum(back * normed, axis=0, keepdims=True)


def ctx_peer(step):
    return {"ctx": lax.rem(lax.axis_index("ctx") + step, CTX)}


def beside():
    c = lax.axis_index("ctx")
    return {"ctx": c + 1 - 2 * lax.rem(c, 2)}


def remote(src, dst, send_sem, recv_sem, where):
    return pltpu.make_async_remote_copy(
        src_ref=src, dst_ref=dst, send_sem=send_sem, recv_sem=recv_sem, device_id=where,
        device_id_type=MESH,
    )


def softmax_parts(q_low, k, bias):
    s = dot(q_low, k, ((1,), (1,))) * (HEAD_SIZE ** -0.5) + bias
    e = jnp.exp(s - jnp.max(s, axis=-1, keepdims=True))
    return e / jnp.sum(e, axis=-1, keepdims=True)


def attention_kernel(
    kv, heads, qkv_ref, cos_ref, sin_ref, gq_ref, gk_ref, bias_ref, o_ref, kv_ref, held,
    send_sem, recv_sem,
):
    c = lax.axis_index("ctx")
    greet([ctx_peer(step) for step in range(1, CTX)])
    micro, rows = held.shape[0], 2 * BLOCK
    q_cols = kv * heads * HEAD_SIZE
    cosine, sine, gq, gk = cos_ref[...], sin_ref[...], gq_ref[...], gk_ref[...]
    mine = pl.ds(pl.multiple_of(c * BLOCK, BLOCK), BLOCK)
    earlier, own = pl.ds(CTX * BLOCK, BLOCK), pl.ds((CTX + 1) * BLOCK, BLOCK)
    copies = []
    for m in range(micro):
        span = slice(m * rows, (m + 1) * rows)
        for h in range(2 * kv):
            cols = slice(h * HEAD_SIZE, (h + 1) * HEAD_SIZE)
            u = qkv_ref[span, q_cols + h * HEAD_SIZE : q_cols + (h + 1) * HEAD_SIZE]
            low = rotated(u, gk, cosine, sine)[0] if h < kv else u.astype(BF16)
            held[m, mine, cols] = low[:BLOCK]
            held[m, own, cols] = low[BLOCK:]
        for step in range(1, CTX):
            part = held.at[m, mine]
            copies.append(
                remote(part, part, send_sem.at[step, m], recv_sem.at[step, m], ctx_peer(step))
            )
        copies.append(
            remote(
                held.at[m, own], held.at[m, earlier], send_sem.at[0, m], recv_sem.at[0, m], beside()
            )
        )
        for copy in copies[-CTX:]:
            copy.start()

    def group(m, h, carry):
        span = slice(m * rows, (m + 1) * rows)
        k = held[m, :, pl.ds(pl.multiple_of(h * HEAD_SIZE, HEAD_SIZE), HEAD_SIZE)]
        v = held[m, :, pl.ds(pl.multiple_of((kv + h) * HEAD_SIZE, HEAD_SIZE), HEAD_SIZE)]
        for e in range(heads):
            cols = pl.ds(pl.multiple_of((h * heads + e) * HEAD_SIZE, HEAD_SIZE), HEAD_SIZE)
            q_low = rotated(qkv_ref[span, cols], gq, cosine, sine)[0]
            p = softmax_parts(q_low, k, bias_ref[...]).astype(BF16)
            o_ref[span, cols] = dot(p, v, ((1,), (0,))).astype(BF16)
        return carry

    for m in range(micro):
        for step in range(1, CTX):
            source = lax.rem(c + CTX - step, CTX)
            part = held.at[m, pl.ds(pl.multiple_of(source * BLOCK, BLOCK), BLOCK)]
            remote(
                part, part, send_sem.at[step, m], recv_sem.at[step, m], ctx_peer(step)
            ).wait_recv()
        copies[(m + 1) * CTX - 1].wait_recv()
        lax.fori_loop(0, kv, functools.partial(group, m), 0)
    kv_ref[...] = held[...]
    for copy in copies:
        copy.wait_send()


def attention_back_kernel(
    kv, heads, qkv_ref, cos_ref, sin_ref, gq_ref, gk_ref, bias_ref, kv_ref, do_ref,
    dqkv_ref, gains_ref, grads, given, given_side, p_all, ds_all, q_all, do_all,
    send_sem, recv_sem,
):
    c = lax.axis_index("ctx")
    greet([ctx_peer(step) for step in range(1, CTX)])
    micro, rows = grads.shape[0], 2 * BLOCK
    q_cols = kv * heads * HEAD_SIZE
    scale = HEAD_SIZE ** -0.5
    cosine, sine, gq, gk = cos_ref[...], sin_ref[...], gq_ref[...], gk_ref[...]
    mine = pl.ds(pl.multiple_of(c * BLOCK, BLOCK), BLOCK)
    earlier, own = pl.ds(CTX * BLOCK, BLOCK), pl.ds((CTX + 1) * BLOCK, BLOCK)

    def group(m, h, total):
        span = slice(m * rows, (m + 1) * rows)
        k_cols = pl.ds(pl.multiple_of(h * HEAD_SIZE, HEAD_SIZE), HEAD_SIZE)
        v_cols = pl.ds(pl.multiple_of((kv + h) * HEAD_SIZE, HEAD_SIZE), HEAD_SIZE)
        k, v = kv_ref[m, :, k_cols], kv_ref[m, :, v_cols]
        for e in range(heads):
            cols = pl.ds(pl.multiple_of((h * heads + e) * HEAD_SIZE, HEAD_SIZE), HEAD_SIZE)
            stack = slice(e * rows, (e + 1) * rows)
            q_low, normed, scaling = rotated(qkv_ref[span, cols], gq, cosine, sine)
            q_all[stack, :] = q_low
            p = softmax_parts(q_low, k, bias_ref[...])
            p_all[stack, :] = p.astype(BF16)
            do = do_ref[span, cols]
            do_all[stack, :] = do
            dp = dot(do, v, ((1,), (1,)))
            ds = (p * (dp - jnp.sum(dp * p, axis=-1, keepdims=True))).astype(BF16)
            ds_all[stack, :] = ds
            dqr = (dot(ds, k, ((1,), (0,))) * scale).astype(BF16).astype(F32)
            dq, part = rotated_back(dqr, normed, scaling, gq, cosine, sine)
            dqkv_ref[span, cols] = dq.astype(BF16)
            total = total + part
        grads[m, :, v_cols] = dot(p_all[...], do_all[...], ((0,), (0,))).astype(BF16)
        grads[m, :, k_cols] = (dot(ds_all[...], q_all[...], ((0,), (0,))) * scale).astype(BF16)
        return total

    total = jnp.zeros((1, HEAD_SIZE), F32)
    copies = []
    for m in range(micro):
        total = lax.fori_loop(0, kv, functools.partial(group, m), total)
        for step in range(1, CTX):
            peer = lax.rem(c + step, CTX)
            part = grads.at[m, pl.ds(pl.multiple_of(peer * BLOCK, BLOCK), BLOCK)]
            copies.append(
                remote(
                    part, given.at[step - 1, m], send_sem.at[step, m], recv_sem.at[step, m],
                    ctx_peer(step),
                )
            )
        copies.append(
            remote(
                grads.at[m, earlier], given_side.at[m], send_sem.at[0, m], recv_sem.at[0, m],
                beside(),
            )
        )
        for copy in copies[-CTX:]:
            copy.start()
    k_total = jnp.zeros((1, HEAD_SIZE), F32)
    for m in range(micro):
        for copy in copies[m * CTX : (m + 1) * CTX]:
            copy.wait_recv()
        for h in range(2 * kv):
            cols = slice(h * HEAD_SIZE, (h + 1) * HEAD_SIZE)
            at = slice(q_cols + h * HEAD_SIZE, q_cols + (h + 1) * HEAD_SIZE)
            prompt = grads[m, mine, cols].astype(F32)
            for step in range(CTX - 1):
                prompt = prompt + given[step, m, :, cols].astype(F32)
            cont = grads[m, own, cols].astype(F32) + given_side[m, :, cols].astype(F32)
            e = jnp.concatenate([prompt, cont], axis=0).astype(BF16)
            span = slice(m * rows, (m + 1) * rows)
            if h < kv:
                _, normed, scaling = rotated(qkv_ref[span, at], gk, cosine, sine)
                d, part = rotated_back(e.astype(F32), normed, scaling, gk, cosine, sine)
                k_total = k_total + part
                dqkv_ref[span, at] = d.astype(BF16)
            else:
                dqkv_ref[span, at] = e
    gains_ref[0:1, :] = total
    gains_ref[1:2, :] = k_total
    for copy in copies:
        copy.wait_send()


def attention(qkv, cosine, sine, gain_query, gain_key, bias, kv, micro):
    heads = qkv.shape[1] // HEAD_SIZE // kv - 2
    rows, keys = bias.shape
    return pl.pallas_call(
        functools.partial(attention_kernel, kv, heads),
        out_shape=[
            jax.ShapeDtypeStruct((qkv.shape[0], kv * heads * HEAD_SIZE), BF16),
            jax.ShapeDtypeStruct((micro, keys, 2 * kv * HEAD_SIZE), BF16),
        ],
        scratch_shapes=[
            pltpu.VMEM((micro, keys, 2 * kv * HEAD_SIZE), BF16),
            pltpu.SemaphoreType.DMA((CTX, micro)),
            pltpu.SemaphoreType.DMA((CTX, micro)),
        ],
        compiler_params=pltpu.CompilerParams(
            collective_id=2, has_side_effects=True, vmem_limit_bytes=VMEM_LIMIT
        ),
        cost_estimate=pl.CostEstimate(flops=0, bytes_accessed=120_000_000, transcendentals=0),
        name="attention_forward",
    )(qkv, cosine, sine, gain_query, gain_key, bias)


def attention_back(qkv, cosine, sine, gain_query, gain_key, bias, kv_all, d_out, kv):
    heads = qkv.shape[1] // HEAD_SIZE // kv - 2
    rows, keys = bias.shape
    micro, _, kv_cols = kv_all.shape
    return pl.pallas_call(
        functools.partial(attention_back_kernel, kv, heads),
        out_shape=[
            jax.ShapeDtypeStruct(qkv.shape, BF16),
            jax.ShapeDtypeStruct((2, HEAD_SIZE), F32),
        ],
        scratch_shapes=[
            pltpu.VMEM((micro, keys, kv_cols), BF16),
            pltpu.VMEM((CTX - 1, micro, BLOCK, kv_cols), BF16),
            pltpu.VMEM((micro, BLOCK, kv_cols), BF16),
            pltpu.VMEM((heads * rows, keys), BF16),
            pltpu.VMEM((heads * rows, keys), BF16),
            pltpu.VMEM((heads * rows, HEAD_SIZE), BF16),
            pltpu.VMEM((heads * rows, HEAD_SIZE), BF16),
            pltpu.SemaphoreType.DMA((CTX, micro)),
            pltpu.SemaphoreType.DMA((CTX, micro)),
        ],
        compiler_params=pltpu.CompilerParams(
            collective_id=3, has_side_effects=True, vmem_limit_bytes=VMEM_LIMIT
        ),
        cost_estimate=pl.CostEstimate(flops=0, bytes_accessed=120_000_000, transcendentals=0),
        name="attention_backward",
    )(qkv, cosine, sine, gain_query, gain_key, bias, kv_all, d_out)


PART = 256


def other_core():
    f = lax.axis_index("fsdp")
    return {"fsdp": f + 1 - 2 * (f % 2)}


def expert_kernel(
    got_ref, deo_ref, gu_ref, down_ref, back_ref, eo_ref, rows_ref, deos_ref, z_ref, dgu_ref,
    rows, deos, gu, down, own, give, take, load_sem, send_sem, recv_sem, save_sem,
):
    greet([other_core()])
    count, hidden = got_ref.shape[0], down_ref.shape[0]
    parts = count // PART
    near, far = pl.ds(0, count), pl.ds(count, count)
    swaps = [
        remote(got_ref, rows.at[far], send_sem.at[0], recv_sem.at[0], other_core()),
        remote(deo_ref, deos.at[far], send_sem.at[1], recv_sem.at[1], other_core()),
    ]
    loads = [
        pltpu.make_async_copy(src, dst, load_sem.at[n])
        for n, (src, dst) in enumerate(
            ((got_ref, rows.at[near]), (gu_ref, gu), (deo_ref, deos.at[near]), (down_ref, down))
        )
    ]
    saves = [
        pltpu.make_async_copy(rows, rows_ref, save_sem.at[0]),
        pltpu.make_async_copy(deos, deos_ref, save_sem.at[1]),
    ]
    for copy in loads + swaps:
        copy.start()

    def span(i):
        return pl.ds(pl.multiple_of(i * PART, PART), PART)

    def returned(kind, i):
        slot = kind * parts + i
        return remote(
            give.at[kind, span(i)], take.at[kind, span(i)], send_sem.at[2 + slot],
            recv_sem.at[2 + slot], other_core(),
        )

    def through(i):
        pre = dot(rows[span(i), :], gu[...], ((1,), (0,)))
        dz = dot(deos[span(i), :], down[...], ((1,), (1,)))
        g, u = pre[:, :hidden], pre[:, hidden:]
        sig = 1.0 / (1.0 + jnp.exp(-g))
        act = g * sig
        z_ref[span(i), :] = (act * u).astype(BF16)
        dgu_ref[span(i), :hidden] = (dz * u * sig * (1.0 + g * (1.0 - sig))).astype(BF16)
        dgu_ref[span(i), hidden:] = (dz * act).astype(BF16)

    def to_rows(i):
        return dot(dgu_ref[span(i), :], gu[...], ((1,), (1,)))

    def to_outputs(i):
        return dot(z_ref[span(i), :], down[...], ((1,), (0,)))

    def each(body):
        def step(i, carry):
            body(i)
            return carry

        lax.fori_loop(0, parts, step, 0)

    def give_rows(i):
        through(parts + i)
        give[0, span(i), :] = to_rows(parts + i).astype(BF16)
        returned(0, i).start()

    def keep_rows(i):
        own[span(i), :] = to_rows(i)

    def give_outputs(i):
        give[1, span(i), :] = to_outputs(parts + i).astype(BF16)
        returned(1, i).start()

    def end_rows(i):
        returned(0, i).wait()
        back_ref[span(i), :] = (own[span(i), :] + take[0, span(i), :].astype(F32)).astype(BF16)

    def end_outputs(i):
        total = to_outputs(i)
        returned(1, i).wait()
        eo_ref[span(i), :] = (total + take[1, span(i), :].astype(F32)).astype(BF16)

    for copy in loads:
        copy.wait()
    each(through)
    for copy in swaps:
        copy.wait_recv()
    for copy in saves:
        copy.start()
    each(give_rows)
    each(give_outputs)
    each(keep_rows)
    each(end_rows)
    each(end_outputs)
    for copy in swaps:
        copy.wait_send()
    for copy in saves:
        copy.wait()


def expert(got, d_eo, gu, down, collective):
    count, width = got.shape
    hidden = down.shape[0]
    parts = count // PART
    vmem, any_space = (pl.BlockSpec(memory_space=space) for space in (pltpu.VMEM, pl.ANY))
    shapes = [(count, width), (count, width), (2 * count, width), (2 * count, width)]
    shapes += [(2 * count, hidden), (2 * count, 2 * hidden)]
    return pl.pallas_call(
        expert_kernel,
        in_specs=[any_space] * 4,
        out_specs=[vmem] * 2 + [any_space] * 2 + [vmem] * 2,
        out_shape=[jax.ShapeDtypeStruct(shape, BF16) for shape in shapes],
        scratch_shapes=[
            pltpu.VMEM((2 * count, width), BF16),
            pltpu.VMEM((2 * count, width), BF16),
            pltpu.VMEM(gu.shape, BF16),
            pltpu.VMEM(down.shape, BF16),
            pltpu.VMEM((count, width), F32),
            pltpu.VMEM((2, count, width), BF16),
            pltpu.VMEM((2, count, width), BF16),
            pltpu.SemaphoreType.DMA((4,)),
            pltpu.SemaphoreType.DMA((2 + 2 * parts,)),
            pltpu.SemaphoreType.DMA((2 + 2 * parts,)),
            pltpu.SemaphoreType.DMA((2,)),
        ],
        compiler_params=pltpu.CompilerParams(
            collective_id=collective, has_side_effects=True, vmem_limit_bytes=VMEM_LIMIT
        ),
        cost_estimate=pl.CostEstimate(flops=0, bytes_accessed=80_000_000, transcendentals=0),
        name="expert_both_ways",
    )(got, d_eo, gu, down)


def normalize(rows, gain):
    scaling = lax.rsqrt(jnp.mean(rows * rows, axis=-1, keepdims=True) + EPS)
    return rows * scaling * gain, scaling


def normalize_back(rows, scaling, gain, upstream):
    normed = rows * scaling
    gain_grad = jnp.sum((upstream * normed).reshape(-1, rows.shape[-1]), axis=0)
    scaled = upstream * gain
    inner = jnp.mean(scaled * normed, axis=-1, keepdims=True)
    return scaling * (scaled - normed * inner), gain_grad


def swap_tp(value):
    return lax.ppermute(value, "tp", [(0, 1), (1, 0)])


def local(
    x_prompt, x_cont, cot_prompt, cot_cont, ids_prompt, ids_cont, gates_prompt, gates_cont,
    norm_gain, query_weight, key_matrix, value_matrix, out_weight, query_gain, key_gain, moe_gain,
    expert_gate, expert_up, expert_down,
):
    micro = x_prompt.shape[0]
    prompt_rows, cont_rows, width = x_prompt.shape[2], x_cont.shape[2], x_prompt.shape[3]
    block = cont_rows
    rows = 2 * block
    s = lax.axis_index("ctx")
    ctx = lax.axis_size("ctx")
    first = lax.axis_index("tp") == 0
    peers = lax.axis_size(ALL)
    q_cols, kv_cols = query_weight.shape[1], key_matrix.shape[1]
    kv = kv_cols // HEAD_SIZE
    qkv_cols = q_cols + 2 * kv_cols
    shard_rows = query_weight.shape[0]
    hidden = expert_gate.shape[2]
    slots = cont_rows * TOPK // peers

    fsdp, tp = lax.axis_size("fsdp"), lax.axis_size("tp")
    chips = [(2 * y, c, t) for y in range(fsdp // 2) for c in range(ctx) for t in range(tp)]
    groups = [[((f + core) * ctx + c) * tp + t for f, c, t in chips] for core in range(2)]
    expert_of = jnp.array([(f + t) * ctx + c for f, c, t in chips], jnp.int32)

    def exchange(rows_of):
        return lax.all_to_all(
            rows_of, ("fsdp", "ctx", "tp"), split_axis=0, concat_axis=0, tiled=True,
            axis_index_groups=groups,
        )

    def pad(v):
        return jnp.pad(v[:, 0], ((0, 0), (0, block - prompt_rows), (0, 0)))

    x_first, x_second = pad(x_prompt), x_cont[:, 0]
    own_tokens = jnp.where(first, x_second, x_first).astype(F32)
    own_cot = jnp.where(first, cot_cont[:, 0], pad(cot_prompt)).astype(F32)
    ids_pad = jnp.pad(
        ids_prompt[:, 0], ((0, 0), (0, block - prompt_rows), (0, 0)), constant_values=-1
    )
    own_ids = jnp.where(first, ids_cont[:, 0], ids_pad)
    own_gates = jnp.where(first, gates_cont[:, 0], pad(gates_prompt))

    named = own_ids[:, :, :, None] == expert_of
    chosen = jnp.any(named, axis=2)
    weight = jnp.sum(jnp.where(named, own_gates[:, :, :, None], 0.0), axis=2)
    lower = jnp.tril(jnp.ones((block, block), BF16), -1)
    rank = jnp.einsum("ts,mse->mte", lower, chosen.astype(BF16), preferred_element_type=F32)
    place = jnp.where(chosen, rank, -1.0)
    placed = place[:, :, :, None] == jnp.arange(slots, dtype=F32)
    select = placed.astype(BF16).reshape(micro, block, peers * slots)
    same = jnp.arange(micro)[:, None] == jnp.arange(micro)[None, :]
    both = jnp.logical_and(placed[:, :, :, None, :], same[:, None, None, :, None])
    flat = (micro * block, peers * micro * slots)
    select_both = both.astype(BF16).reshape(flat)
    mixing = jnp.where(both, weight[:, :, :, None, None], 0.0).reshape(flat)
    mixing_high = mixing.astype(BF16)
    mixing_low = (mixing - mixing_high.astype(F32)).astype(BF16)
    slot_gate = jnp.sum(mixing, axis=0)

    extra = jnp.concatenate(
        [
            norm_gain[:, None],
            moe_gain[:, None],
            jnp.pad(query_gain, (0, shard_rows - query_gain.shape[0]))[:, None],
            jnp.pad(key_gain, (0, shard_rows - key_gain.shape[0]))[:, None],
            jnp.zeros((shard_rows, 124), BF16),
        ],
        axis=1,
    )
    w_qkv, w_out_extra, gu, down = gather_weights(
        jnp.concatenate([query_weight, key_matrix, value_matrix], axis=1),
        jnp.concatenate([out_weight, extra], axis=1),
        expert_gate[0],
        expert_up[0],
        expert_down[0],
    )
    w_out = w_out_extra[:, :q_cols]
    gains = w_out_extra[:, q_cols:].astype(F32)
    gain_in, gain_moe = gains[:, 0], gains[:, 1]
    head_gains = gains[:, 2:4].reshape(peers, shard_rows, 2)[:, : query_gain.shape[0]]
    head_gains = head_gains.reshape(HEAD_SIZE, 2)
    gain_query, gain_key = head_gains[:, 0], head_gains[:, 1]

    cot_low, w_qkv = lax.optimization_barrier((own_cot.astype(BF16), w_qkv))
    spread = dot(select_both, cot_low.reshape(-1, width), ((0,), (0,))) * slot_gate[:, None]
    d_eo_rows = exchange(spread.astype(BF16))

    offsets = jnp.arange(rows, dtype=jnp.int32)
    is_prompt = offsets < block
    prompt_pos = s * prompt_rows + offsets
    cont_pos = s * cont_rows + offsets - block
    rot_place = jnp.where(is_prompt, prompt_pos, PROMPT + cont_pos % CL).astype(F32)
    steps_freq = jnp.arange(HEAD_SIZE // 2, dtype=F32) * (2.0 / HEAD_SIZE)
    angles = rot_place[:, None] * jnp.power(THETA, -steps_freq)[None, :]
    cosine, sine = jnp.cos(angles), jnp.sin(angles)
    cosine = jnp.concatenate([cosine, cosine], axis=1)
    sine = jnp.concatenate([-sine, sine], axis=1)
    keys = (ctx + 2) * block
    key_index = jnp.arange(keys, dtype=jnp.int32)[None, :]
    key_off = key_index % block
    key_prompt_pos = key_index // block * prompt_rows + key_off
    key_cont = (s - 1) * cont_rows + key_index - ctx * block
    is_cont = jnp.logical_not(is_prompt)[:, None]
    visible = jnp.where(
        key_index < ctx * block,
        jnp.logical_and(
            key_off < prompt_rows,
            jnp.logical_or(is_cont, key_prompt_pos <= prompt_pos[:, None]),
        ),
        jnp.logical_and(
            is_cont,
            jnp.logical_and(
                key_cont // CL == cont_pos[:, None] // CL, key_cont <= cont_pos[:, None]
            ),
        ),
    )
    bias = jnp.where(visible, 0.0, NEG).astype(F32)

    def share_rows(own):
        other = swap_tp(own)
        return jnp.where(first, other, own), jnp.where(first, own, other)

    def sum_own(part):
        part = part.reshape(micro, rows, width)
        given = jnp.where(first, part[:, :block], part[:, block:]).astype(BF16)
        kept = jnp.where(first, part[:, block:], part[:, :block])
        return kept + swap_tp(given).astype(F32)

    tokens = jnp.concatenate([x_first, x_second], axis=1).astype(F32).reshape(-1, width)
    a = normalize(tokens, gain_in)[0].astype(BF16)
    qkv = dot(a, w_qkv, ((1,), (0,)))
    heads_in = (cosine, sine, gain_query[None], gain_key[None], bias)
    o, kv_all = attention(qkv, *heads_in, kv, micro)
    middle = own_tokens + sum_own(dot(o, w_out, ((1,), (1,))))
    b_normed, b_scale = normalize(middle, gain_moe)
    b_low = b_normed.astype(BF16)

    b_low, d_eo_rows = lax.optimization_barrier((b_low, d_eo_rows))
    d_eo_rows = d_eo_rows.reshape(peers, micro, slots, width)
    backs, outputs, wide_terms, tall_terms = [], [], [], []
    for m in range(micro):
        got = exchange(dot(select[m], b_low[m], ((0,), (0,))).astype(BF16))
        back, eo, rows_m, d_eo_m, z_m, d_gu_m = expert(
            got, d_eo_rows[:, m].reshape(-1, width), gu, down, 4 + m
        )
        backs.append(exchange(back))
        outputs.append(eo.reshape(peers, slots, width))
        wide_terms.append((rows_m, d_gu_m))
        tall_terms.append((z_m, d_eo_m))

    def over_rows(terms):
        return sum(dot(left, right, ((0,), (0,))) for left, right in terms).astype(BF16)

    wide_here, tall_here = over_rows(wide_terms), over_rows(tall_terms)

    d_b = jnp.stack([dot(select[m], backs[m], ((1,), (0,))) for m in range(micro)])
    middle_from, moe_total = normalize_back(middle, b_scale, gain_moe, d_b)
    d_h = own_cot + middle_from
    d_attn = jnp.concatenate(share_rows(d_h.astype(BF16)), axis=1).reshape(-1, width)

    late = lax.optimization_barrier((*outputs, backs[-1]))
    eo_back = exchange(jnp.stack(late[:micro], axis=1).reshape(-1, width))

    d_o = dot(d_attn, w_out, ((1,), (0,))).astype(BF16)
    grad_out = dot(d_attn, o, ((0,), (0,))).astype(BF16)
    d_qkv, head_totals = attention_back(qkv, *heads_in, kv_all, d_o, kv)
    d_qkv, eo_back = lax.optimization_barrier((d_qkv, eo_back))
    moe_out = dot(mixing_high, eo_back, ((1,), (0,))) + dot(mixing_low, eo_back, ((1,), (0,)))
    out_first, out_second = share_rows((middle + moe_out.reshape(middle.shape)).astype(BF16))
    input_grad = sum_own(dot(d_qkv, w_qkv, ((1,), (1,))))
    grad_qkv = dot(a, d_qkv, ((0,), (0,))).astype(BF16)
    scale_in = lax.rsqrt(jnp.mean(own_tokens * own_tokens, axis=-1, keepdims=True) + EPS)
    token_from, norm_total = normalize_back(own_tokens, scale_in, gain_in, input_grad)
    grad_first, grad_second = share_rows((d_h + token_from).astype(BF16))

    head_grads = head_totals.T.reshape(peers, -1, 2)
    head_grads = jnp.pad(head_grads, ((0, 0), (0, shard_rows - head_grads.shape[1]), (0, 0)))
    extra_grads = jnp.concatenate(
        [
            norm_total[:, None],
            moe_total[:, None],
            head_grads.reshape(-1, 2),
            jnp.zeros((peers * shard_rows, 124), F32),
        ],
        axis=1,
    ).astype(BF16)
    grad_qkv, out_first, out_second = lax.optimization_barrier((grad_qkv, out_first, out_second))
    share, share_out, wide_there, tall_there = scatter_grads(
        grad_qkv, grad_out, extra_grads, wide_here, tall_here
    )
    grad_wide = jnp.where(native(), wide_here, wide_there).astype(F32)
    grad_down = jnp.where(native(), tall_here, tall_there).astype(F32)
    gain_share = share_out[:, q_cols:]
    head_rows = query_gain.shape[0]

    return (
        out_first[:, None, :prompt_rows],
        out_second[:, None],
        grad_first[:, None, :prompt_rows],
        grad_second[:, None],
        gain_share[:, 0],
        share[:, :q_cols],
        share[:, q_cols : q_cols + kv_cols],
        share[:, q_cols + kv_cols : qkv_cols],
        share_out[:, :q_cols],
        gain_share[:head_rows, 2],
        gain_share[:head_rows, 3],
        gain_share[:, 1],
        grad_wide[None, :, :hidden],
        grad_wide[None, :, hidden:],
        grad_down[None],
    )


def solution(mesh):
    rows = P(None, "fsdp", "ctx", None)
    vector = P(("fsdp", "ctx"))
    matrix = P(("fsdp", "ctx"), "tp")
    wide = P(("fsdp", "ctx"), None, "tp")
    tall = P(("fsdp", "ctx"), "tp", None)
    in_specs = (rows,) * 8 + (vector,) + (matrix,) * 4 + (vector,) * 3 + (wide, wide, tall)
    out_specs = (rows,) * 4 + (vector,) + (matrix,) * 4 + (vector,) * 3 + (wide, wide, tall)
    return jax.shard_map(local, mesh=mesh, in_specs=in_specs, out_specs=out_specs, check_vma=False)
```

```python
import functools

import jax
import jax.numpy as jnp
from jax import lax
from jax.experimental import pallas as pl
from jax.experimental.pallas import tpu as pltpu
from jax.sharding import PartitionSpec as P

HEAD_SIZE = 128
TOPK = 8
PROMPT = 448
CL = 128
EPS = 1e-06
THETA = 1000000.0
NEG = -1e30
F32 = jnp.float32
BF16 = jnp.bfloat16
ALL = ("fsdp", "ctx")
MESH = pl.DeviceIdType.MESH
RING = 4
VMEM_LIMIT = 48 * 1024 * 1024


def place():
    f, c = lax.axis_index("fsdp"), lax.axis_index("ctx")
    return f // 2, f % 2, c // 2, c % 2


def device(y, core, z, x):
    return {"fsdp": y * 2 + core, "ctx": z * 2 + x}


def greet(partners):
    barrier = pltpu.get_barrier_semaphore()
    for partner in partners:
        pl.semaphore_signal(barrier, inc=1, device_id=partner, device_id_type=MESH)
    pl.semaphore_wait(barrier, len(partners))


def neighbours():
    y, core, z, x = place()
    up, down = (lambda v: lax.rem(v + 1, RING)), (lambda v: lax.rem(v + RING - 1, RING))
    return [
        device(y, core, z, 1 - x),
        device(y, 1 - core, z, x),
        device(up(y), core, z, x),
        device(down(y), core, z, x),
        device(y, core, up(z), x),
        device(y, core, down(z), x),
    ]


def other_tp():
    return {"tp": 1 - lax.axis_index("tp")}


def opposite():
    f = lax.axis_index("fsdp")
    return {"fsdp": f + 1 - 2 * (f % 2), "tp": 1 - lax.axis_index("tp")}


def native():
    return lax.axis_index("fsdp") % 2 == lax.axis_index("tp")


def swap_opposite(src, dst, send_sem, recv_sem):
    return pltpu.make_async_remote_copy(
        src_ref=src, dst_ref=dst, send_sem=send_sem, recv_sem=recv_sem, device_id=opposite(),
        device_id_type=MESH,
    )


def gather_kernel(
    a_ref, b_ref, gate_ref, up_ref, down_ref, a_all, b_all, gate_all, up_all, down_all,
    local_sem, send_sem, recv_sem, away_sem, home_sem, give_sem, take_sem,
):
    y, core, z, x = place()
    greet(neighbours() + [opposite()])
    shards = ((gate_ref, gate_all), (up_ref, up_all), (down_ref, down_all))
    moved = [
        swap_opposite(p, q, give_sem.at[n], take_sem.at[n]) for n, (p, q) in enumerate(shards)
    ]
    refs, own = (a_all, b_all), (a_ref, b_ref)
    started = []
    count = [0, 0]

    def chunk(n, i, j):
        return refs[n].at[j, core, i] if n == 0 else refs[n].at[i, core, j]

    def to(n, first, second):
        return device(second, core, first, x) if n == 0 else device(first, core, second, x)

    def send(n, ref, where, slot):
        copy = pltpu.make_async_remote_copy(
            src_ref=ref, dst_ref=ref, send_sem=send_sem.at[n, slot], recv_sem=recv_sem.at[n, slot],
            device_id=where, device_id_type=MESH,
        )
        copy.start()
        started.append(copy)

    def arrived(n, ref, slot):
        pltpu.make_async_remote_copy(
            src_ref=ref, dst_ref=ref, send_sem=send_sem.at[n, slot], recv_sem=recv_sem.at[n, slot],
            device_id=device(y, core, z, x), device_id_type=MESH,
        ).wait_recv()

    homes = []

    def across(n, i, j):
        slot = count[n]
        count[n] += 1
        ref = chunk(n, i, j)
        copy = pltpu.make_async_remote_copy(
            src_ref=ref, dst_ref=ref, send_sem=away_sem.at[n, slot], recv_sem=home_sem.at[n, slot],
            device_id=device(y, 1 - core, z, x), device_id_type=MESH,
        )
        copy.start()
        homes.append(copy)

    def second(n, i, j, k):
        base = 5 + 4 * k
        send(n, chunk(n, i, j), to(n, me[n][0], up(j)), base)
        send(n, chunk(n, i, j), to(n, me[n][0], down(j)), base + 1)
        across(n, i, j)

    up, down = (lambda v: lax.rem(v + 1, RING)), (lambda v: lax.rem(v + RING - 1, RING))
    me = ((z, y), (y, z))
    locals_ = []
    for n in (0, 1):
        i, j = me[n]
        keep = pltpu.make_async_copy(own[n], chunk(n, i, j).at[x], local_sem.at[n])
        keep.start()
        locals_.append(keep)
        copy = pltpu.make_async_remote_copy(
            src_ref=own[n], dst_ref=chunk(n, i, j).at[x], send_sem=send_sem.at[n, 0],
            recv_sem=recv_sem.at[n, 0], device_id=device(y, core, z, 1 - x), device_id_type=MESH,
        )
        copy.start()
        started.append(copy)
    for n in (0, 1):
        i, j = me[n]
        locals_[n].wait()
        arrived(n, chunk(n, i, j).at[1 - x], 0)
        send(n, chunk(n, i, j), to(n, up(i), j), 1)
        send(n, chunk(n, i, j), to(n, down(i), j), 2)
    for n in (0, 1):
        i, j = me[n]
        second(n, i, j, 0)

    @pl.when(jnp.logical_not(native()))
    def _():
        for copy in moved:
            copy.start()

    for n in (0, 1):
        i, j = me[n]
        arrived(n, chunk(n, down(i), j), 1)
        send(n, chunk(n, down(i), j).at[0], to(n, up(i), j), 3)
        second(n, down(i), j, 1)
    for n in (0, 1):
        i, j = me[n]
        arrived(n, chunk(n, up(i), j), 2)
        send(n, chunk(n, up(i), j).at[1], to(n, down(i), j), 4)
        second(n, up(i), j, 2)
    for n in (0, 1):
        i, j = me[n]
        far = lax.rem(i + 2, RING)
        arrived(n, chunk(n, far, j).at[0], 3)
        arrived(n, chunk(n, far, j).at[1], 4)
        second(n, far, j, 3)
    for k in range(4):
        for n in (0, 1):
            i, j = me[n]
            it = (i, down(i), up(i), lax.rem(i + 2, RING))[k]
            base = 5 + 4 * k
            arrived(n, chunk(n, it, down(j)), base)
            send(n, chunk(n, it, down(j)).at[0], to(n, i, up(j)), base + 2)
            across(n, it, down(j))
            arrived(n, chunk(n, it, up(j)), base + 1)
            send(n, chunk(n, it, up(j)).at[1], to(n, i, down(j)), base + 3)
            across(n, it, up(j))
    for k in range(4):
        for n in (0, 1):
            i, j = me[n]
            it = (i, down(i), up(i), lax.rem(i + 2, RING))[k]
            base = 5 + 4 * k
            far = lax.rem(j + 2, RING)
            arrived(n, chunk(n, it, far).at[0], base + 2)
            arrived(n, chunk(n, it, far).at[1], base + 3)
            across(n, it, far)
    for copy in homes:
        copy.wait()
    for copy in started:
        copy.wait_send()

    @pl.when(jnp.logical_not(native()))
    def _():
        for copy in moved:
            copy.wait()


def gather_weights(a, b, gate, up, down):
    rows = a.shape[0]
    shape = (RING, 2, RING, 2, rows)
    any_space = pl.BlockSpec(memory_space=pl.ANY)
    a_all, b_all, *experts = pl.pallas_call(
        gather_kernel,
        in_specs=[pl.BlockSpec(memory_space=pltpu.VMEM)] * 2 + [any_space] * 3,
        out_specs=[any_space] * 5,
        out_shape=[jax.ShapeDtypeStruct(shape + (v.shape[1],), v.dtype) for v in (a, b)]
        + [jax.ShapeDtypeStruct(v.shape, v.dtype) for v in (gate, up, down)],
        scratch_shapes=[
            pltpu.SemaphoreType.DMA((2,)),
            pltpu.SemaphoreType.DMA((2, 21)),
            pltpu.SemaphoreType.DMA((2, 21)),
            pltpu.SemaphoreType.DMA((2, 16)),
            pltpu.SemaphoreType.DMA((2, 16)),
            pltpu.SemaphoreType.DMA((3,)),
            pltpu.SemaphoreType.DMA((3,)),
        ],
        compiler_params=pltpu.CompilerParams(collective_id=0, has_side_effects=True),
        cost_estimate=pl.CostEstimate(flops=0, bytes_accessed=250_000_000, transcendentals=0),
        name="gather_weights",
    )(a, b, gate, up, down)
    return a_all.reshape(-1, a.shape[1]), b_all.reshape(-1, b.shape[1]), *experts


ORDER = (2, 1, 3, 0)
SLICE = 16


def up(v):
    return lax.rem(v + 1, RING)


def down(v):
    return lax.rem(v + RING - 1, RING)


def add_into(target, *terms):
    flat = [target.shape[0]] if len(target.shape) == 3 else []
    for lead in range(flat[0]) if flat else (None,):
        for start in range(0, target.shape[-2], SLICE):
            at = (pl.ds(start, SLICE), slice(None))
            at = at if lead is None else (lead,) + at
            total = terms[0][at].astype(F32)
            for term in terms[1:]:
                total = total + term[at].astype(F32)
            target[at] = total.astype(target.dtype)


def scatter_kernel(
    a_ref, b_ref, extra_ref, wide_ref, tall_ref, a_out, b_out, wide_out, tall_out, a_mine, b_mine, a_theirs, b_theirs, a_one, b_one, a_two, b_two,
    a_first, b_first, a_last, b_last, a_x, b_x, load_sem, send_sem, recv_sem,
    gains_here, gains_there,
    extra_load_sem, extra_send_sem, extra_recv_sem, give_sem, take_sem, gains_sem,
):
    y, core, z, x = place()
    greet(neighbours() + [other_tp(), opposite()])
    moved = [
        swap_opposite(wide_ref, wide_out, give_sem.at[0], take_sem.at[0]),
        swap_opposite(tall_ref, tall_out, give_sem.at[1], take_sem.at[1]),
    ]

    @pl.when(jnp.logical_not(native()))
    def _():
        for copy in moved:
            copy.start()

    grads, outs = (a_ref, b_ref), (a_out, b_out)
    mine, theirs = (a_mine, b_mine), (a_theirs, b_theirs)
    one, two = (a_one, b_one), (a_two, b_two)
    first, last, side = (a_first, b_first), (a_last, b_last), (a_x, b_x)
    me = ((z, y), (y, z))
    sent = []

    def chunk(n, i, j, c):
        return grads[n].at[j, c, i] if n == 0 else grads[n].at[i, c, j]

    def to(n, i, j):
        return device(j, core, i, x) if n == 0 else device(i, core, j, x)

    def copy_of(n, src, dst, slot, where):
        return pltpu.make_async_remote_copy(
            src_ref=src, dst_ref=dst, send_sem=send_sem.at[n, slot], recv_sem=recv_sem.at[n, slot],
            device_id=where, device_id_type=MESH,
        )

    def send(n, src, dst, slot, where):
        copy = copy_of(n, src, dst, slot, where)
        copy.start()
        sent.append(copy)

    def arrived(n, dst, slot):
        copy_of(n, dst, dst, slot, device(y, core, z, x)).wait_recv()

    cols = b_ref.shape[-1]

    def columns(ref, start, count):
        return ref.at[:, :, pl.ds(start, count)]

    def extra_copy(slot):
        ref = columns(theirs[1].at[slot], cols, extra_ref.shape[-1])
        far = extra_ref.at[lax.rem(y + slot // RING, RING), 1 - core, lax.rem(z + slot % RING, RING)]
        return pltpu.make_async_remote_copy(
            src_ref=far, dst_ref=ref, send_sem=extra_send_sem.at[slot],
            recv_sem=extra_recv_sem.at[slot], device_id=device(y, 1 - core, z, x),
            device_id_type=MESH,
        )

    def extra_load(slot):
        near = extra_ref.at[lax.rem(y + slot // RING, RING), core, lax.rem(z + slot % RING, RING)]
        return pltpu.make_async_copy(
            near, columns(mine[1].at[slot], cols, extra_ref.shape[-1]), extra_load_sem.at[slot]
        )

    def load(n, di, dj):
        i, j = me[n]
        slot = di * RING + dj
        target = mine[n].at[slot] if n == 0 else columns(mine[n].at[slot], 0, cols)
        return pltpu.make_async_copy(
            chunk(n, lax.rem(i + di, RING), lax.rem(j + dj, RING), core), target,
            load_sem.at[n, slot],
        )

    for dj in ORDER:
        for di in ORDER:
            for n in (0, 1):
                i, j = me[n]
                slot = di * RING + dj
                there = chunk(n, lax.rem(i + di, RING), lax.rem(j + dj, RING), 1 - core)
                target = theirs[n].at[slot] if n == 0 else columns(theirs[n].at[slot], 0, cols)
                send(n, there, target, slot, device(y, 1 - core, z, x))
                load(n, di, dj).start()
                if n == 1:
                    extra_copy(slot).start()
                    extra_load(slot).start()

    def ready(n, di, dj):
        slot = di * RING + dj
        load(n, di, dj).wait()
        if n == 0:
            arrived(n, theirs[n].at[slot], slot)
        else:
            arrived(n, columns(theirs[n].at[slot], 0, cols), slot)
            extra_load(slot).wait()
            extra_copy(slot).wait_recv()
        return slot

    for di in ORDER:
        for n in (0, 1):
            i, j = me[n]
            slot = ready(n, di, 2)
            add_into(mine[n].at[slot], mine[n].at[slot], theirs[n].at[slot])
            for half in (0, 1):
                send(
                    n, mine[n].at[slot, half], one[n].at[di, half], 16 + di * 2 + half,
                    to(n, i, up(j) if half == 0 else down(j)),
                )
    for di in ORDER:
        for n in (0, 1):
            i, j = me[n]
            for half, dj in ((0, 1), (1, 3)):
                slot = ready(n, di, dj)
                arrived(n, one[n].at[di, half], 16 + di * 2 + half)
                add_into(
                    mine[n].at[slot, half], mine[n].at[slot, half], theirs[n].at[slot, half],
                    one[n].at[di, half],
                )
                add_into(
                    mine[n].at[slot, 1 - half], mine[n].at[slot, 1 - half],
                    theirs[n].at[slot, 1 - half],
                )
                send(
                    n, mine[n].at[slot], two[n].at[di, half], 24 + di * 2 + half,
                    to(n, i, up(j) if half == 0 else down(j)),
                )
    for di in ORDER:
        for n in (0, 1):
            i, j = me[n]
            slot = ready(n, di, 0)
            for half in (0, 1):
                arrived(n, two[n].at[di, half], 24 + di * 2 + half)
            add_into(
                mine[n].at[slot], mine[n].at[slot], theirs[n].at[slot], two[n].at[di, 0],
                two[n].at[di, 1],
            )
            if di == 2:
                for half in (0, 1):
                    send(
                        n, mine[n].at[slot, half], first[n].at[half], 32 + half,
                        to(n, up(i) if half == 0 else down(i), j),
                    )
            elif di != 0:
                half = 0 if di == 1 else 1
                arrived(n, first[n].at[half], 32 + half)
                add_into(mine[n].at[slot, half], mine[n].at[slot, half], first[n].at[half])
                send(
                    n, mine[n].at[slot], last[n].at[half], 34 + half,
                    to(n, up(i) if half == 0 else down(i), j),
                )
    for n in (0, 1):
        for half in (0, 1):
            arrived(n, last[n].at[half], 34 + half)
        add_into(mine[n].at[0], mine[n].at[0], last[n].at[0], last[n].at[1])
        send(n, mine[n].at[0, 1 - x], side[n], 36, device(y, core, z, 1 - x))
    for n in (0, 1):
        arrived(n, side[n], 36)
        add_into(outs[n], mine[n].at[0, x], side[n])
    gains_here[...] = b_out[:, cols:]
    gains = pltpu.make_async_remote_copy(
        src_ref=gains_here, dst_ref=gains_there, send_sem=gains_sem.at[0],
        recv_sem=gains_sem.at[1], device_id=other_tp(), device_id_type=MESH,
    )
    gains.start()
    for copy in sent:
        copy.wait_send()
    for slot in range(RING * RING):
        extra_copy(slot).wait_send()
    gains.wait()
    b_out[:, cols:] = gains_here[...] + gains_there[...]

    @pl.when(jnp.logical_not(native()))
    def _():
        for copy in moved:
            copy.wait()


def scatter_grads(a, b, extra, wide, tall):
    peers = RING * RING * 4
    rows = a.shape[0] // peers
    shape = (RING, 2, RING, 2, rows)
    cols = (a.shape[1], b.shape[1] + extra.shape[1])
    buffers = []
    for lead in ((16, 2), (16, 2), (4, 2), (4, 2, 2), (2,), (2, 2), ()):
        buffers += [pltpu.VMEM(lead + (rows, c), a.dtype) for c in cols]
    any_space = pl.BlockSpec(memory_space=pl.ANY)
    return pl.pallas_call(
        scatter_kernel,
        in_specs=[any_space] * 5,
        out_specs=[pl.BlockSpec(memory_space=pltpu.VMEM)] * 2 + [any_space] * 2,
        out_shape=[jax.ShapeDtypeStruct((rows, c), F32) for c in cols]
        + [jax.ShapeDtypeStruct(v.shape, v.dtype) for v in (wide, tall)],
        scratch_shapes=buffers + [
            pltpu.SemaphoreType.DMA((2, 16)),
            pltpu.SemaphoreType.DMA((2, 37)),
            pltpu.SemaphoreType.DMA((2, 37)),
            pltpu.VMEM((rows, extra.shape[1]), F32),
            pltpu.VMEM((rows, extra.shape[1]), F32),
            pltpu.SemaphoreType.DMA((16,)),
            pltpu.SemaphoreType.DMA((16,)),
            pltpu.SemaphoreType.DMA((16,)),
            pltpu.SemaphoreType.DMA((2,)),
            pltpu.SemaphoreType.DMA((2,)),
            pltpu.SemaphoreType.DMA((2,)),
        ],
        compiler_params=pltpu.CompilerParams(
            collective_id=1, has_side_effects=True, vmem_limit_bytes=44 * 1024 * 1024
        ),
        cost_estimate=pl.CostEstimate(flops=0, bytes_accessed=250_000_000, transcendentals=0),
        name="scatter_grads",
    )(*(v.reshape(shape + (v.shape[1],)) for v in (a, b, extra)), wide, tall)


BLOCK = 64
CTX = 8


def dot(a, b, dims):
    return lax.dot_general(a, b, (dims, ((), ())), preferred_element_type=F32)


def rotated(u, gain, cosine, sine):
    scaling = lax.rsqrt(jnp.mean(u * u, axis=-1, keepdims=True) + EPS)
    normed = u * scaling
    n = normed * gain
    rot = n * cosine + pltpu.roll(n, HEAD_SIZE // 2, 1) * sine
    return rot.astype(BF16), normed, scaling


def rotated_back(e, normed, scaling, gain, cosine, sine):
    back = e * cosine + pltpu.roll(e * sine, HEAD_SIZE // 2, 1)
    scaled = back * gain
    inner = jnp.mean(scaled * normed, axis=-1, keepdims=True)
    return scaling * (scaled - normed * inner), jnp.sum(back * normed, axis=0, keepdims=True)


def ctx_peer(step):
    return {"ctx": lax.rem(lax.axis_index("ctx") + step, CTX)}


def beside():
    c = lax.axis_index("ctx")
    return {"ctx": c + 1 - 2 * lax.rem(c, 2)}


def remote(src, dst, send_sem, recv_sem, where):
    return pltpu.make_async_remote_copy(
        src_ref=src, dst_ref=dst, send_sem=send_sem, recv_sem=recv_sem, device_id=where,
        device_id_type=MESH,
    )


def softmax_parts(q_low, k, bias):
    s = dot(q_low, k, ((1,), (1,))) * (HEAD_SIZE ** -0.5) + bias
    e = jnp.exp(s - jnp.max(s, axis=-1, keepdims=True))
    return e / jnp.sum(e, axis=-1, keepdims=True)


def share_kernel(kv, rows_ref, cos_ref, sin_ref, gk_ref, kv_ref, held, send_sem, recv_sem):
    c = lax.axis_index("ctx")
    greet([ctx_peer(step) for step in range(1, CTX)])
    micro, rows = held.shape[0], 2 * BLOCK
    cosine, sine, gk = cos_ref[...], sin_ref[...], gk_ref[...]
    mine = pl.ds(pl.multiple_of(c * BLOCK, BLOCK), BLOCK)
    earlier, own = pl.ds(CTX * BLOCK, BLOCK), pl.ds((CTX + 1) * BLOCK, BLOCK)
    copies = []
    for m in range(micro):
        span = slice(m * rows, (m + 1) * rows)
        for h in range(2 * kv):
            cols = slice(h * HEAD_SIZE, (h + 1) * HEAD_SIZE)
            u = rows_ref[span, cols]
            low = rotated(u, gk, cosine, sine)[0] if h < kv else u.astype(BF16)
            held[m, mine, cols] = low[:BLOCK]
            held[m, own, cols] = low[BLOCK:]
        for step in range(1, CTX):
            part = held.at[m, mine]
            copies.append(
                remote(part, part, send_sem.at[step, m], recv_sem.at[step, m], ctx_peer(step))
            )
        copies.append(
            remote(
                held.at[m, own], held.at[m, earlier], send_sem.at[0, m], recv_sem.at[0, m], beside()
            )
        )
        for copy in copies[-CTX:]:
            copy.start()
    for m in range(micro):
        for step in range(1, CTX):
            source = lax.rem(c + CTX - step, CTX)
            part = held.at[m, pl.ds(pl.multiple_of(source * BLOCK, BLOCK), BLOCK)]
            remote(
                part, part, send_sem.at[step, m], recv_sem.at[step, m], ctx_peer(step)
            ).wait_recv()
        copies[(m + 1) * CTX - 1].wait_recv()
        kv_ref[m] = held[m]
    for copy in copies:
        copy.wait_send()


def attention_kernel(heads, q_ref, cos_ref, sin_ref, gq_ref, bias_ref, k_ref, v_ref, o_ref):
    cosine, sine, gq = cos_ref[...], sin_ref[...], gq_ref[...]
    for e in range(heads):
        cols = slice(e * HEAD_SIZE, (e + 1) * HEAD_SIZE)
        q_low = rotated(q_ref[:, cols], gq, cosine, sine)[0]
        p = softmax_parts(q_low, k_ref[...], bias_ref[...]).astype(BF16)
        o_ref[:, cols] = dot(p, v_ref[...], ((1,), (0,))).astype(BF16)


def attention_back_kernel(
    kv, heads, qkv_ref, cos_ref, sin_ref, gq_ref, gk_ref, bias_ref, kv_ref, do_ref,
    dqkv_ref, gains_ref, grads, given, given_side, p_all, ds_all, q_all, do_all,
    send_sem, recv_sem,
):
    c = lax.axis_index("ctx")
    greet([ctx_peer(step) for step in range(1, CTX)])
    micro, rows = grads.shape[0], 2 * BLOCK
    q_cols = kv * heads * HEAD_SIZE
    scale = HEAD_SIZE ** -0.5
    cosine, sine, gq, gk = cos_ref[...], sin_ref[...], gq_ref[...], gk_ref[...]
    mine = pl.ds(pl.multiple_of(c * BLOCK, BLOCK), BLOCK)
    earlier, own = pl.ds(CTX * BLOCK, BLOCK), pl.ds((CTX + 1) * BLOCK, BLOCK)

    def group(m, h, total):
        span = slice(m * rows, (m + 1) * rows)
        k_cols = pl.ds(pl.multiple_of(h * HEAD_SIZE, HEAD_SIZE), HEAD_SIZE)
        v_cols = pl.ds(pl.multiple_of((kv + h) * HEAD_SIZE, HEAD_SIZE), HEAD_SIZE)
        k, v = kv_ref[m, :, k_cols], kv_ref[m, :, v_cols]
        for e in range(heads):
            cols = pl.ds(pl.multiple_of((h * heads + e) * HEAD_SIZE, HEAD_SIZE), HEAD_SIZE)
            stack = slice(e * rows, (e + 1) * rows)
            q_low, normed, scaling = rotated(qkv_ref[span, cols], gq, cosine, sine)
            q_all[stack, :] = q_low
            p = softmax_parts(q_low, k, bias_ref[...])
            p_all[stack, :] = p.astype(BF16)
            do = do_ref[span, cols]
            do_all[stack, :] = do
            dp = dot(do, v, ((1,), (1,)))
            ds = (p * (dp - jnp.sum(dp * p, axis=-1, keepdims=True))).astype(BF16)
            ds_all[stack, :] = ds
            dqr = (dot(ds, k, ((1,), (0,))) * scale).astype(BF16).astype(F32)
            dq, part = rotated_back(dqr, normed, scaling, gq, cosine, sine)
            dqkv_ref[span, cols] = dq.astype(BF16)
            total = total + part
        grads[m, :, v_cols] = dot(p_all[...], do_all[...], ((0,), (0,))).astype(BF16)
        grads[m, :, k_cols] = (dot(ds_all[...], q_all[...], ((0,), (0,))) * scale).astype(BF16)
        return total

    total = jnp.zeros((1, HEAD_SIZE), F32)
    copies = []
    for m in range(micro):
        total = lax.fori_loop(0, kv, functools.partial(group, m), total)
        for step in range(1, CTX):
            peer = lax.rem(c + step, CTX)
            part = grads.at[m, pl.ds(pl.multiple_of(peer * BLOCK, BLOCK), BLOCK)]
            copies.append(
                remote(
                    part, given.at[step - 1, m], send_sem.at[step, m], recv_sem.at[step, m],
                    ctx_peer(step),
                )
            )
        copies.append(
            remote(
                grads.at[m, earlier], given_side.at[m], send_sem.at[0, m], recv_sem.at[0, m],
                beside(),
            )
        )
        for copy in copies[-CTX:]:
            copy.start()
    k_total = jnp.zeros((1, HEAD_SIZE), F32)
    for m in range(micro):
        for copy in copies[m * CTX : (m + 1) * CTX]:
            copy.wait_recv()
        for h in range(2 * kv):
            cols = slice(h * HEAD_SIZE, (h + 1) * HEAD_SIZE)
            at = slice(q_cols + h * HEAD_SIZE, q_cols + (h + 1) * HEAD_SIZE)
            prompt = grads[m, mine, cols].astype(F32)
            for step in range(CTX - 1):
                prompt = prompt + given[step, m, :, cols].astype(F32)
            cont = grads[m, own, cols].astype(F32) + given_side[m, :, cols].astype(F32)
            e = jnp.concatenate([prompt, cont], axis=0).astype(BF16)
            span = slice(m * rows, (m + 1) * rows)
            if h < kv:
                _, normed, scaling = rotated(qkv_ref[span, at], gk, cosine, sine)
                d, part = rotated_back(e.astype(F32), normed, scaling, gk, cosine, sine)
                k_total = k_total + part
                dqkv_ref[span, at] = d.astype(BF16)
            else:
                dqkv_ref[span, at] = e
    gains_ref[0:1, :] = total
    gains_ref[1:2, :] = k_total
    for copy in copies:
        copy.wait_send()


def share_keys(qkv, cosine, sine, gain_key, kv, keys, micro):
    rows, cols = qkv.shape[0], 2 * kv * HEAD_SIZE
    last = qkv.shape[1] // cols - 1

    def whole(shape):
        return pl.BlockSpec(shape, lambda i: (0,) * len(shape))

    return pl.pallas_call(
        functools.partial(share_kernel, kv),
        grid=(1,),
        in_specs=[pl.BlockSpec((rows, cols), lambda i: (0, last)), whole(cosine.shape)]
        + [whole(sine.shape), whole(gain_key.shape)],
        out_specs=whole((micro, keys, cols)),
        out_shape=jax.ShapeDtypeStruct((micro, keys, cols), BF16),
        scratch_shapes=[
            pltpu.VMEM((micro, keys, cols), BF16),
            pltpu.SemaphoreType.DMA((CTX, micro)),
            pltpu.SemaphoreType.DMA((CTX, micro)),
        ],
        compiler_params=pltpu.CompilerParams(
            collective_id=2, has_side_effects=True, vmem_limit_bytes=VMEM_LIMIT
        ),
        cost_estimate=pl.CostEstimate(flops=0, bytes_accessed=50_000_000, transcendentals=0),
        name="share_keys",
    )(qkv, cosine, sine, gain_key)


def attention(qkv, cosine, sine, gain_query, bias, kv_all, kv):
    micro, keys, cols = kv_all.shape
    rows = bias.shape[0]
    heads = qkv.shape[1] // HEAD_SIZE // kv - 2
    width = heads * HEAD_SIZE

    def whole(v):
        return pl.BlockSpec(v.shape, lambda m, g: (0,) * v.ndim)

    return pl.pallas_call(
        functools.partial(attention_kernel, heads),
        grid=(micro, kv),
        in_specs=[pl.BlockSpec((rows, width), lambda m, g: (m, g))]
        + [whole(v) for v in (cosine, sine, gain_query, bias)]
        + [
            pl.BlockSpec((None, keys, HEAD_SIZE), lambda m, g: (m, 0, g)),
            pl.BlockSpec((None, keys, HEAD_SIZE), lambda m, g: (m, 0, kv + g)),
        ],
        out_specs=pl.BlockSpec((rows, width), lambda m, g: (m, g)),
        out_shape=jax.ShapeDtypeStruct((micro * rows, kv * width), BF16),
        compiler_params=pltpu.CompilerParams(vmem_limit_bytes=VMEM_LIMIT),
        cost_estimate=pl.CostEstimate(flops=0, bytes_accessed=60_000_000, transcendentals=0),
        name="attention_forward",
    )(qkv, cosine, sine, gain_query, bias, kv_all, kv_all)


def attention_back(qkv, cosine, sine, gain_query, gain_key, bias, kv_all, d_out, kv):
    heads = qkv.shape[1] // HEAD_SIZE // kv - 2
    rows, keys = bias.shape
    micro, _, kv_cols = kv_all.shape
    return pl.pallas_call(
        functools.partial(attention_back_kernel, kv, heads),
        out_shape=[
            jax.ShapeDtypeStruct(qkv.shape, BF16),
            jax.ShapeDtypeStruct((2, HEAD_SIZE), F32),
        ],
        scratch_shapes=[
            pltpu.VMEM((micro, keys, kv_cols), BF16),
            pltpu.VMEM((CTX - 1, micro, BLOCK, kv_cols), BF16),
            pltpu.VMEM((micro, BLOCK, kv_cols), BF16),
            pltpu.VMEM((heads * rows, keys), BF16),
            pltpu.VMEM((heads * rows, keys), BF16),
            pltpu.VMEM((heads * rows, HEAD_SIZE), BF16),
            pltpu.VMEM((heads * rows, HEAD_SIZE), BF16),
            pltpu.SemaphoreType.DMA((CTX, micro)),
            pltpu.SemaphoreType.DMA((CTX, micro)),
        ],
        compiler_params=pltpu.CompilerParams(
            collective_id=3, has_side_effects=True, vmem_limit_bytes=VMEM_LIMIT
        ),
        cost_estimate=pl.CostEstimate(flops=0, bytes_accessed=120_000_000, transcendentals=0),
        name="attention_backward",
    )(qkv, cosine, sine, gain_query, gain_key, bias, kv_all, d_out)


PART = 256


def other_core():
    f = lax.axis_index("fsdp")
    return {"fsdp": f + 1 - 2 * (f % 2)}


def expert_kernel(
    got_ref, deo_ref, gate_ref, up_ref, down_ref, gate_far, up_far, down_far, back_ref, eo_ref, rows_ref, deos_ref, z_ref, dgu_ref,
    rows, deos, gu, down, own, give, take, load_sem, send_sem, recv_sem, save_sem,
):
    greet([other_core()])
    count, hidden = got_ref.shape[0], down_ref.shape[0]
    parts = count // PART
    near, far = pl.ds(0, count), pl.ds(count, count)
    swaps = [
        remote(got_ref, rows.at[far], send_sem.at[0], recv_sem.at[0], other_core()),
        remote(deo_ref, deos.at[far], send_sem.at[1], recv_sem.at[1], other_core()),
    ]
    loads = [
        pltpu.make_async_copy(got_ref, rows.at[near], load_sem.at[0]),
        pltpu.make_async_copy(deo_ref, deos.at[near], load_sem.at[1]),
    ]
    places = (gu.at[:, pl.ds(0, hidden)], gu.at[:, pl.ds(hidden, hidden)], down)
    weights = [
        [pltpu.make_async_copy(src, dst, load_sem.at[2 + n]) for n, (src, dst) in enumerate(pairs)]
        for pairs in (
            zip((gate_ref, up_ref, down_ref), places), zip((gate_far, up_far, down_far), places)
        )
    ]

    def on_weights(act):
        for condition, copies in zip((native(), jnp.logical_not(native())), weights):

            @pl.when(condition)
            def _(copies=copies):
                for copy in copies:
                    act(copy)

    saves = [
        pltpu.make_async_copy(rows, rows_ref, save_sem.at[0]),
        pltpu.make_async_copy(deos, deos_ref, save_sem.at[1]),
    ]
    for copy in loads + swaps:
        copy.start()
    on_weights(lambda copy: copy.start())

    def span(i):
        return pl.ds(pl.multiple_of(i * PART, PART), PART)

    def returned(kind, i):
        slot = kind * parts + i
        return remote(
            give.at[kind, span(i)], take.at[kind, span(i)], send_sem.at[2 + slot],
            recv_sem.at[2 + slot], other_core(),
        )

    def through(i):
        pre = dot(rows[span(i), :], gu[...], ((1,), (0,)))
        dz = dot(deos[span(i), :], down[...], ((1,), (1,)))
        g, u = pre[:, :hidden], pre[:, hidden:]
        sig = 1.0 / (1.0 + jnp.exp(-g))
        act = g * sig
        z_ref[span(i), :] = (act * u).astype(BF16)
        dgu_ref[span(i), :hidden] = (dz * u * sig * (1.0 + g * (1.0 - sig))).astype(BF16)
        dgu_ref[span(i), hidden:] = (dz * act).astype(BF16)

    def to_rows(i):
        return dot(dgu_ref[span(i), :], gu[...], ((1,), (1,)))

    def to_outputs(i):
        return dot(z_ref[span(i), :], down[...], ((1,), (0,)))

    def each(body):
        def step(i, carry):
            body(i)
            return carry

        lax.fori_loop(0, parts, step, 0)

    def give_rows(i):
        through(parts + i)
        give[0, span(i), :] = to_rows(parts + i).astype(BF16)
        returned(0, i).start()

    def keep_rows(i):
        own[span(i), :] = to_rows(i)

    def give_outputs(i):
        give[1, span(i), :] = to_outputs(parts + i).astype(BF16)
        returned(1, i).start()

    def end_rows(i):
        returned(0, i).wait()
        back_ref[span(i), :] = (own[span(i), :] + take[0, span(i), :].astype(F32)).astype(BF16)

    def end_outputs(i):
        total = to_outputs(i)
        returned(1, i).wait()
        eo_ref[span(i), :] = (total + take[1, span(i), :].astype(F32)).astype(BF16)

    for copy in loads:
        copy.wait()
    on_weights(lambda copy: copy.wait())
    each(through)
    for copy in swaps:
        copy.wait_recv()
    for copy in saves:
        copy.start()
    each(give_rows)
    each(give_outputs)
    each(keep_rows)
    each(end_rows)
    each(end_outputs)
    for copy in swaps:
        copy.wait_send()
    for copy in saves:
        copy.wait()


def expert(got, d_eo, own, far, collective):
    count, width = got.shape
    hidden = own[2].shape[0]
    parts = count // PART
    vmem, any_space = (pl.BlockSpec(memory_space=space) for space in (pltpu.VMEM, pl.ANY))
    shapes = [(count, width), (count, width), (2 * count, width), (2 * count, width)]
    shapes += [(2 * count, hidden), (2 * count, 2 * hidden)]
    return pl.pallas_call(
        expert_kernel,
        in_specs=[any_space] * 8,
        out_specs=[vmem] * 2 + [any_space] * 2 + [vmem] * 2,
        out_shape=[jax.ShapeDtypeStruct(shape, BF16) for shape in shapes],
        scratch_shapes=[
            pltpu.VMEM((2 * count, width), BF16),
            pltpu.VMEM((2 * count, width), BF16),
            pltpu.VMEM((width, 2 * hidden), BF16),
            pltpu.VMEM((hidden, width), BF16),
            pltpu.VMEM((count, width), F32),
            pltpu.VMEM((2, count, width), BF16),
            pltpu.VMEM((2, count, width), BF16),
            pltpu.SemaphoreType.DMA((5,)),
            pltpu.SemaphoreType.DMA((2 + 2 * parts,)),
            pltpu.SemaphoreType.DMA((2 + 2 * parts,)),
            pltpu.SemaphoreType.DMA((2,)),
        ],
        compiler_params=pltpu.CompilerParams(
            collective_id=collective, has_side_effects=True, vmem_limit_bytes=VMEM_LIMIT
        ),
        cost_estimate=pl.CostEstimate(flops=0, bytes_accessed=80_000_000, transcendentals=0),
        name="expert_both_ways",
    )(got, d_eo, *own, *far)


def normalize(rows, gain):
    scaling = lax.rsqrt(jnp.mean(rows * rows, axis=-1, keepdims=True) + EPS)
    return rows * scaling * gain, scaling


def normalize_back(rows, scaling, gain, upstream):
    normed = rows * scaling
    gain_grad = jnp.sum((upstream * normed).reshape(-1, rows.shape[-1]), axis=0)
    scaled = upstream * gain
    inner = jnp.mean(scaled * normed, axis=-1, keepdims=True)
    return scaling * (scaled - normed * inner), gain_grad


def swap_tp(value):
    return lax.ppermute(value, "tp", [(0, 1), (1, 0)])


def local(
    x_prompt, x_cont, cot_prompt, cot_cont, ids_prompt, ids_cont, gates_prompt, gates_cont,
    norm_gain, query_weight, key_matrix, value_matrix, out_weight, query_gain, key_gain, moe_gain,
    expert_gate, expert_up, expert_down,
):
    micro = x_prompt.shape[0]
    prompt_rows, cont_rows, width = x_prompt.shape[2], x_cont.shape[2], x_prompt.shape[3]
    block = cont_rows
    rows = 2 * block
    s = lax.axis_index("ctx")
    ctx = lax.axis_size("ctx")
    first = lax.axis_index("tp") == 0
    peers = lax.axis_size(ALL)
    q_cols, kv_cols = query_weight.shape[1], key_matrix.shape[1]
    kv = kv_cols // HEAD_SIZE
    qkv_cols = q_cols + 2 * kv_cols
    shard_rows = query_weight.shape[0]
    hidden = expert_gate.shape[2]
    slots = cont_rows * TOPK // peers

    fsdp, tp = lax.axis_size("fsdp"), lax.axis_size("tp")
    chips = [(2 * y, c, t) for y in range(fsdp // 2) for c in range(ctx) for t in range(tp)]
    groups = [[((f + core) * ctx + c) * tp + t for f, c, t in chips] for core in range(2)]
    expert_of = jnp.array([(f + t) * ctx + c for f, c, t in chips], jnp.int32)

    def exchange(rows_of):
        return lax.all_to_all(
            rows_of, ("fsdp", "ctx", "tp"), split_axis=0, concat_axis=0, tiled=True,
            axis_index_groups=groups,
        )

    def pad(v):
        return jnp.pad(v[:, 0], ((0, 0), (0, block - prompt_rows), (0, 0)))

    x_first, x_second = pad(x_prompt), x_cont[:, 0]
    own_tokens = jnp.where(first, x_second, x_first).astype(F32)
    own_cot = jnp.where(first, cot_cont[:, 0], pad(cot_prompt)).astype(F32)
    ids_pad = jnp.pad(
        ids_prompt[:, 0], ((0, 0), (0, block - prompt_rows), (0, 0)), constant_values=-1
    )
    own_ids = jnp.where(first, ids_cont[:, 0], ids_pad)
    own_gates = jnp.where(first, gates_cont[:, 0], pad(gates_prompt))

    named = own_ids[:, :, :, None] == expert_of
    chosen = jnp.any(named, axis=2)
    weight = jnp.sum(jnp.where(named, own_gates[:, :, :, None], 0.0), axis=2)
    lower = jnp.tril(jnp.ones((block, block), BF16), -1)
    rank = jnp.einsum("ts,mse->mte", lower, chosen.astype(BF16), preferred_element_type=F32)
    place = jnp.where(chosen, rank, -1.0)
    placed = place[:, :, :, None] == jnp.arange(slots, dtype=F32)
    select = placed.astype(BF16).reshape(micro, block, peers * slots)
    same = jnp.arange(micro)[:, None] == jnp.arange(micro)[None, :]
    both = jnp.logical_and(placed[:, :, :, None, :], same[:, None, None, :, None])
    flat = (micro * block, peers * micro * slots)
    select_both = both.astype(BF16).reshape(flat)
    mixing = jnp.where(placed, weight[:, :, :, None], 0.0).reshape(select.shape)
    mixing_high = mixing.astype(BF16)
    mixing_low = (mixing - mixing_high.astype(F32)).astype(BF16)
    slot_gate = jnp.sum(mixing, axis=1).reshape(micro, peers, slots).swapaxes(0, 1).reshape(-1)

    extra = jnp.concatenate(
        [
            norm_gain[:, None],
            moe_gain[:, None],
            jnp.pad(query_gain, (0, shard_rows - query_gain.shape[0]))[:, None],
            jnp.pad(key_gain, (0, shard_rows - key_gain.shape[0]))[:, None],
            jnp.zeros((shard_rows, 124), BF16),
        ],
        axis=1,
    )
    w_qkv, w_out_extra, *far_experts = gather_weights(
        jnp.concatenate([query_weight, key_matrix, value_matrix], axis=1),
        jnp.concatenate([out_weight, extra], axis=1),
        expert_gate[0],
        expert_up[0],
        expert_down[0],
    )
    w_out = w_out_extra[:, :q_cols]
    gains = w_out_extra[:, q_cols:].astype(F32)
    gain_in, gain_moe = gains[:, 0], gains[:, 1]
    head_gains = gains[:, 2:4].reshape(peers, shard_rows, 2)[:, : query_gain.shape[0]]
    head_gains = head_gains.reshape(HEAD_SIZE, 2)
    gain_query, gain_key = head_gains[:, 0], head_gains[:, 1]

    offsets = jnp.arange(rows, dtype=jnp.int32)
    is_prompt = offsets < block
    prompt_pos = s * prompt_rows + offsets
    cont_pos = s * cont_rows + offsets - block
    rot_place = jnp.where(is_prompt, prompt_pos, PROMPT + cont_pos % CL).astype(F32)
    steps_freq = jnp.arange(HEAD_SIZE // 2, dtype=F32) * (2.0 / HEAD_SIZE)
    angles = rot_place[:, None] * jnp.power(THETA, -steps_freq)[None, :]
    cosine, sine = jnp.cos(angles), jnp.sin(angles)
    cosine = jnp.concatenate([cosine, cosine], axis=1)
    sine = jnp.concatenate([-sine, sine], axis=1)
    keys = (ctx + 2) * block
    key_index = jnp.arange(keys, dtype=jnp.int32)[None, :]
    key_off = key_index % block
    key_prompt_pos = key_index // block * prompt_rows + key_off
    key_cont = (s - 1) * cont_rows + key_index - ctx * block
    is_cont = jnp.logical_not(is_prompt)[:, None]
    visible = jnp.where(
        key_index < ctx * block,
        jnp.logical_and(
            key_off < prompt_rows,
            jnp.logical_or(is_cont, key_prompt_pos <= prompt_pos[:, None]),
        ),
        jnp.logical_and(
            is_cont,
            jnp.logical_and(
                key_cont // CL == cont_pos[:, None] // CL, key_cont <= cont_pos[:, None]
            ),
        ),
    )
    bias = jnp.where(visible, 0.0, NEG).astype(F32)

    def share_rows(own):
        other = swap_tp(own)
        return jnp.where(first, other, own), jnp.where(first, own, other)

    def sum_own(part):
        part = part.reshape(micro, rows, width)
        given = jnp.where(first, part[:, :block], part[:, block:]).astype(BF16)
        kept = jnp.where(first, part[:, block:], part[:, :block])
        return kept + swap_tp(given).astype(F32)

    tokens = jnp.concatenate([x_first, x_second], axis=1).astype(F32).reshape(-1, width)
    a = normalize(tokens, gain_in)[0].astype(BF16)
    qkv = dot(a, w_qkv, ((1,), (0,)))
    heads_in = (cosine, sine, gain_query[None], gain_key[None], bias)
    kv_all = share_keys(qkv, cosine, sine, gain_key[None], kv, keys, micro)

    spread = dot(select_both, own_cot.astype(BF16).reshape(-1, width), ((0,), (0,)))
    spread = (spread * slot_gate[:, None]).astype(BF16)
    spread, kv_all = lax.optimization_barrier((spread, kv_all))
    d_eo_rows = exchange(spread)
    o = attention(qkv, cosine, sine, gain_query[None], bias, kv_all, kv)
    middle = own_tokens + sum_own(dot(o, w_out, ((1,), (1,))))
    b_normed, b_scale = normalize(middle, gain_moe)
    b_low = b_normed.astype(BF16)

    b_low, d_eo_rows = lax.optimization_barrier((b_low, d_eo_rows))
    d_eo_rows = d_eo_rows.reshape(peers, micro, slots, width)
    backs, outputs, wide_terms, tall_terms = [], [], [], []
    for m in range(micro):
        got = exchange(dot(select[m], b_low[m], ((0,), (0,))).astype(BF16))
        back, eo, rows_m, d_eo_m, z_m, d_gu_m = expert(
            got, d_eo_rows[:, m].reshape(-1, width), (expert_gate[0], expert_up[0], expert_down[0]),
            far_experts, 4 + m,
        )
        backs.append(exchange(back))
        outputs.append(eo)
        wide_terms.append((rows_m, d_gu_m))
        tall_terms.append((z_m, d_eo_m))

    def over_rows(terms):
        return sum(dot(left, right, ((0,), (0,))) for left, right in terms).astype(BF16)

    wide_here, tall_here = over_rows(wide_terms), over_rows(tall_terms)

    d_b = jnp.stack([dot(select[m], backs[m], ((1,), (0,))) for m in range(micro)])
    middle_from, moe_total = normalize_back(middle, b_scale, gain_moe, d_b)
    d_h = own_cot + middle_from
    d_attn = jnp.concatenate(share_rows(d_h.astype(BF16)), axis=1).reshape(-1, width)

    late, d_attn = lax.optimization_barrier((outputs[0], d_attn))
    eo_back = [exchange(late)]

    d_o = dot(d_attn, w_out, ((1,), (0,))).astype(BF16)
    grad_out = dot(d_attn, o, ((0,), (0,))).astype(BF16)
    d_qkv, head_totals = attention_back(qkv, *heads_in, kv_all, d_o, kv)
    for m in range(1, micro):
        late, d_qkv, eo_back[m - 1] = lax.optimization_barrier((outputs[m], d_qkv, eo_back[m - 1]))
        eo_back.append(exchange(late))
    moe_out = [
        dot(high, eo, ((1,), (0,))) + dot(low, eo, ((1,), (0,)))
        for high, low, eo in zip(mixing_high, mixing_low, eo_back)
    ]
    out_first, out_second = share_rows((middle + jnp.stack(moe_out)).astype(BF16))
    input_grad = sum_own(dot(d_qkv, w_qkv, ((1,), (1,))))
    grad_qkv = dot(a, d_qkv, ((0,), (0,))).astype(BF16)
    scale_in = lax.rsqrt(jnp.mean(own_tokens * own_tokens, axis=-1, keepdims=True) + EPS)
    token_from, norm_total = normalize_back(own_tokens, scale_in, gain_in, input_grad)
    grad_first, grad_second = share_rows((d_h + token_from).astype(BF16))

    head_grads = head_totals.T.reshape(peers, -1, 2)
    head_grads = jnp.pad(head_grads, ((0, 0), (0, shard_rows - head_grads.shape[1]), (0, 0)))
    extra_grads = jnp.concatenate(
        [
            norm_total[:, None],
            moe_total[:, None],
            head_grads.reshape(-1, 2),
            jnp.zeros((peers * shard_rows, 124), F32),
        ],
        axis=1,
    ).astype(BF16)
    grad_qkv, out_first, out_second = lax.optimization_barrier((grad_qkv, out_first, out_second))
    share, share_out, wide_there, tall_there = scatter_grads(
        grad_qkv, grad_out, extra_grads, wide_here, tall_here
    )
    grad_wide = jnp.where(native(), wide_here, wide_there).astype(F32)
    grad_down = jnp.where(native(), tall_here, tall_there).astype(F32)
    gain_share = share_out[:, q_cols:]
    head_rows = query_gain.shape[0]

    return (
        out_first[:, None, :prompt_rows],
        out_second[:, None],
        grad_first[:, None, :prompt_rows],
        grad_second[:, None],
        gain_share[:, 0],
        share[:, :q_cols],
        share[:, q_cols : q_cols + kv_cols],
        share[:, q_cols + kv_cols : qkv_cols],
        share_out[:, :q_cols],
        gain_share[:head_rows, 2],
        gain_share[:head_rows, 3],
        gain_share[:, 1],
        grad_wide[None, :, :hidden],
        grad_wide[None, :, hidden:],
        grad_down[None],
    )


def solution(mesh):
    rows = P(None, "fsdp", "ctx", None)
    vector = P(("fsdp", "ctx"))
    matrix = P(("fsdp", "ctx"), "tp")
    wide = P(("fsdp", "ctx"), None, "tp")
    tall = P(("fsdp", "ctx"), "tp", None)
    in_specs = (rows,) * 8 + (vector,) + (matrix,) * 4 + (vector,) * 3 + (wide, wide, tall)
    out_specs = (rows,) * 4 + (vector,) + (matrix,) * 4 + (vector,) * 3 + (wide, wide, tall)
    return jax.shard_map(local, mesh=mesh, in_specs=in_specs, out_specs=out_specs, check_vma=False)
```

```python
import functools

import jax
import jax.numpy as jnp
from jax import lax
from jax.experimental import pallas as pl
from jax.experimental.pallas import tpu as pltpu
from jax.sharding import PartitionSpec as P

HEAD_SIZE = 128
TOPK = 8
PROMPT = 448
CL = 128
EPS = 1e-06
THETA = 1000000.0
NEG = -1e30
F32 = jnp.float32
BF16 = jnp.bfloat16
ALL = ("fsdp", "ctx")
MESH = pl.DeviceIdType.MESH
RING = 4
VMEM_LIMIT = 48 * 1024 * 1024


def place():
    f, c = lax.axis_index("fsdp"), lax.axis_index("ctx")
    return f // 2, f % 2, c // 2, c % 2


def device(y, core, z, x):
    return {"fsdp": y * 2 + core, "ctx": z * 2 + x}


def greet(partners):
    barrier = pltpu.get_barrier_semaphore()
    for partner in partners:
        pl.semaphore_signal(barrier, inc=1, device_id=partner, device_id_type=MESH)
    pl.semaphore_wait(barrier, len(partners))


def neighbours():
    y, core, z, x = place()
    up, down = (lambda v: lax.rem(v + 1, RING)), (lambda v: lax.rem(v + RING - 1, RING))
    return [
        device(y, core, z, 1 - x),
        device(y, 1 - core, z, x),
        device(up(y), core, z, x),
        device(down(y), core, z, x),
        device(y, core, up(z), x),
        device(y, core, down(z), x),
    ]


def other_tp():
    return {"tp": 1 - lax.axis_index("tp")}


def opposite():
    f = lax.axis_index("fsdp")
    return {"fsdp": f + 1 - 2 * (f % 2), "tp": 1 - lax.axis_index("tp")}


def native():
    return lax.axis_index("fsdp") % 2 == lax.axis_index("tp")


def swap_opposite(src, dst, send_sem, recv_sem):
    return pltpu.make_async_remote_copy(
        src_ref=src, dst_ref=dst, send_sem=send_sem, recv_sem=recv_sem, device_id=opposite(),
        device_id_type=MESH,
    )


def gather_kernel(
    query_ref, key_ref, value_ref, out_ref, extra_ref, gate_ref, up_ref, down_ref,
    a_all, b_all, gate_all, up_all, down_all, a_own, b_own, local_sem, send_sem, recv_sem, away_sem, home_sem, give_sem, take_sem,
):
    y, core, z, x = place()
    for own, refs in ((a_own, (query_ref, key_ref, value_ref)), (b_own, (out_ref, extra_ref))):
        at = 0
        for ref in refs:
            own[:, at : at + ref.shape[1]] = ref[...]
            at += ref.shape[1]
    greet(neighbours() + [opposite()])
    shards = ((gate_ref, gate_all), (up_ref, up_all), (down_ref, down_all))
    moved = [
        swap_opposite(p, q, give_sem.at[n], take_sem.at[n]) for n, (p, q) in enumerate(shards)
    ]
    refs, own = (a_all, b_all), (a_own, b_own)
    started = []
    count = [0, 0]

    def chunk(n, i, j):
        return refs[n].at[j, core, i] if n == 0 else refs[n].at[i, core, j]

    def to(n, first, second):
        return device(second, core, first, x) if n == 0 else device(first, core, second, x)

    def send(n, ref, where, slot):
        copy = pltpu.make_async_remote_copy(
            src_ref=ref, dst_ref=ref, send_sem=send_sem.at[n, slot], recv_sem=recv_sem.at[n, slot],
            device_id=where, device_id_type=MESH,
        )
        copy.start()
        started.append(copy)

    def arrived(n, ref, slot):
        pltpu.make_async_remote_copy(
            src_ref=ref, dst_ref=ref, send_sem=send_sem.at[n, slot], recv_sem=recv_sem.at[n, slot],
            device_id=device(y, core, z, x), device_id_type=MESH,
        ).wait_recv()

    homes = []

    def across(n, i, j):
        slot = count[n]
        count[n] += 1
        ref = chunk(n, i, j)
        copy = pltpu.make_async_remote_copy(
            src_ref=ref, dst_ref=ref, send_sem=away_sem.at[n, slot], recv_sem=home_sem.at[n, slot],
            device_id=device(y, 1 - core, z, x), device_id_type=MESH,
        )
        copy.start()
        homes.append(copy)

    def second(n, i, j, k):
        base = 5 + 4 * k
        send(n, chunk(n, i, j), to(n, me[n][0], up(j)), base)
        send(n, chunk(n, i, j), to(n, me[n][0], down(j)), base + 1)
        across(n, i, j)

    up, down = (lambda v: lax.rem(v + 1, RING)), (lambda v: lax.rem(v + RING - 1, RING))
    me = ((z, y), (y, z))
    locals_ = []
    for n in (0, 1):
        i, j = me[n]
        keep = pltpu.make_async_copy(own[n], chunk(n, i, j).at[x], local_sem.at[n])
        keep.start()
        locals_.append(keep)
        copy = pltpu.make_async_remote_copy(
            src_ref=own[n], dst_ref=chunk(n, i, j).at[x], send_sem=send_sem.at[n, 0],
            recv_sem=recv_sem.at[n, 0], device_id=device(y, core, z, 1 - x), device_id_type=MESH,
        )
        copy.start()
        started.append(copy)
    for n in (0, 1):
        i, j = me[n]
        locals_[n].wait()
        arrived(n, chunk(n, i, j).at[1 - x], 0)
        send(n, chunk(n, i, j), to(n, up(i), j), 1)
        send(n, chunk(n, i, j), to(n, down(i), j), 2)
    for n in (0, 1):
        i, j = me[n]
        second(n, i, j, 0)

    @pl.when(jnp.logical_not(native()))
    def _():
        for copy in moved:
            copy.start()

    for n in (0, 1):
        i, j = me[n]
        arrived(n, chunk(n, down(i), j), 1)
        send(n, chunk(n, down(i), j).at[0], to(n, up(i), j), 3)
        second(n, down(i), j, 1)
    for n in (0, 1):
        i, j = me[n]
        arrived(n, chunk(n, up(i), j), 2)
        send(n, chunk(n, up(i), j).at[1], to(n, down(i), j), 4)
        second(n, up(i), j, 2)
    for n in (0, 1):
        i, j = me[n]
        far = lax.rem(i + 2, RING)
        arrived(n, chunk(n, far, j).at[0], 3)
        arrived(n, chunk(n, far, j).at[1], 4)
        second(n, far, j, 3)
    for k in range(4):
        for n in (0, 1):
            i, j = me[n]
            it = (i, down(i), up(i), lax.rem(i + 2, RING))[k]
            base = 5 + 4 * k
            arrived(n, chunk(n, it, down(j)), base)
            send(n, chunk(n, it, down(j)).at[0], to(n, i, up(j)), base + 2)
            across(n, it, down(j))
            arrived(n, chunk(n, it, up(j)), base + 1)
            send(n, chunk(n, it, up(j)).at[1], to(n, i, down(j)), base + 3)
            across(n, it, up(j))
    for k in range(4):
        for n in (0, 1):
            i, j = me[n]
            it = (i, down(i), up(i), lax.rem(i + 2, RING))[k]
            base = 5 + 4 * k
            far = lax.rem(j + 2, RING)
            arrived(n, chunk(n, it, far).at[0], base + 2)
            arrived(n, chunk(n, it, far).at[1], base + 3)
            across(n, it, far)
    for copy in homes:
        copy.wait()
    for copy in started:
        copy.wait_send()

    @pl.when(jnp.logical_not(native()))
    def _():
        for copy in moved:
            copy.wait()


def gather_weights(query, key, value, out, extra, gate, up, down):
    rows = query.shape[0]
    cols = (query.shape[1] + key.shape[1] + value.shape[1], out.shape[1] + extra.shape[1])
    shape = (RING, 2, RING, 2, rows)
    any_space = pl.BlockSpec(memory_space=pl.ANY)
    a_all, b_all, *experts = pl.pallas_call(
        gather_kernel,
        in_specs=[pl.BlockSpec(memory_space=pltpu.VMEM)] * 5 + [any_space] * 3,
        out_specs=[any_space] * 5,
        out_shape=[jax.ShapeDtypeStruct(shape + (c,), query.dtype) for c in cols]
        + [jax.ShapeDtypeStruct(v.shape, v.dtype) for v in (gate, up, down)],
        scratch_shapes=[pltpu.VMEM((rows, c), query.dtype) for c in cols] + [
            pltpu.SemaphoreType.DMA((2,)),
            pltpu.SemaphoreType.DMA((2, 21)),
            pltpu.SemaphoreType.DMA((2, 21)),
            pltpu.SemaphoreType.DMA((2, 16)),
            pltpu.SemaphoreType.DMA((2, 16)),
            pltpu.SemaphoreType.DMA((3,)),
            pltpu.SemaphoreType.DMA((3,)),
        ],
        compiler_params=pltpu.CompilerParams(collective_id=0, has_side_effects=True),
        cost_estimate=pl.CostEstimate(flops=0, bytes_accessed=250_000_000, transcendentals=0),
        name="gather_weights",
    )(query, key, value, out, extra, gate, up, down)
    return a_all.reshape(-1, cols[0]), b_all.reshape(-1, cols[1]), *experts


ORDER = (2, 1, 3, 0)
SLICE = 16


def up(v):
    return lax.rem(v + 1, RING)


def down(v):
    return lax.rem(v + RING - 1, RING)


def add_into(target, *terms):
    flat = [target.shape[0]] if len(target.shape) == 3 else []
    for lead in range(flat[0]) if flat else (None,):
        for start in range(0, target.shape[-2], SLICE):
            at = (pl.ds(start, SLICE), slice(None))
            at = at if lead is None else (lead,) + at
            total = terms[0][at].astype(F32)
            for term in terms[1:]:
                total = total + term[at].astype(F32)
            target[at] = total.astype(target.dtype)


def scatter_kernel(
    a_ref, b_ref, extra_ref, wide_ref, tall_ref, a_out, b_out, wide_out, tall_out, a_mine, b_mine, a_theirs, b_theirs, a_one, b_one, a_two, b_two,
    a_first, b_first, a_last, b_last, a_x, b_x, load_sem, send_sem, recv_sem,
    gains_here, gains_there,
    extra_load_sem, extra_send_sem, extra_recv_sem, give_sem, take_sem, gains_sem,
):
    y, core, z, x = place()
    greet(neighbours() + [other_tp(), opposite()])
    moved = [
        swap_opposite(wide_ref, wide_out, give_sem.at[0], take_sem.at[0]),
        swap_opposite(tall_ref, tall_out, give_sem.at[1], take_sem.at[1]),
    ]

    @pl.when(jnp.logical_not(native()))
    def _():
        for copy in moved:
            copy.start()

    grads, outs = (a_ref, b_ref), (a_out, b_out)
    mine, theirs = (a_mine, b_mine), (a_theirs, b_theirs)
    one, two = (a_one, b_one), (a_two, b_two)
    first, last, side = (a_first, b_first), (a_last, b_last), (a_x, b_x)
    me = ((z, y), (y, z))
    sent = []

    def chunk(n, i, j, c):
        return grads[n].at[j, c, i] if n == 0 else grads[n].at[i, c, j]

    def to(n, i, j):
        return device(j, core, i, x) if n == 0 else device(i, core, j, x)

    def copy_of(n, src, dst, slot, where):
        return pltpu.make_async_remote_copy(
            src_ref=src, dst_ref=dst, send_sem=send_sem.at[n, slot], recv_sem=recv_sem.at[n, slot],
            device_id=where, device_id_type=MESH,
        )

    def send(n, src, dst, slot, where):
        copy = copy_of(n, src, dst, slot, where)
        copy.start()
        sent.append(copy)

    def arrived(n, dst, slot):
        copy_of(n, dst, dst, slot, device(y, core, z, x)).wait_recv()

    cols = b_ref.shape[-1]

    def columns(ref, start, count):
        return ref.at[:, :, pl.ds(start, count)]

    def extra_copy(slot):
        ref = columns(theirs[1].at[slot], cols, extra_ref.shape[-1])
        far = extra_ref.at[lax.rem(y + slot // RING, RING), 1 - core, lax.rem(z + slot % RING, RING)]
        return pltpu.make_async_remote_copy(
            src_ref=far, dst_ref=ref, send_sem=extra_send_sem.at[slot],
            recv_sem=extra_recv_sem.at[slot], device_id=device(y, 1 - core, z, x),
            device_id_type=MESH,
        )

    def extra_load(slot):
        near = extra_ref.at[lax.rem(y + slot // RING, RING), core, lax.rem(z + slot % RING, RING)]
        return pltpu.make_async_copy(
            near, columns(mine[1].at[slot], cols, extra_ref.shape[-1]), extra_load_sem.at[slot]
        )

    def load(n, di, dj):
        i, j = me[n]
        slot = di * RING + dj
        target = mine[n].at[slot] if n == 0 else columns(mine[n].at[slot], 0, cols)
        return pltpu.make_async_copy(
            chunk(n, lax.rem(i + di, RING), lax.rem(j + dj, RING), core), target,
            load_sem.at[n, slot],
        )

    for dj in ORDER:
        for di in ORDER:
            for n in (0, 1):
                i, j = me[n]
                slot = di * RING + dj
                there = chunk(n, lax.rem(i + di, RING), lax.rem(j + dj, RING), 1 - core)
                target = theirs[n].at[slot] if n == 0 else columns(theirs[n].at[slot], 0, cols)
                send(n, there, target, slot, device(y, 1 - core, z, x))
                load(n, di, dj).start()
                if n == 1:
                    extra_copy(slot).start()
                    extra_load(slot).start()

    def ready(n, di, dj):
        slot = di * RING + dj
        load(n, di, dj).wait()
        if n == 0:
            arrived(n, theirs[n].at[slot], slot)
        else:
            arrived(n, columns(theirs[n].at[slot], 0, cols), slot)
            extra_load(slot).wait()
            extra_copy(slot).wait_recv()
        return slot

    for di in ORDER:
        for n in (0, 1):
            i, j = me[n]
            slot = ready(n, di, 2)
            add_into(mine[n].at[slot], mine[n].at[slot], theirs[n].at[slot])
            for half in (0, 1):
                send(
                    n, mine[n].at[slot, half], one[n].at[di, half], 16 + di * 2 + half,
                    to(n, i, up(j) if half == 0 else down(j)),
                )
    for di in ORDER:
        for n in (0, 1):
            i, j = me[n]
            for half, dj in ((0, 1), (1, 3)):
                slot = ready(n, di, dj)
                arrived(n, one[n].at[di, half], 16 + di * 2 + half)
                add_into(
                    mine[n].at[slot, half], mine[n].at[slot, half], theirs[n].at[slot, half],
                    one[n].at[di, half],
                )
                add_into(
                    mine[n].at[slot, 1 - half], mine[n].at[slot, 1 - half],
                    theirs[n].at[slot, 1 - half],
                )
                send(
                    n, mine[n].at[slot], two[n].at[di, half], 24 + di * 2 + half,
                    to(n, i, up(j) if half == 0 else down(j)),
                )
    for di in ORDER:
        for n in (0, 1):
            i, j = me[n]
            slot = ready(n, di, 0)
            for half in (0, 1):
                arrived(n, two[n].at[di, half], 24 + di * 2 + half)
            add_into(
                mine[n].at[slot], mine[n].at[slot], theirs[n].at[slot], two[n].at[di, 0],
                two[n].at[di, 1],
            )
            if di == 2:
                for half in (0, 1):
                    send(
                        n, mine[n].at[slot, half], first[n].at[half], 32 + half,
                        to(n, up(i) if half == 0 else down(i), j),
                    )
            elif di != 0:
                half = 0 if di == 1 else 1
                arrived(n, first[n].at[half], 32 + half)
                add_into(mine[n].at[slot, half], mine[n].at[slot, half], first[n].at[half])
                send(
                    n, mine[n].at[slot], last[n].at[half], 34 + half,
                    to(n, up(i) if half == 0 else down(i), j),
                )
    for n in (0, 1):
        for half in (0, 1):
            arrived(n, last[n].at[half], 34 + half)
        add_into(mine[n].at[0], mine[n].at[0], last[n].at[0], last[n].at[1])
        send(n, mine[n].at[0, 1 - x], side[n], 36, device(y, core, z, 1 - x))
    for n in (0, 1):
        arrived(n, side[n], 36)
        add_into(outs[n], mine[n].at[0, x], side[n])
    gains_here[...] = b_out[:, cols:]
    gains = pltpu.make_async_remote_copy(
        src_ref=gains_here, dst_ref=gains_there, send_sem=gains_sem.at[0],
        recv_sem=gains_sem.at[1], device_id=other_tp(), device_id_type=MESH,
    )
    gains.start()
    for copy in sent:
        copy.wait_send()
    for slot in range(RING * RING):
        extra_copy(slot).wait_send()
    gains.wait()
    b_out[:, cols:] = gains_here[...] + gains_there[...]

    @pl.when(jnp.logical_not(native()))
    def _():
        for copy in moved:
            copy.wait()


def scatter_grads(a, b, extra, wide, tall):
    peers = RING * RING * 4
    rows = a.shape[0] // peers
    shape = (RING, 2, RING, 2, rows)
    cols = (a.shape[1], b.shape[1] + extra.shape[1])
    buffers = []
    for lead in ((16, 2), (16, 2), (4, 2), (4, 2, 2), (2,), (2, 2), ()):
        buffers += [pltpu.VMEM(lead + (rows, c), a.dtype) for c in cols]
    any_space = pl.BlockSpec(memory_space=pl.ANY)
    return pl.pallas_call(
        scatter_kernel,
        in_specs=[any_space] * 5,
        out_specs=[pl.BlockSpec(memory_space=pltpu.VMEM)] * 2 + [any_space] * 2,
        out_shape=[jax.ShapeDtypeStruct((rows, c), F32) for c in cols]
        + [jax.ShapeDtypeStruct(v.shape, v.dtype) for v in (wide, tall)],
        scratch_shapes=buffers + [
            pltpu.SemaphoreType.DMA((2, 16)),
            pltpu.SemaphoreType.DMA((2, 37)),
            pltpu.SemaphoreType.DMA((2, 37)),
            pltpu.VMEM((rows, extra.shape[1]), F32),
            pltpu.VMEM((rows, extra.shape[1]), F32),
            pltpu.SemaphoreType.DMA((16,)),
            pltpu.SemaphoreType.DMA((16,)),
            pltpu.SemaphoreType.DMA((16,)),
            pltpu.SemaphoreType.DMA((2,)),
            pltpu.SemaphoreType.DMA((2,)),
            pltpu.SemaphoreType.DMA((2,)),
        ],
        compiler_params=pltpu.CompilerParams(
            collective_id=1, has_side_effects=True, vmem_limit_bytes=44 * 1024 * 1024
        ),
        cost_estimate=pl.CostEstimate(flops=0, bytes_accessed=250_000_000, transcendentals=0),
        name="scatter_grads",
    )(*(v.reshape(shape + (v.shape[1],)) for v in (a, b, extra)), wide, tall)


BLOCK = 64
CTX = 8


def dot(a, b, dims):
    return lax.dot_general(a, b, (dims, ((), ())), preferred_element_type=F32)


def rotated(u, gain, cosine, sine):
    scaling = lax.rsqrt(jnp.mean(u * u, axis=-1, keepdims=True) + EPS)
    normed = u * scaling
    n = normed * gain
    rot = n * cosine + pltpu.roll(n, HEAD_SIZE // 2, 1) * sine
    return rot.astype(BF16), normed, scaling


def rotated_back(e, normed, scaling, gain, cosine, sine):
    back = e * cosine + pltpu.roll(e * sine, HEAD_SIZE // 2, 1)
    scaled = back * gain
    inner = jnp.mean(scaled * normed, axis=-1, keepdims=True)
    return scaling * (scaled - normed * inner), jnp.sum(back * normed, axis=0, keepdims=True)


def ctx_peer(step):
    return {"ctx": lax.rem(lax.axis_index("ctx") + step, CTX)}


def beside():
    c = lax.axis_index("ctx")
    return {"ctx": c + 1 - 2 * lax.rem(c, 2)}


def remote(src, dst, send_sem, recv_sem, where):
    return pltpu.make_async_remote_copy(
        src_ref=src, dst_ref=dst, send_sem=send_sem, recv_sem=recv_sem, device_id=where,
        device_id_type=MESH,
    )


def softmax_parts(q_low, k, bias):
    s = dot(q_low, k, ((1,), (1,))) * (HEAD_SIZE ** -0.5) + bias
    e = jnp.exp(s - jnp.max(s, axis=-1, keepdims=True))
    return e / jnp.sum(e, axis=-1, keepdims=True)


def share_kernel(kv, rows_ref, cos_ref, sin_ref, gk_ref, kv_ref, held, send_sem, recv_sem):
    c = lax.axis_index("ctx")
    greet([ctx_peer(step) for step in range(1, CTX)])
    micro, rows = held.shape[0], 2 * BLOCK
    cosine, sine, gk = cos_ref[...], sin_ref[...], gk_ref[...]
    mine = pl.ds(pl.multiple_of(c * BLOCK, BLOCK), BLOCK)
    earlier, own = pl.ds(CTX * BLOCK, BLOCK), pl.ds((CTX + 1) * BLOCK, BLOCK)
    copies = []
    for m in range(micro):
        span = slice(m * rows, (m + 1) * rows)
        for h in range(2 * kv):
            cols = slice(h * HEAD_SIZE, (h + 1) * HEAD_SIZE)
            u = rows_ref[span, cols]
            low = rotated(u, gk, cosine, sine)[0] if h < kv else u.astype(BF16)
            held[m, mine, cols] = low[:BLOCK]
            held[m, own, cols] = low[BLOCK:]
        for step in range(1, CTX):
            part = held.at[m, mine]
            copies.append(
                remote(part, part, send_sem.at[step, m], recv_sem.at[step, m], ctx_peer(step))
            )
        copies.append(
            remote(
                held.at[m, own], held.at[m, earlier], send_sem.at[0, m], recv_sem.at[0, m], beside()
            )
        )
        for copy in copies[-CTX:]:
            copy.start()
    for m in range(micro):
        for step in range(1, CTX):
            source = lax.rem(c + CTX - step, CTX)
            part = held.at[m, pl.ds(pl.multiple_of(source * BLOCK, BLOCK), BLOCK)]
            remote(
                part, part, send_sem.at[step, m], recv_sem.at[step, m], ctx_peer(step)
            ).wait_recv()
        copies[(m + 1) * CTX - 1].wait_recv()
        kv_ref[m] = held[m]
    for copy in copies:
        copy.wait_send()


def attention_kernel(heads, q_ref, cos_ref, sin_ref, gq_ref, bias_ref, k_ref, v_ref, o_ref):
    cosine, sine, gq = cos_ref[...], sin_ref[...], gq_ref[...]
    for e in range(heads):
        cols = slice(e * HEAD_SIZE, (e + 1) * HEAD_SIZE)
        q_low = rotated(q_ref[:, cols], gq, cosine, sine)[0]
        p = softmax_parts(q_low, k_ref[...], bias_ref[...]).astype(BF16)
        o_ref[:, cols] = dot(p, v_ref[...], ((1,), (0,))).astype(BF16)


def attention_back_kernel(
    kv, heads, qkv_ref, cos_ref, sin_ref, gq_ref, gk_ref, bias_ref, kv_ref, do_ref,
    dqkv_ref, gains_ref, grads, given, given_side, p_all, ds_all, q_all, do_all,
    send_sem, recv_sem,
):
    c = lax.axis_index("ctx")
    greet([ctx_peer(step) for step in range(1, CTX)])
    micro, rows = grads.shape[0], 2 * BLOCK
    q_cols = kv * heads * HEAD_SIZE
    scale = HEAD_SIZE ** -0.5
    cosine, sine, gq, gk = cos_ref[...], sin_ref[...], gq_ref[...], gk_ref[...]
    mine = pl.ds(pl.multiple_of(c * BLOCK, BLOCK), BLOCK)
    earlier, own = pl.ds(CTX * BLOCK, BLOCK), pl.ds((CTX + 1) * BLOCK, BLOCK)

    def head_cols(h):
        return pl.ds(pl.multiple_of(h * HEAD_SIZE, HEAD_SIZE), HEAD_SIZE)

    def keys_back(m, h, carry):
        span = slice(m * rows, (m + 1) * rows)
        k, v = kv_ref[m, :, head_cols(h)], kv_ref[m, :, head_cols(kv + h)]
        for e in range(heads):
            cols = head_cols(h * heads + e)
            stack = slice(e * rows, (e + 1) * rows)
            q_low = rotated(qkv_ref[span, cols], gq, cosine, sine)[0]
            q_all[stack, :] = q_low
            p = softmax_parts(q_low, k, bias_ref[...])
            p_all[stack, :] = p.astype(BF16)
            do = do_ref[span, cols]
            do_all[stack, :] = do
            dp = dot(do, v, ((1,), (1,)))
            ds = (p * (dp - jnp.sum(dp * p, axis=-1, keepdims=True))).astype(BF16)
            ds_all[m * kv + h, stack, :] = ds
        grads[m, :, head_cols(kv + h)] = dot(p_all[...], do_all[...], ((0,), (0,))).astype(BF16)
        d_k = dot(ds_all[m * kv + h], q_all[...], ((0,), (0,))) * scale
        grads[m, :, head_cols(h)] = d_k.astype(BF16)
        return carry

    def queries_back(m, h, total):
        span = slice(m * rows, (m + 1) * rows)
        k = kv_ref[m, :, head_cols(h)]
        for e in range(heads):
            cols = head_cols(h * heads + e)
            ds = ds_all[m * kv + h, e * rows : (e + 1) * rows, :]
            dqr = (dot(ds, k, ((1,), (0,))) * scale).astype(BF16).astype(F32)
            u = qkv_ref[span, cols]
            scaling = lax.rsqrt(jnp.mean(u * u, axis=-1, keepdims=True) + EPS)
            dq, part = rotated_back(dqr, u * scaling, scaling, gq, cosine, sine)
            dqkv_ref[span, cols] = dq.astype(BF16)
            total = total + part
        return total

    copies = []
    for m in range(micro):
        lax.fori_loop(0, kv, functools.partial(keys_back, m), 0)
        for step in range(1, CTX):
            peer = lax.rem(c + step, CTX)
            part = grads.at[m, pl.ds(pl.multiple_of(peer * BLOCK, BLOCK), BLOCK)]
            copies.append(
                remote(
                    part, given.at[step - 1, m], send_sem.at[step, m], recv_sem.at[step, m],
                    ctx_peer(step),
                )
            )
        copies.append(
            remote(
                grads.at[m, earlier], given_side.at[m], send_sem.at[0, m], recv_sem.at[0, m],
                beside(),
            )
        )
        for copy in copies[-CTX:]:
            copy.start()
    total = jnp.zeros((1, HEAD_SIZE), F32)
    for m in range(micro):
        total = lax.fori_loop(0, kv, functools.partial(queries_back, m), total)
    k_total = jnp.zeros((1, HEAD_SIZE), F32)
    for m in range(micro):
        for copy in copies[m * CTX : (m + 1) * CTX]:
            copy.wait_recv()
        for h in range(2 * kv):
            cols = slice(h * HEAD_SIZE, (h + 1) * HEAD_SIZE)
            at = slice(q_cols + h * HEAD_SIZE, q_cols + (h + 1) * HEAD_SIZE)
            prompt = grads[m, mine, cols].astype(F32)
            for step in range(CTX - 1):
                prompt = prompt + given[step, m, :, cols].astype(F32)
            cont = grads[m, own, cols].astype(F32) + given_side[m, :, cols].astype(F32)
            e = jnp.concatenate([prompt, cont], axis=0).astype(BF16)
            span = slice(m * rows, (m + 1) * rows)
            if h < kv:
                _, normed, scaling = rotated(qkv_ref[span, at], gk, cosine, sine)
                d, part = rotated_back(e.astype(F32), normed, scaling, gk, cosine, sine)
                k_total = k_total + part
                dqkv_ref[span, at] = d.astype(BF16)
            else:
                dqkv_ref[span, at] = e
    gains_ref[0:1, :] = total
    gains_ref[1:2, :] = k_total
    for copy in copies:
        copy.wait_send()


def share_keys(qkv, cosine, sine, gain_key, kv, keys, micro):
    rows, cols = qkv.shape[0], 2 * kv * HEAD_SIZE
    last = qkv.shape[1] // cols - 1

    def whole(shape):
        return pl.BlockSpec(shape, lambda i: (0,) * len(shape))

    return pl.pallas_call(
        functools.partial(share_kernel, kv),
        grid=(1,),
        in_specs=[pl.BlockSpec((rows, cols), lambda i: (0, last)), whole(cosine.shape)]
        + [whole(sine.shape), whole(gain_key.shape)],
        out_specs=whole((micro, keys, cols)),
        out_shape=jax.ShapeDtypeStruct((micro, keys, cols), BF16),
        scratch_shapes=[
            pltpu.VMEM((micro, keys, cols), BF16),
            pltpu.SemaphoreType.DMA((CTX, micro)),
            pltpu.SemaphoreType.DMA((CTX, micro)),
        ],
        compiler_params=pltpu.CompilerParams(
            collective_id=2, has_side_effects=True, vmem_limit_bytes=VMEM_LIMIT
        ),
        cost_estimate=pl.CostEstimate(flops=0, bytes_accessed=50_000_000, transcendentals=0),
        name="share_keys",
    )(qkv, cosine, sine, gain_key)


def attention(qkv, cosine, sine, gain_query, bias, kv_all, kv):
    micro, keys, cols = kv_all.shape
    rows = bias.shape[0]
    heads = qkv.shape[1] // HEAD_SIZE // kv - 2
    width = heads * HEAD_SIZE

    def whole(v):
        return pl.BlockSpec(v.shape, lambda m, g: (0,) * v.ndim)

    return pl.pallas_call(
        functools.partial(attention_kernel, heads),
        grid=(micro, kv),
        in_specs=[pl.BlockSpec((rows, width), lambda m, g: (m, g))]
        + [whole(v) for v in (cosine, sine, gain_query, bias)]
        + [
            pl.BlockSpec((None, keys, HEAD_SIZE), lambda m, g: (m, 0, g)),
            pl.BlockSpec((None, keys, HEAD_SIZE), lambda m, g: (m, 0, kv + g)),
        ],
        out_specs=pl.BlockSpec((rows, width), lambda m, g: (m, g)),
        out_shape=jax.ShapeDtypeStruct((micro * rows, kv * width), BF16),
        compiler_params=pltpu.CompilerParams(vmem_limit_bytes=VMEM_LIMIT),
        cost_estimate=pl.CostEstimate(flops=0, bytes_accessed=60_000_000, transcendentals=0),
        name="attention_forward",
    )(qkv, cosine, sine, gain_query, bias, kv_all, kv_all)


def attention_back(qkv, cosine, sine, gain_query, gain_key, bias, kv_all, d_out, kv):
    heads = qkv.shape[1] // HEAD_SIZE // kv - 2
    rows, keys = bias.shape
    micro, _, kv_cols = kv_all.shape
    return pl.pallas_call(
        functools.partial(attention_back_kernel, kv, heads),
        out_shape=[
            jax.ShapeDtypeStruct(qkv.shape, BF16),
            jax.ShapeDtypeStruct((2, HEAD_SIZE), F32),
        ],
        scratch_shapes=[
            pltpu.VMEM((micro, keys, kv_cols), BF16),
            pltpu.VMEM((CTX - 1, micro, BLOCK, kv_cols), BF16),
            pltpu.VMEM((micro, BLOCK, kv_cols), BF16),
            pltpu.VMEM((heads * rows, keys), BF16),
            pltpu.VMEM((micro * kv, heads * rows, keys), BF16),
            pltpu.VMEM((heads * rows, HEAD_SIZE), BF16),
            pltpu.VMEM((heads * rows, HEAD_SIZE), BF16),
            pltpu.SemaphoreType.DMA((CTX, micro)),
            pltpu.SemaphoreType.DMA((CTX, micro)),
        ],
        compiler_params=pltpu.CompilerParams(
            collective_id=3, has_side_effects=True, vmem_limit_bytes=VMEM_LIMIT
        ),
        cost_estimate=pl.CostEstimate(flops=0, bytes_accessed=120_000_000, transcendentals=0),
        name="attention_backward",
    )(qkv, cosine, sine, gain_query, gain_key, bias, kv_all, d_out)


CHIPS = RING * RING * RING
GROUP = 16
MIX = 27


def chip_at(slot, sign):
    f, c, t = lax.axis_index("fsdp"), lax.axis_index("ctx"), lax.axis_index("tp")
    k = slot * MIX % CHIPS
    turn = RING * sign
    y = (f // 2 + turn + sign * (k // (RING * RING))) % RING
    z = (c // 2 + turn + sign * (k // RING % RING)) % RING
    x = (t * 2 + c % 2 + turn + sign * (k % RING)) % RING
    return y, z, x


def device_at(slot, sign):
    y, z, x = chip_at(slot, sign)
    return {"fsdp": y * 2 + lax.axis_index("fsdp") % 2, "ctx": z * 2 + x % 2, "tp": x // 2}


def chip_number(slot, sign):
    y, z, x = chip_at(slot, sign)
    return (y * 2 * RING + z * 2 + x % 2) * 2 + x // 2


def other_core():
    f = lax.axis_index("fsdp")
    return {"fsdp": f + 1 - 2 * (f % 2)}


def moe_kernel(
    send_ref, deo_ref, gate_ref, up_ref, down_ref, gate_far, up_far, down_far,
    back_ref, eo_ref, rows_ref, deos_ref, z_ref, dgu_ref,
    rows, deos, gu, down, give, take,
    go_sem, come_sem, load_sem, weight_sem, share_send, share_recv, part_send, part_recv,
    save_sem, back_send, back_recv, eo_sem,
):
    size, hidden = send_ref.shape[1], down_ref.shape[0]
    count = GROUP * size
    groups = CHIPS // GROUP
    total = CHIPS * size

    def each(body, low, high):
        def step(i, carry):
            body(i)
            return carry

        lax.fori_loop(low, high, step, 0)

    barrier = pltpu.get_barrier_semaphore()
    each(
        lambda s: pl.semaphore_signal(
            barrier, inc=1, device_id=device_at(s, 1), device_id_type=MESH
        ),
        1, CHIPS,
    )
    pl.semaphore_signal(barrier, inc=1, device_id=other_core(), device_id_type=MESH)
    pl.semaphore_wait(barrier, CHIPS)

    def slot_rows(s):
        return pl.ds(pl.multiple_of(s * size, size), size)

    def group_rows(g):
        return pl.ds(pl.multiple_of(g * count, count), count)

    def go(s):
        return remote(
            send_ref.at[s], rows.at[0, slot_rows(s)], go_sem.at[s], come_sem.at[s], device_at(s, 1)
        )

    def stay(s):
        return pltpu.make_async_copy(send_ref.at[s], rows.at[0, slot_rows(s)], come_sem.at[s])

    def load(s):
        return pltpu.make_async_copy(
            deo_ref.at[chip_number(s, -1)], deos.at[0, slot_rows(s)], load_sem.at[s]
        )

    def back(s):
        return remote(
            rows.at[0, slot_rows(s)], back_ref.at[s], back_send.at[s], back_recv.at[s],
            device_at(s, -1),
        )

    def back_stay():
        return pltpu.make_async_copy(rows.at[0, slot_rows(0)], back_ref.at[0], back_recv.at[0])

    def out(s):
        return pltpu.make_async_copy(
            deos.at[0, slot_rows(s)], eo_ref.at[chip_number(s, -1)], eo_sem.at[s]
        )

    def share(n, g):
        ref = (rows, deos)[n]
        return remote(
            ref.at[0, group_rows(g)], ref.at[1, group_rows(g)], share_send.at[n, g],
            share_recv.at[n, g], other_core(),
        )

    def part(n, g):
        return remote(
            give.at[n, group_rows(g)], take.at[n, group_rows(g)], part_send.at[n, g],
            part_recv.at[n, g], other_core(),
        )

    def save(n, side, g):
        ref, to = ((rows, rows_ref), (deos, deos_ref))[n]
        return pltpu.make_async_copy(
            ref.at[side, group_rows(g)], to.at[side, group_rows(g)], save_sem.at[n, side, g]
        )

    places = (gu.at[:, pl.ds(0, hidden)], gu.at[:, pl.ds(hidden, hidden)], down)
    weights = [
        [pltpu.make_async_copy(src, dst, weight_sem.at[n]) for n, (src, dst) in enumerate(pairs)]
        for pairs in (
            zip((gate_ref, up_ref, down_ref), places), zip((gate_far, up_far, down_far), places)
        )
    ]

    def on_weights(act):
        for condition, copies in zip((native(), jnp.logical_not(native())), weights):

            @pl.when(condition)
            def _(copies=copies):
                for copy in copies:
                    act(copy)

    stay(0).start()
    each(lambda s: go(s).start(), 1, CHIPS)
    each(lambda s: load(s).start(), 0, CHIPS)
    on_weights(lambda copy: copy.start())

    def through(side, g):
        at = group_rows(g)
        kept = pl.ds(pl.multiple_of(side * total + g * count, count), count)
        pre = dot(rows[side, at, :], gu[...], ((1,), (0,)))
        dz = dot(deos[side, at, :], down[...], ((1,), (1,)))
        gate, u = pre[:, :hidden], pre[:, hidden:]
        sig = 1.0 / (1.0 + jnp.exp(-gate))
        act = gate * sig
        z_ref[kept, :] = (act * u).astype(BF16)
        dgu_ref[kept, :hidden] = (dz * u * sig * (1.0 + gate * (1.0 - sig))).astype(BF16)
        dgu_ref[kept, hidden:] = (dz * act).astype(BF16)

    def to_rows(side, g):
        kept = pl.ds(pl.multiple_of(side * total + g * count, count), count)
        return dot(dgu_ref[kept, :], gu[...], ((1,), (1,)))

    def to_outputs(side, g):
        kept = pl.ds(pl.multiple_of(side * total + g * count, count), count)
        return dot(z_ref[kept, :], down[...], ((1,), (0,)))

    on_weights(lambda copy: copy.wait())

    def group(g):
        first, last = g * GROUP, (g + 1) * GROUP

        @pl.when(g == 0)
        def _():
            stay(0).wait()

        each(lambda s: go(s).wait_recv(), lax.max(first, 1), last)
        each(lambda s: load(s).wait(), first, last)
        for n in (0, 1):
            share(n, g).start()
            save(n, 0, g).start()
        through(0, g)
        for n in (0, 1):
            share(n, g).wait_recv()
            save(n, 1, g).start()
        through(1, g)
        give[0, group_rows(g), :] = to_rows(1, g).astype(BF16)
        part(0, g).start()
        give[1, group_rows(g), :] = to_outputs(1, g).astype(BF16)
        part(1, g).start()
        own = to_rows(0, g)
        part(0, g).wait_recv()
        share(0, g).wait_send()
        save(0, 0, g).wait()
        at = group_rows(g)
        rows[0, at, :] = (own + take[0, at, :].astype(F32)).astype(BF16)

        @pl.when(g == 0)
        def _():
            back_stay().start()

        each(lambda s: back(s).start(), lax.max(first, 1), last)
        own = to_outputs(0, g)
        part(1, g).wait_recv()
        share(1, g).wait_send()
        save(1, 0, g).wait()
        deos[0, at, :] = (own + take[1, at, :].astype(F32)).astype(BF16)
        each(lambda s: out(s).start(), first, last)

    each(group, 0, groups)

    def finish(g):
        for n in (0, 1):
            part(n, g).wait_send()
            save(n, 1, g).wait()

    each(finish, 0, groups)
    each(lambda s: out(s).wait(), 0, CHIPS)
    back_stay().wait()
    each(lambda s: go(s).wait_send(), 1, CHIPS)
    each(lambda s: back(s).wait(), 1, CHIPS)


def moe(send, d_eo, own, far):
    chips, size, width = send.shape
    hidden = own[2].shape[0]
    total, groups = chips * size, chips // GROUP
    vmem, any_space = (pl.BlockSpec(memory_space=space) for space in (pltpu.VMEM, pl.ANY))
    shapes = [send.shape, send.shape, (2, total, width), (2, total, width)]
    shapes += [(2 * total, hidden), (2 * total, 2 * hidden)]
    dma = pltpu.SemaphoreType.DMA
    return pl.pallas_call(
        moe_kernel,
        in_specs=[any_space] * 8,
        out_specs=[any_space] * 4 + [vmem] * 2,
        out_shape=[jax.ShapeDtypeStruct(shape, BF16) for shape in shapes],
        scratch_shapes=[
            pltpu.VMEM((2, total, width), BF16),
            pltpu.VMEM((2, total, width), BF16),
            pltpu.VMEM((width, 2 * hidden), BF16),
            pltpu.VMEM((hidden, width), BF16),
            pltpu.VMEM((2, total, width), BF16),
            pltpu.VMEM((2, total, width), BF16),
            dma((chips,)), dma((chips,)), dma((chips,)), dma((3,)),
            dma((2, groups)), dma((2, groups)), dma((2, groups)), dma((2, groups)),
            dma((2, 2, groups)), dma((chips,)), dma((chips,)), dma((chips,)),
        ],
        compiler_params=pltpu.CompilerParams(
            collective_id=4, has_side_effects=True, vmem_limit_bytes=56 * 1024 * 1024
        ),
        cost_estimate=pl.CostEstimate(flops=0, bytes_accessed=400_000_000, transcendentals=0),
        name="experts",
    )(send, d_eo, *own, *far)


def normalize(rows, gain):
    scaling = lax.rsqrt(jnp.mean(rows * rows, axis=-1, keepdims=True) + EPS)
    return rows * scaling * gain, scaling


def normalize_back(rows, scaling, gain, upstream):
    normed = rows * scaling
    gain_grad = jnp.sum((upstream * normed).reshape(-1, rows.shape[-1]), axis=0)
    scaled = upstream * gain
    inner = jnp.mean(scaled * normed, axis=-1, keepdims=True)
    return scaling * (scaled - normed * inner), gain_grad


def swap_tp(value):
    return lax.ppermute(value, "tp", [(0, 1), (1, 0)])


def local(
    x_prompt, x_cont, cot_prompt, cot_cont, ids_prompt, ids_cont, gates_prompt, gates_cont,
    norm_gain, query_weight, key_matrix, value_matrix, out_weight, query_gain, key_gain, moe_gain,
    expert_gate, expert_up, expert_down,
):
    micro = x_prompt.shape[0]
    prompt_rows, cont_rows, width = x_prompt.shape[2], x_cont.shape[2], x_prompt.shape[3]
    block = cont_rows
    rows = 2 * block
    s = lax.axis_index("ctx")
    ctx = lax.axis_size("ctx")
    first = lax.axis_index("tp") == 0
    peers = lax.axis_size(ALL)
    q_cols, kv_cols = query_weight.shape[1], key_matrix.shape[1]
    kv = kv_cols // HEAD_SIZE
    qkv_cols = q_cols + 2 * kv_cols
    shard_rows = query_weight.shape[0]
    hidden = expert_gate.shape[2]
    slots = cont_rows * TOPK // peers

    fsdp, tp = lax.axis_size("fsdp"), lax.axis_size("tp")
    chips = [(2 * y, c, t) for y in range(fsdp // 2) for c in range(ctx) for t in range(tp)]
    groups = [[((f + core) * ctx + c) * tp + t for f, c, t in chips] for core in range(2)]
    expert_of = jnp.array([(f + t) * ctx + c for f, c, t in chips], jnp.int32)

    def exchange(rows_of):
        return lax.all_to_all(
            rows_of, ("fsdp", "ctx", "tp"), split_axis=0, concat_axis=0, tiled=True,
            axis_index_groups=groups,
        )

    def pad(v):
        return jnp.pad(v[:, 0], ((0, 0), (0, block - prompt_rows), (0, 0)))

    x_first, x_second = pad(x_prompt), x_cont[:, 0]
    own_tokens = jnp.where(first, x_second, x_first).astype(F32)
    own_cot = jnp.where(first, cot_cont[:, 0], pad(cot_prompt)).astype(F32)
    ids_pad = jnp.pad(
        ids_prompt[:, 0], ((0, 0), (0, block - prompt_rows), (0, 0)), constant_values=-1
    )
    own_ids = jnp.where(first, ids_cont[:, 0], ids_pad)
    own_gates = jnp.where(first, gates_cont[:, 0], pad(gates_prompt))

    lower = jnp.tril(jnp.ones((block, block), BF16), -1)
    same = jnp.arange(micro)[:, None] == jnp.arange(micro)[None, :]
    flat = (micro * block, peers * micro * slots)

    def routing(experts):
        named = own_ids[:, :, :, None] == experts
        chosen = jnp.any(named, axis=2)
        weight = jnp.sum(jnp.where(named, own_gates[:, :, :, None], 0.0), axis=2)
        rank = jnp.einsum("ts,mse->mte", lower, chosen.astype(BF16), preferred_element_type=F32)
        place = jnp.where(chosen, rank, -1.0)
        placed = place[:, :, :, None] == jnp.arange(slots, dtype=F32)
        both = jnp.logical_and(placed[:, :, :, None, :], same[:, None, None, :, None])
        return both, weight[:, :, :, None, None]

    placed, weight = routing(expert_of)
    select = placed.astype(BF16).reshape(flat)
    mixing = jnp.where(placed, weight, 0.0).reshape(flat)
    mixing_high = mixing.astype(BF16)
    mixing_low = (mixing - mixing_high.astype(F32)).astype(BF16)
    slot_gate = jnp.sum(mixing, axis=0)
    y, z, x = chip_at(jnp.arange(peers, dtype=jnp.int32), 1)
    select_near = routing((2 * y + x // 2) * ctx + 2 * z + x % 2)[0].astype(BF16).reshape(flat)

    def lanes(v):
        return jnp.pad(v, [(0, 0)] * (v.ndim - 1) + [(0, HEAD_SIZE - v.shape[-1])])

    extra = jnp.stack([lanes(v) for v in (norm_gain, moe_gain, query_gain, key_gain)])
    extra = jnp.pad(extra, ((0, shard_rows - extra.shape[0]), (0, 0)))
    own_experts = (expert_gate[0], expert_up[0], expert_down[0])
    w_qkv, w_out_extra, *far_experts = gather_weights(
        query_weight, key_matrix, value_matrix, out_weight, extra, *own_experts
    )
    w_out = w_out_extra[:, :q_cols]
    gains = w_out_extra[:, q_cols:].reshape(peers, shard_rows, HEAD_SIZE)[:, :4].astype(F32)
    gain_in, gain_moe = (gains[:, n, :shard_rows].reshape(-1) for n in (0, 1))
    head_rows = query_gain.shape[0]
    gain_query, gain_key = (gains[:, n, :head_rows].reshape(-1) for n in (2, 3))

    offsets = jnp.arange(rows, dtype=jnp.int32)
    is_prompt = offsets < block
    prompt_pos = s * prompt_rows + offsets
    cont_pos = s * cont_rows + offsets - block
    rot_place = jnp.where(is_prompt, prompt_pos, PROMPT + cont_pos % CL).astype(F32)
    steps_freq = jnp.arange(HEAD_SIZE // 2, dtype=F32) * (2.0 / HEAD_SIZE)
    angles = rot_place[:, None] * jnp.power(THETA, -steps_freq)[None, :]
    cosine, sine = jnp.cos(angles), jnp.sin(angles)
    cosine = jnp.concatenate([cosine, cosine], axis=1)
    sine = jnp.concatenate([-sine, sine], axis=1)
    keys = (ctx + 2) * block
    key_index = jnp.arange(keys, dtype=jnp.int32)[None, :]
    key_off = key_index % block
    key_prompt_pos = key_index // block * prompt_rows + key_off
    key_cont = (s - 1) * cont_rows + key_index - ctx * block
    is_cont = jnp.logical_not(is_prompt)[:, None]
    visible = jnp.where(
        key_index < ctx * block,
        jnp.logical_and(
            key_off < prompt_rows,
            jnp.logical_or(is_cont, key_prompt_pos <= prompt_pos[:, None]),
        ),
        jnp.logical_and(
            is_cont,
            jnp.logical_and(
                key_cont // CL == cont_pos[:, None] // CL, key_cont <= cont_pos[:, None]
            ),
        ),
    )
    bias = jnp.where(visible, 0.0, NEG).astype(F32)

    def share_rows(own):
        other = swap_tp(own)
        return jnp.where(first, other, own), jnp.where(first, own, other)

    def sum_own(part):
        part = part.reshape(micro, rows, width)
        given = jnp.where(first, part[:, :block], part[:, block:]).astype(BF16)
        kept = jnp.where(first, part[:, block:], part[:, :block])
        return kept + swap_tp(given).astype(F32)

    tokens = jnp.concatenate([x_first, x_second], axis=1).astype(F32).reshape(-1, width)
    a = normalize(tokens, gain_in)[0].astype(BF16)
    qkv = dot(a, w_qkv, ((1,), (0,)))
    heads_in = (cosine, sine, gain_query[None], gain_key[None], bias)
    kv_all = share_keys(qkv, cosine, sine, gain_key[None], kv, keys, micro)

    spread = dot(select, own_cot.astype(BF16).reshape(-1, width), ((0,), (0,)))
    spread = (spread * slot_gate[:, None]).astype(BF16)
    spread, kv_all = lax.optimization_barrier((spread, kv_all))
    d_eo_rows = exchange(spread).reshape(peers, micro * slots, width)
    o = attention(qkv, cosine, sine, gain_query[None], bias, kv_all, kv)
    middle = own_tokens + sum_own(dot(o, w_out, ((1,), (1,))))
    b_normed, b_scale = normalize(middle, gain_moe)
    b_low = b_normed.astype(BF16)

    send = dot(select_near, b_low.reshape(-1, width), ((0,), (0,))).astype(BF16)
    back, eo, rows_in, d_eo_in, z, d_gu = moe(
        send.reshape(d_eo_rows.shape), d_eo_rows, own_experts, far_experts
    )
    wide_here = dot(rows_in.reshape(-1, width), d_gu, ((0,), (0,))).astype(BF16)
    tall_here = dot(z, d_eo_in.reshape(-1, width), ((0,), (0,))).astype(BF16)
    d_b = dot(select_near, back.reshape(-1, width), ((1,), (0,))).reshape(middle.shape)
    middle_from, moe_total = normalize_back(middle, b_scale, gain_moe, d_b)
    d_h = own_cot + middle_from
    d_attn = jnp.concatenate(share_rows(d_h.astype(BF16)), axis=1).reshape(-1, width)

    late, d_attn = lax.optimization_barrier((eo, d_attn))
    eo_back = exchange(late.reshape(-1, width))

    d_o = dot(d_attn, w_out, ((1,), (0,))).astype(BF16)
    grad_out = dot(d_attn, o, ((0,), (0,))).astype(BF16)
    d_qkv, head_totals = attention_back(qkv, *heads_in, kv_all, d_o, kv)
    d_qkv, eo_back = lax.optimization_barrier((d_qkv, eo_back))
    moe_out = dot(mixing_high, eo_back, ((1,), (0,))) + dot(mixing_low, eo_back, ((1,), (0,)))
    out_first, out_second = share_rows((middle + moe_out.reshape(middle.shape)).astype(BF16))
    input_grad = sum_own(dot(d_qkv, w_qkv, ((1,), (1,))))
    grad_qkv = dot(a, d_qkv, ((0,), (0,))).astype(BF16)
    scale_in = lax.rsqrt(jnp.mean(own_tokens * own_tokens, axis=-1, keepdims=True) + EPS)
    token_from, norm_total = normalize_back(own_tokens, scale_in, gain_in, input_grad)
    grad_first, grad_second = share_rows((d_h + token_from).astype(BF16))

    extra_grads = jnp.stack(
        [
            lanes(v.reshape(peers, -1))
            for v in (norm_total, moe_total, head_totals[0], head_totals[1])
        ],
        axis=1,
    )
    extra_grads = jnp.pad(extra_grads, ((0, 0), (0, shard_rows - extra_grads.shape[1]), (0, 0)))
    extra_grads = extra_grads.reshape(-1, HEAD_SIZE).astype(BF16)
    grad_qkv, out_first, out_second = lax.optimization_barrier((grad_qkv, out_first, out_second))
    share, share_out, wide_there, tall_there = scatter_grads(
        grad_qkv, grad_out, extra_grads, wide_here, tall_here
    )
    grad_wide = jnp.where(native(), wide_here, wide_there).astype(F32)
    grad_down = jnp.where(native(), tall_here, tall_there).astype(F32)
    gain_share = share_out[:, q_cols:]
    return (
        out_first[:, None, :prompt_rows],
        out_second[:, None],
        grad_first[:, None, :prompt_rows],
        grad_second[:, None],
        gain_share[0, :shard_rows],
        share[:, :q_cols],
        share[:, q_cols : q_cols + kv_cols],
        share[:, q_cols + kv_cols : qkv_cols],
        share_out[:, :q_cols],
        gain_share[2, :head_rows],
        gain_share[3, :head_rows],
        gain_share[1, :shard_rows],
        grad_wide[None, :, :hidden],
        grad_wide[None, :, hidden:],
        grad_down[None],
    )


def solution(mesh):
    rows = P(None, "fsdp", "ctx", None)
    vector = P(("fsdp", "ctx"))
    matrix = P(("fsdp", "ctx"), "tp")
    wide = P(("fsdp", "ctx"), None, "tp")
    tall = P(("fsdp", "ctx"), "tp", None)
    in_specs = (rows,) * 8 + (vector,) + (matrix,) * 4 + (vector,) * 3 + (wide, wide, tall)
    out_specs = (rows,) * 4 + (vector,) + (matrix,) * 4 + (vector,) * 3 + (wide, wide, tall)
    return jax.shard_map(local, mesh=mesh, in_specs=in_specs, out_specs=out_specs, check_vma=False)
```

```python
import functools

import jax
import jax.numpy as jnp
from jax import lax
from jax.experimental import pallas as pl
from jax.experimental.pallas import tpu as pltpu
from jax.sharding import PartitionSpec as P

HEAD_SIZE = 128
TOPK = 8
PROMPT = 448
CL = 128
EPS = 1e-06
THETA = 1000000.0
NEG = -1e30
F32 = jnp.float32
BF16 = jnp.bfloat16
ALL = ("fsdp", "ctx")
MESH = pl.DeviceIdType.MESH
RING = 4
VMEM_LIMIT = 48 * 1024 * 1024


def dot(a, b, dims):
    return lax.dot_general(a, b, (dims, ((), ())), preferred_element_type=F32)


def place():
    f, c = lax.axis_index("fsdp"), lax.axis_index("ctx")
    return f // 2, f % 2, c // 2, c % 2


def device(y, core, z, x):
    return {"fsdp": y * 2 + core, "ctx": z * 2 + x}


def greet(partners):
    barrier = pltpu.get_barrier_semaphore()
    for partner in partners:
        pl.semaphore_signal(barrier, inc=1, device_id=partner, device_id_type=MESH)
    pl.semaphore_wait(barrier, len(partners))


def neighbours():
    y, core, z, x = place()
    up, down = (lambda v: lax.rem(v + 1, RING)), (lambda v: lax.rem(v + RING - 1, RING))
    return [
        device(y, core, z, 1 - x),
        device(y, 1 - core, z, x),
        device(up(y), core, z, x),
        device(down(y), core, z, x),
        device(y, core, up(z), x),
        device(y, core, down(z), x),
    ]


def other_tp():
    return {"tp": 1 - lax.axis_index("tp")}


def opposite():
    f = lax.axis_index("fsdp")
    return {"fsdp": f + 1 - 2 * (f % 2), "tp": 1 - lax.axis_index("tp")}


def native():
    return lax.axis_index("fsdp") % 2 == lax.axis_index("tp")


def swap_opposite(src, dst, send_sem, recv_sem):
    return pltpu.make_async_remote_copy(
        src_ref=src, dst_ref=dst, send_sem=send_sem, recv_sem=recv_sem, device_id=opposite(),
        device_id_type=MESH,
    )


def route(ids, gates, experts, size, select_ref, high_ref, low_ref):
    tokens, slots = ids.shape[0], select_ref.shape[1]
    block, places = tokens // 2, size // 2
    chosen = jnp.zeros((tokens, experts.shape[1]), F32)
    weight = jnp.zeros((tokens, experts.shape[1]), F32)
    for k in range(ids.shape[1]):
        same = ids[:, k : k + 1] == experts
        chosen = chosen + jnp.where(same, 1.0, 0.0)
        weight = weight + jnp.where(same, gates[:, k : k + 1], 0.0)
    t = lax.broadcasted_iota(jnp.int32, (tokens, tokens), 0)
    u = lax.broadcasted_iota(jnp.int32, (tokens, tokens), 1)
    earlier = jnp.logical_and(u < t, (u >= block) == (t >= block))
    rank = dot(jnp.where(earlier, 1.0, 0.0).astype(BF16), chosen.astype(BF16), ((1,), (0,)))
    rank = jnp.where(chosen > 0.0, rank, -1.0).astype(BF16)
    e = lax.broadcasted_iota(jnp.int32, (experts.shape[1], slots), 0)
    j = lax.broadcasted_iota(jnp.int32, (experts.shape[1], slots), 1)
    spread = jnp.where(jnp.logical_and(j >= e * size, j < (e + 1) * size), 1.0, 0.0).astype(BF16)
    j = lax.broadcasted_iota(jnp.int32, (tokens, slots), 1)
    later = lax.broadcasted_iota(jnp.int32, (tokens, slots), 0) >= block
    place = (j & (places - 1)).astype(F32)
    mine = ((j & places) != 0) == later
    there = jnp.logical_and(dot(rank, spread, ((1,), (0,))) == place, mine)
    select_ref[...] = jnp.where(there, 1.0, 0.0).astype(BF16)
    if high_ref is not None:
        high = weight.astype(BF16)
        low = (weight - high.astype(F32)).astype(BF16)
        high_ref[...] = jnp.where(there, dot(high, spread, ((1,), (0,))), 0.0).astype(BF16)
        low_ref[...] = jnp.where(there, dot(low, spread, ((1,), (0,))), 0.0).astype(BF16)


def gather_kernel(
    query_ref, key_ref, value_ref, out_ref, extra_ref, ids_ref, gates_ref, experts_ref, cot_ref,
    gate_ref, up_ref, down_ref,
    a_all, b_all, gate_all, up_all, down_all, near_ref, high_ref, low_ref, rows_ref,
    a_own, b_own, select, rows, rows_sem, local_sem, send_sem, recv_sem, away_sem, home_sem, give_sem, take_sem,
):
    y, core, z, x = place()
    for own, refs in ((a_own, (query_ref, key_ref, value_ref)), (b_own, (out_ref, extra_ref))):
        at = 0
        for ref in refs:
            own[:, at : at + ref.shape[1]] = ref[...]
            at += ref.shape[1]
    greet(neighbours() + [opposite()])
    shards = ((gate_ref, gate_all), (up_ref, up_all), (down_ref, down_all))
    moved = [
        swap_opposite(p, q, give_sem.at[n], take_sem.at[n]) for n, (p, q) in enumerate(shards)
    ]
    refs, own = (a_all, b_all), (a_own, b_own)
    started = []
    count = [0, 0]

    def chunk(n, i, j):
        return refs[n].at[j, core, i] if n == 0 else refs[n].at[i, core, j]

    def to(n, first, second):
        return device(second, core, first, x) if n == 0 else device(first, core, second, x)

    def send(n, ref, where, slot):
        copy = pltpu.make_async_remote_copy(
            src_ref=ref, dst_ref=ref, send_sem=send_sem.at[n, slot], recv_sem=recv_sem.at[n, slot],
            device_id=where, device_id_type=MESH,
        )
        copy.start()
        started.append(copy)

    def arrived(n, ref, slot):
        pltpu.make_async_remote_copy(
            src_ref=ref, dst_ref=ref, send_sem=send_sem.at[n, slot], recv_sem=recv_sem.at[n, slot],
            device_id=device(y, core, z, x), device_id_type=MESH,
        ).wait_recv()

    homes = []

    def across(n, i, j):
        slot = count[n]
        count[n] += 1
        ref = chunk(n, i, j)
        copy = pltpu.make_async_remote_copy(
            src_ref=ref, dst_ref=ref, send_sem=away_sem.at[n, slot], recv_sem=home_sem.at[n, slot],
            device_id=device(y, 1 - core, z, x), device_id_type=MESH,
        )
        copy.start()
        homes.append(copy)

    def second(n, i, j, k):
        base = 5 + 4 * k
        send(n, chunk(n, i, j), to(n, me[n][0], up(j)), base)
        send(n, chunk(n, i, j), to(n, me[n][0], down(j)), base + 1)
        across(n, i, j)

    up, down = (lambda v: lax.rem(v + 1, RING)), (lambda v: lax.rem(v + RING - 1, RING))
    me = ((z, y), (y, z))
    locals_ = []
    for n in (0, 1):
        i, j = me[n]
        keep = pltpu.make_async_copy(own[n], chunk(n, i, j).at[x], local_sem.at[n])
        keep.start()
        locals_.append(keep)
        copy = pltpu.make_async_remote_copy(
            src_ref=own[n], dst_ref=chunk(n, i, j).at[x], send_sem=send_sem.at[n, 0],
            recv_sem=recv_sem.at[n, 0], device_id=device(y, core, z, 1 - x), device_id_type=MESH,
        )
        copy.start()
        started.append(copy)
    size = rows.shape[0] // (RING * RING * RING)
    ids, gates = ids_ref[...], gates_ref[...]
    route(ids, gates, experts_ref[0:1, :], size, select, high_ref, low_ref)
    route(ids, gates, experts_ref[1:2, :], size, near_ref, None, None)
    for n in (0, 1):
        i, j = me[n]
        locals_[n].wait()
        arrived(n, chunk(n, i, j).at[1 - x], 0)
        send(n, chunk(n, i, j), to(n, up(i), j), 1)
        send(n, chunk(n, i, j), to(n, down(i), j), 2)
    for n in (0, 1):
        i, j = me[n]
        second(n, i, j, 0)

    @pl.when(jnp.logical_not(native()))
    def _():
        for copy in moved:
            copy.start()

    part = 256
    for at in range(0, rows.shape[0], part):
        lanes = slice(at, at + part)
        total = dot(high_ref[:, lanes], cot_ref[...], ((0,), (0,)))
        total = total + dot(low_ref[:, lanes], cot_ref[...], ((0,), (0,)))
        rows[lanes, :] = total.astype(BF16)
    keep_rows = pltpu.make_async_copy(rows, rows_ref, rows_sem)
    keep_rows.start()
    for n in (0, 1):
        i, j = me[n]
        arrived(n, chunk(n, down(i), j), 1)
        send(n, chunk(n, down(i), j).at[0], to(n, up(i), j), 3)
        second(n, down(i), j, 1)
    for n in (0, 1):
        i, j = me[n]
        arrived(n, chunk(n, up(i), j), 2)
        send(n, chunk(n, up(i), j).at[1], to(n, down(i), j), 4)
        second(n, up(i), j, 2)
    for n in (0, 1):
        i, j = me[n]
        far = lax.rem(i + 2, RING)
        arrived(n, chunk(n, far, j).at[0], 3)
        arrived(n, chunk(n, far, j).at[1], 4)
        second(n, far, j, 3)
    for k in range(4):
        for n in (0, 1):
            i, j = me[n]
            it = (i, down(i), up(i), lax.rem(i + 2, RING))[k]
            base = 5 + 4 * k
            arrived(n, chunk(n, it, down(j)), base)
            send(n, chunk(n, it, down(j)).at[0], to(n, i, up(j)), base + 2)
            across(n, it, down(j))
            arrived(n, chunk(n, it, up(j)), base + 1)
            send(n, chunk(n, it, up(j)).at[1], to(n, i, down(j)), base + 3)
            across(n, it, up(j))
    for k in range(4):
        for n in (0, 1):
            i, j = me[n]
            it = (i, down(i), up(i), lax.rem(i + 2, RING))[k]
            base = 5 + 4 * k
            far = lax.rem(j + 2, RING)
            arrived(n, chunk(n, it, far).at[0], base + 2)
            arrived(n, chunk(n, it, far).at[1], base + 3)
            across(n, it, far)
    keep_rows.wait()
    for copy in homes:
        copy.wait()
    for copy in started:
        copy.wait_send()

    @pl.when(jnp.logical_not(native()))
    def _():
        for copy in moved:
            copy.wait()


def gather_weights(query, key, value, out, extra, ids, gates, experts, cot, slots, gate, up, down):
    rows = query.shape[0]
    cols = (query.shape[1] + key.shape[1] + value.shape[1], out.shape[1] + extra.shape[1])
    shape = (RING, 2, RING, 2, rows)
    vmem, any_space = (pl.BlockSpec(memory_space=space) for space in (pltpu.VMEM, pl.ANY))
    tokens, width = cot.shape
    routing = [jax.ShapeDtypeStruct((tokens, slots), BF16)] * 3
    a_all, b_all, *rest = pl.pallas_call(
        gather_kernel,
        in_specs=[vmem] * 9 + [any_space] * 3,
        out_specs=[any_space] * 5 + [vmem] * 3 + [any_space],
        out_shape=[jax.ShapeDtypeStruct(shape + (c,), query.dtype) for c in cols]
        + [jax.ShapeDtypeStruct(v.shape, v.dtype) for v in (gate, up, down)]
        + routing + [jax.ShapeDtypeStruct((slots, width), BF16)],
        scratch_shapes=[pltpu.VMEM((rows, c), query.dtype) for c in cols] + [
            pltpu.VMEM((tokens, slots), BF16),
            pltpu.VMEM((slots, width), BF16),
            pltpu.SemaphoreType.DMA,
            pltpu.SemaphoreType.DMA((2,)),
            pltpu.SemaphoreType.DMA((2, 21)),
            pltpu.SemaphoreType.DMA((2, 21)),
            pltpu.SemaphoreType.DMA((2, 16)),
            pltpu.SemaphoreType.DMA((2, 16)),
            pltpu.SemaphoreType.DMA((3,)),
            pltpu.SemaphoreType.DMA((3,)),
        ],
        compiler_params=pltpu.CompilerParams(
            collective_id=0, has_side_effects=True, vmem_limit_bytes=VMEM_LIMIT
        ),
        cost_estimate=pl.CostEstimate(flops=0, bytes_accessed=250_000_000, transcendentals=0),
        name="gather_weights",
    )(query, key, value, out, extra, ids, gates, experts, cot, gate, up, down)
    return a_all.reshape(-1, cols[0]), b_all.reshape(-1, cols[1]), rest[:3], rest[3:]


ORDER = (2, 1, 3, 0)
SLICE = 16


def up(v):
    return lax.rem(v + 1, RING)


def down(v):
    return lax.rem(v + RING - 1, RING)


def add_into(target, *terms):
    flat = [target.shape[0]] if len(target.shape) == 3 else []
    for lead in range(flat[0]) if flat else (None,):
        for start in range(0, target.shape[-2], SLICE):
            at = (pl.ds(start, SLICE), slice(None))
            at = at if lead is None else (lead,) + at
            total = terms[0][at].astype(F32)
            for term in terms[1:]:
                total = total + term[at].astype(F32)
            target[at] = total.astype(target.dtype)


def scatter_kernel(
    a_ref, b_ref, extra_ref, wide_ref, tall_ref, a_out, b_out, wide_out, tall_out, a_mine, b_mine, a_theirs, b_theirs, a_one, b_one, a_two, b_two,
    a_first, b_first, a_last, b_last, a_x, b_x, load_sem, send_sem, recv_sem,
    gains_here, gains_there,
    extra_load_sem, extra_send_sem, extra_recv_sem, give_sem, take_sem, gains_sem,
):
    y, core, z, x = place()
    greet(neighbours() + [other_tp(), opposite()])
    moved = [
        swap_opposite(wide_ref, wide_out, give_sem.at[0], take_sem.at[0]),
        swap_opposite(tall_ref, tall_out, give_sem.at[1], take_sem.at[1]),
    ]

    @pl.when(jnp.logical_not(native()))
    def _():
        for copy in moved:
            copy.start()

    grads, outs = (a_ref, b_ref), (a_out, b_out)
    mine, theirs = (a_mine, b_mine), (a_theirs, b_theirs)
    one, two = (a_one, b_one), (a_two, b_two)
    first, last, side = (a_first, b_first), (a_last, b_last), (a_x, b_x)
    me = ((z, y), (y, z))
    sent = []

    def chunk(n, i, j, c):
        return grads[n].at[j, c, i] if n == 0 else grads[n].at[i, c, j]

    def to(n, i, j):
        return device(j, core, i, x) if n == 0 else device(i, core, j, x)

    def copy_of(n, src, dst, slot, where):
        return pltpu.make_async_remote_copy(
            src_ref=src, dst_ref=dst, send_sem=send_sem.at[n, slot], recv_sem=recv_sem.at[n, slot],
            device_id=where, device_id_type=MESH,
        )

    def send(n, src, dst, slot, where):
        copy = copy_of(n, src, dst, slot, where)
        copy.start()
        sent.append(copy)

    def arrived(n, dst, slot):
        copy_of(n, dst, dst, slot, device(y, core, z, x)).wait_recv()

    cols = b_ref.shape[-1]

    def columns(ref, start, count):
        return ref.at[:, :, pl.ds(start, count)]

    def extra_copy(slot):
        ref = columns(theirs[1].at[slot], cols, extra_ref.shape[-1])
        far = extra_ref.at[lax.rem(y + slot // RING, RING), 1 - core, lax.rem(z + slot % RING, RING)]
        return pltpu.make_async_remote_copy(
            src_ref=far, dst_ref=ref, send_sem=extra_send_sem.at[slot],
            recv_sem=extra_recv_sem.at[slot], device_id=device(y, 1 - core, z, x),
            device_id_type=MESH,
        )

    def extra_load(slot):
        near = extra_ref.at[lax.rem(y + slot // RING, RING), core, lax.rem(z + slot % RING, RING)]
        return pltpu.make_async_copy(
            near, columns(mine[1].at[slot], cols, extra_ref.shape[-1]), extra_load_sem.at[slot]
        )

    def load(n, di, dj):
        i, j = me[n]
        slot = di * RING + dj
        target = mine[n].at[slot] if n == 0 else columns(mine[n].at[slot], 0, cols)
        return pltpu.make_async_copy(
            chunk(n, lax.rem(i + di, RING), lax.rem(j + dj, RING), core), target,
            load_sem.at[n, slot],
        )

    for dj in ORDER:
        for di in ORDER:
            for n in (0, 1):
                i, j = me[n]
                slot = di * RING + dj
                there = chunk(n, lax.rem(i + di, RING), lax.rem(j + dj, RING), 1 - core)
                target = theirs[n].at[slot] if n == 0 else columns(theirs[n].at[slot], 0, cols)
                send(n, there, target, slot, device(y, 1 - core, z, x))
                load(n, di, dj).start()
                if n == 1:
                    extra_copy(slot).start()
                    extra_load(slot).start()

    def ready(n, di, dj):
        slot = di * RING + dj
        load(n, di, dj).wait()
        if n == 0:
            arrived(n, theirs[n].at[slot], slot)
        else:
            arrived(n, columns(theirs[n].at[slot], 0, cols), slot)
            extra_load(slot).wait()
            extra_copy(slot).wait_recv()
        return slot

    for di in ORDER:
        for n in (0, 1):
            i, j = me[n]
            slot = ready(n, di, 2)
            add_into(mine[n].at[slot], mine[n].at[slot], theirs[n].at[slot])
            for half in (0, 1):
                send(
                    n, mine[n].at[slot, half], one[n].at[di, half], 16 + di * 2 + half,
                    to(n, i, up(j) if half == 0 else down(j)),
                )
    for di in ORDER:
        for n in (0, 1):
            i, j = me[n]
            for half, dj in ((0, 1), (1, 3)):
                slot = ready(n, di, dj)
                arrived(n, one[n].at[di, half], 16 + di * 2 + half)
                add_into(
                    mine[n].at[slot, half], mine[n].at[slot, half], theirs[n].at[slot, half],
                    one[n].at[di, half],
                )
                add_into(
                    mine[n].at[slot, 1 - half], mine[n].at[slot, 1 - half],
                    theirs[n].at[slot, 1 - half],
                )
                send(
                    n, mine[n].at[slot], two[n].at[di, half], 24 + di * 2 + half,
                    to(n, i, up(j) if half == 0 else down(j)),
                )
    for di in ORDER:
        for n in (0, 1):
            i, j = me[n]
            slot = ready(n, di, 0)
            for half in (0, 1):
                arrived(n, two[n].at[di, half], 24 + di * 2 + half)
            add_into(
                mine[n].at[slot], mine[n].at[slot], theirs[n].at[slot], two[n].at[di, 0],
                two[n].at[di, 1],
            )
            if di == 2:
                for half in (0, 1):
                    send(
                        n, mine[n].at[slot, half], first[n].at[half], 32 + half,
                        to(n, up(i) if half == 0 else down(i), j),
                    )
            elif di != 0:
                half = 0 if di == 1 else 1
                arrived(n, first[n].at[half], 32 + half)
                add_into(mine[n].at[slot, half], mine[n].at[slot, half], first[n].at[half])
                send(
                    n, mine[n].at[slot], last[n].at[half], 34 + half,
                    to(n, up(i) if half == 0 else down(i), j),
                )
    for n in (0, 1):
        for half in (0, 1):
            arrived(n, last[n].at[half], 34 + half)
        add_into(mine[n].at[0], mine[n].at[0], last[n].at[0], last[n].at[1])
        send(n, mine[n].at[0, 1 - x], side[n], 36, device(y, core, z, 1 - x))
    for n in (0, 1):
        arrived(n, side[n], 36)
        add_into(outs[n], mine[n].at[0, x], side[n])
    gains_here[...] = b_out[:, cols:]
    gains = pltpu.make_async_remote_copy(
        src_ref=gains_here, dst_ref=gains_there, send_sem=gains_sem.at[0],
        recv_sem=gains_sem.at[1], device_id=other_tp(), device_id_type=MESH,
    )
    gains.start()
    for copy in sent:
        copy.wait_send()
    for slot in range(RING * RING):
        extra_copy(slot).wait_send()
    gains.wait()
    b_out[:, cols:] = gains_here[...] + gains_there[...]

    @pl.when(jnp.logical_not(native()))
    def _():
        for copy in moved:
            copy.wait()


def scatter_grads(a, b, extra, wide, tall):
    peers = RING * RING * 4
    rows = a.shape[0] // peers
    shape = (RING, 2, RING, 2, rows)
    cols = (a.shape[1], b.shape[1] + extra.shape[1])
    buffers = []
    for lead in ((16, 2), (16, 2), (4, 2), (4, 2, 2), (2,), (2, 2), ()):
        buffers += [pltpu.VMEM(lead + (rows, c), a.dtype) for c in cols]
    any_space = pl.BlockSpec(memory_space=pl.ANY)
    return pl.pallas_call(
        scatter_kernel,
        in_specs=[any_space] * 5,
        out_specs=[pl.BlockSpec(memory_space=pltpu.VMEM)] * 2 + [any_space] * 2,
        out_shape=[jax.ShapeDtypeStruct((rows, c), F32) for c in cols]
        + [jax.ShapeDtypeStruct(v.shape, v.dtype) for v in (wide, tall)],
        scratch_shapes=buffers + [
            pltpu.SemaphoreType.DMA((2, 16)),
            pltpu.SemaphoreType.DMA((2, 37)),
            pltpu.SemaphoreType.DMA((2, 37)),
            pltpu.VMEM((rows, extra.shape[1]), F32),
            pltpu.VMEM((rows, extra.shape[1]), F32),
            pltpu.SemaphoreType.DMA((16,)),
            pltpu.SemaphoreType.DMA((16,)),
            pltpu.SemaphoreType.DMA((16,)),
            pltpu.SemaphoreType.DMA((2,)),
            pltpu.SemaphoreType.DMA((2,)),
            pltpu.SemaphoreType.DMA((2,)),
        ],
        compiler_params=pltpu.CompilerParams(
            collective_id=1, has_side_effects=True, vmem_limit_bytes=44 * 1024 * 1024
        ),
        cost_estimate=pl.CostEstimate(flops=0, bytes_accessed=250_000_000, transcendentals=0),
        name="scatter_grads",
    )(*(v.reshape(shape + (v.shape[1],)) for v in (a, b, extra)), wide, tall)


BLOCK = 64
CTX = 8


def rotated(u, gain, cosine, sine):
    scaling = lax.rsqrt(jnp.mean(u * u, axis=-1, keepdims=True) + EPS)
    normed = u * scaling
    n = normed * gain
    rot = n * cosine + pltpu.roll(n, HEAD_SIZE // 2, 1) * sine
    return rot.astype(BF16), normed, scaling


def rotated_back(e, normed, scaling, gain, cosine, sine):
    back = e * cosine + pltpu.roll(e * sine, HEAD_SIZE // 2, 1)
    scaled = back * gain
    inner = jnp.mean(scaled * normed, axis=-1, keepdims=True)
    return scaling * (scaled - normed * inner), jnp.sum(back * normed, axis=0, keepdims=True)


def ctx_peer(step):
    return {"ctx": lax.rem(lax.axis_index("ctx") + step, CTX)}


def beside():
    c = lax.axis_index("ctx")
    return {"ctx": c + 1 - 2 * lax.rem(c, 2)}


def remote(src, dst, send_sem, recv_sem, where):
    return pltpu.make_async_remote_copy(
        src_ref=src, dst_ref=dst, send_sem=send_sem, recv_sem=recv_sem, device_id=where,
        device_id_type=MESH,
    )


def softmax_parts(q_low, k, bias):
    s = dot(q_low, k, ((1,), (1,))) * (HEAD_SIZE ** -0.5) + bias
    e = jnp.exp(s - jnp.max(s, axis=-1, keepdims=True))
    return e / jnp.sum(e, axis=-1, keepdims=True)


def share_kernel(kv, rows_ref, cos_ref, sin_ref, gk_ref, kv_ref, held, send_sem, recv_sem):
    c = lax.axis_index("ctx")
    greet([ctx_peer(step) for step in range(1, CTX)])
    micro, rows = held.shape[0], 2 * BLOCK
    cosine, sine, gk = cos_ref[...], sin_ref[...], gk_ref[...]
    mine = pl.ds(pl.multiple_of(c * BLOCK, BLOCK), BLOCK)
    earlier, own = pl.ds(CTX * BLOCK, BLOCK), pl.ds((CTX + 1) * BLOCK, BLOCK)
    copies = []
    for m in range(micro):
        span = slice(m * rows, (m + 1) * rows)
        for h in range(2 * kv):
            cols = slice(h * HEAD_SIZE, (h + 1) * HEAD_SIZE)
            u = rows_ref[span, cols]
            low = rotated(u, gk, cosine, sine)[0] if h < kv else u.astype(BF16)
            held[m, mine, cols] = low[:BLOCK]
            held[m, own, cols] = low[BLOCK:]
        for step in range(1, CTX):
            part = held.at[m, mine]
            copies.append(
                remote(part, part, send_sem.at[step, m], recv_sem.at[step, m], ctx_peer(step))
            )
        copies.append(
            remote(
                held.at[m, own], held.at[m, earlier], send_sem.at[0, m], recv_sem.at[0, m], beside()
            )
        )
        for copy in copies[-CTX:]:
            copy.start()
    for m in range(micro):
        for step in range(1, CTX):
            source = lax.rem(c + CTX - step, CTX)
            part = held.at[m, pl.ds(pl.multiple_of(source * BLOCK, BLOCK), BLOCK)]
            remote(
                part, part, send_sem.at[step, m], recv_sem.at[step, m], ctx_peer(step)
            ).wait_recv()
        copies[(m + 1) * CTX - 1].wait_recv()
        kv_ref[m] = held[m]
    for copy in copies:
        copy.wait_send()


def attention_kernel(heads, q_ref, cos_ref, sin_ref, gq_ref, bias_ref, k_ref, v_ref, o_ref):
    cosine, sine, gq = cos_ref[...], sin_ref[...], gq_ref[...]
    for e in range(heads):
        cols = slice(e * HEAD_SIZE, (e + 1) * HEAD_SIZE)
        q_low = rotated(q_ref[:, cols], gq, cosine, sine)[0]
        p = softmax_parts(q_low, k_ref[...], bias_ref[...]).astype(BF16)
        o_ref[:, cols] = dot(p, v_ref[...], ((1,), (0,))).astype(BF16)


def attention_back_kernel(
    kv, heads, qkv_ref, cos_ref, sin_ref, gq_ref, gk_ref, bias_ref, kv_ref, do_ref,
    dqkv_ref, gains_ref, grads, given, given_side, p_all, ds_all, q_all, do_all,
    send_sem, recv_sem,
):
    c = lax.axis_index("ctx")
    greet([ctx_peer(step) for step in range(1, CTX)])
    micro, rows = grads.shape[0], 2 * BLOCK
    q_cols = kv * heads * HEAD_SIZE
    scale = HEAD_SIZE ** -0.5
    cosine, sine, gq, gk = cos_ref[...], sin_ref[...], gq_ref[...], gk_ref[...]
    mine = pl.ds(pl.multiple_of(c * BLOCK, BLOCK), BLOCK)
    earlier, own = pl.ds(CTX * BLOCK, BLOCK), pl.ds((CTX + 1) * BLOCK, BLOCK)

    def head_cols(h):
        return pl.ds(pl.multiple_of(h * HEAD_SIZE, HEAD_SIZE), HEAD_SIZE)

    def keys_back(m, h, carry):
        span = slice(m * rows, (m + 1) * rows)
        k, v = kv_ref[m, :, head_cols(h)], kv_ref[m, :, head_cols(kv + h)]
        for e in range(heads):
            cols = head_cols(h * heads + e)
            stack = slice(e * rows, (e + 1) * rows)
            q_low = rotated(qkv_ref[span, cols], gq, cosine, sine)[0]
            q_all[stack, :] = q_low
            p = softmax_parts(q_low, k, bias_ref[...])
            p_all[stack, :] = p.astype(BF16)
            do = do_ref[span, cols]
            do_all[stack, :] = do
            dp = dot(do, v, ((1,), (1,)))
            ds = (p * (dp - jnp.sum(dp * p, axis=-1, keepdims=True))).astype(BF16)
            ds_all[m * kv + h, stack, :] = ds
        grads[m, :, head_cols(kv + h)] = dot(p_all[...], do_all[...], ((0,), (0,))).astype(BF16)
        d_k = dot(ds_all[m * kv + h], q_all[...], ((0,), (0,))) * scale
        grads[m, :, head_cols(h)] = d_k.astype(BF16)
        return carry

    def queries_back(m, h, total):
        span = slice(m * rows, (m + 1) * rows)
        k = kv_ref[m, :, head_cols(h)]
        for e in range(heads):
            cols = head_cols(h * heads + e)
            ds = ds_all[m * kv + h, e * rows : (e + 1) * rows, :]
            dqr = (dot(ds, k, ((1,), (0,))) * scale).astype(BF16).astype(F32)
            u = qkv_ref[span, cols]
            scaling = lax.rsqrt(jnp.mean(u * u, axis=-1, keepdims=True) + EPS)
            dq, part = rotated_back(dqr, u * scaling, scaling, gq, cosine, sine)
            dqkv_ref[span, cols] = dq.astype(BF16)
            total = total + part
        return total

    copies = []
    for m in range(micro):
        lax.fori_loop(0, kv, functools.partial(keys_back, m), 0)
        for step in range(1, CTX):
            peer = lax.rem(c + step, CTX)
            part = grads.at[m, pl.ds(pl.multiple_of(peer * BLOCK, BLOCK), BLOCK)]
            copies.append(
                remote(
                    part, given.at[step - 1, m], send_sem.at[step, m], recv_sem.at[step, m],
                    ctx_peer(step),
                )
            )
        copies.append(
            remote(
                grads.at[m, earlier], given_side.at[m], send_sem.at[0, m], recv_sem.at[0, m],
                beside(),
            )
        )
        for copy in copies[-CTX:]:
            copy.start()
    total = jnp.zeros((1, HEAD_SIZE), F32)
    for m in range(micro):
        total = lax.fori_loop(0, kv, functools.partial(queries_back, m), total)
    k_total = jnp.zeros((1, HEAD_SIZE), F32)
    for m in range(micro):
        for copy in copies[m * CTX : (m + 1) * CTX]:
            copy.wait_recv()
        for h in range(2 * kv):
            cols = slice(h * HEAD_SIZE, (h + 1) * HEAD_SIZE)
            at = slice(q_cols + h * HEAD_SIZE, q_cols + (h + 1) * HEAD_SIZE)
            prompt = grads[m, mine, cols].astype(F32)
            for step in range(CTX - 1):
                prompt = prompt + given[step, m, :, cols].astype(F32)
            cont = grads[m, own, cols].astype(F32) + given_side[m, :, cols].astype(F32)
            e = jnp.concatenate([prompt, cont], axis=0).astype(BF16)
            span = slice(m * rows, (m + 1) * rows)
            if h < kv:
                _, normed, scaling = rotated(qkv_ref[span, at], gk, cosine, sine)
                d, part = rotated_back(e.astype(F32), normed, scaling, gk, cosine, sine)
                k_total = k_total + part
                dqkv_ref[span, at] = d.astype(BF16)
            else:
                dqkv_ref[span, at] = e
    gains_ref[0:1, :] = total
    gains_ref[1:2, :] = k_total
    for copy in copies:
        copy.wait_send()


def share_keys(qkv, cosine, sine, gain_key, kv, keys, micro):
    rows, cols = qkv.shape[0], 2 * kv * HEAD_SIZE
    last = qkv.shape[1] // cols - 1

    def whole(shape):
        return pl.BlockSpec(shape, lambda i: (0,) * len(shape))

    return pl.pallas_call(
        functools.partial(share_kernel, kv),
        grid=(1,),
        in_specs=[pl.BlockSpec((rows, cols), lambda i: (0, last)), whole(cosine.shape)]
        + [whole(sine.shape), whole(gain_key.shape)],
        out_specs=whole((micro, keys, cols)),
        out_shape=jax.ShapeDtypeStruct((micro, keys, cols), BF16),
        scratch_shapes=[
            pltpu.VMEM((micro, keys, cols), BF16),
            pltpu.SemaphoreType.DMA((CTX, micro)),
            pltpu.SemaphoreType.DMA((CTX, micro)),
        ],
        compiler_params=pltpu.CompilerParams(
            collective_id=2, has_side_effects=True, vmem_limit_bytes=VMEM_LIMIT
        ),
        cost_estimate=pl.CostEstimate(flops=0, bytes_accessed=50_000_000, transcendentals=0),
        name="share_keys",
    )(qkv, cosine, sine, gain_key)


def attention(qkv, cosine, sine, gain_query, bias, kv_all, kv):
    micro, keys, cols = kv_all.shape
    rows = bias.shape[0]
    heads = qkv.shape[1] // HEAD_SIZE // kv - 2
    width = heads * HEAD_SIZE

    def whole(v):
        return pl.BlockSpec(v.shape, lambda m, g: (0,) * v.ndim)

    return pl.pallas_call(
        functools.partial(attention_kernel, heads),
        grid=(micro, kv),
        in_specs=[pl.BlockSpec((rows, width), lambda m, g: (m, g))]
        + [whole(v) for v in (cosine, sine, gain_query, bias)]
        + [
            pl.BlockSpec((None, keys, HEAD_SIZE), lambda m, g: (m, 0, g)),
            pl.BlockSpec((None, keys, HEAD_SIZE), lambda m, g: (m, 0, kv + g)),
        ],
        out_specs=pl.BlockSpec((rows, width), lambda m, g: (m, g)),
        out_shape=jax.ShapeDtypeStruct((micro * rows, kv * width), BF16),
        compiler_params=pltpu.CompilerParams(vmem_limit_bytes=VMEM_LIMIT),
        cost_estimate=pl.CostEstimate(flops=0, bytes_accessed=60_000_000, transcendentals=0),
        name="attention_forward",
    )(qkv, cosine, sine, gain_query, bias, kv_all, kv_all)


def attention_back(qkv, cosine, sine, gain_query, gain_key, bias, kv_all, d_out, kv):
    heads = qkv.shape[1] // HEAD_SIZE // kv - 2
    rows, keys = bias.shape
    micro, _, kv_cols = kv_all.shape
    return pl.pallas_call(
        functools.partial(attention_back_kernel, kv, heads),
        out_shape=[
            jax.ShapeDtypeStruct(qkv.shape, BF16),
            jax.ShapeDtypeStruct((2, HEAD_SIZE), F32),
        ],
        scratch_shapes=[
            pltpu.VMEM((micro, keys, kv_cols), BF16),
            pltpu.VMEM((CTX - 1, micro, BLOCK, kv_cols), BF16),
            pltpu.VMEM((micro, BLOCK, kv_cols), BF16),
            pltpu.VMEM((heads * rows, keys), BF16),
            pltpu.VMEM((micro * kv, heads * rows, keys), BF16),
            pltpu.VMEM((heads * rows, HEAD_SIZE), BF16),
            pltpu.VMEM((heads * rows, HEAD_SIZE), BF16),
            pltpu.SemaphoreType.DMA((CTX, micro)),
            pltpu.SemaphoreType.DMA((CTX, micro)),
        ],
        compiler_params=pltpu.CompilerParams(
            collective_id=3, has_side_effects=True, vmem_limit_bytes=VMEM_LIMIT
        ),
        cost_estimate=pl.CostEstimate(flops=0, bytes_accessed=120_000_000, transcendentals=0),
        name="attention_backward",
    )(qkv, cosine, sine, gain_query, gain_key, bias, kv_all, d_out)


CHIPS = RING * RING * RING
GROUP = 16
MIX = 11
AHEAD = 2
TILE = 256


def chip_at(slot, sign):
    f, c, t = lax.axis_index("fsdp"), lax.axis_index("ctx"), lax.axis_index("tp")
    k = lax.rem(slot * MIX, CHIPS) * sign
    turn = 0 if sign > 0 else RING
    far = [lax.div(k, RING * RING), lax.rem(lax.div(k, RING), RING), lax.rem(k, RING)]
    own = [lax.div(f, 2), lax.div(c, 2), t * 2 + lax.rem(c, 2)]
    return [lax.rem(o + d + turn, RING) for o, d in zip(own, far)]


def device_at(slot, sign):
    y, z, x = chip_at(slot, sign)
    core = lax.rem(lax.axis_index("fsdp"), 2)
    return {"fsdp": y * 2 + core, "ctx": z * 2 + lax.rem(x, 2), "tp": lax.div(x, 2)}


def chip_number(slot, sign):
    y, z, x = chip_at(slot, sign)
    return (y * 2 * RING + z * 2 + lax.rem(x, 2)) * 2 + lax.div(x, 2)


def other_core():
    f = lax.axis_index("fsdp")
    return {"fsdp": f + 1 - 2 * (f % 2)}


def moe_kernel(
    send_ref, deo_ref, gate_ref, up_ref, down_ref, gate_far, up_far, down_far,
    back_ref, eo_ref, wide_ref, tall_ref,
    rows, deos, gu, down, z, dgu, wide, tall, give, take,
    go_sem, come_sem, load_sem, weight_sem, share_send, share_recv, part_send, part_recv,
    back_send, back_recv, eo_sem,
):
    size, hidden = send_ref.shape[1], down_ref.shape[0]
    count = GROUP * size
    groups = CHIPS // GROUP
    width = down_ref.shape[1]

    def each(body, low, high):
        def step(i, carry):
            body(i)
            return carry

        lax.fori_loop(low, high, step, 0)

    barrier = pltpu.get_barrier_semaphore()
    each(
        lambda s: pl.semaphore_signal(
            barrier, inc=1, device_id=device_at(s, 1), device_id_type=MESH
        ),
        1, CHIPS,
    )
    pl.semaphore_signal(barrier, inc=1, device_id=other_core(), device_id_type=MESH)
    pl.semaphore_wait(barrier, CHIPS)

    def slot_rows(s):
        return pl.ds(pl.multiple_of(s * size, size), size)

    def group_rows(g):
        return pl.ds(pl.multiple_of(g * count, count), count)

    def go(s):
        return remote(
            send_ref.at[s], rows.at[0, slot_rows(s)], go_sem.at[s], come_sem.at[s], device_at(s, 1)
        )

    def stay(s):
        return pltpu.make_async_copy(send_ref.at[s], rows.at[0, slot_rows(s)], come_sem.at[s])

    def load(s):
        return pltpu.make_async_copy(
            deo_ref.at[chip_number(s, -1)], deos.at[0, slot_rows(s)], load_sem.at[s]
        )

    def sent_rows(n, s):
        slot = lax.rem(lax.div(s, GROUP), 2)
        return give.at[n, slot, slot_rows(lax.rem(s, GROUP))]

    def back(s):
        return remote(
            sent_rows(0, s), back_ref.at[s], back_send.at[s], back_recv.at[s], device_at(s, -1)
        )

    def back_stay():
        return pltpu.make_async_copy(
            give.at[0, 0, pl.ds(0, size)], back_ref.at[0], back_recv.at[0]
        )

    def out(s):
        return pltpu.make_async_copy(
            sent_rows(1, s), eo_ref.at[chip_number(s, -1)], eo_sem.at[s]
        )

    def share(n, g):
        ref = (rows, deos)[n]
        return remote(
            ref.at[0, group_rows(g)], ref.at[1, group_rows(g)], share_send.at[n, g],
            share_recv.at[n, g], other_core(),
        )

    def part(n, g):
        slot = lax.rem(g, 2)
        return remote(
            give.at[n, slot], take.at[n, slot], part_send.at[n, g], part_recv.at[n, g],
            other_core(),
        )

    places = (gu.at[:, pl.ds(0, hidden)], gu.at[:, pl.ds(hidden, hidden)], down)
    weights = [
        [pltpu.make_async_copy(src, dst, weight_sem.at[n]) for n, (src, dst) in enumerate(pairs)]
        for pairs in (
            zip((gate_ref, up_ref, down_ref), places), zip((gate_far, up_far, down_far), places)
        )
    ]

    def on_weights(act):
        for condition, copies in zip((native(), jnp.logical_not(native())), weights):

            @pl.when(condition)
            def _(copies=copies):
                for copy in copies:
                    act(copy)

    stay(0).start()
    each(lambda s: go(s).start(), 1, AHEAD * GROUP)
    each(lambda s: load(s).start(), 0, CHIPS)
    on_weights(lambda copy: copy.start())

    def tiles(body):
        each(lambda i: body(pl.ds(pl.multiple_of(i * TILE, TILE), TILE)), 0, width // TILE)

    def clear(at):
        wide[at, :] = jnp.zeros((TILE, 2 * hidden), F32)
        tall[:, at] = jnp.zeros((hidden, TILE), F32)

    tiles(clear)

    def through(side, g):
        at = group_rows(g)
        pre = dot(rows[side, at, :], gu[...], ((1,), (0,)))
        dz = dot(deos[side, at, :], down[...], ((1,), (1,)))
        gate, u = pre[:, :hidden], pre[:, hidden:]
        sig = 1.0 / (1.0 + jnp.exp(-gate))
        act = gate * sig
        z[side] = (act * u).astype(BF16)
        dgu[side, :, :hidden] = (dz * u * sig * (1.0 + gate * (1.0 - sig))).astype(BF16)
        dgu[side, :, hidden:] = (dz * act).astype(BF16)

    def to_rows(side):
        return dot(dgu[side], gu[...], ((1,), (1,)))

    def to_outputs(side):
        return dot(z[side], down[...], ((1,), (0,)))

    on_weights(lambda copy: copy.wait())

    def group(g):
        first, last, slot = g * GROUP, (g + 1) * GROUP, lax.rem(g, 2)

        @pl.when(g == 0)
        def _():
            stay(0).wait()

        each(lambda s: go(s).wait_recv(), lax.max(first, 1), last)
        each(lambda s: load(s).wait(), first, last)
        each(
            lambda s: go(s).start(), lax.min(first + AHEAD * GROUP, CHIPS),
            lax.min(last + AHEAD * GROUP, CHIPS),
        )
        for n in (0, 1):
            share(n, g).start()
        through(0, g)
        for n in (0, 1):
            share(n, g).wait_recv()
        through(1, g)

        @pl.when(g >= 2)
        def _():
            @pl.when(g == 2)
            def _():
                back_stay().wait()

            each(lambda s: back(s).wait_send(), lax.max(first - 2 * GROUP, 1), last - 2 * GROUP)
            each(lambda s: out(s).wait(), first - 2 * GROUP, last - 2 * GROUP)

        give[0, slot] = to_rows(1).astype(BF16)
        part(0, g).start()
        give[1, slot] = to_outputs(1).astype(BF16)
        part(1, g).start()
        own = to_rows(0)
        part(0, g).wait()
        give[0, slot] = (own + take[0, slot].astype(F32)).astype(BF16)

        @pl.when(g == 0)
        def _():
            back_stay().start()

        each(lambda s: back(s).start(), lax.max(first, 1), last)
        own = to_outputs(0)
        part(1, g).wait()
        give[1, slot] = (own + take[1, slot].astype(F32)).astype(BF16)
        each(lambda s: out(s).start(), first, last)
        at = group_rows(g)

        def weight_grads(cols):
            wide[cols, :] += dot(rows[0, at, cols], dgu[0], ((0,), (0,))) + dot(
                rows[1, at, cols], dgu[1], ((0,), (0,))
            )
            tall[:, cols] += dot(z[0], deos[0, at, cols], ((0,), (0,))) + dot(
                z[1], deos[1, at, cols], ((0,), (0,))
            )

        tiles(weight_grads)

    each(group, 0, groups)

    def store(at):
        wide_ref[at, :] = wide[at, :].astype(BF16)
        tall_ref[:, at] = tall[:, at].astype(BF16)

    tiles(store)
    for g in range(groups):
        for n in (0, 1):
            share(n, g).wait_send()
    each(lambda s: out(s).wait(), (groups - 2) * GROUP, CHIPS)
    each(lambda s: back(s).wait_send(), (groups - 2) * GROUP, CHIPS)
    each(lambda s: go(s).wait_send(), 1, CHIPS)
    each(lambda s: back(s).wait_recv(), 1, CHIPS)


def moe(send, d_eo, own, far):
    chips, size, width = send.shape
    hidden = own[2].shape[0]
    total, groups = chips * size, chips // GROUP
    count = GROUP * size
    vmem, any_space = (pl.BlockSpec(memory_space=space) for space in (pltpu.VMEM, pl.ANY))
    shapes = [send.shape, send.shape, (width, 2 * hidden), (hidden, width)]
    dma = pltpu.SemaphoreType.DMA
    return pl.pallas_call(
        moe_kernel,
        in_specs=[any_space] * 8,
        out_specs=[any_space] * 2 + [vmem] * 2,
        out_shape=[jax.ShapeDtypeStruct(shape, BF16) for shape in shapes],
        scratch_shapes=[
            pltpu.VMEM((2, total, width), BF16),
            pltpu.VMEM((2, total, width), BF16),
            pltpu.VMEM((width, 2 * hidden), BF16),
            pltpu.VMEM((hidden, width), BF16),
            pltpu.VMEM((2, count, hidden), BF16),
            pltpu.VMEM((2, count, 2 * hidden), BF16),
            pltpu.VMEM((width, 2 * hidden), F32),
            pltpu.VMEM((hidden, width), F32),
            pltpu.VMEM((2, 2, count, width), BF16),
            pltpu.VMEM((2, 2, count, width), BF16),
            dma((chips,)), dma((chips,)), dma((chips,)), dma((3,)),
            dma((2, groups)), dma((2, groups)), dma((2, groups)), dma((2, groups)),
            dma((chips,)), dma((chips,)), dma((chips,)),
        ],
        compiler_params=pltpu.CompilerParams(
            collective_id=4, has_side_effects=True, vmem_limit_bytes=56 * 1024 * 1024
        ),
        cost_estimate=pl.CostEstimate(flops=0, bytes_accessed=400_000_000, transcendentals=0),
        name="experts",
    )(send, d_eo, *own, *far)


def normalize(rows, gain):
    scaling = lax.rsqrt(jnp.mean(rows * rows, axis=-1, keepdims=True) + EPS)
    return rows * scaling * gain, scaling


def normalize_back(rows, scaling, gain, upstream):
    normed = rows * scaling
    gain_grad = jnp.sum((upstream * normed).reshape(-1, rows.shape[-1]), axis=0)
    scaled = upstream * gain
    inner = jnp.mean(scaled * normed, axis=-1, keepdims=True)
    return scaling * (scaled - normed * inner), gain_grad


def swap_tp(value):
    return lax.ppermute(value, "tp", [(0, 1), (1, 0)])


def local(
    x_prompt, x_cont, cot_prompt, cot_cont, ids_prompt, ids_cont, gates_prompt, gates_cont,
    norm_gain, query_weight, key_matrix, value_matrix, out_weight, query_gain, key_gain, moe_gain,
    expert_gate, expert_up, expert_down,
):
    micro = x_prompt.shape[0]
    prompt_rows, cont_rows, width = x_prompt.shape[2], x_cont.shape[2], x_prompt.shape[3]
    block = cont_rows
    rows = 2 * block
    s = lax.axis_index("ctx")
    ctx = lax.axis_size("ctx")
    first = lax.axis_index("tp") == 0
    peers = lax.axis_size(ALL)
    q_cols, kv_cols = query_weight.shape[1], key_matrix.shape[1]
    kv = kv_cols // HEAD_SIZE
    qkv_cols = q_cols + 2 * kv_cols
    shard_rows = query_weight.shape[0]
    hidden = expert_gate.shape[2]
    slots = cont_rows * TOPK // peers

    fsdp, tp = lax.axis_size("fsdp"), lax.axis_size("tp")
    chips = [(2 * y, c, t) for y in range(fsdp // 2) for c in range(ctx) for t in range(tp)]
    groups = [[((f + core) * ctx + c) * tp + t for f, c, t in chips] for core in range(2)]
    expert_of = jnp.array([(f + t) * ctx + c for f, c, t in chips], jnp.int32)

    def exchange(rows_of):
        return lax.all_to_all(
            rows_of, ("fsdp", "ctx", "tp"), split_axis=0, concat_axis=0, tiled=True,
            axis_index_groups=groups,
        )

    def pad(v):
        return jnp.pad(v[:, 0], ((0, 0), (0, block - prompt_rows), (0, 0)))

    x_first, x_second = pad(x_prompt), x_cont[:, 0]
    own_tokens = jnp.where(first, x_second, x_first).astype(F32)
    own_cot = jnp.where(first, cot_cont[:, 0], pad(cot_prompt))
    ids_pad = jnp.pad(
        ids_prompt[:, 0], ((0, 0), (0, block - prompt_rows), (0, 0)), constant_values=-1
    )
    own_ids = jnp.where(first, ids_cont[:, 0], ids_pad)
    own_gates = jnp.where(first, gates_cont[:, 0], pad(gates_prompt))

    y, z, x = chip_at(jnp.arange(peers, dtype=jnp.int32), 1)
    near = (2 * y + x // 2) * ctx + 2 * z + x % 2
    order = jnp.pad(jnp.stack([expert_of, near]), ((0, 0), (0, HEAD_SIZE - peers)), constant_values=-2)

    def lanes(v):
        return jnp.pad(v, [(0, 0)] * (v.ndim - 1) + [(0, HEAD_SIZE - v.shape[-1])])

    extra = jnp.stack([lanes(v) for v in (norm_gain, moe_gain, query_gain, key_gain)])
    extra = jnp.pad(extra, ((0, shard_rows - extra.shape[0]), (0, 0)))
    own_experts = (expert_gate[0], expert_up[0], expert_down[0])
    w_qkv, w_out_extra, far_experts, routing = gather_weights(
        query_weight, key_matrix, value_matrix, out_weight, extra,
        own_ids.reshape(-1, TOPK), own_gates.reshape(-1, TOPK), order,
        own_cot.reshape(-1, width), peers * micro * slots, *own_experts,
    )
    select_near, mixing_high, mixing_low, spread = routing
    w_out = w_out_extra[:, :q_cols]
    gains = w_out_extra[:, q_cols:].reshape(peers, shard_rows, HEAD_SIZE)[:, :4].astype(F32)
    gain_in, gain_moe = (gains[:, n, :shard_rows].reshape(-1) for n in (0, 1))
    head_rows = query_gain.shape[0]
    gain_query, gain_key = (gains[:, n, :head_rows].reshape(-1) for n in (2, 3))

    offsets = jnp.arange(rows, dtype=jnp.int32)
    is_prompt = offsets < block
    prompt_pos = s * prompt_rows + offsets
    cont_pos = s * cont_rows + offsets - block
    rot_place = jnp.where(is_prompt, prompt_pos, PROMPT + cont_pos % CL).astype(F32)
    steps_freq = jnp.arange(HEAD_SIZE // 2, dtype=F32) * (2.0 / HEAD_SIZE)
    angles = rot_place[:, None] * jnp.power(THETA, -steps_freq)[None, :]
    cosine, sine = jnp.cos(angles), jnp.sin(angles)
    cosine = jnp.concatenate([cosine, cosine], axis=1)
    sine = jnp.concatenate([-sine, sine], axis=1)
    keys = (ctx + 2) * block
    key_index = jnp.arange(keys, dtype=jnp.int32)[None, :]
    key_off = key_index % block
    key_prompt_pos = key_index // block * prompt_rows + key_off
    key_cont = (s - 1) * cont_rows + key_index - ctx * block
    is_cont = jnp.logical_not(is_prompt)[:, None]
    visible = jnp.where(
        key_index < ctx * block,
        jnp.logical_and(
            key_off < prompt_rows,
            jnp.logical_or(is_cont, key_prompt_pos <= prompt_pos[:, None]),
        ),
        jnp.logical_and(
            is_cont,
            jnp.logical_and(
                key_cont // CL == cont_pos[:, None] // CL, key_cont <= cont_pos[:, None]
            ),
        ),
    )
    bias = jnp.where(visible, 0.0, NEG).astype(F32)

    def share_rows(own):
        other = swap_tp(own)
        return jnp.where(first, other, own), jnp.where(first, own, other)

    def sum_own(part):
        part = part.reshape(micro, rows, width)
        given = jnp.where(first, part[:, :block], part[:, block:]).astype(BF16)
        kept = jnp.where(first, part[:, block:], part[:, :block])
        return kept + swap_tp(given).astype(F32)

    tokens = jnp.concatenate([x_first, x_second], axis=1).astype(F32).reshape(-1, width)
    a = normalize(tokens, gain_in)[0].astype(BF16)
    qkv = dot(a, w_qkv, ((1,), (0,)))
    heads_in = (cosine, sine, gain_query[None], gain_key[None], bias)
    kv_all = share_keys(qkv, cosine, sine, gain_key[None], kv, keys, micro)

    spread, kv_all = lax.optimization_barrier((spread, kv_all))
    d_eo_rows = exchange(spread).reshape(peers, micro * slots, width)
    o = attention(qkv, cosine, sine, gain_query[None], bias, kv_all, kv)
    middle = own_tokens + sum_own(dot(o, w_out, ((1,), (1,))))
    b_normed, b_scale = normalize(middle, gain_moe)
    b_low = b_normed.astype(BF16)

    send = dot(select_near, b_low.reshape(-1, width), ((0,), (0,))).astype(BF16)
    back, eo, wide_here, tall_here = moe(
        send.reshape(d_eo_rows.shape), d_eo_rows, own_experts, far_experts
    )
    d_b = dot(select_near, back.reshape(-1, width), ((1,), (0,))).reshape(middle.shape)
    middle_from, moe_total = normalize_back(middle, b_scale, gain_moe, d_b)
    d_h = own_cot.astype(F32) + middle_from
    d_attn = jnp.concatenate(share_rows(d_h.astype(BF16)), axis=1).reshape(-1, width)

    late, d_attn = lax.optimization_barrier((eo, d_attn))
    eo_back = exchange(late.reshape(-1, width))

    d_o = dot(d_attn, w_out, ((1,), (0,))).astype(BF16)
    d_qkv, head_totals = attention_back(qkv, *heads_in, kv_all, d_o, kv)
    input_part, d_attn, eo_back = lax.optimization_barrier(
        (dot(d_qkv, w_qkv, ((1,), (1,))), d_attn, eo_back)
    )
    input_grad = sum_own(input_part)
    grad_out = dot(d_attn, o, ((0,), (0,))).astype(BF16)
    moe_out = dot(mixing_high, eo_back, ((1,), (0,))) + dot(mixing_low, eo_back, ((1,), (0,)))
    out_first, out_second = share_rows((middle + moe_out.reshape(middle.shape)).astype(BF16))
    grad_qkv = dot(a, d_qkv, ((0,), (0,))).astype(BF16)
    scale_in = lax.rsqrt(jnp.mean(own_tokens * own_tokens, axis=-1, keepdims=True) + EPS)
    token_from, norm_total = normalize_back(own_tokens, scale_in, gain_in, input_grad)
    grad_first, grad_second = share_rows((d_h + token_from).astype(BF16))

    extra_grads = jnp.stack(
        [
            lanes(v.reshape(peers, -1))
            for v in (norm_total, moe_total, head_totals[0], head_totals[1])
        ],
        axis=1,
    )
    extra_grads = jnp.pad(extra_grads, ((0, 0), (0, shard_rows - extra_grads.shape[1]), (0, 0)))
    extra_grads = extra_grads.reshape(-1, HEAD_SIZE).astype(BF16)
    share, share_out, wide_there, tall_there = scatter_grads(
        grad_qkv, grad_out, extra_grads, wide_here, tall_here
    )
    grad_wide = jnp.where(native(), wide_here, wide_there).astype(F32)
    grad_down = jnp.where(native(), tall_here, tall_there).astype(F32)
    gain_share = share_out[:, q_cols:]
    return (
        out_first[:, None, :prompt_rows],
        out_second[:, None],
        grad_first[:, None, :prompt_rows],
        grad_second[:, None],
        gain_share[0, :shard_rows],
        share[:, :q_cols],
        share[:, q_cols : q_cols + kv_cols],
        share[:, q_cols + kv_cols : qkv_cols],
        share_out[:, :q_cols],
        gain_share[2, :head_rows],
        gain_share[3, :head_rows],
        gain_share[1, :shard_rows],
        grad_wide[None, :, :hidden],
        grad_wide[None, :, hidden:],
        grad_down[None],
    )


def solution(mesh):
    rows = P(None, "fsdp", "ctx", None)
    vector = P(("fsdp", "ctx"))
    matrix = P(("fsdp", "ctx"), "tp")
    wide = P(("fsdp", "ctx"), None, "tp")
    tall = P(("fsdp", "ctx"), "tp", None)
    in_specs = (rows,) * 8 + (vector,) + (matrix,) * 4 + (vector,) * 3 + (wide, wide, tall)
    out_specs = (rows,) * 4 + (vector,) + (matrix,) * 4 + (vector,) * 3 + (wide, wide, tall)
    return jax.shard_map(local, mesh=mesh, in_specs=in_specs, out_specs=out_specs, check_vma=False)
```

```python
import functools

import jax
import jax.numpy as jnp
from jax import lax
from jax.experimental import pallas as pl
from jax.experimental.pallas import tpu as pltpu
from jax.sharding import PartitionSpec as P

HEAD_SIZE = 128
TOPK = 8
PROMPT = 448
CL = 128
EPS = 1e-06
THETA = 1000000.0
NEG = -1e30
F32 = jnp.float32
BF16 = jnp.bfloat16
ALL = ("fsdp", "ctx")
MESH = pl.DeviceIdType.MESH
RING = 4
VMEM_LIMIT = 48 * 1024 * 1024


def dot(a, b, dims):
    return lax.dot_general(a, b, (dims, ((), ())), preferred_element_type=F32)


def remote(src, dst, send_sem, recv_sem, where):
    return pltpu.make_async_remote_copy(
        src_ref=src, dst_ref=dst, send_sem=send_sem, recv_sem=recv_sem, device_id=where,
        device_id_type=MESH,
    )


def place():
    f, c = lax.axis_index("fsdp"), lax.axis_index("ctx")
    return f // 2, f % 2, c // 2, c % 2


def device(y, core, z, x):
    return {"fsdp": y * 2 + core, "ctx": z * 2 + x}


def greet(partners):
    barrier = pltpu.get_barrier_semaphore()
    for partner in partners:
        pl.semaphore_signal(barrier, inc=1, device_id=partner, device_id_type=MESH)
    pl.semaphore_wait(barrier, len(partners))


def neighbours():
    y, core, z, x = place()
    up, down = (lambda v: lax.rem(v + 1, RING)), (lambda v: lax.rem(v + RING - 1, RING))
    return [
        device(y, core, z, 1 - x),
        device(y, 1 - core, z, x),
        device(up(y), core, z, x),
        device(down(y), core, z, x),
        device(y, core, up(z), x),
        device(y, core, down(z), x),
    ]


def other_tp():
    return {"tp": 1 - lax.axis_index("tp")}


def opposite():
    f = lax.axis_index("fsdp")
    return {"fsdp": f + 1 - 2 * (f % 2), "tp": 1 - lax.axis_index("tp")}


def native():
    return lax.axis_index("fsdp") % 2 == lax.axis_index("tp")


def swap_opposite(src, dst, send_sem, recv_sem):
    return pltpu.make_async_remote_copy(
        src_ref=src, dst_ref=dst, send_sem=send_sem, recv_sem=recv_sem, device_id=opposite(),
        device_id_type=MESH,
    )


def route(ids, gates, experts, size, select_ref, mix_ref):
    tokens, slots = ids.shape[0], mix_ref.shape[1]
    block, places = tokens // 2, size // 2
    chosen = jnp.zeros((tokens, experts.shape[1]), F32)
    weight = jnp.zeros((tokens, experts.shape[1]), F32)
    for k in range(ids.shape[1]):
        same = ids[:, k : k + 1] == experts
        chosen = chosen + jnp.where(same, 1.0, 0.0)
        weight = weight + jnp.where(same, gates[:, k : k + 1], 0.0)
    t = lax.broadcasted_iota(jnp.int32, (tokens, tokens), 0)
    u = lax.broadcasted_iota(jnp.int32, (tokens, tokens), 1)
    earlier = jnp.logical_and(u < t, (u >= block) == (t >= block))
    rank = dot(jnp.where(earlier, 1.0, 0.0).astype(BF16), chosen.astype(BF16), ((1,), (0,)))
    rank = jnp.where(chosen > 0.0, rank, -1.0).astype(BF16)
    e = lax.broadcasted_iota(jnp.int32, (experts.shape[1], slots), 0)
    j = lax.broadcasted_iota(jnp.int32, (experts.shape[1], slots), 1)
    spread = jnp.where(jnp.logical_and(j >= e * size, j < (e + 1) * size), 1.0, 0.0).astype(BF16)
    j = lax.broadcasted_iota(jnp.int32, (tokens, slots), 1)
    later = lax.broadcasted_iota(jnp.int32, (tokens, slots), 0) >= block
    place = (j & (places - 1)).astype(F32)
    mine = ((j & places) != 0) == later
    there = jnp.logical_and(dot(rank, spread, ((1,), (0,))) == place, mine)
    if select_ref is not None:
        select_ref[...] = jnp.where(there, 1.0, 0.0).astype(BF16)
    high = weight.astype(BF16)
    low = (weight - high.astype(F32)).astype(BF16)
    mix_ref[0:tokens, :] = jnp.where(there, dot(high, spread, ((1,), (0,))), 0.0).astype(BF16)
    mix_ref[tokens:, :] = jnp.where(there, dot(low, spread, ((1,), (0,))), 0.0).astype(BF16)


def gather_kernel(
    query_ref, key_ref, value_ref, out_ref, extra_ref, ids_ref, gates_ref, experts_ref, cot_ref,
    gate_ref, up_ref, down_ref,
    a_all, b_all, gate_all, up_all, down_all, near_ref, mix_ref, rows_ref,
    a_own, b_own, mix, rows, rows_sem, local_sem, send_sem, recv_sem, away_sem, home_sem, give_sem, take_sem,
):
    y, core, z, x = place()
    for own, refs in ((a_own, (query_ref, key_ref, value_ref)), (b_own, (out_ref, extra_ref))):
        at = 0
        for ref in refs:
            own[:, at : at + ref.shape[1]] = ref[...]
            at += ref.shape[1]
    greet(neighbours() + [opposite()])
    shards = ((gate_ref, gate_all), (up_ref, up_all), (down_ref, down_all))
    moved = [
        swap_opposite(p, q, give_sem.at[n], take_sem.at[n]) for n, (p, q) in enumerate(shards)
    ]
    refs, own = (a_all, b_all), (a_own, b_own)
    started = []
    count = [0, 0]

    def chunk(n, i, j):
        return refs[n].at[j, core, i] if n == 0 else refs[n].at[i, core, j]

    def to(n, first, second):
        return device(second, core, first, x) if n == 0 else device(first, core, second, x)

    def send(n, ref, where, slot):
        copy = pltpu.make_async_remote_copy(
            src_ref=ref, dst_ref=ref, send_sem=send_sem.at[n, slot], recv_sem=recv_sem.at[n, slot],
            device_id=where, device_id_type=MESH,
        )
        copy.start()
        started.append(copy)

    def arrived(n, ref, slot):
        pltpu.make_async_remote_copy(
            src_ref=ref, dst_ref=ref, send_sem=send_sem.at[n, slot], recv_sem=recv_sem.at[n, slot],
            device_id=device(y, core, z, x), device_id_type=MESH,
        ).wait_recv()

    homes = []

    def across(n, i, j):
        slot = count[n]
        count[n] += 1
        ref = chunk(n, i, j)
        copy = pltpu.make_async_remote_copy(
            src_ref=ref, dst_ref=ref, send_sem=away_sem.at[n, slot], recv_sem=home_sem.at[n, slot],
            device_id=device(y, 1 - core, z, x), device_id_type=MESH,
        )
        copy.start()
        homes.append(copy)

    def second(n, i, j, k):
        base = 5 + 4 * k
        send(n, chunk(n, i, j), to(n, me[n][0], up(j)), base)
        send(n, chunk(n, i, j), to(n, me[n][0], down(j)), base + 1)
        across(n, i, j)

    up, down = (lambda v: lax.rem(v + 1, RING)), (lambda v: lax.rem(v + RING - 1, RING))
    me = ((z, y), (y, z))
    locals_ = []
    for n in (0, 1):
        i, j = me[n]
        keep = pltpu.make_async_copy(own[n], chunk(n, i, j).at[x], local_sem.at[n])
        keep.start()
        locals_.append(keep)
        copy = pltpu.make_async_remote_copy(
            src_ref=own[n], dst_ref=chunk(n, i, j).at[x], send_sem=send_sem.at[n, 0],
            recv_sem=recv_sem.at[n, 0], device_id=device(y, core, z, 1 - x), device_id_type=MESH,
        )
        copy.start()
        started.append(copy)
    size = rows.shape[0] // (RING * RING * RING)
    ids, gates = ids_ref[...], gates_ref[...]
    route(ids, gates, experts_ref[0:1, :], size, None, mix)
    route(ids, gates, experts_ref[1:2, :], size, near_ref, mix_ref)
    for n in (0, 1):
        i, j = me[n]
        locals_[n].wait()
        arrived(n, chunk(n, i, j).at[1 - x], 0)
        send(n, chunk(n, i, j), to(n, up(i), j), 1)
        send(n, chunk(n, i, j), to(n, down(i), j), 2)
    for n in (0, 1):
        i, j = me[n]
        second(n, i, j, 0)

    @pl.when(jnp.logical_not(native()))
    def _():
        for copy in moved:
            copy.start()

    part, tokens = 256, cot_ref.shape[0]
    for at in range(0, rows.shape[0], part):
        lanes = slice(at, at + part)
        total = dot(mix[0:tokens, lanes], cot_ref[...], ((0,), (0,)))
        total = total + dot(mix[tokens:, lanes], cot_ref[...], ((0,), (0,)))
        rows[lanes, :] = total.astype(BF16)
    keep_rows = pltpu.make_async_copy(rows, rows_ref, rows_sem)
    keep_rows.start()
    for n in (0, 1):
        i, j = me[n]
        arrived(n, chunk(n, down(i), j), 1)
        send(n, chunk(n, down(i), j).at[0], to(n, up(i), j), 3)
        second(n, down(i), j, 1)
    for n in (0, 1):
        i, j = me[n]
        arrived(n, chunk(n, up(i), j), 2)
        send(n, chunk(n, up(i), j).at[1], to(n, down(i), j), 4)
        second(n, up(i), j, 2)
    for n in (0, 1):
        i, j = me[n]
        far = lax.rem(i + 2, RING)
        arrived(n, chunk(n, far, j).at[0], 3)
        arrived(n, chunk(n, far, j).at[1], 4)
        second(n, far, j, 3)
    for k in range(4):
        for n in (0, 1):
            i, j = me[n]
            it = (i, down(i), up(i), lax.rem(i + 2, RING))[k]
            base = 5 + 4 * k
            arrived(n, chunk(n, it, down(j)), base)
            send(n, chunk(n, it, down(j)).at[0], to(n, i, up(j)), base + 2)
            across(n, it, down(j))
            arrived(n, chunk(n, it, up(j)), base + 1)
            send(n, chunk(n, it, up(j)).at[1], to(n, i, down(j)), base + 3)
            across(n, it, up(j))
    for k in range(4):
        for n in (0, 1):
            i, j = me[n]
            it = (i, down(i), up(i), lax.rem(i + 2, RING))[k]
            base = 5 + 4 * k
            far = lax.rem(j + 2, RING)
            arrived(n, chunk(n, it, far).at[0], base + 2)
            arrived(n, chunk(n, it, far).at[1], base + 3)
            across(n, it, far)
    keep_rows.wait()
    for copy in homes:
        copy.wait()
    for copy in started:
        copy.wait_send()

    @pl.when(jnp.logical_not(native()))
    def _():
        for copy in moved:
            copy.wait()


def gather_weights(query, key, value, out, extra, ids, gates, experts, cot, slots, gate, up, down):
    rows = query.shape[0]
    cols = (query.shape[1] + key.shape[1] + value.shape[1], out.shape[1] + extra.shape[1])
    shape = (RING, 2, RING, 2, rows)
    vmem, any_space = (pl.BlockSpec(memory_space=space) for space in (pltpu.VMEM, pl.ANY))
    tokens, width = cot.shape
    routing = [jax.ShapeDtypeStruct((n * tokens, slots), BF16) for n in (1, 2)]
    a_all, b_all, *rest = pl.pallas_call(
        gather_kernel,
        in_specs=[vmem] * 9 + [any_space] * 3,
        out_specs=[any_space] * 5 + [vmem] * 2 + [any_space],
        out_shape=[jax.ShapeDtypeStruct(shape + (c,), query.dtype) for c in cols]
        + [jax.ShapeDtypeStruct(v.shape, v.dtype) for v in (gate, up, down)]
        + routing + [jax.ShapeDtypeStruct((slots, width), BF16)],
        scratch_shapes=[pltpu.VMEM((rows, c), query.dtype) for c in cols] + [
            pltpu.VMEM((2 * tokens, slots), BF16),
            pltpu.VMEM((slots, width), BF16),
            pltpu.SemaphoreType.DMA,
            pltpu.SemaphoreType.DMA((2,)),
            pltpu.SemaphoreType.DMA((2, 21)),
            pltpu.SemaphoreType.DMA((2, 21)),
            pltpu.SemaphoreType.DMA((2, 16)),
            pltpu.SemaphoreType.DMA((2, 16)),
            pltpu.SemaphoreType.DMA((3,)),
            pltpu.SemaphoreType.DMA((3,)),
        ],
        compiler_params=pltpu.CompilerParams(
            collective_id=0, has_side_effects=True, vmem_limit_bytes=VMEM_LIMIT
        ),
        cost_estimate=pl.CostEstimate(flops=0, bytes_accessed=250_000_000, transcendentals=0),
        name="gather_weights",
    )(query, key, value, out, extra, ids, gates, experts, cot, gate, up, down)
    return a_all.reshape(-1, cols[0]), b_all.reshape(-1, cols[1]), rest[:3], rest[3:]


ORDER = (2, 1, 3, 0)
SLICE = 16


def up(v):
    return lax.rem(v + 1, RING)


def down(v):
    return lax.rem(v + RING - 1, RING)


def add_into(target, *terms):
    flat = [target.shape[0]] if len(target.shape) == 3 else []
    for lead in range(flat[0]) if flat else (None,):
        for start in range(0, target.shape[-2], SLICE):
            at = (pl.ds(start, SLICE), slice(None))
            at = at if lead is None else (lead,) + at
            total = terms[0][at].astype(F32)
            for term in terms[1:]:
                total = total + term[at].astype(F32)
            target[at] = total.astype(target.dtype)


def scatter_kernel(
    a_ref, b_ref, extra_ref, wide_ref, tall_ref, y_ref, x_ref,
    a_out, b_out, wide_out, tall_out, y_out, x_out, a_mine, b_mine, a_theirs, b_theirs, a_one, b_one, a_two, b_two,
    a_first, b_first, a_last, b_last, a_x, b_x, load_sem, send_sem, recv_sem,
    gains_here, gains_there,
    extra_load_sem, extra_send_sem, extra_recv_sem, give_sem, take_sem, gains_sem, token_sem,
):
    y, core, z, x = place()
    greet(neighbours() + [other_tp(), opposite()])
    moved = [
        swap_opposite(wide_ref, wide_out, give_sem.at[0], take_sem.at[0]),
        swap_opposite(tall_ref, tall_out, give_sem.at[1], take_sem.at[1]),
    ]

    tokens = [
        pltpu.make_async_remote_copy(
            src_ref=src, dst_ref=dst, send_sem=token_sem.at[n, 0], recv_sem=token_sem.at[n, 1],
            device_id=other_tp(), device_id_type=MESH,
        )
        for n, (src, dst) in enumerate(((y_ref, y_out), (x_ref, x_out)))
    ]
    for copy in tokens:
        copy.start()

    @pl.when(jnp.logical_not(native()))
    def _():
        for copy in moved:
            copy.start()

    grads, outs = (a_ref, b_ref), (a_out, b_out)
    mine, theirs = (a_mine, b_mine), (a_theirs, b_theirs)
    one, two = (a_one, b_one), (a_two, b_two)
    first, last, side = (a_first, b_first), (a_last, b_last), (a_x, b_x)
    me = ((z, y), (y, z))
    sent = []

    def chunk(n, i, j, c):
        return grads[n].at[j, c, i] if n == 0 else grads[n].at[i, c, j]

    def to(n, i, j):
        return device(j, core, i, x) if n == 0 else device(i, core, j, x)

    def copy_of(n, src, dst, slot, where):
        return pltpu.make_async_remote_copy(
            src_ref=src, dst_ref=dst, send_sem=send_sem.at[n, slot], recv_sem=recv_sem.at[n, slot],
            device_id=where, device_id_type=MESH,
        )

    def send(n, src, dst, slot, where):
        copy = copy_of(n, src, dst, slot, where)
        copy.start()
        sent.append(copy)

    def arrived(n, dst, slot):
        copy_of(n, dst, dst, slot, device(y, core, z, x)).wait_recv()

    cols = b_ref.shape[-1]

    def columns(ref, start, count):
        return ref.at[:, :, pl.ds(start, count)]

    def extra_copy(slot):
        ref = columns(theirs[1].at[slot], cols, extra_ref.shape[-1])
        far = extra_ref.at[lax.rem(y + slot // RING, RING), 1 - core, lax.rem(z + slot % RING, RING)]
        return pltpu.make_async_remote_copy(
            src_ref=far, dst_ref=ref, send_sem=extra_send_sem.at[slot],
            recv_sem=extra_recv_sem.at[slot], device_id=device(y, 1 - core, z, x),
            device_id_type=MESH,
        )

    def extra_load(slot):
        near = extra_ref.at[lax.rem(y + slot // RING, RING), core, lax.rem(z + slot % RING, RING)]
        return pltpu.make_async_copy(
            near, columns(mine[1].at[slot], cols, extra_ref.shape[-1]), extra_load_sem.at[slot]
        )

    def load(n, di, dj):
        i, j = me[n]
        slot = di * RING + dj
        target = mine[n].at[slot] if n == 0 else columns(mine[n].at[slot], 0, cols)
        return pltpu.make_async_copy(
            chunk(n, lax.rem(i + di, RING), lax.rem(j + dj, RING), core), target,
            load_sem.at[n, slot],
        )

    for dj in ORDER:
        for di in ORDER:
            for n in (0, 1):
                i, j = me[n]
                slot = di * RING + dj
                there = chunk(n, lax.rem(i + di, RING), lax.rem(j + dj, RING), 1 - core)
                target = theirs[n].at[slot] if n == 0 else columns(theirs[n].at[slot], 0, cols)
                send(n, there, target, slot, device(y, 1 - core, z, x))
                load(n, di, dj).start()
                if n == 1:
                    extra_copy(slot).start()
                    extra_load(slot).start()

    def ready(n, di, dj):
        slot = di * RING + dj
        load(n, di, dj).wait()
        if n == 0:
            arrived(n, theirs[n].at[slot], slot)
        else:
            arrived(n, columns(theirs[n].at[slot], 0, cols), slot)
            extra_load(slot).wait()
            extra_copy(slot).wait_recv()
        return slot

    for di in ORDER:
        for n in (0, 1):
            i, j = me[n]
            slot = ready(n, di, 2)
            add_into(mine[n].at[slot], mine[n].at[slot], theirs[n].at[slot])
            for half in (0, 1):
                send(
                    n, mine[n].at[slot, half], one[n].at[di, half], 16 + di * 2 + half,
                    to(n, i, up(j) if half == 0 else down(j)),
                )
    for di in ORDER:
        for n in (0, 1):
            i, j = me[n]
            for half, dj in ((0, 1), (1, 3)):
                slot = ready(n, di, dj)
                arrived(n, one[n].at[di, half], 16 + di * 2 + half)
                add_into(
                    mine[n].at[slot, half], mine[n].at[slot, half], theirs[n].at[slot, half],
                    one[n].at[di, half],
                )
                add_into(
                    mine[n].at[slot, 1 - half], mine[n].at[slot, 1 - half],
                    theirs[n].at[slot, 1 - half],
                )
                send(
                    n, mine[n].at[slot], two[n].at[di, half], 24 + di * 2 + half,
                    to(n, i, up(j) if half == 0 else down(j)),
                )
    for di in ORDER:
        for n in (0, 1):
            i, j = me[n]
            slot = ready(n, di, 0)
            for half in (0, 1):
                arrived(n, two[n].at[di, half], 24 + di * 2 + half)
            add_into(
                mine[n].at[slot], mine[n].at[slot], theirs[n].at[slot], two[n].at[di, 0],
                two[n].at[di, 1],
            )
            if di == 2:
                for half in (0, 1):
                    send(
                        n, mine[n].at[slot, half], first[n].at[half], 32 + half,
                        to(n, up(i) if half == 0 else down(i), j),
                    )
            elif di != 0:
                half = 0 if di == 1 else 1
                arrived(n, first[n].at[half], 32 + half)
                add_into(mine[n].at[slot, half], mine[n].at[slot, half], first[n].at[half])
                send(
                    n, mine[n].at[slot], last[n].at[half], 34 + half,
                    to(n, up(i) if half == 0 else down(i), j),
                )
    for n in (0, 1):
        for half in (0, 1):
            arrived(n, last[n].at[half], 34 + half)
        add_into(mine[n].at[0], mine[n].at[0], last[n].at[0], last[n].at[1])
        send(n, mine[n].at[0, 1 - x], side[n], 36, device(y, core, z, 1 - x))
    for n in (0, 1):
        arrived(n, side[n], 36)
        add_into(outs[n], mine[n].at[0, x], side[n])
    gains_here[...] = b_out[:, cols:]
    gains = pltpu.make_async_remote_copy(
        src_ref=gains_here, dst_ref=gains_there, send_sem=gains_sem.at[0],
        recv_sem=gains_sem.at[1], device_id=other_tp(), device_id_type=MESH,
    )
    gains.start()
    for copy in sent:
        copy.wait_send()
    for slot in range(RING * RING):
        extra_copy(slot).wait_send()
    gains.wait()
    for copy in tokens:
        copy.wait()
    b_out[:, cols:] = gains_here[...] + gains_there[...]

    @pl.when(jnp.logical_not(native()))
    def _():
        for copy in moved:
            copy.wait()


def scatter_grads(a, b, extra, wide, tall, y, x):
    peers = RING * RING * 4
    rows = a.shape[0] // peers
    shape = (RING, 2, RING, 2, rows)
    cols = (a.shape[1], b.shape[1] + extra.shape[1])
    buffers = []
    for lead in ((16, 2), (16, 2), (4, 2), (4, 2, 2), (2,), (2, 2), ()):
        buffers += [pltpu.VMEM(lead + (rows, c), a.dtype) for c in cols]
    any_space = pl.BlockSpec(memory_space=pl.ANY)
    return pl.pallas_call(
        scatter_kernel,
        in_specs=[any_space] * 7,
        out_specs=[pl.BlockSpec(memory_space=pltpu.VMEM)] * 2 + [any_space] * 4,
        out_shape=[jax.ShapeDtypeStruct((rows, c), F32) for c in cols]
        + [jax.ShapeDtypeStruct(v.shape, v.dtype) for v in (wide, tall, y, x)],
        scratch_shapes=buffers + [
            pltpu.SemaphoreType.DMA((2, 16)),
            pltpu.SemaphoreType.DMA((2, 37)),
            pltpu.SemaphoreType.DMA((2, 37)),
            pltpu.VMEM((rows, extra.shape[1]), F32),
            pltpu.VMEM((rows, extra.shape[1]), F32),
            pltpu.SemaphoreType.DMA((16,)),
            pltpu.SemaphoreType.DMA((16,)),
            pltpu.SemaphoreType.DMA((16,)),
            pltpu.SemaphoreType.DMA((2,)),
            pltpu.SemaphoreType.DMA((2,)),
            pltpu.SemaphoreType.DMA((2,)),
            pltpu.SemaphoreType.DMA((2, 2)),
        ],
        compiler_params=pltpu.CompilerParams(
            collective_id=1, has_side_effects=True, vmem_limit_bytes=44 * 1024 * 1024
        ),
        cost_estimate=pl.CostEstimate(flops=0, bytes_accessed=250_000_000, transcendentals=0),
        name="scatter_grads",
    )(*(v.reshape(shape + (v.shape[1],)) for v in (a, b, extra)), wide, tall, y, x)


CHIPS = RING * RING * RING
GROUP = 16
MIX = 11
AHEAD = 2
TILE = 256


def chip_at(slot, sign):
    f, c, t = lax.axis_index("fsdp"), lax.axis_index("ctx"), lax.axis_index("tp")
    k = lax.rem(slot * MIX, CHIPS) * sign
    turn = 0 if sign > 0 else RING
    far = [lax.div(k, RING * RING), lax.rem(lax.div(k, RING), RING), lax.rem(k, RING)]
    own = [lax.div(f, 2), lax.div(c, 2), t * 2 + lax.rem(c, 2)]
    return [lax.rem(o + d + turn, RING) for o, d in zip(own, far)]


def device_at(slot, sign):
    y, z, x = chip_at(slot, sign)
    core = lax.rem(lax.axis_index("fsdp"), 2)
    return {"fsdp": y * 2 + core, "ctx": z * 2 + lax.rem(x, 2), "tp": lax.div(x, 2)}


def chip_number(slot, sign):
    y, z, x = chip_at(slot, sign)
    return (y * 2 * RING + z * 2 + lax.rem(x, 2)) * 2 + lax.div(x, 2)


def other_core():
    f = lax.axis_index("fsdp")
    return {"fsdp": f + 1 - 2 * (f % 2)}


def moe_kernel(
    send_ref, deo_ref, gate_ref, up_ref, down_ref, gate_far, up_far, down_far,
    back_ref, eo_ref, wide_ref, tall_ref,
    rows, deos, gu, down, z, dgu, wide, tall, give, take,
    go_sem, come_sem, load_sem, weight_sem, share_send, share_recv, part_send, part_recv,
    back_send, back_recv, eo_sem,
):
    size, hidden = send_ref.shape[1], down_ref.shape[0]
    count = GROUP * size
    groups = CHIPS // GROUP
    width = down_ref.shape[1]

    def each(body, low, high):
        def step(i, carry):
            body(i)
            return carry

        lax.fori_loop(low, high, step, 0)

    barrier = pltpu.get_barrier_semaphore()
    each(
        lambda s: pl.semaphore_signal(
            barrier, inc=1, device_id=device_at(s, 1), device_id_type=MESH
        ),
        1, CHIPS,
    )
    pl.semaphore_signal(barrier, inc=1, device_id=other_core(), device_id_type=MESH)
    pl.semaphore_wait(barrier, CHIPS)

    def slot_rows(s):
        return pl.ds(pl.multiple_of(s * size, size), size)

    def group_rows(g):
        return pl.ds(pl.multiple_of(g * count, count), count)

    def go(s):
        return remote(
            send_ref.at[s], rows.at[0, slot_rows(s)], go_sem.at[s], come_sem.at[s], device_at(s, 1)
        )

    def stay(s):
        return pltpu.make_async_copy(send_ref.at[s], rows.at[0, slot_rows(s)], come_sem.at[s])

    def load(s):
        return pltpu.make_async_copy(
            deo_ref.at[chip_number(s, -1)], deos.at[0, slot_rows(s)], load_sem.at[s]
        )

    def sent_rows(n, s):
        slot = lax.rem(lax.div(s, GROUP), 2)
        return give.at[n, slot, slot_rows(lax.rem(s, GROUP))]

    def back(s):
        return remote(
            sent_rows(0, s), back_ref.at[s], back_send.at[s], back_recv.at[s], device_at(s, -1)
        )

    def back_stay():
        return pltpu.make_async_copy(
            give.at[0, 0, pl.ds(0, size)], back_ref.at[0], back_recv.at[0]
        )

    def out(s):
        return pltpu.make_async_copy(
            sent_rows(1, s), eo_ref.at[s], eo_sem.at[s]
        )

    def share(n, g):
        ref = (rows, deos)[n]
        return remote(
            ref.at[0, group_rows(g)], ref.at[1, group_rows(g)], share_send.at[n, g],
            share_recv.at[n, g], other_core(),
        )

    def part(n, g):
        slot = lax.rem(g, 2)
        return remote(
            give.at[n, slot], take.at[n, slot], part_send.at[n, g], part_recv.at[n, g],
            other_core(),
        )

    places = (gu.at[:, pl.ds(0, hidden)], gu.at[:, pl.ds(hidden, hidden)], down)
    weights = [
        [pltpu.make_async_copy(src, dst, weight_sem.at[n]) for n, (src, dst) in enumerate(pairs)]
        for pairs in (
            zip((gate_ref, up_ref, down_ref), places), zip((gate_far, up_far, down_far), places)
        )
    ]

    def on_weights(act):
        for condition, copies in zip((native(), jnp.logical_not(native())), weights):

            @pl.when(condition)
            def _(copies=copies):
                for copy in copies:
                    act(copy)

    stay(0).start()
    each(lambda s: go(s).start(), 1, AHEAD * GROUP)
    each(lambda s: load(s).start(), 0, CHIPS)
    on_weights(lambda copy: copy.start())

    def tiles(body):
        each(lambda i: body(pl.ds(pl.multiple_of(i * TILE, TILE), TILE)), 0, width // TILE)

    def clear(at):
        wide[at, :] = jnp.zeros((TILE, 2 * hidden), F32)
        tall[:, at] = jnp.zeros((hidden, TILE), F32)

    tiles(clear)

    def through(side, g):
        at = group_rows(g)
        pre = dot(rows[side, at, :], gu[...], ((1,), (0,)))
        dz = dot(deos[side, at, :], down[...], ((1,), (1,)))
        gate, u = pre[:, :hidden], pre[:, hidden:]
        sig = 1.0 / (1.0 + jnp.exp(-gate))
        act = gate * sig
        z[side] = (act * u).astype(BF16)
        dgu[side, :, :hidden] = (dz * u * sig * (1.0 + gate * (1.0 - sig))).astype(BF16)
        dgu[side, :, hidden:] = (dz * act).astype(BF16)

    def to_rows(side):
        return dot(dgu[side], gu[...], ((1,), (1,)))

    def to_outputs(side):
        return dot(z[side], down[...], ((1,), (0,)))

    on_weights(lambda copy: copy.wait())

    def group(g):
        first, last, slot = g * GROUP, (g + 1) * GROUP, lax.rem(g, 2)

        @pl.when(g == 0)
        def _():
            stay(0).wait()

        each(lambda s: go(s).wait_recv(), lax.max(first, 1), last)
        each(lambda s: load(s).wait(), first, last)
        each(
            lambda s: go(s).start(), lax.min(first + AHEAD * GROUP, CHIPS),
            lax.min(last + AHEAD * GROUP, CHIPS),
        )
        for n in (0, 1):
            share(n, g).start()
        through(0, g)
        for n in (0, 1):
            share(n, g).wait_recv()
        through(1, g)

        @pl.when(g >= 2)
        def _():
            @pl.when(g == 2)
            def _():
                back_stay().wait()

            each(lambda s: back(s).wait_send(), lax.max(first - 2 * GROUP, 1), last - 2 * GROUP)
            each(lambda s: out(s).wait(), first - 2 * GROUP, last - 2 * GROUP)

        give[0, slot] = to_rows(1).astype(BF16)
        part(0, g).start()
        give[1, slot] = to_outputs(1).astype(BF16)
        part(1, g).start()
        own = to_rows(0)
        part(0, g).wait()
        give[0, slot] = (own + take[0, slot].astype(F32)).astype(BF16)

        @pl.when(g == 0)
        def _():
            back_stay().start()

        each(lambda s: back(s).start(), lax.max(first, 1), last)
        own = to_outputs(0)
        part(1, g).wait()
        give[1, slot] = (own + take[1, slot].astype(F32)).astype(BF16)
        each(lambda s: out(s).start(), first, last)
        at = group_rows(g)

        def weight_grads(cols):
            wide[cols, :] += dot(rows[0, at, cols], dgu[0], ((0,), (0,))) + dot(
                rows[1, at, cols], dgu[1], ((0,), (0,))
            )
            tall[:, cols] += dot(z[0], deos[0, at, cols], ((0,), (0,))) + dot(
                z[1], deos[1, at, cols], ((0,), (0,))
            )

        tiles(weight_grads)

    each(group, 0, groups)

    def store(at):
        wide_ref[at, :] = wide[at, :].astype(BF16)
        tall_ref[:, at] = tall[:, at].astype(BF16)

    tiles(store)
    for g in range(groups):
        for n in (0, 1):
            share(n, g).wait_send()
    each(lambda s: out(s).wait(), (groups - 2) * GROUP, CHIPS)
    each(lambda s: back(s).wait_send(), (groups - 2) * GROUP, CHIPS)
    each(lambda s: go(s).wait_send(), 1, CHIPS)
    each(lambda s: back(s).wait_recv(), 1, CHIPS)


def moe(send, d_eo, own, far):
    chips, size, width = send.shape
    hidden = own[2].shape[0]
    total, groups = chips * size, chips // GROUP
    count = GROUP * size
    vmem, any_space = (pl.BlockSpec(memory_space=space) for space in (pltpu.VMEM, pl.ANY))
    shapes = [send.shape, send.shape, (width, 2 * hidden), (hidden, width)]
    dma = pltpu.SemaphoreType.DMA
    return pl.pallas_call(
        moe_kernel,
        in_specs=[any_space] * 8,
        out_specs=[any_space] * 2 + [vmem] * 2,
        out_shape=[jax.ShapeDtypeStruct(shape, BF16) for shape in shapes],
        scratch_shapes=[
            pltpu.VMEM((2, total, width), BF16),
            pltpu.VMEM((2, total, width), BF16),
            pltpu.VMEM((width, 2 * hidden), BF16),
            pltpu.VMEM((hidden, width), BF16),
            pltpu.VMEM((2, count, hidden), BF16),
            pltpu.VMEM((2, count, 2 * hidden), BF16),
            pltpu.VMEM((width, 2 * hidden), F32),
            pltpu.VMEM((hidden, width), F32),
            pltpu.VMEM((2, 2, count, width), BF16),
            pltpu.VMEM((2, 2, count, width), BF16),
            dma((chips,)), dma((chips,)), dma((chips,)), dma((3,)),
            dma((2, groups)), dma((2, groups)), dma((2, groups)), dma((2, groups)),
            dma((chips,)), dma((chips,)), dma((chips,)),
        ],
        compiler_params=pltpu.CompilerParams(
            collective_id=4, has_side_effects=True, vmem_limit_bytes=56 * 1024 * 1024
        ),
        cost_estimate=pl.CostEstimate(flops=0, bytes_accessed=400_000_000, transcendentals=0),
        name="experts",
    )(send, d_eo, *own, *far)


BLOCK = 64
CTX = 8
WIDE = 256


def rotated(u, gain, cosine, sine):
    scaling = lax.rsqrt(jnp.mean(u * u, axis=-1, keepdims=True) + EPS)
    normed = u * scaling
    n = normed * gain
    rot = n * cosine + pltpu.roll(n, HEAD_SIZE // 2, 1) * sine
    return rot.astype(BF16), normed, scaling


def rotated_back(e, normed, scaling, gain, cosine, sine):
    back = e * cosine + pltpu.roll(e * sine, HEAD_SIZE // 2, 1)
    scaled = back * gain
    inner = jnp.mean(scaled * normed, axis=-1, keepdims=True)
    return scaling * (scaled - normed * inner), jnp.sum(back * normed, axis=0, keepdims=True)


def ctx_peer(step):
    return {"ctx": lax.rem(lax.axis_index("ctx") + step, CTX)}


def beside():
    c = lax.axis_index("ctx")
    return {"ctx": c + 1 - 2 * lax.rem(c, 2)}


def softmax_parts(q_low, k, bias):
    s = dot(q_low, k, ((1,), (1,))) * (HEAD_SIZE ** -0.5) + bias
    e = jnp.exp(s - jnp.max(s, axis=-1, keepdims=True))
    return e / jnp.sum(e, axis=-1, keepdims=True)


def share_kernel(kv, rows_ref, cos_ref, sin_ref, gk_ref, kv_ref, held, send_sem, recv_sem):
    c = lax.axis_index("ctx")
    greet([ctx_peer(step) for step in range(1, CTX)])
    micro, rows = held.shape[0], 2 * BLOCK
    cosine, sine, gk = cos_ref[...], sin_ref[...], gk_ref[...]
    mine = pl.ds(pl.multiple_of(c * BLOCK, BLOCK), BLOCK)
    earlier, own = pl.ds(CTX * BLOCK, BLOCK), pl.ds((CTX + 1) * BLOCK, BLOCK)
    copies = []
    for m in range(micro):
        span = slice(m * rows, (m + 1) * rows)
        for h in range(2 * kv):
            cols = slice(h * HEAD_SIZE, (h + 1) * HEAD_SIZE)
            u = rows_ref[span, cols]
            low = rotated(u, gk, cosine, sine)[0] if h < kv else u.astype(BF16)
            held[m, mine, cols] = low[:BLOCK]
            held[m, own, cols] = low[BLOCK:]
        for step in range(1, CTX):
            part = held.at[m, mine]
            copies.append(
                remote(part, part, send_sem.at[step, m], recv_sem.at[step, m], ctx_peer(step))
            )
        copies.append(
            remote(
                held.at[m, own], held.at[m, earlier], send_sem.at[0, m], recv_sem.at[0, m], beside()
            )
        )
        for copy in copies[-CTX:]:
            copy.start()
    for m in range(micro):
        for step in range(1, CTX):
            source = lax.rem(c + CTX - step, CTX)
            part = held.at[m, pl.ds(pl.multiple_of(source * BLOCK, BLOCK), BLOCK)]
            remote(
                part, part, send_sem.at[step, m], recv_sem.at[step, m], ctx_peer(step)
            ).wait_recv()
        copies[(m + 1) * CTX - 1].wait_recv()
        kv_ref[m] = held[m]
    for copy in copies:
        copy.wait_send()


def attention_kernel(heads, q_ref, cos_ref, sin_ref, gq_ref, bias_ref, k_ref, v_ref, o_ref):
    cosine, sine, gq = cos_ref[...], sin_ref[...], gq_ref[...]
    for e in range(heads):
        cols = slice(e * HEAD_SIZE, (e + 1) * HEAD_SIZE)
        q_low = rotated(q_ref[:, cols], gq, cosine, sine)[0]
        p = softmax_parts(q_low, k_ref[...], bias_ref[...]).astype(BF16)
        o_ref[:, cols] = dot(p, v_ref[...], ((1,), (0,))).astype(BF16)


def backward_kernel(
    kv, heads, qkv_ref, cos_ref, sin_ref, gq_ref, gk_ref, bias_ref, kv_ref, dattn_ref, o_ref, a_ref,
    w_out_ref, w_qkv_ref, eo_ref,
    given_grad_ref, gains_ref, grad_qkv_ref, grad_out_ref, eo_back_ref,
    w_out, w_qkv, do_ref, dqkv_ref, part_sum, wide_tile, tall_tile, grads, given, given_side,
    p_all, ds_all, q_all, do_all, swap_give, swap_take,
    send_sem, recv_sem, load_sem, tile_sem, swap_sem, eo_send, eo_recv,
):
    c, tp = lax.axis_index("ctx"), lax.axis_index("tp")
    width = w_out.shape[0]

    def each(body, low, high):
        def step(i, carry):
            body(i)
            return carry

        lax.fori_loop(low, high, step, 0)

    barrier = pltpu.get_barrier_semaphore()
    each(
        lambda s: pl.semaphore_signal(
            barrier, inc=1, device_id=device_at(s, 1), device_id_type=MESH
        ),
        1, CHIPS,
    )
    loads = [
        pltpu.make_async_copy(w_out_ref.at[:, pl.ds(0, w_out.shape[1])], w_out, load_sem.at[0]),
        pltpu.make_async_copy(w_qkv_ref, w_qkv, load_sem.at[1]),
    ]
    for copy in loads:
        copy.start()
    pl.semaphore_wait(barrier, CHIPS - 1)

    def output(s):
        return remote(
            eo_ref.at[s], eo_back_ref.at[s], eo_send.at[s], eo_recv.at[s], device_at(s, -1)
        )

    def outputs(quarter):
        each(lambda s: output(s).start(), max(quarter * GROUP, 1), (quarter + 1) * GROUP)

    stay = pltpu.make_async_copy(eo_ref.at[0], eo_back_ref.at[0], eo_recv.at[0])
    stay.start()
    outputs(0)
    micro, rows = grads.shape[0], 2 * BLOCK
    q_cols = kv * heads * HEAD_SIZE
    scale = HEAD_SIZE ** -0.5
    cosine, sine, gq, gk = cos_ref[...], sin_ref[...], gq_ref[...], gk_ref[...]
    mine = pl.ds(pl.multiple_of(c * BLOCK, BLOCK), BLOCK)
    earlier, own = pl.ds(CTX * BLOCK, BLOCK), pl.ds((CTX + 1) * BLOCK, BLOCK)

    def tile(i):
        return pl.ds(pl.multiple_of(i * WIDE, WIDE), WIDE)

    loads[0].wait()

    def outputs_back(i):
        do_ref[:, tile(i)] = dot(dattn_ref[...], w_out[:, tile(i)], ((1,), (0,))).astype(BF16)

    each(outputs_back, 0, w_out.shape[1] // WIDE)

    def head_cols(h):
        return pl.ds(pl.multiple_of(h * HEAD_SIZE, HEAD_SIZE), HEAD_SIZE)

    def keys_back(m, h, carry):
        span = slice(m * rows, (m + 1) * rows)
        k, v = kv_ref[m, :, head_cols(h)], kv_ref[m, :, head_cols(kv + h)]
        for e in range(heads):
            cols = head_cols(h * heads + e)
            stack = slice(e * rows, (e + 1) * rows)
            q_low = rotated(qkv_ref[span, cols], gq, cosine, sine)[0]
            q_all[stack, :] = q_low
            p = softmax_parts(q_low, k, bias_ref[...])
            p_all[stack, :] = p.astype(BF16)
            do = do_ref[span, cols]
            do_all[stack, :] = do
            dp = dot(do, v, ((1,), (1,)))
            ds = (p * (dp - jnp.sum(dp * p, axis=-1, keepdims=True))).astype(BF16)
            ds_all[m * kv + h, stack, :] = ds
        grads[m, :, head_cols(kv + h)] = dot(p_all[...], do_all[...], ((0,), (0,))).astype(BF16)
        d_k = dot(ds_all[m * kv + h], q_all[...], ((0,), (0,))) * scale
        grads[m, :, head_cols(h)] = d_k.astype(BF16)
        return carry

    def queries_back(m, h, total):
        span = slice(m * rows, (m + 1) * rows)
        k = kv_ref[m, :, head_cols(h)]
        for e in range(heads):
            cols = head_cols(h * heads + e)
            ds = ds_all[m * kv + h, e * rows : (e + 1) * rows, :]
            dqr = (dot(ds, k, ((1,), (0,))) * scale).astype(BF16).astype(F32)
            u = qkv_ref[span, cols]
            scaling = lax.rsqrt(jnp.mean(u * u, axis=-1, keepdims=True) + EPS)
            dq, part = rotated_back(dqr, u * scaling, scaling, gq, cosine, sine)
            dqkv_ref[span, cols] = dq.astype(BF16)
            total = total + part
        return total

    copies = []
    for m in range(micro):
        lax.fori_loop(0, kv, functools.partial(keys_back, m), 0)
        for step in range(1, CTX):
            peer = lax.rem(c + step, CTX)
            part = grads.at[m, pl.ds(pl.multiple_of(peer * BLOCK, BLOCK), BLOCK)]
            copies.append(
                remote(
                    part, given.at[step - 1, m], send_sem.at[step, m], recv_sem.at[step, m],
                    ctx_peer(step),
                )
            )
        copies.append(
            remote(
                grads.at[m, earlier], given_side.at[m], send_sem.at[0, m], recv_sem.at[0, m],
                beside(),
            )
        )
        for copy in copies[-CTX:]:
            copy.start()
        outputs(1 + m)
    total = jnp.zeros((1, HEAD_SIZE), F32)
    for m in range(micro):
        total = lax.fori_loop(0, kv, functools.partial(queries_back, m), total)
    outputs(3)

    def tiles_out(buffer, left, right, out_ref, sems):
        def copy_out(i):
            slot = lax.rem(i, 2)
            return pltpu.make_async_copy(buffer.at[slot], out_ref.at[tile(i)], sems.at[i])

        def step(i):
            @pl.when(i >= 2)
            def _():
                copy_out(i - 2).wait()

            value = dot(left[:, tile(i)], right[...], ((0,), (0,)))
            buffer[lax.rem(i, 2)] = value.astype(BF16)
            copy_out(i).start()

        count = width // WIDE
        each(step, 0, count)
        return lambda: each(lambda i: copy_out(i).wait(), count - 2, count)

    end_out = tiles_out(tall_tile, dattn_ref, o_ref, grad_out_ref, tile_sem.at[0])
    loads[1].wait()

    def queries_in(i):
        part_sum[:, tile(i)] = dot(dqkv_ref[:, :q_cols], w_qkv[tile(i), :q_cols], ((1,), (1,)))

    each(queries_in, 0, width // WIDE)
    k_total = jnp.zeros((1, HEAD_SIZE), F32)
    for m in range(micro):
        for copy in copies[m * CTX : (m + 1) * CTX]:
            copy.wait_recv()
        for h in range(2 * kv):
            cols = slice(h * HEAD_SIZE, (h + 1) * HEAD_SIZE)
            at = slice(q_cols + h * HEAD_SIZE, q_cols + (h + 1) * HEAD_SIZE)
            prompt = grads[m, mine, cols].astype(F32)
            for step in range(CTX - 1):
                prompt = prompt + given[step, m, :, cols].astype(F32)
            cont = grads[m, own, cols].astype(F32) + given_side[m, :, cols].astype(F32)
            e = jnp.concatenate([prompt, cont], axis=0).astype(BF16)
            span = slice(m * rows, (m + 1) * rows)
            if h < kv:
                _, normed, scaling = rotated(qkv_ref[span, at], gk, cosine, sine)
                d, part = rotated_back(e.astype(F32), normed, scaling, gk, cosine, sine)
                k_total = k_total + part
                dqkv_ref[span, at] = d.astype(BF16)
            else:
                dqkv_ref[span, at] = e
    gains_ref[0:1, :] = total
    gains_ref[1:2, :] = k_total

    def keys_in(i):
        part_sum[:, tile(i)] += dot(dqkv_ref[:, q_cols:], w_qkv[tile(i), q_cols:], ((1,), (1,)))

    each(keys_in, 0, width // WIDE)
    for m in range(micro):
        away = pl.ds(pl.multiple_of(m * rows + tp * BLOCK, BLOCK), BLOCK)
        swap_give[m * BLOCK : (m + 1) * BLOCK, :] = part_sum[away, :].astype(BF16)
    swap = remote(swap_give, swap_take, swap_sem.at[0], swap_sem.at[1], {"tp": 1 - tp})
    swap.start()
    end_qkv = tiles_out(wide_tile, a_ref, dqkv_ref, grad_qkv_ref, tile_sem.at[1])
    swap.wait()
    for m in range(micro):
        kept = pl.ds(pl.multiple_of(m * rows + (1 - tp) * BLOCK, BLOCK), BLOCK)
        span = slice(m * BLOCK, (m + 1) * BLOCK)
        given_grad_ref[span, :] = part_sum[kept, :] + swap_take[span, :].astype(F32)
    for copy in copies:
        copy.wait_send()
    end_out()
    end_qkv()
    stay.wait()
    each(lambda s: output(s).wait(), 1, CHIPS)


def share_keys(qkv, cosine, sine, gain_key, kv, keys, micro):
    rows, cols = qkv.shape[0], 2 * kv * HEAD_SIZE
    last = qkv.shape[1] // cols - 1

    def whole(shape):
        return pl.BlockSpec(shape, lambda i: (0,) * len(shape))

    return pl.pallas_call(
        functools.partial(share_kernel, kv),
        grid=(1,),
        in_specs=[pl.BlockSpec((rows, cols), lambda i: (0, last)), whole(cosine.shape)]
        + [whole(sine.shape), whole(gain_key.shape)],
        out_specs=whole((micro, keys, cols)),
        out_shape=jax.ShapeDtypeStruct((micro, keys, cols), BF16),
        scratch_shapes=[
            pltpu.VMEM((micro, keys, cols), BF16),
            pltpu.SemaphoreType.DMA((CTX, micro)),
            pltpu.SemaphoreType.DMA((CTX, micro)),
        ],
        compiler_params=pltpu.CompilerParams(
            collective_id=2, has_side_effects=True, vmem_limit_bytes=VMEM_LIMIT
        ),
        cost_estimate=pl.CostEstimate(flops=0, bytes_accessed=50_000_000, transcendentals=0),
        name="share_keys",
    )(qkv, cosine, sine, gain_key)


def attention(qkv, cosine, sine, gain_query, bias, kv_all, kv):
    micro, keys, cols = kv_all.shape
    rows = bias.shape[0]
    heads = qkv.shape[1] // HEAD_SIZE // kv - 2
    width = heads * HEAD_SIZE

    def whole(v):
        return pl.BlockSpec(v.shape, lambda m, g: (0,) * v.ndim)

    return pl.pallas_call(
        functools.partial(attention_kernel, heads),
        grid=(micro, kv),
        in_specs=[pl.BlockSpec((rows, width), lambda m, g: (m, g))]
        + [whole(v) for v in (cosine, sine, gain_query, bias)]
        + [
            pl.BlockSpec((None, keys, HEAD_SIZE), lambda m, g: (m, 0, g)),
            pl.BlockSpec((None, keys, HEAD_SIZE), lambda m, g: (m, 0, kv + g)),
        ],
        out_specs=pl.BlockSpec((rows, width), lambda m, g: (m, g)),
        out_shape=jax.ShapeDtypeStruct((micro * rows, kv * width), BF16),
        compiler_params=pltpu.CompilerParams(vmem_limit_bytes=VMEM_LIMIT),
        cost_estimate=pl.CostEstimate(flops=0, bytes_accessed=60_000_000, transcendentals=0),
        name="attention_forward",
    )(qkv, cosine, sine, gain_query, bias, kv_all, kv_all)


def backward(qkv, heads_in, kv_all, d_attn, o, a, w_out, w_qkv, eo, kv):
    heads = qkv.shape[1] // HEAD_SIZE // kv - 2
    bias = heads_in[-1]
    rows, keys = bias.shape
    micro, _, kv_cols = kv_all.shape
    width, cols = w_qkv.shape
    total, q_cols = qkv.shape[0], kv * heads * HEAD_SIZE
    vmem, any_space = (pl.BlockSpec(memory_space=space) for space in (pltpu.VMEM, pl.ANY))
    dma = pltpu.SemaphoreType.DMA
    return pl.pallas_call(
        functools.partial(backward_kernel, kv, heads),
        in_specs=[vmem] * 10 + [any_space] * 3,
        out_specs=[vmem] * 2 + [any_space] * 3,
        out_shape=[
            jax.ShapeDtypeStruct((micro * BLOCK, width), F32),
            jax.ShapeDtypeStruct((2, HEAD_SIZE), F32),
            jax.ShapeDtypeStruct((width, cols), BF16),
            jax.ShapeDtypeStruct((width, q_cols), BF16),
            jax.ShapeDtypeStruct(eo.shape, BF16),
        ],
        scratch_shapes=[
            pltpu.VMEM((width, q_cols), BF16),
            pltpu.VMEM((width, cols), BF16),
            pltpu.VMEM((total, q_cols), BF16),
            pltpu.VMEM((total, cols), BF16),
            pltpu.VMEM((total, width), F32),
            pltpu.VMEM((2, WIDE, cols), BF16),
            pltpu.VMEM((2, WIDE, q_cols), BF16),
            pltpu.VMEM((micro, keys, kv_cols), BF16),
            pltpu.VMEM((CTX - 1, micro, BLOCK, kv_cols), BF16),
            pltpu.VMEM((micro, BLOCK, kv_cols), BF16),
            pltpu.VMEM((heads * rows, keys), BF16),
            pltpu.VMEM((micro * kv, heads * rows, keys), BF16),
            pltpu.VMEM((heads * rows, HEAD_SIZE), BF16),
            pltpu.VMEM((heads * rows, HEAD_SIZE), BF16),
            pltpu.VMEM((micro * BLOCK, width), BF16),
            pltpu.VMEM((micro * BLOCK, width), BF16),
            dma((CTX, micro)), dma((CTX, micro)), dma((2,)), dma((2, width // WIDE)), dma((2,)),
            dma((CHIPS,)), dma((CHIPS,)),
        ],
        compiler_params=pltpu.CompilerParams(
            collective_id=3, has_side_effects=True, vmem_limit_bytes=56 * 1024 * 1024
        ),
        cost_estimate=pl.CostEstimate(flops=0, bytes_accessed=250_000_000, transcendentals=0),
        name="attention_backward",
    )(qkv, *heads_in, kv_all, d_attn, o, a, w_out, w_qkv, eo)


def normalize(rows, gain):
    scaling = lax.rsqrt(jnp.mean(rows * rows, axis=-1, keepdims=True) + EPS)
    return rows * scaling * gain, scaling


def normalize_back(rows, scaling, gain, upstream):
    normed = rows * scaling
    gain_grad = jnp.sum((upstream * normed).reshape(-1, rows.shape[-1]), axis=0)
    scaled = upstream * gain
    inner = jnp.mean(scaled * normed, axis=-1, keepdims=True)
    return scaling * (scaled - normed * inner), gain_grad


def swap_tp(value):
    return lax.ppermute(value, "tp", [(0, 1), (1, 0)])


def local(
    x_prompt, x_cont, cot_prompt, cot_cont, ids_prompt, ids_cont, gates_prompt, gates_cont,
    norm_gain, query_weight, key_matrix, value_matrix, out_weight, query_gain, key_gain, moe_gain,
    expert_gate, expert_up, expert_down,
):
    micro = x_prompt.shape[0]
    prompt_rows, cont_rows, width = x_prompt.shape[2], x_cont.shape[2], x_prompt.shape[3]
    block = cont_rows
    rows = 2 * block
    s = lax.axis_index("ctx")
    ctx = lax.axis_size("ctx")
    first = lax.axis_index("tp") == 0
    peers = lax.axis_size(ALL)
    q_cols, kv_cols = query_weight.shape[1], key_matrix.shape[1]
    kv = kv_cols // HEAD_SIZE
    qkv_cols = q_cols + 2 * kv_cols
    shard_rows = query_weight.shape[0]
    hidden = expert_gate.shape[2]
    slots = cont_rows * TOPK // peers

    fsdp, tp = lax.axis_size("fsdp"), lax.axis_size("tp")
    chips = [(2 * y, c, t) for y in range(fsdp // 2) for c in range(ctx) for t in range(tp)]
    groups = [[((f + core) * ctx + c) * tp + t for f, c, t in chips] for core in range(2)]
    expert_of = jnp.array([(f + t) * ctx + c for f, c, t in chips], jnp.int32)

    def exchange(rows_of):
        return lax.all_to_all(
            rows_of, ("fsdp", "ctx", "tp"), split_axis=0, concat_axis=0, tiled=True,
            axis_index_groups=groups,
        )

    def pad(v):
        return jnp.pad(v[:, 0], ((0, 0), (0, block - prompt_rows), (0, 0)))

    x_first, x_second = pad(x_prompt), x_cont[:, 0]
    own_tokens = jnp.where(first, x_second, x_first).astype(F32)
    own_cot = jnp.where(first, cot_cont[:, 0], pad(cot_prompt))
    ids_pad = jnp.pad(
        ids_prompt[:, 0], ((0, 0), (0, block - prompt_rows), (0, 0)), constant_values=-1
    )
    own_ids = jnp.where(first, ids_cont[:, 0], ids_pad)
    own_gates = jnp.where(first, gates_cont[:, 0], pad(gates_prompt))

    y, z, x = chip_at(jnp.arange(peers, dtype=jnp.int32), 1)
    near = (2 * y + x // 2) * ctx + 2 * z + x % 2
    order = jnp.pad(jnp.stack([expert_of, near]), ((0, 0), (0, HEAD_SIZE - peers)), constant_values=-2)

    def lanes(v):
        return jnp.pad(v, [(0, 0)] * (v.ndim - 1) + [(0, HEAD_SIZE - v.shape[-1])])

    extra = jnp.stack([lanes(v) for v in (norm_gain, moe_gain, query_gain, key_gain)])
    extra = jnp.pad(extra, ((0, shard_rows - extra.shape[0]), (0, 0)))
    own_experts = (expert_gate[0], expert_up[0], expert_down[0])
    w_qkv, w_out_extra, far_experts, routing = gather_weights(
        query_weight, key_matrix, value_matrix, out_weight, extra,
        own_ids.reshape(-1, TOPK), own_gates.reshape(-1, TOPK), order,
        own_cot.reshape(-1, width), peers * micro * slots, *own_experts,
    )
    select_near, mixing, spread = routing
    w_out = w_out_extra[:, :q_cols]
    gains = w_out_extra[:, q_cols:].reshape(peers, shard_rows, HEAD_SIZE)[:, :4].astype(F32)
    gain_in, gain_moe = (gains[:, n, :shard_rows].reshape(-1) for n in (0, 1))
    head_rows = query_gain.shape[0]
    gain_query, gain_key = (gains[:, n, :head_rows].reshape(-1) for n in (2, 3))

    offsets = jnp.arange(rows, dtype=jnp.int32)
    is_prompt = offsets < block
    prompt_pos = s * prompt_rows + offsets
    cont_pos = s * cont_rows + offsets - block
    rot_place = jnp.where(is_prompt, prompt_pos, PROMPT + cont_pos % CL).astype(F32)
    steps_freq = jnp.arange(HEAD_SIZE // 2, dtype=F32) * (2.0 / HEAD_SIZE)
    angles = rot_place[:, None] * jnp.power(THETA, -steps_freq)[None, :]
    cosine, sine = jnp.cos(angles), jnp.sin(angles)
    cosine = jnp.concatenate([cosine, cosine], axis=1)
    sine = jnp.concatenate([-sine, sine], axis=1)
    keys = (ctx + 2) * block
    key_index = jnp.arange(keys, dtype=jnp.int32)[None, :]
    key_off = key_index % block
    key_prompt_pos = key_index // block * prompt_rows + key_off
    key_cont = (s - 1) * cont_rows + key_index - ctx * block
    is_cont = jnp.logical_not(is_prompt)[:, None]
    visible = jnp.where(
        key_index < ctx * block,
        jnp.logical_and(
            key_off < prompt_rows,
            jnp.logical_or(is_cont, key_prompt_pos <= prompt_pos[:, None]),
        ),
        jnp.logical_and(
            is_cont,
            jnp.logical_and(
                key_cont // CL == cont_pos[:, None] // CL, key_cont <= cont_pos[:, None]
            ),
        ),
    )
    bias = jnp.where(visible, 0.0, NEG).astype(F32)

    def arranged(own, other):
        return jnp.where(first, other, own), jnp.where(first, own, other)

    def sum_own(part):
        part = part.reshape(micro, rows, width)
        given = jnp.where(first, part[:, :block], part[:, block:]).astype(BF16)
        kept = jnp.where(first, part[:, block:], part[:, :block])
        return kept + swap_tp(given).astype(F32)

    tokens = jnp.concatenate([x_first, x_second], axis=1).astype(F32).reshape(-1, width)
    a = normalize(tokens, gain_in)[0].astype(BF16)
    qkv = dot(a, w_qkv, ((1,), (0,)))
    heads_in = (cosine, sine, gain_query[None], gain_key[None], bias)
    kv_all = share_keys(qkv, cosine, sine, gain_key[None], kv, keys, micro)

    spread, kv_all = lax.optimization_barrier((spread, kv_all))
    d_eo_rows = exchange(spread).reshape(peers, micro * slots, width)
    o = attention(qkv, cosine, sine, gain_query[None], bias, kv_all, kv)
    middle = own_tokens + sum_own(dot(o, w_out, ((1,), (1,))))
    b_normed, b_scale = normalize(middle, gain_moe)
    b_low = b_normed.astype(BF16)

    send = dot(select_near, b_low.reshape(-1, width), ((0,), (0,))).astype(BF16)
    back, eo, wide_here, tall_here = moe(
        send.reshape(d_eo_rows.shape), d_eo_rows, own_experts, far_experts
    )
    d_b = dot(select_near, back.reshape(-1, width), ((1,), (0,))).reshape(middle.shape)
    middle_from, moe_total = normalize_back(middle, b_scale, gain_moe, d_b)
    d_h = own_cot.astype(F32) + middle_from
    d_h_low = d_h.astype(BF16)
    d_attn = jnp.concatenate(arranged(d_h_low, swap_tp(d_h_low)), axis=1).reshape(-1, width)

    input_grad, head_totals, grad_qkv, grad_out, eo_back = backward(
        qkv, heads_in, kv_all, d_attn, o, a, w_out_extra, w_qkv, eo, kv
    )
    moe_out = dot(mixing, eo_back.reshape(-1, width), ((1,), (0,)))
    moe_out = (moe_out[: micro * block] + moe_out[micro * block :]).reshape(middle.shape)
    y_own = (middle + moe_out).astype(BF16)
    scale_in = lax.rsqrt(jnp.mean(own_tokens * own_tokens, axis=-1, keepdims=True) + EPS)
    token_from, norm_total = normalize_back(
        own_tokens, scale_in, gain_in, input_grad.reshape(own_tokens.shape)
    )
    x_own = (d_h + token_from).astype(BF16)

    extra_grads = jnp.stack(
        [
            lanes(v.reshape(peers, -1))
            for v in (norm_total, moe_total, head_totals[0], head_totals[1])
        ],
        axis=1,
    )
    extra_grads = jnp.pad(extra_grads, ((0, 0), (0, shard_rows - extra_grads.shape[1]), (0, 0)))
    extra_grads = extra_grads.reshape(-1, HEAD_SIZE).astype(BF16)
    share, share_out, wide_there, tall_there, y_other, x_other = scatter_grads(
        grad_qkv, grad_out, extra_grads, wide_here, tall_here, y_own, x_own
    )
    out_first, out_second = arranged(y_own, y_other)
    grad_first, grad_second = arranged(x_own, x_other)
    grad_wide = jnp.where(native(), wide_here, wide_there).astype(F32)
    grad_down = jnp.where(native(), tall_here, tall_there).astype(F32)
    gain_share = share_out[:, q_cols:]
    return (
        out_first[:, None, :prompt_rows],
        out_second[:, None],
        grad_first[:, None, :prompt_rows],
        grad_second[:, None],
        gain_share[0, :shard_rows],
        share[:, :q_cols],
        share[:, q_cols : q_cols + kv_cols],
        share[:, q_cols + kv_cols : qkv_cols],
        share_out[:, :q_cols],
        gain_share[2, :head_rows],
        gain_share[3, :head_rows],
        gain_share[1, :shard_rows],
        grad_wide[None, :, :hidden],
        grad_wide[None, :, hidden:],
        grad_down[None],
    )


def solution(mesh):
    rows = P(None, "fsdp", "ctx", None)
    vector = P(("fsdp", "ctx"))
    matrix = P(("fsdp", "ctx"), "tp")
    wide = P(("fsdp", "ctx"), None, "tp")
    tall = P(("fsdp", "ctx"), "tp", None)
    in_specs = (rows,) * 8 + (vector,) + (matrix,) * 4 + (vector,) * 3 + (wide, wide, tall)
    out_specs = (rows,) * 4 + (vector,) + (matrix,) * 4 + (vector,) * 3 + (wide, wide, tall)
    return jax.shard_map(local, mesh=mesh, in_specs=in_specs, out_specs=out_specs, check_vma=False)
```

```python
import functools

import jax
import jax.numpy as jnp
from jax import lax
from jax.experimental import pallas as pl
from jax.experimental.pallas import tpu as pltpu
from jax.sharding import PartitionSpec as P

HEAD_SIZE = 128
TOPK = 8
PROMPT = 448
CL = 128
EPS = 1e-06
THETA = 1000000.0
NEG = -1e30
F32 = jnp.float32
BF16 = jnp.bfloat16
ALL = ("fsdp", "ctx")
MESH = pl.DeviceIdType.MESH
RING = 4
VMEM_LIMIT = 48 * 1024 * 1024


def dot(a, b, dims):
    return lax.dot_general(a, b, (dims, ((), ())), preferred_element_type=F32)


def remote(src, dst, send_sem, recv_sem, where):
    return pltpu.make_async_remote_copy(
        src_ref=src, dst_ref=dst, send_sem=send_sem, recv_sem=recv_sem, device_id=where,
        device_id_type=MESH,
    )


def place():
    f, c = lax.axis_index("fsdp"), lax.axis_index("ctx")
    return f // 2, f % 2, c // 2, c % 2


def device(y, core, z, x):
    return {"fsdp": y * 2 + core, "ctx": z * 2 + x}


def greet(partners):
    barrier = pltpu.get_barrier_semaphore()
    for partner in partners:
        pl.semaphore_signal(barrier, inc=1, device_id=partner, device_id_type=MESH)
    pl.semaphore_wait(barrier, len(partners))


def neighbours():
    y, core, z, x = place()
    up, down = (lambda v: lax.rem(v + 1, RING)), (lambda v: lax.rem(v + RING - 1, RING))
    return [
        device(y, core, z, 1 - x),
        device(y, 1 - core, z, x),
        device(up(y), core, z, x),
        device(down(y), core, z, x),
        device(y, core, up(z), x),
        device(y, core, down(z), x),
    ]


def other_tp():
    return {"tp": 1 - lax.axis_index("tp")}


def opposite():
    f = lax.axis_index("fsdp")
    return {"fsdp": f + 1 - 2 * (f % 2), "tp": 1 - lax.axis_index("tp")}


def native():
    return lax.axis_index("fsdp") % 2 == lax.axis_index("tp")


def swap_opposite(src, dst, send_sem, recv_sem):
    return pltpu.make_async_remote_copy(
        src_ref=src, dst_ref=dst, send_sem=send_sem, recv_sem=recv_sem, device_id=opposite(),
        device_id_type=MESH,
    )


def route(ids, gates, experts, size, select_ref, mix_ref):
    tokens, slots = ids.shape[0], mix_ref.shape[1]
    block, places = tokens // 2, size // 2
    chosen = jnp.zeros((tokens, experts.shape[1]), F32)
    weight = jnp.zeros((tokens, experts.shape[1]), F32)
    for k in range(ids.shape[1]):
        same = ids[:, k : k + 1] == experts
        chosen = chosen + jnp.where(same, 1.0, 0.0)
        weight = weight + jnp.where(same, gates[:, k : k + 1], 0.0)
    t = lax.broadcasted_iota(jnp.int32, (tokens, tokens), 0)
    u = lax.broadcasted_iota(jnp.int32, (tokens, tokens), 1)
    earlier = jnp.logical_and(u < t, (u >= block) == (t >= block))
    rank = dot(jnp.where(earlier, 1.0, 0.0).astype(BF16), chosen.astype(BF16), ((1,), (0,)))
    rank = jnp.where(chosen > 0.0, rank, -1.0).astype(BF16)
    e = lax.broadcasted_iota(jnp.int32, (experts.shape[1], slots), 0)
    j = lax.broadcasted_iota(jnp.int32, (experts.shape[1], slots), 1)
    spread = jnp.where(jnp.logical_and(j >= e * size, j < (e + 1) * size), 1.0, 0.0).astype(BF16)
    j = lax.broadcasted_iota(jnp.int32, (tokens, slots), 1)
    later = lax.broadcasted_iota(jnp.int32, (tokens, slots), 0) >= block
    place = (j & (places - 1)).astype(F32)
    mine = ((j & places) != 0) == later
    there = jnp.logical_and(dot(rank, spread, ((1,), (0,))) == place, mine)
    select_ref[...] = jnp.where(there, 1.0, 0.0).astype(BF16)
    high = weight.astype(BF16)
    low = (weight - high.astype(F32)).astype(BF16)
    mix_ref[0:tokens, :] = jnp.where(there, dot(high, spread, ((1,), (0,))), 0.0).astype(BF16)
    mix_ref[tokens:, :] = jnp.where(there, dot(low, spread, ((1,), (0,))), 0.0).astype(BF16)


def gather_kernel(
    query_ref, key_ref, value_ref, out_ref, extra_ref, ids_ref, gates_ref, experts_ref, cot_ref,
    gate_ref, up_ref, down_ref,
    a_all, b_all, gate_all, up_all, down_all, near_ref, mix_ref, rows_ref,
    a_own, b_own, rows, rows_sem, local_sem, send_sem, recv_sem, away_sem, home_sem, give_sem, take_sem,
):
    y, core, z, x = place()
    for own, refs in ((a_own, (query_ref, key_ref, value_ref)), (b_own, (out_ref, extra_ref))):
        at = 0
        for ref in refs:
            own[:, at : at + ref.shape[1]] = ref[...]
            at += ref.shape[1]
    greet(neighbours() + [opposite()])
    shards = ((gate_ref, gate_all), (up_ref, up_all), (down_ref, down_all))
    moved = [
        swap_opposite(p, q, give_sem.at[n], take_sem.at[n]) for n, (p, q) in enumerate(shards)
    ]
    refs, own = (a_all, b_all), (a_own, b_own)
    started = []
    count = [0, 0]

    def chunk(n, i, j):
        return refs[n].at[j, core, i] if n == 0 else refs[n].at[i, core, j]

    def to(n, first, second):
        return device(second, core, first, x) if n == 0 else device(first, core, second, x)

    def send(n, ref, where, slot):
        copy = pltpu.make_async_remote_copy(
            src_ref=ref, dst_ref=ref, send_sem=send_sem.at[n, slot], recv_sem=recv_sem.at[n, slot],
            device_id=where, device_id_type=MESH,
        )
        copy.start()
        started.append(copy)

    def arrived(n, ref, slot):
        pltpu.make_async_remote_copy(
            src_ref=ref, dst_ref=ref, send_sem=send_sem.at[n, slot], recv_sem=recv_sem.at[n, slot],
            device_id=device(y, core, z, x), device_id_type=MESH,
        ).wait_recv()

    homes = []

    def across(n, i, j):
        slot = count[n]
        count[n] += 1
        ref = chunk(n, i, j)
        copy = pltpu.make_async_remote_copy(
            src_ref=ref, dst_ref=ref, send_sem=away_sem.at[n, slot], recv_sem=home_sem.at[n, slot],
            device_id=device(y, 1 - core, z, x), device_id_type=MESH,
        )
        copy.start()
        homes.append(copy)

    def second(n, i, j, k):
        base = 5 + 4 * k
        send(n, chunk(n, i, j), to(n, me[n][0], up(j)), base)
        send(n, chunk(n, i, j), to(n, me[n][0], down(j)), base + 1)
        across(n, i, j)

    up, down = (lambda v: lax.rem(v + 1, RING)), (lambda v: lax.rem(v + RING - 1, RING))
    me = ((z, y), (y, z))
    locals_ = []
    for n in (0, 1):
        i, j = me[n]
        keep = pltpu.make_async_copy(own[n], chunk(n, i, j).at[x], local_sem.at[n])
        keep.start()
        locals_.append(keep)
        copy = pltpu.make_async_remote_copy(
            src_ref=own[n], dst_ref=chunk(n, i, j).at[x], send_sem=send_sem.at[n, 0],
            recv_sem=recv_sem.at[n, 0], device_id=device(y, core, z, 1 - x), device_id_type=MESH,
        )
        copy.start()
        started.append(copy)
    size = rows.shape[0] // (RING * RING * RING)
    ids, gates = ids_ref[...], gates_ref[...]
    route(ids, gates, experts_ref[...], size, near_ref, mix_ref)
    for n in (0, 1):
        i, j = me[n]
        locals_[n].wait()
        arrived(n, chunk(n, i, j).at[1 - x], 0)
        send(n, chunk(n, i, j), to(n, up(i), j), 1)
        send(n, chunk(n, i, j), to(n, down(i), j), 2)
    for n in (0, 1):
        i, j = me[n]
        second(n, i, j, 0)

    @pl.when(jnp.logical_not(native()))
    def _():
        for copy in moved:
            copy.start()

    part, tokens = 256, cot_ref.shape[0]
    for at in range(0, rows.shape[0], part):
        lanes = slice(at, at + part)
        total = dot(mix_ref[0:tokens, lanes], cot_ref[...], ((0,), (0,)))
        total = total + dot(mix_ref[tokens:, lanes], cot_ref[...], ((0,), (0,)))
        rows[lanes, :] = total.astype(BF16)
    keep_rows = pltpu.make_async_copy(rows, rows_ref, rows_sem)
    keep_rows.start()
    for n in (0, 1):
        i, j = me[n]
        arrived(n, chunk(n, down(i), j), 1)
        send(n, chunk(n, down(i), j).at[0], to(n, up(i), j), 3)
        second(n, down(i), j, 1)
    for n in (0, 1):
        i, j = me[n]
        arrived(n, chunk(n, up(i), j), 2)
        send(n, chunk(n, up(i), j).at[1], to(n, down(i), j), 4)
        second(n, up(i), j, 2)
    for n in (0, 1):
        i, j = me[n]
        far = lax.rem(i + 2, RING)
        arrived(n, chunk(n, far, j).at[0], 3)
        arrived(n, chunk(n, far, j).at[1], 4)
        second(n, far, j, 3)
    for k in range(4):
        for n in (0, 1):
            i, j = me[n]
            it = (i, down(i), up(i), lax.rem(i + 2, RING))[k]
            base = 5 + 4 * k
            arrived(n, chunk(n, it, down(j)), base)
            send(n, chunk(n, it, down(j)).at[0], to(n, i, up(j)), base + 2)
            across(n, it, down(j))
            arrived(n, chunk(n, it, up(j)), base + 1)
            send(n, chunk(n, it, up(j)).at[1], to(n, i, down(j)), base + 3)
            across(n, it, up(j))
    for k in range(4):
        for n in (0, 1):
            i, j = me[n]
            it = (i, down(i), up(i), lax.rem(i + 2, RING))[k]
            base = 5 + 4 * k
            far = lax.rem(j + 2, RING)
            arrived(n, chunk(n, it, far).at[0], base + 2)
            arrived(n, chunk(n, it, far).at[1], base + 3)
            across(n, it, far)
    keep_rows.wait()
    for copy in homes:
        copy.wait()
    for copy in started:
        copy.wait_send()

    @pl.when(jnp.logical_not(native()))
    def _():
        for copy in moved:
            copy.wait()


def gather_weights(query, key, value, out, extra, ids, gates, experts, cot, slots, gate, up, down):
    rows = query.shape[0]
    cols = (query.shape[1] + key.shape[1] + value.shape[1], out.shape[1] + extra.shape[1])
    shape = (RING, 2, RING, 2, rows)
    vmem, any_space = (pl.BlockSpec(memory_space=space) for space in (pltpu.VMEM, pl.ANY))
    tokens, width = cot.shape
    routing = [jax.ShapeDtypeStruct((n * tokens, slots), BF16) for n in (1, 2)]
    a_all, b_all, *rest = pl.pallas_call(
        gather_kernel,
        in_specs=[vmem] * 9 + [any_space] * 3,
        out_specs=[any_space] * 5 + [vmem] * 2 + [any_space],
        out_shape=[jax.ShapeDtypeStruct(shape + (c,), query.dtype) for c in cols]
        + [jax.ShapeDtypeStruct(v.shape, v.dtype) for v in (gate, up, down)]
        + routing + [jax.ShapeDtypeStruct((slots, width), BF16)],
        scratch_shapes=[pltpu.VMEM((rows, c), query.dtype) for c in cols] + [
            pltpu.VMEM((slots, width), BF16),
            pltpu.SemaphoreType.DMA,
            pltpu.SemaphoreType.DMA((2,)),
            pltpu.SemaphoreType.DMA((2, 21)),
            pltpu.SemaphoreType.DMA((2, 21)),
            pltpu.SemaphoreType.DMA((2, 16)),
            pltpu.SemaphoreType.DMA((2, 16)),
            pltpu.SemaphoreType.DMA((3,)),
            pltpu.SemaphoreType.DMA((3,)),
        ],
        compiler_params=pltpu.CompilerParams(
            collective_id=0, has_side_effects=True, vmem_limit_bytes=VMEM_LIMIT
        ),
        cost_estimate=pl.CostEstimate(flops=0, bytes_accessed=250_000_000, transcendentals=0),
        name="gather_weights",
    )(query, key, value, out, extra, ids, gates, experts, cot, gate, up, down)
    return a_all.reshape(-1, cols[0]), b_all.reshape(-1, cols[1]), rest[:3], rest[3:]


ORDER = (2, 1, 3, 0)
SLICE = 16


def up(v):
    return lax.rem(v + 1, RING)


def down(v):
    return lax.rem(v + RING - 1, RING)


def add_into(target, *terms):
    flat = [target.shape[0]] if len(target.shape) == 3 else []
    for lead in range(flat[0]) if flat else (None,):
        for start in range(0, target.shape[-2], SLICE):
            at = (pl.ds(start, SLICE), slice(None))
            at = at if lead is None else (lead,) + at
            total = terms[0][at].astype(F32)
            for term in terms[1:]:
                total = total + term[at].astype(F32)
            target[at] = total.astype(target.dtype)


def scatter_kernel(
    a_ref, b_ref, extra_ref, wide_ref, tall_ref, y_ref, x_ref,
    a_out, b_out, wide_out, tall_out, y_out, x_out, a_mine, b_mine, a_theirs, b_theirs, a_one, b_one, a_two, b_two,
    a_first, b_first, a_last, b_last, a_x, b_x, load_sem, send_sem, recv_sem,
    gains_here, gains_there,
    extra_load_sem, extra_send_sem, extra_recv_sem, give_sem, take_sem, gains_sem, token_sem,
):
    y, core, z, x = place()
    greet(neighbours() + [other_tp(), opposite()])
    moved = [
        swap_opposite(wide_ref, wide_out, give_sem.at[0], take_sem.at[0]),
        swap_opposite(tall_ref, tall_out, give_sem.at[1], take_sem.at[1]),
    ]

    tokens = [
        pltpu.make_async_remote_copy(
            src_ref=src, dst_ref=dst, send_sem=token_sem.at[n, 0], recv_sem=token_sem.at[n, 1],
            device_id=other_tp(), device_id_type=MESH,
        )
        for n, (src, dst) in enumerate(((y_ref, y_out), (x_ref, x_out)))
    ]
    for copy in tokens:
        copy.start()

    @pl.when(jnp.logical_not(native()))
    def _():
        for copy in moved:
            copy.start()

    grads, outs = (a_ref, b_ref), (a_out, b_out)
    mine, theirs = (a_mine, b_mine), (a_theirs, b_theirs)
    one, two = (a_one, b_one), (a_two, b_two)
    first, last, side = (a_first, b_first), (a_last, b_last), (a_x, b_x)
    me = ((z, y), (y, z))
    sent = []

    def chunk(n, i, j, c):
        return grads[n].at[j, c, i] if n == 0 else grads[n].at[i, c, j]

    def to(n, i, j):
        return device(j, core, i, x) if n == 0 else device(i, core, j, x)

    def copy_of(n, src, dst, slot, where):
        return pltpu.make_async_remote_copy(
            src_ref=src, dst_ref=dst, send_sem=send_sem.at[n, slot], recv_sem=recv_sem.at[n, slot],
            device_id=where, device_id_type=MESH,
        )

    def send(n, src, dst, slot, where):
        copy = copy_of(n, src, dst, slot, where)
        copy.start()
        sent.append(copy)

    def arrived(n, dst, slot):
        copy_of(n, dst, dst, slot, device(y, core, z, x)).wait_recv()

    cols = b_ref.shape[-1]

    def columns(ref, start, count):
        return ref.at[:, :, pl.ds(start, count)]

    def extra_copy(slot):
        ref = columns(theirs[1].at[slot], cols, extra_ref.shape[-1])
        far = extra_ref.at[lax.rem(y + slot // RING, RING), 1 - core, lax.rem(z + slot % RING, RING)]
        return pltpu.make_async_remote_copy(
            src_ref=far, dst_ref=ref, send_sem=extra_send_sem.at[slot],
            recv_sem=extra_recv_sem.at[slot], device_id=device(y, 1 - core, z, x),
            device_id_type=MESH,
        )

    def extra_load(slot):
        near = extra_ref.at[lax.rem(y + slot // RING, RING), core, lax.rem(z + slot % RING, RING)]
        return pltpu.make_async_copy(
            near, columns(mine[1].at[slot], cols, extra_ref.shape[-1]), extra_load_sem.at[slot]
        )

    def load(n, di, dj):
        i, j = me[n]
        slot = di * RING + dj
        target = mine[n].at[slot] if n == 0 else columns(mine[n].at[slot], 0, cols)
        return pltpu.make_async_copy(
            chunk(n, lax.rem(i + di, RING), lax.rem(j + dj, RING), core), target,
            load_sem.at[n, slot],
        )

    for dj in ORDER:
        for di in ORDER:
            for n in (0, 1):
                i, j = me[n]
                slot = di * RING + dj
                there = chunk(n, lax.rem(i + di, RING), lax.rem(j + dj, RING), 1 - core)
                target = theirs[n].at[slot] if n == 0 else columns(theirs[n].at[slot], 0, cols)
                send(n, there, target, slot, device(y, 1 - core, z, x))
                load(n, di, dj).start()
                if n == 1:
                    extra_copy(slot).start()
                    extra_load(slot).start()

    def ready(n, di, dj):
        slot = di * RING + dj
        load(n, di, dj).wait()
        if n == 0:
            arrived(n, theirs[n].at[slot], slot)
        else:
            arrived(n, columns(theirs[n].at[slot], 0, cols), slot)
            extra_load(slot).wait()
            extra_copy(slot).wait_recv()
        return slot

    for di in ORDER:
        for n in (0, 1):
            i, j = me[n]
            slot = ready(n, di, 2)
            add_into(mine[n].at[slot], mine[n].at[slot], theirs[n].at[slot])
            for half in (0, 1):
                send(
                    n, mine[n].at[slot, half], one[n].at[di, half], 16 + di * 2 + half,
                    to(n, i, up(j) if half == 0 else down(j)),
                )
    for di in ORDER:
        for n in (0, 1):
            i, j = me[n]
            for half, dj in ((0, 1), (1, 3)):
                slot = ready(n, di, dj)
                arrived(n, one[n].at[di, half], 16 + di * 2 + half)
                add_into(
                    mine[n].at[slot, half], mine[n].at[slot, half], theirs[n].at[slot, half],
                    one[n].at[di, half],
                )
                add_into(
                    mine[n].at[slot, 1 - half], mine[n].at[slot, 1 - half],
                    theirs[n].at[slot, 1 - half],
                )
                send(
                    n, mine[n].at[slot], two[n].at[di, half], 24 + di * 2 + half,
                    to(n, i, up(j) if half == 0 else down(j)),
                )
    for di in ORDER:
        for n in (0, 1):
            i, j = me[n]
            slot = ready(n, di, 0)
            for half in (0, 1):
                arrived(n, two[n].at[di, half], 24 + di * 2 + half)
            add_into(
                mine[n].at[slot], mine[n].at[slot], theirs[n].at[slot], two[n].at[di, 0],
                two[n].at[di, 1],
            )
            if di == 2:
                for half in (0, 1):
                    send(
                        n, mine[n].at[slot, half], first[n].at[half], 32 + half,
                        to(n, up(i) if half == 0 else down(i), j),
                    )
            elif di != 0:
                half = 0 if di == 1 else 1
                arrived(n, first[n].at[half], 32 + half)
                add_into(mine[n].at[slot, half], mine[n].at[slot, half], first[n].at[half])
                send(
                    n, mine[n].at[slot], last[n].at[half], 34 + half,
                    to(n, up(i) if half == 0 else down(i), j),
                )
    for n in (0, 1):
        for half in (0, 1):
            arrived(n, last[n].at[half], 34 + half)
        add_into(mine[n].at[0], mine[n].at[0], last[n].at[0], last[n].at[1])
        send(n, mine[n].at[0, 1 - x], side[n], 36, device(y, core, z, 1 - x))
    for n in (0, 1):
        arrived(n, side[n], 36)
        add_into(outs[n], mine[n].at[0, x], side[n])
    gains_here[...] = b_out[:, cols:]
    gains = pltpu.make_async_remote_copy(
        src_ref=gains_here, dst_ref=gains_there, send_sem=gains_sem.at[0],
        recv_sem=gains_sem.at[1], device_id=other_tp(), device_id_type=MESH,
    )
    gains.start()
    for copy in sent:
        copy.wait_send()
    for slot in range(RING * RING):
        extra_copy(slot).wait_send()
    gains.wait()
    for copy in tokens:
        copy.wait()
    b_out[:, cols:] = gains_here[...] + gains_there[...]

    @pl.when(jnp.logical_not(native()))
    def _():
        for copy in moved:
            copy.wait()


def scatter_grads(a, b, extra, wide, tall, y, x):
    peers = RING * RING * 4
    rows = a.shape[0] // peers
    shape = (RING, 2, RING, 2, rows)
    cols = (a.shape[1], b.shape[1] + extra.shape[1])
    buffers = []
    for lead in ((16, 2), (16, 2), (4, 2), (4, 2, 2), (2,), (2, 2), ()):
        buffers += [pltpu.VMEM(lead + (rows, c), a.dtype) for c in cols]
    any_space = pl.BlockSpec(memory_space=pl.ANY)
    return pl.pallas_call(
        scatter_kernel,
        in_specs=[any_space] * 7,
        out_specs=[pl.BlockSpec(memory_space=pltpu.VMEM)] * 2 + [any_space] * 4,
        out_shape=[jax.ShapeDtypeStruct((rows, c), F32) for c in cols]
        + [jax.ShapeDtypeStruct(v.shape, v.dtype) for v in (wide, tall, y, x)],
        scratch_shapes=buffers + [
            pltpu.SemaphoreType.DMA((2, 16)),
            pltpu.SemaphoreType.DMA((2, 37)),
            pltpu.SemaphoreType.DMA((2, 37)),
            pltpu.VMEM((rows, extra.shape[1]), F32),
            pltpu.VMEM((rows, extra.shape[1]), F32),
            pltpu.SemaphoreType.DMA((16,)),
            pltpu.SemaphoreType.DMA((16,)),
            pltpu.SemaphoreType.DMA((16,)),
            pltpu.SemaphoreType.DMA((2,)),
            pltpu.SemaphoreType.DMA((2,)),
            pltpu.SemaphoreType.DMA((2,)),
            pltpu.SemaphoreType.DMA((2, 2)),
        ],
        compiler_params=pltpu.CompilerParams(
            collective_id=1, has_side_effects=True, vmem_limit_bytes=44 * 1024 * 1024
        ),
        cost_estimate=pl.CostEstimate(flops=0, bytes_accessed=250_000_000, transcendentals=0),
        name="scatter_grads",
    )(*(v.reshape(shape + (v.shape[1],)) for v in (a, b, extra)), wide, tall, y, x)


CHIPS = RING * RING * RING
GROUP = 16
MIX = 11
AHEAD = 2
TILE = 256


def chip_at(slot, sign):
    f, c, t = lax.axis_index("fsdp"), lax.axis_index("ctx"), lax.axis_index("tp")
    k = lax.rem(slot * MIX, CHIPS) * sign
    turn = 0 if sign > 0 else RING
    far = [lax.div(k, RING * RING), lax.rem(lax.div(k, RING), RING), lax.rem(k, RING)]
    own = [lax.div(f, 2), lax.div(c, 2), t * 2 + lax.rem(c, 2)]
    return [lax.rem(o + d + turn, RING) for o, d in zip(own, far)]


def device_at(slot, sign):
    y, z, x = chip_at(slot, sign)
    core = lax.rem(lax.axis_index("fsdp"), 2)
    return {"fsdp": y * 2 + core, "ctx": z * 2 + lax.rem(x, 2), "tp": lax.div(x, 2)}


def other_core():
    f = lax.axis_index("fsdp")
    return {"fsdp": f + 1 - 2 * (f % 2)}


def moe_kernel(
    send_ref, deo_ref, gate_ref, up_ref, down_ref, gate_far, up_far, down_far,
    back_ref, eo_ref, wide_ref, tall_ref,
    rows, deos, gu, down, z, dgu, wide, tall, give, take,
    go_sem, come_sem, load_sem, weight_sem, share_send, share_recv, part_send, part_recv,
    back_send, back_recv, eo_sem,
):
    size, hidden = send_ref.shape[1], down_ref.shape[0]
    count = GROUP * size
    groups = CHIPS // GROUP
    width = down_ref.shape[1]

    def each(body, low, high):
        def step(i, carry):
            body(i)
            return carry

        lax.fori_loop(low, high, step, 0)

    barrier = pltpu.get_barrier_semaphore()
    each(
        lambda s: pl.semaphore_signal(
            barrier, inc=1, device_id=device_at(s, 1), device_id_type=MESH
        ),
        1, CHIPS,
    )
    pl.semaphore_signal(barrier, inc=1, device_id=other_core(), device_id_type=MESH)
    pl.semaphore_wait(barrier, CHIPS)

    def slot_rows(s):
        return pl.ds(pl.multiple_of(s * size, size), size)

    def group_rows(g):
        return pl.ds(pl.multiple_of(g * count, count), count)

    def go(s):
        return remote(
            send_ref.at[s], rows.at[0, slot_rows(s)], go_sem.at[s], come_sem.at[s], device_at(s, 1)
        )

    def stay(s):
        return pltpu.make_async_copy(send_ref.at[s], rows.at[0, slot_rows(s)], come_sem.at[s])

    def load(s):
        return pltpu.make_async_copy(
            deo_ref.at[s], deos.at[0, slot_rows(s)], load_sem.at[s]
        )

    def sent_rows(n, s):
        slot = lax.rem(lax.div(s, GROUP), 2)
        return give.at[n, slot, slot_rows(lax.rem(s, GROUP))]

    def back(s):
        return remote(
            sent_rows(0, s), back_ref.at[s], back_send.at[s], back_recv.at[s], device_at(s, -1)
        )

    def back_stay():
        return pltpu.make_async_copy(
            give.at[0, 0, pl.ds(0, size)], back_ref.at[0], back_recv.at[0]
        )

    def out(s):
        return pltpu.make_async_copy(
            sent_rows(1, s), eo_ref.at[s], eo_sem.at[s]
        )

    def share(n, g):
        ref = (rows, deos)[n]
        return remote(
            ref.at[0, group_rows(g)], ref.at[1, group_rows(g)], share_send.at[n, g],
            share_recv.at[n, g], other_core(),
        )

    def part(n, g):
        slot = lax.rem(g, 2)
        return remote(
            give.at[n, slot], take.at[n, slot], part_send.at[n, g], part_recv.at[n, g],
            other_core(),
        )

    places = (gu.at[:, pl.ds(0, hidden)], gu.at[:, pl.ds(hidden, hidden)], down)
    weights = [
        [pltpu.make_async_copy(src, dst, weight_sem.at[n]) for n, (src, dst) in enumerate(pairs)]
        for pairs in (
            zip((gate_ref, up_ref, down_ref), places), zip((gate_far, up_far, down_far), places)
        )
    ]

    def on_weights(act):
        for condition, copies in zip((native(), jnp.logical_not(native())), weights):

            @pl.when(condition)
            def _(copies=copies):
                for copy in copies:
                    act(copy)

    stay(0).start()
    each(lambda s: go(s).start(), 1, AHEAD * GROUP)
    each(lambda s: load(s).start(), 0, CHIPS)
    on_weights(lambda copy: copy.start())

    def tiles(body):
        each(lambda i: body(pl.ds(pl.multiple_of(i * TILE, TILE), TILE)), 0, width // TILE)

    def clear(at):
        wide[at, :] = jnp.zeros((TILE, 2 * hidden), F32)
        tall[:, at] = jnp.zeros((hidden, TILE), F32)

    tiles(clear)

    def through(side, g):
        at = group_rows(g)
        pre = dot(rows[side, at, :], gu[...], ((1,), (0,)))
        dz = dot(deos[side, at, :], down[...], ((1,), (1,)))
        gate, u = pre[:, :hidden], pre[:, hidden:]
        sig = 1.0 / (1.0 + jnp.exp(-gate))
        act = gate * sig
        z[side] = (act * u).astype(BF16)
        dgu[side, :, :hidden] = (dz * u * sig * (1.0 + gate * (1.0 - sig))).astype(BF16)
        dgu[side, :, hidden:] = (dz * act).astype(BF16)

    def to_rows(side):
        return dot(dgu[side], gu[...], ((1,), (1,)))

    def to_outputs(side):
        return dot(z[side], down[...], ((1,), (0,)))

    on_weights(lambda copy: copy.wait())

    def group(g):
        first, last, slot = g * GROUP, (g + 1) * GROUP, lax.rem(g, 2)

        @pl.when(g == 0)
        def _():
            stay(0).wait()

        each(lambda s: go(s).wait_recv(), lax.max(first, 1), last)
        each(lambda s: load(s).wait(), first, last)
        each(
            lambda s: go(s).start(), lax.min(first + AHEAD * GROUP, CHIPS),
            lax.min(last + AHEAD * GROUP, CHIPS),
        )
        for n in (0, 1):
            share(n, g).start()
        through(0, g)
        for n in (0, 1):
            share(n, g).wait_recv()
        through(1, g)

        @pl.when(g >= 2)
        def _():
            @pl.when(g == 2)
            def _():
                back_stay().wait()

            each(lambda s: back(s).wait_send(), lax.max(first - 2 * GROUP, 1), last - 2 * GROUP)
            each(lambda s: out(s).wait(), first - 2 * GROUP, last - 2 * GROUP)

        give[0, slot] = to_rows(1).astype(BF16)
        part(0, g).start()
        give[1, slot] = to_outputs(1).astype(BF16)
        part(1, g).start()
        own = to_rows(0)
        part(0, g).wait()
        give[0, slot] = (own + take[0, slot].astype(F32)).astype(BF16)

        @pl.when(g == 0)
        def _():
            back_stay().start()

        each(lambda s: back(s).start(), lax.max(first, 1), last)
        own = to_outputs(0)
        part(1, g).wait()
        give[1, slot] = (own + take[1, slot].astype(F32)).astype(BF16)
        each(lambda s: out(s).start(), first, last)
        at = group_rows(g)

        def weight_grads(cols):
            wide[cols, :] += dot(rows[0, at, cols], dgu[0], ((0,), (0,))) + dot(
                rows[1, at, cols], dgu[1], ((0,), (0,))
            )
            tall[:, cols] += dot(z[0], deos[0, at, cols], ((0,), (0,))) + dot(
                z[1], deos[1, at, cols], ((0,), (0,))
            )

        tiles(weight_grads)

    each(group, 0, groups)

    def store(at):
        wide_ref[at, :] = wide[at, :].astype(BF16)
        tall_ref[:, at] = tall[:, at].astype(BF16)

    tiles(store)
    for g in range(groups):
        for n in (0, 1):
            share(n, g).wait_send()
    each(lambda s: out(s).wait(), (groups - 2) * GROUP, CHIPS)
    each(lambda s: back(s).wait_send(), (groups - 2) * GROUP, CHIPS)
    each(lambda s: go(s).wait_send(), 1, CHIPS)
    each(lambda s: back(s).wait_recv(), 1, CHIPS)


def moe(send, d_eo, own, far):
    chips, size, width = send.shape
    hidden = own[2].shape[0]
    total, groups = chips * size, chips // GROUP
    count = GROUP * size
    vmem, any_space = (pl.BlockSpec(memory_space=space) for space in (pltpu.VMEM, pl.ANY))
    shapes = [send.shape, send.shape, (width, 2 * hidden), (hidden, width)]
    dma = pltpu.SemaphoreType.DMA
    return pl.pallas_call(
        moe_kernel,
        in_specs=[any_space] * 8,
        out_specs=[any_space] * 2 + [vmem] * 2,
        out_shape=[jax.ShapeDtypeStruct(shape, BF16) for shape in shapes],
        scratch_shapes=[
            pltpu.VMEM((2, total, width), BF16),
            pltpu.VMEM((2, total, width), BF16),
            pltpu.VMEM((width, 2 * hidden), BF16),
            pltpu.VMEM((hidden, width), BF16),
            pltpu.VMEM((2, count, hidden), BF16),
            pltpu.VMEM((2, count, 2 * hidden), BF16),
            pltpu.VMEM((width, 2 * hidden), F32),
            pltpu.VMEM((hidden, width), F32),
            pltpu.VMEM((2, 2, count, width), BF16),
            pltpu.VMEM((2, 2, count, width), BF16),
            dma((chips,)), dma((chips,)), dma((chips,)), dma((3,)),
            dma((2, groups)), dma((2, groups)), dma((2, groups)), dma((2, groups)),
            dma((chips,)), dma((chips,)), dma((chips,)),
        ],
        compiler_params=pltpu.CompilerParams(
            collective_id=4, has_side_effects=True, vmem_limit_bytes=56 * 1024 * 1024
        ),
        cost_estimate=pl.CostEstimate(flops=0, bytes_accessed=400_000_000, transcendentals=0),
        name="experts",
    )(send, d_eo, *own, *far)


BLOCK = 64
CTX = 8
WIDE = 256


def rotated(u, gain, cosine, sine):
    scaling = lax.rsqrt(jnp.mean(u * u, axis=-1, keepdims=True) + EPS)
    normed = u * scaling
    n = normed * gain
    rot = n * cosine + pltpu.roll(n, HEAD_SIZE // 2, 1) * sine
    return rot.astype(BF16), normed, scaling


def rotated_back(e, normed, scaling, gain, cosine, sine):
    back = e * cosine + pltpu.roll(e * sine, HEAD_SIZE // 2, 1)
    scaled = back * gain
    inner = jnp.mean(scaled * normed, axis=-1, keepdims=True)
    return scaling * (scaled - normed * inner), jnp.sum(back * normed, axis=0, keepdims=True)


def ctx_peer(step):
    return {"ctx": lax.rem(lax.axis_index("ctx") + step, CTX)}


def beside():
    c = lax.axis_index("ctx")
    return {"ctx": c + 1 - 2 * lax.rem(c, 2)}


def softmax_parts(q_low, k, bias):
    s = dot(q_low, k, ((1,), (1,))) * (HEAD_SIZE ** -0.5) + bias
    e = jnp.exp(s - jnp.max(s, axis=-1, keepdims=True))
    return e / jnp.sum(e, axis=-1, keepdims=True)


def each(body, low, high):
    def step(i, carry):
        body(i)
        return carry

    lax.fori_loop(low, high, step, 0)


def greet_chips():
    barrier = pltpu.get_barrier_semaphore()
    each(
        lambda s: pl.semaphore_signal(
            barrier, inc=1, device_id=device_at(s, 1), device_id_type=MESH
        ),
        1, CHIPS,
    )
    return lambda: pl.semaphore_wait(barrier, CHIPS - 1)


def tile(i):
    return pl.ds(pl.multiple_of(i * WIDE, WIDE), WIDE)


def head_cols(h):
    return pl.ds(pl.multiple_of(h * HEAD_SIZE, HEAD_SIZE), HEAD_SIZE)


def forward_kernel(
    kv, heads, tokens_ref, gain_in_ref, gain_moe_ref, cos_ref, sin_ref, gq_ref, gk_ref, bias_ref,
    select_ref, w_qkv_ref, w_out_ref, rows_ref,
    a_ref, qkv_ref, kv_ref, o_ref, middle_ref, send_ref, came_ref,
    w_qkv, w_out, held, part_sum, swap_give, swap_take, send_rows,
    send_sem, recv_sem, load_sem, swap_sem, out_sem, go_sem, come_sem,
):
    c, tp = lax.axis_index("ctx"), lax.axis_index("tp")
    micro, rows = held.shape[0], 2 * BLOCK
    q_cols = kv * heads * HEAD_SIZE
    width = w_out.shape[0]
    entered = greet_chips()
    loads = [
        pltpu.make_async_copy(w_qkv_ref, w_qkv, load_sem.at[0]),
        pltpu.make_async_copy(w_out_ref.at[:, pl.ds(0, w_out.shape[1])], w_out, load_sem.at[1]),
    ]
    for copy in loads:
        copy.start()

    def go(s):
        return remote(
            rows_ref.at[s], came_ref.at[s], go_sem.at[s], come_sem.at[s], device_at(s, 1)
        )

    def rows_out(quarter):
        each(lambda s: go(s).start(), max(quarter * GROUP, 1), (quarter + 1) * GROUP)

    stay = pltpu.make_async_copy(rows_ref.at[0], came_ref.at[0], come_sem.at[0])
    stay.start()
    cosine, sine, gq, gk = cos_ref[...], sin_ref[...], gq_ref[...], gk_ref[...]
    mine = pl.ds(pl.multiple_of(c * BLOCK, BLOCK), BLOCK)
    earlier, own = pl.ds(CTX * BLOCK, BLOCK), pl.ds((CTX + 1) * BLOCK, BLOCK)

    def block(i):
        return pl.ds(pl.multiple_of(i * BLOCK, BLOCK), BLOCK)

    def norm_in(i):
        u = tokens_ref[block(i), :].astype(F32)
        scaling = lax.rsqrt(jnp.mean(u * u, axis=-1, keepdims=True) + EPS)
        a_ref[block(i), :] = (u * scaling * gain_in_ref[...]).astype(BF16)

    each(norm_in, 0, micro * 2)
    loads[0].wait()

    def project(i):
        qkv_ref[:, tile(i)] = dot(a_ref[...], w_qkv[:, tile(i)], ((1,), (0,)))

    each(project, q_cols // WIDE, w_qkv.shape[1] // WIDE)
    entered()
    copies = []
    for m in range(micro):
        span = slice(m * rows, (m + 1) * rows)
        for h in range(2 * kv):
            cols = slice(h * HEAD_SIZE, (h + 1) * HEAD_SIZE)
            u = qkv_ref[span, q_cols + h * HEAD_SIZE : q_cols + (h + 1) * HEAD_SIZE]
            low = rotated(u, gk, cosine, sine)[0] if h < kv else u.astype(BF16)
            held[m, mine, cols] = low[:BLOCK]
            held[m, own, cols] = low[BLOCK:]
        for step in range(1, CTX):
            part = held.at[m, mine]
            copies.append(
                remote(part, part, send_sem.at[step, m], recv_sem.at[step, m], ctx_peer(step))
            )
        copies.append(
            remote(
                held.at[m, own], held.at[m, earlier], send_sem.at[0, m], recv_sem.at[0, m], beside()
            )
        )
        for copy in copies[-CTX:]:
            copy.start()
    rows_out(0)
    each(project, 0, q_cols // WIDE)

    def group(m, h, carry):
        span = slice(m * rows, (m + 1) * rows)
        k, v = held[m, :, head_cols(h)], held[m, :, head_cols(kv + h)]
        for e in range(heads):
            cols = head_cols(h * heads + e)
            q_low = rotated(qkv_ref[span, cols], gq, cosine, sine)[0]
            p = softmax_parts(q_low, k, bias_ref[...]).astype(BF16)
            o_ref[span, cols] = dot(p, v, ((1,), (0,))).astype(BF16)
        return carry

    def arrived(m):
        for step in range(1, CTX):
            source = lax.rem(c + CTX - step, CTX)
            part = held.at[m, pl.ds(pl.multiple_of(source * BLOCK, BLOCK), BLOCK)]
            remote(
                part, part, send_sem.at[step, m], recv_sem.at[step, m], ctx_peer(step)
            ).wait_recv()
        copies[(m + 1) * CTX - 1].wait_recv()

    for m in range(micro):
        arrived(m)
        if m == micro - 1:
            for quarter in range(1, CHIPS // GROUP):
                rows_out(quarter)
        lax.fori_loop(0, kv, functools.partial(group, m), 0)
        kv_ref[m] = held[m]
    loads[1].wait()

    def join(i):
        part_sum[:, tile(i)] = dot(o_ref[...], w_out[tile(i), :], ((1,), (1,)))

    each(join, 0, width // WIDE)
    for m in range(micro):
        away = pl.ds(pl.multiple_of(m * rows + tp * BLOCK, BLOCK), BLOCK)
        swap_give[m * BLOCK : (m + 1) * BLOCK, :] = part_sum[away, :].astype(BF16)
    swap = remote(swap_give, swap_take, swap_sem.at[0], swap_sem.at[1], {"tp": 1 - tp})
    swap.start()
    swap.wait()
    for m in range(micro):
        kept = pl.ds(pl.multiple_of(m * rows + (1 - tp) * BLOCK, BLOCK), BLOCK)
        span = slice(m * BLOCK, (m + 1) * BLOCK)
        total = part_sum[kept, :] + swap_take[span, :].astype(F32)
        u = tokens_ref[kept, :].astype(F32) + total
        middle_ref[span, :] = u
        scaling = lax.rsqrt(jnp.mean(u * u, axis=-1, keepdims=True) + EPS)
        swap_give[span, :] = (u * scaling * gain_moe_ref[...]).astype(BF16)

    def pick(i):
        value = dot(select_ref[:, tile(i)], swap_give[...], ((0,), (0,)))
        send_rows[tile(i), :] = value.astype(BF16)

    each(pick, 0, send_rows.shape[0] // WIDE)
    out = pltpu.make_async_copy(send_rows, send_ref, out_sem)
    out.start()
    out.wait()
    stay.wait()
    for copy in copies:
        copy.wait_send()
    each(lambda s: go(s).wait(), 1, CHIPS)


def backward_kernel(
    kv, heads, qkv_ref, cos_ref, sin_ref, gq_ref, gk_ref, bias_ref, kv_ref, dattn_ref, o_ref, a_ref,
    w_out_ref, w_qkv_ref, eo_ref,
    given_grad_ref, gains_ref, grad_qkv_ref, grad_out_ref, eo_back_ref,
    w_out, w_qkv, do_ref, dqkv_ref, part_sum, wide_tile, tall_tile, grads, given, given_side,
    p_all, ds_all, q_all, do_all, swap_give, swap_take,
    send_sem, recv_sem, load_sem, tile_sem, swap_sem, eo_send, eo_recv,
):
    c, tp = lax.axis_index("ctx"), lax.axis_index("tp")
    width = w_out.shape[0]

    entered = greet_chips()
    loads = [
        pltpu.make_async_copy(w_out_ref.at[:, pl.ds(0, w_out.shape[1])], w_out, load_sem.at[0]),
        pltpu.make_async_copy(w_qkv_ref, w_qkv, load_sem.at[1]),
    ]
    for copy in loads:
        copy.start()
    entered()

    def output(s):
        return remote(
            eo_ref.at[s], eo_back_ref.at[s], eo_send.at[s], eo_recv.at[s], device_at(s, -1)
        )

    def outputs(quarter):
        each(lambda s: output(s).start(), max(quarter * GROUP, 1), (quarter + 1) * GROUP)

    stay = pltpu.make_async_copy(eo_ref.at[0], eo_back_ref.at[0], eo_recv.at[0])
    stay.start()
    outputs(0)
    micro, rows = grads.shape[0], 2 * BLOCK
    q_cols = kv * heads * HEAD_SIZE
    scale = HEAD_SIZE ** -0.5
    cosine, sine, gq, gk = cos_ref[...], sin_ref[...], gq_ref[...], gk_ref[...]
    mine = pl.ds(pl.multiple_of(c * BLOCK, BLOCK), BLOCK)
    earlier, own = pl.ds(CTX * BLOCK, BLOCK), pl.ds((CTX + 1) * BLOCK, BLOCK)

    loads[0].wait()

    def outputs_back(i):
        do_ref[:, tile(i)] = dot(dattn_ref[...], w_out[:, tile(i)], ((1,), (0,))).astype(BF16)

    each(outputs_back, 0, w_out.shape[1] // WIDE)

    def keys_back(m, h, carry):
        span = slice(m * rows, (m + 1) * rows)
        k, v = kv_ref[m, :, head_cols(h)], kv_ref[m, :, head_cols(kv + h)]
        for e in range(heads):
            cols = head_cols(h * heads + e)
            stack = slice(e * rows, (e + 1) * rows)
            q_low = rotated(qkv_ref[span, cols], gq, cosine, sine)[0]
            q_all[stack, :] = q_low
            p = softmax_parts(q_low, k, bias_ref[...])
            p_all[stack, :] = p.astype(BF16)
            do = do_ref[span, cols]
            do_all[stack, :] = do
            dp = dot(do, v, ((1,), (1,)))
            ds = (p * (dp - jnp.sum(dp * p, axis=-1, keepdims=True))).astype(BF16)
            ds_all[m * kv + h, stack, :] = ds
        grads[m, :, head_cols(kv + h)] = dot(p_all[...], do_all[...], ((0,), (0,))).astype(BF16)
        d_k = dot(ds_all[m * kv + h], q_all[...], ((0,), (0,))) * scale
        grads[m, :, head_cols(h)] = d_k.astype(BF16)
        return carry

    def queries_back(m, h, total):
        span = slice(m * rows, (m + 1) * rows)
        k = kv_ref[m, :, head_cols(h)]
        for e in range(heads):
            cols = head_cols(h * heads + e)
            ds = ds_all[m * kv + h, e * rows : (e + 1) * rows, :]
            dqr = (dot(ds, k, ((1,), (0,))) * scale).astype(BF16).astype(F32)
            u = qkv_ref[span, cols]
            scaling = lax.rsqrt(jnp.mean(u * u, axis=-1, keepdims=True) + EPS)
            dq, part = rotated_back(dqr, u * scaling, scaling, gq, cosine, sine)
            dqkv_ref[span, cols] = dq.astype(BF16)
            total = total + part
        return total

    copies = []
    for m in range(micro):
        lax.fori_loop(0, kv, functools.partial(keys_back, m), 0)
        for step in range(1, CTX):
            peer = lax.rem(c + step, CTX)
            part = grads.at[m, pl.ds(pl.multiple_of(peer * BLOCK, BLOCK), BLOCK)]
            copies.append(
                remote(
                    part, given.at[step - 1, m], send_sem.at[step, m], recv_sem.at[step, m],
                    ctx_peer(step),
                )
            )
        copies.append(
            remote(
                grads.at[m, earlier], given_side.at[m], send_sem.at[0, m], recv_sem.at[0, m],
                beside(),
            )
        )
        for copy in copies[-CTX:]:
            copy.start()
        outputs(1 + m)
    total = jnp.zeros((1, HEAD_SIZE), F32)
    for m in range(micro):
        total = lax.fori_loop(0, kv, functools.partial(queries_back, m), total)
    outputs(3)

    def tiles_out(buffer, left, right, out_ref, sems):
        def copy_out(i):
            slot = lax.rem(i, 2)
            return pltpu.make_async_copy(buffer.at[slot], out_ref.at[tile(i)], sems.at[i])

        def step(i):
            @pl.when(i >= 2)
            def _():
                copy_out(i - 2).wait()

            value = dot(left[:, tile(i)], right[...], ((0,), (0,)))
            buffer[lax.rem(i, 2)] = value.astype(BF16)
            copy_out(i).start()

        count = width // WIDE
        each(step, 0, count)
        return lambda: each(lambda i: copy_out(i).wait(), count - 2, count)

    end_out = tiles_out(tall_tile, dattn_ref, o_ref, grad_out_ref, tile_sem.at[0])
    loads[1].wait()

    def queries_in(i):
        part_sum[:, tile(i)] = dot(dqkv_ref[:, :q_cols], w_qkv[tile(i), :q_cols], ((1,), (1,)))

    each(queries_in, 0, width // WIDE)
    k_total = jnp.zeros((1, HEAD_SIZE), F32)
    for m in range(micro):
        for copy in copies[m * CTX : (m + 1) * CTX]:
            copy.wait_recv()
        for h in range(2 * kv):
            cols = slice(h * HEAD_SIZE, (h + 1) * HEAD_SIZE)
            at = slice(q_cols + h * HEAD_SIZE, q_cols + (h + 1) * HEAD_SIZE)
            prompt = grads[m, mine, cols].astype(F32)
            for step in range(CTX - 1):
                prompt = prompt + given[step, m, :, cols].astype(F32)
            cont = grads[m, own, cols].astype(F32) + given_side[m, :, cols].astype(F32)
            e = jnp.concatenate([prompt, cont], axis=0).astype(BF16)
            span = slice(m * rows, (m + 1) * rows)
            if h < kv:
                _, normed, scaling = rotated(qkv_ref[span, at], gk, cosine, sine)
                d, part = rotated_back(e.astype(F32), normed, scaling, gk, cosine, sine)
                k_total = k_total + part
                dqkv_ref[span, at] = d.astype(BF16)
            else:
                dqkv_ref[span, at] = e
    gains_ref[0:1, :] = total
    gains_ref[1:2, :] = k_total

    def keys_in(i):
        part_sum[:, tile(i)] += dot(dqkv_ref[:, q_cols:], w_qkv[tile(i), q_cols:], ((1,), (1,)))

    each(keys_in, 0, width // WIDE)
    for m in range(micro):
        away = pl.ds(pl.multiple_of(m * rows + tp * BLOCK, BLOCK), BLOCK)
        swap_give[m * BLOCK : (m + 1) * BLOCK, :] = part_sum[away, :].astype(BF16)
    swap = remote(swap_give, swap_take, swap_sem.at[0], swap_sem.at[1], {"tp": 1 - tp})
    swap.start()
    end_qkv = tiles_out(wide_tile, a_ref, dqkv_ref, grad_qkv_ref, tile_sem.at[1])
    swap.wait()
    for m in range(micro):
        kept = pl.ds(pl.multiple_of(m * rows + (1 - tp) * BLOCK, BLOCK), BLOCK)
        span = slice(m * BLOCK, (m + 1) * BLOCK)
        given_grad_ref[span, :] = part_sum[kept, :] + swap_take[span, :].astype(F32)
    for copy in copies:
        copy.wait_send()
    end_out()
    end_qkv()
    stay.wait()
    each(lambda s: output(s).wait(), 1, CHIPS)


def forward(tokens, gain_in, gain_moe, heads_in, select, w_qkv, w_out, moe_rows, kv):
    total, width = tokens.shape
    cols = w_qkv.shape[1]
    heads = cols // HEAD_SIZE // kv - 2
    q_cols, kv_cols = kv * heads * HEAD_SIZE, 2 * kv * HEAD_SIZE
    rows, keys = heads_in[-1].shape
    micro = total // rows
    vmem, any_space = (pl.BlockSpec(memory_space=space) for space in (pltpu.VMEM, pl.ANY))
    dma = pltpu.SemaphoreType.DMA
    return pl.pallas_call(
        functools.partial(forward_kernel, kv, heads),
        in_specs=[vmem] * 9 + [any_space] * 3,
        out_specs=[vmem] * 5 + [any_space] * 2,
        out_shape=[
            jax.ShapeDtypeStruct((total, width), BF16),
            jax.ShapeDtypeStruct((total, cols), F32),
            jax.ShapeDtypeStruct((micro, keys, kv_cols), BF16),
            jax.ShapeDtypeStruct((total, q_cols), BF16),
            jax.ShapeDtypeStruct((micro * BLOCK, width), F32),
            jax.ShapeDtypeStruct((select.shape[1], width), BF16),
            jax.ShapeDtypeStruct(moe_rows.shape, BF16),
        ],
        scratch_shapes=[
            pltpu.VMEM((width, cols), BF16),
            pltpu.VMEM((width, q_cols), BF16),
            pltpu.VMEM((micro, keys, kv_cols), BF16),
            pltpu.VMEM((total, width), F32),
            pltpu.VMEM((micro * BLOCK, width), BF16),
            pltpu.VMEM((micro * BLOCK, width), BF16),
            pltpu.VMEM((select.shape[1], width), BF16),
            dma((CTX, micro)), dma((CTX, micro)), dma((2,)), dma((2,)), dma,
            dma((CHIPS,)), dma((CHIPS,)),
        ],
        compiler_params=pltpu.CompilerParams(
            collective_id=2, has_side_effects=True, vmem_limit_bytes=56 * 1024 * 1024
        ),
        cost_estimate=pl.CostEstimate(flops=0, bytes_accessed=250_000_000, transcendentals=0),
        name="attention_forward",
    )(tokens, gain_in, gain_moe, *heads_in, select, w_qkv, w_out, moe_rows)


def backward(qkv, heads_in, kv_all, d_attn, o, a, w_out, w_qkv, eo, kv):
    heads = qkv.shape[1] // HEAD_SIZE // kv - 2
    bias = heads_in[-1]
    rows, keys = bias.shape
    micro, _, kv_cols = kv_all.shape
    width, cols = w_qkv.shape
    total, q_cols = qkv.shape[0], kv * heads * HEAD_SIZE
    vmem, any_space = (pl.BlockSpec(memory_space=space) for space in (pltpu.VMEM, pl.ANY))
    dma = pltpu.SemaphoreType.DMA
    return pl.pallas_call(
        functools.partial(backward_kernel, kv, heads),
        in_specs=[vmem] * 10 + [any_space] * 3,
        out_specs=[vmem] * 2 + [any_space] * 3,
        out_shape=[
            jax.ShapeDtypeStruct((micro * BLOCK, width), F32),
            jax.ShapeDtypeStruct((2, HEAD_SIZE), F32),
            jax.ShapeDtypeStruct((width, cols), BF16),
            jax.ShapeDtypeStruct((width, q_cols), BF16),
            jax.ShapeDtypeStruct(eo.shape, BF16),
        ],
        scratch_shapes=[
            pltpu.VMEM((width, q_cols), BF16),
            pltpu.VMEM((width, cols), BF16),
            pltpu.VMEM((total, q_cols), BF16),
            pltpu.VMEM((total, cols), BF16),
            pltpu.VMEM((total, width), F32),
            pltpu.VMEM((2, WIDE, cols), BF16),
            pltpu.VMEM((2, WIDE, q_cols), BF16),
            pltpu.VMEM((micro, keys, kv_cols), BF16),
            pltpu.VMEM((CTX - 1, micro, BLOCK, kv_cols), BF16),
            pltpu.VMEM((micro, BLOCK, kv_cols), BF16),
            pltpu.VMEM((heads * rows, keys), BF16),
            pltpu.VMEM((micro * kv, heads * rows, keys), BF16),
            pltpu.VMEM((heads * rows, HEAD_SIZE), BF16),
            pltpu.VMEM((heads * rows, HEAD_SIZE), BF16),
            pltpu.VMEM((micro * BLOCK, width), BF16),
            pltpu.VMEM((micro * BLOCK, width), BF16),
            dma((CTX, micro)), dma((CTX, micro)), dma((2,)), dma((2, width // WIDE)), dma((2,)),
            dma((CHIPS,)), dma((CHIPS,)),
        ],
        compiler_params=pltpu.CompilerParams(
            collective_id=3, has_side_effects=True, vmem_limit_bytes=56 * 1024 * 1024
        ),
        cost_estimate=pl.CostEstimate(flops=0, bytes_accessed=250_000_000, transcendentals=0),
        name="attention_backward",
    )(qkv, *heads_in, kv_all, d_attn, o, a, w_out, w_qkv, eo)


def normalize_back(rows, scaling, gain, upstream):
    normed = rows * scaling
    gain_grad = jnp.sum((upstream * normed).reshape(-1, rows.shape[-1]), axis=0)
    scaled = upstream * gain
    inner = jnp.mean(scaled * normed, axis=-1, keepdims=True)
    return scaling * (scaled - normed * inner), gain_grad


def swap_tp(value):
    return lax.ppermute(value, "tp", [(0, 1), (1, 0)])


def local(
    x_prompt, x_cont, cot_prompt, cot_cont, ids_prompt, ids_cont, gates_prompt, gates_cont,
    norm_gain, query_weight, key_matrix, value_matrix, out_weight, query_gain, key_gain, moe_gain,
    expert_gate, expert_up, expert_down,
):
    micro = x_prompt.shape[0]
    prompt_rows, cont_rows, width = x_prompt.shape[2], x_cont.shape[2], x_prompt.shape[3]
    block = cont_rows
    rows = 2 * block
    s = lax.axis_index("ctx")
    ctx = lax.axis_size("ctx")
    first = lax.axis_index("tp") == 0
    peers = lax.axis_size(ALL)
    q_cols, kv_cols = query_weight.shape[1], key_matrix.shape[1]
    kv = kv_cols // HEAD_SIZE
    qkv_cols = q_cols + 2 * kv_cols
    shard_rows = query_weight.shape[0]
    hidden = expert_gate.shape[2]
    slots = cont_rows * TOPK // peers

    def pad(v):
        return jnp.pad(v[:, 0], ((0, 0), (0, block - prompt_rows), (0, 0)))

    x_first, x_second = pad(x_prompt), x_cont[:, 0]
    own_tokens = jnp.where(first, x_second, x_first).astype(F32)
    own_cot = jnp.where(first, cot_cont[:, 0], pad(cot_prompt))
    ids_pad = jnp.pad(
        ids_prompt[:, 0], ((0, 0), (0, block - prompt_rows), (0, 0)), constant_values=-1
    )
    own_ids = jnp.where(first, ids_cont[:, 0], ids_pad)
    own_gates = jnp.where(first, gates_cont[:, 0], pad(gates_prompt))

    y, z, x = chip_at(jnp.arange(peers, dtype=jnp.int32), 1)
    near = (2 * y + x // 2) * ctx + 2 * z + x % 2
    order = jnp.pad(near, (0, HEAD_SIZE - peers), constant_values=-2)[None]

    def lanes(v):
        return jnp.pad(v, [(0, 0)] * (v.ndim - 1) + [(0, HEAD_SIZE - v.shape[-1])])

    extra = jnp.stack([lanes(v) for v in (norm_gain, moe_gain, query_gain, key_gain)])
    extra = jnp.pad(extra, ((0, shard_rows - extra.shape[0]), (0, 0)))
    own_experts = (expert_gate[0], expert_up[0], expert_down[0])
    w_qkv, w_out_extra, far_experts, routing = gather_weights(
        query_weight, key_matrix, value_matrix, out_weight, extra,
        own_ids.reshape(-1, TOPK), own_gates.reshape(-1, TOPK), order,
        own_cot.reshape(-1, width), peers * micro * slots, *own_experts,
    )
    select_near, mixing, spread = routing
    gains = w_out_extra[:, q_cols:].reshape(peers, shard_rows, HEAD_SIZE)[:, :4].astype(F32)
    gain_in, gain_moe = (gains[:, n, :shard_rows].reshape(-1) for n in (0, 1))
    head_rows = query_gain.shape[0]
    gain_query, gain_key = (gains[:, n, :head_rows].reshape(-1) for n in (2, 3))

    offsets = jnp.arange(rows, dtype=jnp.int32)
    is_prompt = offsets < block
    prompt_pos = s * prompt_rows + offsets
    cont_pos = s * cont_rows + offsets - block
    rot_place = jnp.where(is_prompt, prompt_pos, PROMPT + cont_pos % CL).astype(F32)
    steps_freq = jnp.arange(HEAD_SIZE // 2, dtype=F32) * (2.0 / HEAD_SIZE)
    angles = rot_place[:, None] * jnp.power(THETA, -steps_freq)[None, :]
    cosine, sine = jnp.cos(angles), jnp.sin(angles)
    cosine = jnp.concatenate([cosine, cosine], axis=1)
    sine = jnp.concatenate([-sine, sine], axis=1)
    keys = (ctx + 2) * block
    key_index = jnp.arange(keys, dtype=jnp.int32)[None, :]
    key_off = key_index % block
    key_prompt_pos = key_index // block * prompt_rows + key_off
    key_cont = (s - 1) * cont_rows + key_index - ctx * block
    is_cont = jnp.logical_not(is_prompt)[:, None]
    visible = jnp.where(
        key_index < ctx * block,
        jnp.logical_and(
            key_off < prompt_rows,
            jnp.logical_or(is_cont, key_prompt_pos <= prompt_pos[:, None]),
        ),
        jnp.logical_and(
            is_cont,
            jnp.logical_and(
                key_cont // CL == cont_pos[:, None] // CL, key_cont <= cont_pos[:, None]
            ),
        ),
    )
    bias = jnp.where(visible, 0.0, NEG).astype(F32)

    def arranged(own, other):
        return jnp.where(first, other, own), jnp.where(first, own, other)

    heads_in = (cosine, sine, gain_query[None], gain_key[None], bias)
    tokens = jnp.concatenate([x_first, x_second], axis=1).reshape(-1, width)
    slot_shape = (peers, micro * slots, width)
    a, qkv, kv_all, o, middle, send, d_eo_rows = forward(
        tokens, gain_in[None], gain_moe[None], heads_in, select_near, w_qkv, w_out_extra,
        spread.reshape(slot_shape), kv,
    )
    middle = middle.reshape(own_tokens.shape)
    b_scale = lax.rsqrt(jnp.mean(middle * middle, axis=-1, keepdims=True) + EPS)

    back, eo, wide_here, tall_here = moe(
        send.reshape(slot_shape), d_eo_rows, own_experts, far_experts
    )
    d_b = dot(select_near, back.reshape(-1, width), ((1,), (0,))).reshape(middle.shape)
    middle_from, moe_total = normalize_back(middle, b_scale, gain_moe, d_b)
    d_h = own_cot.astype(F32) + middle_from
    d_h_low = d_h.astype(BF16)
    d_attn = jnp.concatenate(arranged(d_h_low, swap_tp(d_h_low)), axis=1).reshape(-1, width)

    input_grad, head_totals, grad_qkv, grad_out, eo_back = backward(
        qkv, heads_in, kv_all, d_attn, o, a, w_out_extra, w_qkv, eo, kv
    )
    moe_out = dot(mixing, eo_back.reshape(-1, width), ((1,), (0,)))
    moe_out = (moe_out[: micro * block] + moe_out[micro * block :]).reshape(middle.shape)
    y_own = (middle + moe_out).astype(BF16)
    scale_in = lax.rsqrt(jnp.mean(own_tokens * own_tokens, axis=-1, keepdims=True) + EPS)
    token_from, norm_total = normalize_back(
        own_tokens, scale_in, gain_in, input_grad.reshape(own_tokens.shape)
    )
    x_own = (d_h + token_from).astype(BF16)

    extra_grads = jnp.stack(
        [
            lanes(v.reshape(peers, -1))
            for v in (norm_total, moe_total, head_totals[0], head_totals[1])
        ],
        axis=1,
    )
    extra_grads = jnp.pad(extra_grads, ((0, 0), (0, shard_rows - extra_grads.shape[1]), (0, 0)))
    extra_grads = extra_grads.reshape(-1, HEAD_SIZE).astype(BF16)
    share, share_out, wide_there, tall_there, y_other, x_other = scatter_grads(
        grad_qkv, grad_out, extra_grads, wide_here, tall_here, y_own, x_own
    )
    out_first, out_second = arranged(y_own, y_other)
    grad_first, grad_second = arranged(x_own, x_other)
    grad_wide = jnp.where(native(), wide_here, wide_there).astype(F32)
    grad_down = jnp.where(native(), tall_here, tall_there).astype(F32)
    gain_share = share_out[:, q_cols:]
    return (
        out_first[:, None, :prompt_rows],
        out_second[:, None],
        grad_first[:, None, :prompt_rows],
        grad_second[:, None],
        gain_share[0, :shard_rows],
        share[:, :q_cols],
        share[:, q_cols : q_cols + kv_cols],
        share[:, q_cols + kv_cols : qkv_cols],
        share_out[:, :q_cols],
        gain_share[2, :head_rows],
        gain_share[3, :head_rows],
        gain_share[1, :shard_rows],
        grad_wide[None, :, :hidden],
        grad_wide[None, :, hidden:],
        grad_down[None],
    )


def solution(mesh):
    rows = P(None, "fsdp", "ctx", None)
    vector = P(("fsdp", "ctx"))
    matrix = P(("fsdp", "ctx"), "tp")
    wide = P(("fsdp", "ctx"), None, "tp")
    tall = P(("fsdp", "ctx"), "tp", None)
    in_specs = (rows,) * 8 + (vector,) + (matrix,) * 4 + (vector,) * 3 + (wide, wide, tall)
    out_specs = (rows,) * 4 + (vector,) + (matrix,) * 4 + (vector,) * 3 + (wide, wide, tall)
    return jax.shard_map(local, mesh=mesh, in_specs=in_specs, out_specs=out_specs, check_vma=False)
```

```python
import functools

import jax
import jax.numpy as jnp
from jax import lax
from jax.experimental import pallas as pl
from jax.experimental.pallas import tpu as pltpu
from jax.sharding import PartitionSpec as P

HEAD_SIZE = 128
TOPK = 8
PROMPT = 448
CL = 128
EPS = 1e-06
THETA = 1000000.0
NEG = -1e30
F32 = jnp.float32
BF16 = jnp.bfloat16
ALL = ("fsdp", "ctx")
MESH = pl.DeviceIdType.MESH
RING = 4
VMEM_LIMIT = 48 * 1024 * 1024


def dot(a, b, dims):
    return lax.dot_general(a, b, (dims, ((), ())), preferred_element_type=F32)


def remote(src, dst, send_sem, recv_sem, where):
    return pltpu.make_async_remote_copy(
        src_ref=src, dst_ref=dst, send_sem=send_sem, recv_sem=recv_sem, device_id=where,
        device_id_type=MESH,
    )


def place():
    f, c = lax.axis_index("fsdp"), lax.axis_index("ctx")
    return f // 2, f % 2, c // 2, c % 2


def device(y, core, z, x):
    return {"fsdp": y * 2 + core, "ctx": z * 2 + x}


def greet(partners):
    barrier = pltpu.get_barrier_semaphore()
    for partner in partners:
        pl.semaphore_signal(barrier, inc=1, device_id=partner, device_id_type=MESH)
    pl.semaphore_wait(barrier, len(partners))


def neighbours():
    y, core, z, x = place()
    up, down = (lambda v: lax.rem(v + 1, RING)), (lambda v: lax.rem(v + RING - 1, RING))
    return [
        device(y, core, z, 1 - x),
        device(y, 1 - core, z, x),
        device(up(y), core, z, x),
        device(down(y), core, z, x),
        device(y, core, up(z), x),
        device(y, core, down(z), x),
    ]


def other_tp():
    return {"tp": 1 - lax.axis_index("tp")}


def opposite():
    f = lax.axis_index("fsdp")
    return {"fsdp": f + 1 - 2 * (f % 2), "tp": 1 - lax.axis_index("tp")}


def native():
    return lax.axis_index("fsdp") % 2 == lax.axis_index("tp")


def swap_opposite(src, dst, send_sem, recv_sem):
    return pltpu.make_async_remote_copy(
        src_ref=src, dst_ref=dst, send_sem=send_sem, recv_sem=recv_sem, device_id=opposite(),
        device_id_type=MESH,
    )


def route(ids, gates, experts, size, select_ref, mix_ref):
    tokens, slots = ids.shape[0], mix_ref.shape[1]
    block, places = tokens // 2, size // 2
    chosen = jnp.zeros((tokens, experts.shape[1]), F32)
    weight = jnp.zeros((tokens, experts.shape[1]), F32)
    for k in range(ids.shape[1]):
        same = ids[:, k : k + 1] == experts
        chosen = chosen + jnp.where(same, 1.0, 0.0)
        weight = weight + jnp.where(same, gates[:, k : k + 1], 0.0)
    t = lax.broadcasted_iota(jnp.int32, (tokens, tokens), 0)
    u = lax.broadcasted_iota(jnp.int32, (tokens, tokens), 1)
    earlier = jnp.logical_and(u < t, (u >= block) == (t >= block))
    rank = dot(jnp.where(earlier, 1.0, 0.0).astype(BF16), chosen.astype(BF16), ((1,), (0,)))
    rank = jnp.where(chosen > 0.0, rank, -1.0).astype(BF16)
    e = lax.broadcasted_iota(jnp.int32, (experts.shape[1], slots), 0)
    j = lax.broadcasted_iota(jnp.int32, (experts.shape[1], slots), 1)
    spread = jnp.where(jnp.logical_and(j >= e * size, j < (e + 1) * size), 1.0, 0.0).astype(BF16)
    j = lax.broadcasted_iota(jnp.int32, (tokens, slots), 1)
    later = lax.broadcasted_iota(jnp.int32, (tokens, slots), 0) >= block
    place = (j & (places - 1)).astype(F32)
    mine = ((j & places) != 0) == later
    there = jnp.logical_and(dot(rank, spread, ((1,), (0,))) == place, mine)
    select_ref[...] = jnp.where(there, 1.0, 0.0).astype(BF16)
    high = weight.astype(BF16)
    low = (weight - high.astype(F32)).astype(BF16)
    mix_ref[0:tokens, :] = jnp.where(there, dot(high, spread, ((1,), (0,))), 0.0).astype(BF16)
    mix_ref[tokens:, :] = jnp.where(there, dot(low, spread, ((1,), (0,))), 0.0).astype(BF16)


def gather_kernel(
    query_ref, key_ref, value_ref, out_ref, extra_ref, ids_ref, gates_ref, experts_ref, cot_ref,
    gate_ref, up_ref, down_ref,
    a_all, b_all, gate_all, up_all, down_all, near_out, mix_out, rows_ref,
    a_own, b_own, ids_own, gates_own, cot_own, near_ref, mix_ref, rows, rows_sem, small_sem, local_sem, send_sem, recv_sem, away_sem, home_sem, give_sem, take_sem,
):
    y, core, z, x = place()
    smalls = [
        pltpu.make_async_copy(src, dst, small_sem.at[n])
        for n, (src, dst) in enumerate(
            ((ids_ref, ids_own), (gates_ref, gates_own), (cot_ref, cot_own),
             (near_ref, near_out), (mix_ref, mix_out))
        )
    ]
    for copy in smalls[:3]:
        copy.start()
    for own, refs in ((a_own, (query_ref, key_ref, value_ref)), (b_own, (out_ref, extra_ref))):
        at = 0
        for ref in refs:
            own[:, at : at + ref.shape[1]] = ref[...]
            at += ref.shape[1]
    greet(neighbours() + [opposite()])
    shards = ((gate_ref, gate_all), (up_ref, up_all), (down_ref, down_all))
    moved = [
        swap_opposite(p, q, give_sem.at[n], take_sem.at[n]) for n, (p, q) in enumerate(shards)
    ]
    refs, own = (a_all, b_all), (a_own, b_own)
    started = []
    count = [0, 0]

    def chunk(n, i, j):
        return refs[n].at[j, core, i] if n == 0 else refs[n].at[i, core, j]

    def to(n, first, second):
        return device(second, core, first, x) if n == 0 else device(first, core, second, x)

    def send(n, ref, where, slot):
        copy = pltpu.make_async_remote_copy(
            src_ref=ref, dst_ref=ref, send_sem=send_sem.at[n, slot], recv_sem=recv_sem.at[n, slot],
            device_id=where, device_id_type=MESH,
        )
        copy.start()
        started.append(copy)

    def arrived(n, ref, slot):
        pltpu.make_async_remote_copy(
            src_ref=ref, dst_ref=ref, send_sem=send_sem.at[n, slot], recv_sem=recv_sem.at[n, slot],
            device_id=device(y, core, z, x), device_id_type=MESH,
        ).wait_recv()

    homes = []

    def across(n, i, j):
        slot = count[n]
        count[n] += 1
        ref = chunk(n, i, j)
        copy = pltpu.make_async_remote_copy(
            src_ref=ref, dst_ref=ref, send_sem=away_sem.at[n, slot], recv_sem=home_sem.at[n, slot],
            device_id=device(y, 1 - core, z, x), device_id_type=MESH,
        )
        copy.start()
        homes.append(copy)

    def second(n, i, j, k):
        base = 5 + 4 * k
        send(n, chunk(n, i, j), to(n, me[n][0], up(j)), base)
        send(n, chunk(n, i, j), to(n, me[n][0], down(j)), base + 1)
        across(n, i, j)

    up, down = (lambda v: lax.rem(v + 1, RING)), (lambda v: lax.rem(v + RING - 1, RING))
    me = ((z, y), (y, z))
    locals_ = []
    for n in (0, 1):
        i, j = me[n]
        keep = pltpu.make_async_copy(own[n], chunk(n, i, j).at[x], local_sem.at[n])
        keep.start()
        locals_.append(keep)
        copy = pltpu.make_async_remote_copy(
            src_ref=own[n], dst_ref=chunk(n, i, j).at[x], send_sem=send_sem.at[n, 0],
            recv_sem=recv_sem.at[n, 0], device_id=device(y, core, z, 1 - x), device_id_type=MESH,
        )
        copy.start()
        started.append(copy)
    size = rows.shape[0] // (RING * RING * RING)
    for copy in smalls[:3]:
        copy.wait()
    ids, gates = ids_own[...], gates_own[...]
    route(ids, gates, experts_ref[...], size, near_ref, mix_ref)
    for copy in smalls[3:]:
        copy.start()
    for n in (0, 1):
        i, j = me[n]
        locals_[n].wait()
        arrived(n, chunk(n, i, j).at[1 - x], 0)
        send(n, chunk(n, i, j), to(n, up(i), j), 1)
        send(n, chunk(n, i, j), to(n, down(i), j), 2)
    for n in (0, 1):
        i, j = me[n]
        second(n, i, j, 0)

    @pl.when(jnp.logical_not(native()))
    def _():
        for copy in moved:
            copy.start()

    part, tokens = 256, cot_ref.shape[0]
    for at in range(0, rows.shape[0], part):
        lanes = slice(at, at + part)
        total = dot(mix_ref[0:tokens, lanes], cot_own[...], ((0,), (0,)))
        total = total + dot(mix_ref[tokens:, lanes], cot_own[...], ((0,), (0,)))
        rows[lanes, :] = total.astype(BF16)
    keep_rows = pltpu.make_async_copy(rows, rows_ref, rows_sem)
    keep_rows.start()
    for n in (0, 1):
        i, j = me[n]
        arrived(n, chunk(n, down(i), j), 1)
        send(n, chunk(n, down(i), j).at[0], to(n, up(i), j), 3)
        second(n, down(i), j, 1)
    for n in (0, 1):
        i, j = me[n]
        arrived(n, chunk(n, up(i), j), 2)
        send(n, chunk(n, up(i), j).at[1], to(n, down(i), j), 4)
        second(n, up(i), j, 2)
    for n in (0, 1):
        i, j = me[n]
        far = lax.rem(i + 2, RING)
        arrived(n, chunk(n, far, j).at[0], 3)
        arrived(n, chunk(n, far, j).at[1], 4)
        second(n, far, j, 3)
    for k in range(4):
        for n in (0, 1):
            i, j = me[n]
            it = (i, down(i), up(i), lax.rem(i + 2, RING))[k]
            base = 5 + 4 * k
            arrived(n, chunk(n, it, down(j)), base)
            send(n, chunk(n, it, down(j)).at[0], to(n, i, up(j)), base + 2)
            across(n, it, down(j))
            arrived(n, chunk(n, it, up(j)), base + 1)
            send(n, chunk(n, it, up(j)).at[1], to(n, i, down(j)), base + 3)
            across(n, it, up(j))
    for k in range(4):
        for n in (0, 1):
            i, j = me[n]
            it = (i, down(i), up(i), lax.rem(i + 2, RING))[k]
            base = 5 + 4 * k
            far = lax.rem(j + 2, RING)
            arrived(n, chunk(n, it, far).at[0], base + 2)
            arrived(n, chunk(n, it, far).at[1], base + 3)
            across(n, it, far)
    keep_rows.wait()
    for copy in smalls[3:]:
        copy.wait()
    for copy in homes:
        copy.wait()
    for copy in started:
        copy.wait_send()

    @pl.when(jnp.logical_not(native()))
    def _():
        for copy in moved:
            copy.wait()


def gather_weights(query, key, value, out, extra, ids, gates, experts, cot, slots, gate, up, down):
    rows = query.shape[0]
    cols = (query.shape[1] + key.shape[1] + value.shape[1], out.shape[1] + extra.shape[1])
    shape = (RING, 2, RING, 2, rows)
    vmem, any_space = (pl.BlockSpec(memory_space=space) for space in (pltpu.VMEM, pl.ANY))
    tokens, width = cot.shape
    routing = [jax.ShapeDtypeStruct((n * tokens, slots), BF16) for n in (1, 2)]
    a_all, b_all, *rest = pl.pallas_call(
        gather_kernel,
        in_specs=[vmem] * 5 + [any_space] * 2 + [vmem] + [any_space] * 4,
        out_specs=[any_space] * 8,
        out_shape=[jax.ShapeDtypeStruct(shape + (c,), query.dtype) for c in cols]
        + [jax.ShapeDtypeStruct(v.shape, v.dtype) for v in (gate, up, down)]
        + routing + [jax.ShapeDtypeStruct((slots, width), BF16)],
        scratch_shapes=[pltpu.VMEM((rows, c), query.dtype) for c in cols] + [
            pltpu.VMEM(ids.shape, ids.dtype),
            pltpu.VMEM(gates.shape, gates.dtype),
            pltpu.VMEM(cot.shape, cot.dtype),
            pltpu.VMEM((tokens, slots), BF16),
            pltpu.VMEM((2 * tokens, slots), BF16),
            pltpu.VMEM((slots, width), BF16),
            pltpu.SemaphoreType.DMA,
            pltpu.SemaphoreType.DMA((5,)),
            pltpu.SemaphoreType.DMA((2,)),
            pltpu.SemaphoreType.DMA((2, 21)),
            pltpu.SemaphoreType.DMA((2, 21)),
            pltpu.SemaphoreType.DMA((2, 16)),
            pltpu.SemaphoreType.DMA((2, 16)),
            pltpu.SemaphoreType.DMA((3,)),
            pltpu.SemaphoreType.DMA((3,)),
        ],
        compiler_params=pltpu.CompilerParams(
            collective_id=0, has_side_effects=True, vmem_limit_bytes=VMEM_LIMIT
        ),
        cost_estimate=pl.CostEstimate(flops=0, bytes_accessed=250_000_000, transcendentals=0),
        name="gather_weights",
    )(query, key, value, out, extra, ids, gates, experts, cot, gate, up, down)
    return a_all.reshape(-1, cols[0]), b_all.reshape(-1, cols[1]), rest[:3], rest[3:]


ORDER = (2, 1, 3, 0)
SLICE = 16


def up(v):
    return lax.rem(v + 1, RING)


def down(v):
    return lax.rem(v + RING - 1, RING)


def add_into(target, *terms):
    flat = [target.shape[0]] if len(target.shape) == 3 else []
    for lead in range(flat[0]) if flat else (None,):
        for start in range(0, target.shape[-2], SLICE):
            at = (pl.ds(start, SLICE), slice(None))
            at = at if lead is None else (lead,) + at
            total = terms[0][at].astype(F32)
            for term in terms[1:]:
                total = total + term[at].astype(F32)
            target[at] = total.astype(target.dtype)


def scatter_kernel(
    a_ref, b_ref, extra_ref, wide_ref, tall_ref, y_ref, x_ref,
    a_out, b_out, wide_out, tall_out, y_out, x_out, a_mine, b_mine, a_theirs, b_theirs, a_one, b_one, a_two, b_two,
    a_first, b_first, a_last, b_last, a_x, b_x, load_sem, send_sem, recv_sem,
    gains_here, gains_there,
    extra_load_sem, extra_send_sem, extra_recv_sem, give_sem, take_sem, gains_sem, token_sem,
):
    y, core, z, x = place()
    greet(neighbours() + [other_tp(), opposite()])
    moved = [
        swap_opposite(wide_ref, wide_out, give_sem.at[0], take_sem.at[0]),
        swap_opposite(tall_ref, tall_out, give_sem.at[1], take_sem.at[1]),
    ]

    tokens = [
        pltpu.make_async_remote_copy(
            src_ref=src, dst_ref=dst, send_sem=token_sem.at[n, 0], recv_sem=token_sem.at[n, 1],
            device_id=other_tp(), device_id_type=MESH,
        )
        for n, (src, dst) in enumerate(((y_ref, y_out), (x_ref, x_out)))
    ]
    for copy in tokens:
        copy.start()

    @pl.when(jnp.logical_not(native()))
    def _():
        for copy in moved:
            copy.start()

    grads, outs = (a_ref, b_ref), (a_out, b_out)
    mine, theirs = (a_mine, b_mine), (a_theirs, b_theirs)
    one, two = (a_one, b_one), (a_two, b_two)
    first, last, side = (a_first, b_first), (a_last, b_last), (a_x, b_x)
    me = ((z, y), (y, z))
    sent = []

    def chunk(n, i, j, c):
        return grads[n].at[j, c, i] if n == 0 else grads[n].at[i, c, j]

    def to(n, i, j):
        return device(j, core, i, x) if n == 0 else device(i, core, j, x)

    def copy_of(n, src, dst, slot, where):
        return pltpu.make_async_remote_copy(
            src_ref=src, dst_ref=dst, send_sem=send_sem.at[n, slot], recv_sem=recv_sem.at[n, slot],
            device_id=where, device_id_type=MESH,
        )

    def send(n, src, dst, slot, where):
        copy = copy_of(n, src, dst, slot, where)
        copy.start()
        sent.append(copy)

    def arrived(n, dst, slot):
        copy_of(n, dst, dst, slot, device(y, core, z, x)).wait_recv()

    cols = b_ref.shape[-1]

    def columns(ref, start, count):
        return ref.at[:, :, pl.ds(start, count)]

    def extra_copy(slot):
        ref = columns(theirs[1].at[slot], cols, extra_ref.shape[-1])
        far = extra_ref.at[lax.rem(y + slot // RING, RING), 1 - core, lax.rem(z + slot % RING, RING)]
        return pltpu.make_async_remote_copy(
            src_ref=far, dst_ref=ref, send_sem=extra_send_sem.at[slot],
            recv_sem=extra_recv_sem.at[slot], device_id=device(y, 1 - core, z, x),
            device_id_type=MESH,
        )

    def extra_load(slot):
        near = extra_ref.at[lax.rem(y + slot // RING, RING), core, lax.rem(z + slot % RING, RING)]
        return pltpu.make_async_copy(
            near, columns(mine[1].at[slot], cols, extra_ref.shape[-1]), extra_load_sem.at[slot]
        )

    def load(n, di, dj):
        i, j = me[n]
        slot = di * RING + dj
        target = mine[n].at[slot] if n == 0 else columns(mine[n].at[slot], 0, cols)
        return pltpu.make_async_copy(
            chunk(n, lax.rem(i + di, RING), lax.rem(j + dj, RING), core), target,
            load_sem.at[n, slot],
        )

    for dj in ORDER:
        for di in ORDER:
            for n in (0, 1):
                i, j = me[n]
                slot = di * RING + dj
                there = chunk(n, lax.rem(i + di, RING), lax.rem(j + dj, RING), 1 - core)
                target = theirs[n].at[slot] if n == 0 else columns(theirs[n].at[slot], 0, cols)
                send(n, there, target, slot, device(y, 1 - core, z, x))
                load(n, di, dj).start()
                if n == 1:
                    extra_copy(slot).start()
                    extra_load(slot).start()

    def ready(n, di, dj):
        slot = di * RING + dj
        load(n, di, dj).wait()
        if n == 0:
            arrived(n, theirs[n].at[slot], slot)
        else:
            arrived(n, columns(theirs[n].at[slot], 0, cols), slot)
            extra_load(slot).wait()
            extra_copy(slot).wait_recv()
        return slot

    for di in ORDER:
        for n in (0, 1):
            i, j = me[n]
            slot = ready(n, di, 2)
            add_into(mine[n].at[slot], mine[n].at[slot], theirs[n].at[slot])
            for half in (0, 1):
                send(
                    n, mine[n].at[slot, half], one[n].at[di, half], 16 + di * 2 + half,
                    to(n, i, up(j) if half == 0 else down(j)),
                )
    for di in ORDER:
        for n in (0, 1):
            i, j = me[n]
            for half, dj in ((0, 1), (1, 3)):
                slot = ready(n, di, dj)
                arrived(n, one[n].at[di, half], 16 + di * 2 + half)
                add_into(
                    mine[n].at[slot, half], mine[n].at[slot, half], theirs[n].at[slot, half],
                    one[n].at[di, half],
                )
                add_into(
                    mine[n].at[slot, 1 - half], mine[n].at[slot, 1 - half],
                    theirs[n].at[slot, 1 - half],
                )
                send(
                    n, mine[n].at[slot], two[n].at[di, half], 24 + di * 2 + half,
                    to(n, i, up(j) if half == 0 else down(j)),
                )
    for di in ORDER:
        for n in (0, 1):
            i, j = me[n]
            slot = ready(n, di, 0)
            for half in (0, 1):
                arrived(n, two[n].at[di, half], 24 + di * 2 + half)
            add_into(
                mine[n].at[slot], mine[n].at[slot], theirs[n].at[slot], two[n].at[di, 0],
                two[n].at[di, 1],
            )
            if di == 2:
                for half in (0, 1):
                    send(
                        n, mine[n].at[slot, half], first[n].at[half], 32 + half,
                        to(n, up(i) if half == 0 else down(i), j),
                    )
            elif di != 0:
                half = 0 if di == 1 else 1
                arrived(n, first[n].at[half], 32 + half)
                add_into(mine[n].at[slot, half], mine[n].at[slot, half], first[n].at[half])
                send(
                    n, mine[n].at[slot], last[n].at[half], 34 + half,
                    to(n, up(i) if half == 0 else down(i), j),
                )
    for n in (0, 1):
        for half in (0, 1):
            arrived(n, last[n].at[half], 34 + half)
        add_into(mine[n].at[0], mine[n].at[0], last[n].at[0], last[n].at[1])
        send(n, mine[n].at[0, 1 - x], side[n], 36, device(y, core, z, 1 - x))
    for n in (0, 1):
        arrived(n, side[n], 36)
        add_into(outs[n], mine[n].at[0, x], side[n])
    gains_here[...] = b_out[:, cols:]
    gains = pltpu.make_async_remote_copy(
        src_ref=gains_here, dst_ref=gains_there, send_sem=gains_sem.at[0],
        recv_sem=gains_sem.at[1], device_id=other_tp(), device_id_type=MESH,
    )
    gains.start()
    for copy in sent:
        copy.wait_send()
    for slot in range(RING * RING):
        extra_copy(slot).wait_send()
    gains.wait()
    for copy in tokens:
        copy.wait()
    b_out[:, cols:] = gains_here[...] + gains_there[...]

    @pl.when(jnp.logical_not(native()))
    def _():
        for copy in moved:
            copy.wait()


def scatter_grads(a, b, extra, wide, tall, y, x):
    peers = RING * RING * 4
    rows = a.shape[0] // peers
    shape = (RING, 2, RING, 2, rows)
    cols = (a.shape[1], b.shape[1] + extra.shape[1])
    buffers = []
    for lead in ((16, 2), (16, 2), (4, 2), (4, 2, 2), (2,), (2, 2), ()):
        buffers += [pltpu.VMEM(lead + (rows, c), a.dtype) for c in cols]
    any_space = pl.BlockSpec(memory_space=pl.ANY)
    return pl.pallas_call(
        scatter_kernel,
        in_specs=[any_space] * 7,
        out_specs=[pl.BlockSpec(memory_space=pltpu.VMEM)] * 2 + [any_space] * 4,
        out_shape=[jax.ShapeDtypeStruct((rows, c), F32) for c in cols]
        + [jax.ShapeDtypeStruct(v.shape, v.dtype) for v in (wide, tall, y, x)],
        scratch_shapes=buffers + [
            pltpu.SemaphoreType.DMA((2, 16)),
            pltpu.SemaphoreType.DMA((2, 37)),
            pltpu.SemaphoreType.DMA((2, 37)),
            pltpu.VMEM((rows, extra.shape[1]), F32),
            pltpu.VMEM((rows, extra.shape[1]), F32),
            pltpu.SemaphoreType.DMA((16,)),
            pltpu.SemaphoreType.DMA((16,)),
            pltpu.SemaphoreType.DMA((16,)),
            pltpu.SemaphoreType.DMA((2,)),
            pltpu.SemaphoreType.DMA((2,)),
            pltpu.SemaphoreType.DMA((2,)),
            pltpu.SemaphoreType.DMA((2, 2)),
        ],
        compiler_params=pltpu.CompilerParams(
            collective_id=1, has_side_effects=True, vmem_limit_bytes=44 * 1024 * 1024
        ),
        cost_estimate=pl.CostEstimate(flops=0, bytes_accessed=250_000_000, transcendentals=0),
        name="scatter_grads",
    )(*(v.reshape(shape + (v.shape[1],)) for v in (a, b, extra)), wide, tall, y, x)


CHIPS = RING * RING * RING
GROUP = 16
MIX = 11
EARLY = 32
TILE = 256


def chip_at(slot, sign):
    f, c, t = lax.axis_index("fsdp"), lax.axis_index("ctx"), lax.axis_index("tp")
    k = lax.rem(slot * MIX, CHIPS) * sign
    turn = 0 if sign > 0 else RING
    far = [lax.div(k, RING * RING), lax.rem(lax.div(k, RING), RING), lax.rem(k, RING)]
    own = [lax.div(f, 2), lax.div(c, 2), t * 2 + lax.rem(c, 2)]
    return [lax.rem(o + d + turn, RING) for o, d in zip(own, far)]


def device_at(slot, sign):
    y, z, x = chip_at(slot, sign)
    core = lax.rem(lax.axis_index("fsdp"), 2)
    return {"fsdp": y * 2 + core, "ctx": z * 2 + lax.rem(x, 2), "tp": lax.div(x, 2)}


def signal_chips(barrier):
    f, c, t = lax.axis_index("fsdp"), lax.axis_index("ctx"), lax.axis_index("tp")
    y, z, x = lax.div(f, 2), lax.div(c, 2), t * 2 + lax.rem(c, 2)
    core = lax.rem(f, 2)
    line = [lax.rem(x + d, RING) for d in range(RING)]
    line = [(lax.rem(v, 2), lax.div(v, 2)) for v in line]

    def plane(i, carry):
        far_y = lax.rem(y + lax.div(i, RING), RING) * 2 + core
        far_z = lax.rem(z + lax.rem(i, RING), RING) * 2
        for d, (low, high) in enumerate(line):

            @pl.when(jnp.logical_or(i > 0, d > 0))
            def _(low=low, high=high):
                pl.semaphore_signal(
                    barrier, inc=1, device_id={"fsdp": far_y, "ctx": far_z + low, "tp": high},
                    device_id_type=MESH,
                )

        return carry

    lax.fori_loop(0, RING * RING, plane, 0)


def other_core():
    f = lax.axis_index("fsdp")
    return {"fsdp": f + 1 - 2 * (f % 2)}


def moe_kernel(
    send_ref, deo_ref, late_ref, gate_ref, up_ref, down_ref, gate_far, up_far, down_far,
    back_ref, eo_ref, wide_ref, tall_ref,
    rows, deos, gu, down, z, dgu, wide, tall, give, take,
    go_sem, come_sem, load_sem, weight_sem, share_send, share_recv, part_send, part_recv,
    back_send, back_recv, eo_sem, late_sem,
):
    size, hidden = send_ref.shape[1], down_ref.shape[0]
    count = GROUP * size
    groups = CHIPS // GROUP
    width = down_ref.shape[1]

    def each(body, low, high):
        def step(i, carry):
            body(i)
            return carry

        lax.fori_loop(low, high, step, 0)

    barrier = pltpu.get_barrier_semaphore()
    signal_chips(barrier)
    pl.semaphore_signal(barrier, inc=1, device_id=other_core(), device_id_type=MESH)
    pl.semaphore_wait(barrier, CHIPS)

    def slot_rows(s):
        return pl.ds(pl.multiple_of(s * size, size), size)

    def group_rows(g):
        return pl.ds(pl.multiple_of(g * count, count), count)

    def go(s):
        return remote(
            send_ref.at[s], rows.at[0, slot_rows(s)], go_sem.at[s], come_sem.at[s], device_at(s, 1)
        )

    def stay(s):
        return pltpu.make_async_copy(send_ref.at[s], rows.at[0, slot_rows(s)], come_sem.at[s])

    def load(s):
        return pltpu.make_async_copy(
            deo_ref.at[s], deos.at[0, slot_rows(s)], load_sem.at[s]
        )

    def go_late(s):
        return remote(
            late_ref.at[s], deos.at[0, slot_rows(s)], late_sem.at[s], load_sem.at[s],
            device_at(s, 1),
        )

    def sent_rows(n, s):
        slot = lax.rem(lax.div(s, GROUP), 2)
        return give.at[n, slot, slot_rows(lax.rem(s, GROUP))]

    def back(s):
        return remote(
            sent_rows(0, s), back_ref.at[s], back_send.at[s], back_recv.at[s], device_at(s, -1)
        )

    def back_stay():
        return pltpu.make_async_copy(
            give.at[0, 0, pl.ds(0, size)], back_ref.at[0], back_recv.at[0]
        )

    def out(s):
        return pltpu.make_async_copy(
            sent_rows(1, s), eo_ref.at[s], eo_sem.at[s]
        )

    def share(n, g):
        ref = (rows, deos)[n]
        return remote(
            ref.at[0, group_rows(g)], ref.at[1, group_rows(g)], share_send.at[n, g],
            share_recv.at[n, g], other_core(),
        )

    def part(n, g):
        slot = lax.rem(g, 2)
        return remote(
            give.at[n, slot], take.at[n, slot], part_send.at[n, g], part_recv.at[n, g],
            other_core(),
        )

    places = (gu.at[:, pl.ds(0, hidden)], gu.at[:, pl.ds(hidden, hidden)], down)
    weights = [
        [pltpu.make_async_copy(src, dst, weight_sem.at[n]) for n, (src, dst) in enumerate(pairs)]
        for pairs in (
            zip((gate_ref, up_ref, down_ref), places), zip((gate_far, up_far, down_far), places)
        )
    ]

    def on_weights(act):
        for condition, copies in zip((native(), jnp.logical_not(native())), weights):

            @pl.when(condition)
            def _(copies=copies):
                for copy in copies:
                    act(copy)

    stay(0).start()
    each(lambda s: go(s).start(), 1, EARLY)
    each(lambda s: load(s).start(), 0, EARLY)
    on_weights(lambda copy: copy.start())

    def tiles(body):
        each(lambda i: body(pl.ds(pl.multiple_of(i * TILE, TILE), TILE)), 0, width // TILE)

    def clear(at):
        wide[at, :] = jnp.zeros((TILE, 2 * hidden), F32)
        tall[:, at] = jnp.zeros((hidden, TILE), F32)

    tiles(clear)

    def through(side, g):
        at = group_rows(g)
        pre = dot(rows[side, at, :], gu[...], ((1,), (0,)))
        dz = dot(deos[side, at, :], down[...], ((1,), (1,)))
        gate, u = pre[:, :hidden], pre[:, hidden:]
        sig = 1.0 / (1.0 + jnp.exp(-gate))
        act = gate * sig
        z[side] = (act * u).astype(BF16)
        dgu[side, :, :hidden] = (dz * u * sig * (1.0 + gate * (1.0 - sig))).astype(BF16)
        dgu[side, :, hidden:] = (dz * act).astype(BF16)

    def to_rows(side):
        return dot(dgu[side], gu[...], ((1,), (1,)))

    def to_outputs(side):
        return dot(z[side], down[...], ((1,), (0,)))

    on_weights(lambda copy: copy.wait())

    def group(g):
        first, last, slot = g * GROUP, (g + 1) * GROUP, lax.rem(g, 2)

        @pl.when(g == 0)
        def _():
            stay(0).wait()

        each(lambda s: go(s).wait_recv(), lax.max(first, 1), last)
        each(lambda s: load(s).wait(), lax.min(first, EARLY), lax.min(last, EARLY))
        each(lambda s: go_late(s).wait_recv(), lax.max(first, EARLY), lax.max(last, EARLY))

        def go_both(s):
            go(s).start()
            go_late(s).start()

        each(go_both, lax.min(first + EARLY, CHIPS), lax.min(last + EARLY, CHIPS))
        for n in (0, 1):
            share(n, g).start()
        through(0, g)
        for n in (0, 1):
            share(n, g).wait_recv()
        through(1, g)

        @pl.when(g >= 2)
        def _():
            @pl.when(g == 2)
            def _():
                back_stay().wait()

            each(lambda s: back(s).wait_send(), lax.max(first - 2 * GROUP, 1), last - 2 * GROUP)
            each(lambda s: out(s).wait(), first - 2 * GROUP, last - 2 * GROUP)

        give[0, slot] = to_rows(1).astype(BF16)
        part(0, g).start()
        give[1, slot] = to_outputs(1).astype(BF16)
        part(1, g).start()
        own = to_rows(0)
        part(0, g).wait()
        give[0, slot] = (own + take[0, slot].astype(F32)).astype(BF16)

        @pl.when(g == 0)
        def _():
            back_stay().start()

        each(lambda s: back(s).start(), lax.max(first, 1), last)
        own = to_outputs(0)
        part(1, g).wait()
        give[1, slot] = (own + take[1, slot].astype(F32)).astype(BF16)
        each(lambda s: out(s).start(), first, last)
        at = group_rows(g)

        def weight_grads(cols):
            wide[cols, :] += dot(rows[0, at, cols], dgu[0], ((0,), (0,))) + dot(
                rows[1, at, cols], dgu[1], ((0,), (0,))
            )
            tall[:, cols] += dot(z[0], deos[0, at, cols], ((0,), (0,))) + dot(
                z[1], deos[1, at, cols], ((0,), (0,))
            )

        tiles(weight_grads)

    each(group, 0, groups)

    def store(at):
        wide_ref[at, :] = wide[at, :].astype(BF16)
        tall_ref[:, at] = tall[:, at].astype(BF16)

    tiles(store)
    for g in range(groups):
        for n in (0, 1):
            share(n, g).wait_send()
    each(lambda s: out(s).wait(), (groups - 2) * GROUP, CHIPS)
    each(lambda s: back(s).wait_send(), (groups - 2) * GROUP, CHIPS)
    each(lambda s: go(s).wait_send(), 1, CHIPS)
    each(lambda s: go_late(s).wait_send(), EARLY, CHIPS)
    each(lambda s: back(s).wait_recv(), 1, CHIPS)


def moe(send, d_eo, d_eo_late, own, far):
    chips, size, width = send.shape
    hidden = own[2].shape[0]
    total, groups = chips * size, chips // GROUP
    count = GROUP * size
    vmem, any_space = (pl.BlockSpec(memory_space=space) for space in (pltpu.VMEM, pl.ANY))
    shapes = [send.shape, send.shape, (width, 2 * hidden), (hidden, width)]
    dma = pltpu.SemaphoreType.DMA
    return pl.pallas_call(
        moe_kernel,
        in_specs=[any_space] * 9,
        out_specs=[any_space] * 2 + [vmem] * 2,
        out_shape=[jax.ShapeDtypeStruct(shape, BF16) for shape in shapes],
        scratch_shapes=[
            pltpu.VMEM((2, total, width), BF16),
            pltpu.VMEM((2, total, width), BF16),
            pltpu.VMEM((width, 2 * hidden), BF16),
            pltpu.VMEM((hidden, width), BF16),
            pltpu.VMEM((2, count, hidden), BF16),
            pltpu.VMEM((2, count, 2 * hidden), BF16),
            pltpu.VMEM((width, 2 * hidden), F32),
            pltpu.VMEM((hidden, width), F32),
            pltpu.VMEM((2, 2, count, width), BF16),
            pltpu.VMEM((2, 2, count, width), BF16),
            dma((chips,)), dma((chips,)), dma((chips,)), dma((3,)),
            dma((2, groups)), dma((2, groups)), dma((2, groups)), dma((2, groups)),
            dma((chips,)), dma((chips,)), dma((chips,)), dma((chips,)),
        ],
        compiler_params=pltpu.CompilerParams(
            collective_id=4, has_side_effects=True, vmem_limit_bytes=56 * 1024 * 1024
        ),
        cost_estimate=pl.CostEstimate(flops=0, bytes_accessed=400_000_000, transcendentals=0),
        name="experts",
    )(send, d_eo, d_eo_late, *own, *far)


BLOCK = 64
CTX = 8
WIDE = 256


def rotated(u, gain, cosine, sine):
    scaling = lax.rsqrt(jnp.mean(u * u, axis=-1, keepdims=True) + EPS)
    normed = u * scaling
    n = normed * gain
    rot = n * cosine + pltpu.roll(n, HEAD_SIZE // 2, 1) * sine
    return rot.astype(BF16), normed, scaling


def rotated_back(e, normed, scaling, gain, cosine, sine):
    back = e * cosine + pltpu.roll(e * sine, HEAD_SIZE // 2, 1)
    scaled = back * gain
    inner = jnp.mean(scaled * normed, axis=-1, keepdims=True)
    return scaling * (scaled - normed * inner), jnp.sum(back * normed, axis=0, keepdims=True)


def ctx_peer(step):
    return {"ctx": lax.rem(lax.axis_index("ctx") + step, CTX)}


def beside():
    c = lax.axis_index("ctx")
    return {"ctx": c + 1 - 2 * lax.rem(c, 2)}


def softmax_parts(q_low, k, bias):
    s = dot(q_low, k, ((1,), (1,))) * (HEAD_SIZE ** -0.5) + bias
    e = jnp.exp(s - jnp.max(s, axis=-1, keepdims=True))
    return e / jnp.sum(e, axis=-1, keepdims=True)


def each(body, low, high):
    def step(i, carry):
        body(i)
        return carry

    lax.fori_loop(low, high, step, 0)


def greet_chips():
    barrier = pltpu.get_barrier_semaphore()
    signal_chips(barrier)
    return lambda: pl.semaphore_wait(barrier, CHIPS - 1)


def tile(i):
    return pl.ds(pl.multiple_of(i * WIDE, WIDE), WIDE)


def head_cols(h):
    return pl.ds(pl.multiple_of(h * HEAD_SIZE, HEAD_SIZE), HEAD_SIZE)


def forward_kernel(
    kv, heads, tokens_ref, gain_in_ref, gain_moe_ref, cos_ref, sin_ref, gq_ref, gk_ref, bias_ref,
    select_ref, w_qkv_ref, w_out_ref, rows_ref,
    a_ref, qkv_ref, kv_ref, o_ref, middle_ref, send_ref, came_ref,
    w_qkv, w_out, held, part_sum, swap_give, swap_take, send_rows,
    send_sem, recv_sem, load_sem, swap_sem, out_sem, go_sem, come_sem,
):
    c, tp = lax.axis_index("ctx"), lax.axis_index("tp")
    micro, rows = held.shape[0], 2 * BLOCK
    q_cols = kv * heads * HEAD_SIZE
    width = w_out.shape[0]
    entered = greet_chips()
    loads = [
        pltpu.make_async_copy(w_qkv_ref, w_qkv, load_sem.at[0]),
        pltpu.make_async_copy(w_out_ref.at[:, pl.ds(0, w_out.shape[1])], w_out, load_sem.at[1]),
    ]
    for copy in loads:
        copy.start()

    def go(s):
        return remote(
            rows_ref.at[s], came_ref.at[s], go_sem.at[s], come_sem.at[s], device_at(s, 1)
        )

    stay = pltpu.make_async_copy(rows_ref.at[0], came_ref.at[0], come_sem.at[0])
    stay.start()
    cosine, sine, gq, gk = cos_ref[...], sin_ref[...], gq_ref[...], gk_ref[...]
    mine = pl.ds(pl.multiple_of(c * BLOCK, BLOCK), BLOCK)
    earlier, own = pl.ds(CTX * BLOCK, BLOCK), pl.ds((CTX + 1) * BLOCK, BLOCK)

    def block(i):
        return pl.ds(pl.multiple_of(i * BLOCK, BLOCK), BLOCK)

    def norm_in(i):
        u = tokens_ref[block(i), :].astype(F32)
        scaling = lax.rsqrt(jnp.mean(u * u, axis=-1, keepdims=True) + EPS)
        a_ref[block(i), :] = (u * scaling * gain_in_ref[...]).astype(BF16)

    each(norm_in, 0, micro * 2)
    loads[0].wait()

    def project(i):
        qkv_ref[:, tile(i)] = dot(a_ref[...], w_qkv[:, tile(i)], ((1,), (0,)))

    each(project, q_cols // WIDE, w_qkv.shape[1] // WIDE)
    entered()
    copies = []
    for m in range(micro):
        span = slice(m * rows, (m + 1) * rows)
        for h in range(2 * kv):
            cols = slice(h * HEAD_SIZE, (h + 1) * HEAD_SIZE)
            u = qkv_ref[span, q_cols + h * HEAD_SIZE : q_cols + (h + 1) * HEAD_SIZE]
            low = rotated(u, gk, cosine, sine)[0] if h < kv else u.astype(BF16)
            held[m, mine, cols] = low[:BLOCK]
            held[m, own, cols] = low[BLOCK:]
        for step in range(1, CTX):
            part = held.at[m, mine]
            copies.append(
                remote(part, part, send_sem.at[step, m], recv_sem.at[step, m], ctx_peer(step))
            )
        copies.append(
            remote(
                held.at[m, own], held.at[m, earlier], send_sem.at[0, m], recv_sem.at[0, m], beside()
            )
        )
        for copy in copies[-CTX:]:
            copy.start()
    each(lambda s: go(s).start(), 1, EARLY)
    each(project, 0, q_cols // WIDE)

    def group(m, h, carry):
        span = slice(m * rows, (m + 1) * rows)
        k, v = held[m, :, head_cols(h)], held[m, :, head_cols(kv + h)]
        for e in range(heads):
            cols = head_cols(h * heads + e)
            q_low = rotated(qkv_ref[span, cols], gq, cosine, sine)[0]
            p = softmax_parts(q_low, k, bias_ref[...]).astype(BF16)
            o_ref[span, cols] = dot(p, v, ((1,), (0,))).astype(BF16)
        return carry

    def arrived(m):
        for step in range(1, CTX):
            source = lax.rem(c + CTX - step, CTX)
            part = held.at[m, pl.ds(pl.multiple_of(source * BLOCK, BLOCK), BLOCK)]
            remote(
                part, part, send_sem.at[step, m], recv_sem.at[step, m], ctx_peer(step)
            ).wait_recv()
        copies[(m + 1) * CTX - 1].wait_recv()

    for m in range(micro):
        arrived(m)
        lax.fori_loop(0, kv, functools.partial(group, m), 0)
        kv_ref[m] = held[m]
    loads[1].wait()

    def join(i):
        part_sum[:, tile(i)] = dot(o_ref[...], w_out[tile(i), :], ((1,), (1,)))

    each(join, 0, width // WIDE)
    for m in range(micro):
        away = pl.ds(pl.multiple_of(m * rows + tp * BLOCK, BLOCK), BLOCK)
        swap_give[m * BLOCK : (m + 1) * BLOCK, :] = part_sum[away, :].astype(BF16)
    swap = remote(swap_give, swap_take, swap_sem.at[0], swap_sem.at[1], {"tp": 1 - tp})
    swap.start()
    swap.wait()
    for m in range(micro):
        kept = pl.ds(pl.multiple_of(m * rows + (1 - tp) * BLOCK, BLOCK), BLOCK)
        span = slice(m * BLOCK, (m + 1) * BLOCK)
        total = part_sum[kept, :] + swap_take[span, :].astype(F32)
        u = tokens_ref[kept, :].astype(F32) + total
        middle_ref[span, :] = u
        scaling = lax.rsqrt(jnp.mean(u * u, axis=-1, keepdims=True) + EPS)
        swap_give[span, :] = (u * scaling * gain_moe_ref[...]).astype(BF16)

    def pick(i):
        value = dot(select_ref[:, tile(i)], swap_give[...], ((0,), (0,)))
        send_rows[tile(i), :] = value.astype(BF16)

    each(pick, 0, send_rows.shape[0] // WIDE)
    out = pltpu.make_async_copy(send_rows, send_ref, out_sem)
    out.start()
    out.wait()
    stay.wait()
    for copy in copies:
        copy.wait_send()
    each(lambda s: go(s).wait(), 1, EARLY)


def backward_kernel(
    kv, heads, qkv_ref, cos_ref, sin_ref, gq_ref, gk_ref, bias_ref, kv_ref, dattn_ref, o_ref, a_ref,
    w_out_ref, w_qkv_ref, eo_ref,
    given_grad_ref, gains_ref, grad_qkv_ref, grad_out_ref, eo_back_ref,
    w_out, w_qkv, do_ref, dqkv_ref, part_sum, wide_tile, tall_tile, grads, given, given_side,
    p_all, ds_all, q_all, do_all, swap_give, swap_take,
    send_sem, recv_sem, load_sem, tile_sem, swap_sem, eo_send, eo_recv,
):
    c, tp = lax.axis_index("ctx"), lax.axis_index("tp")
    width = w_out.shape[0]

    entered = greet_chips()
    loads = [
        pltpu.make_async_copy(w_out_ref.at[:, pl.ds(0, w_out.shape[1])], w_out, load_sem.at[0]),
        pltpu.make_async_copy(w_qkv_ref, w_qkv, load_sem.at[1]),
    ]
    for copy in loads:
        copy.start()
    entered()

    def output(s):
        return remote(
            eo_ref.at[s], eo_back_ref.at[s], eo_send.at[s], eo_recv.at[s], device_at(s, -1)
        )

    def outputs(quarter):
        each(lambda s: output(s).start(), max(quarter * GROUP, 1), (quarter + 1) * GROUP)

    stay = pltpu.make_async_copy(eo_ref.at[0], eo_back_ref.at[0], eo_recv.at[0])
    stay.start()
    outputs(0)
    micro, rows = grads.shape[0], 2 * BLOCK
    q_cols = kv * heads * HEAD_SIZE
    scale = HEAD_SIZE ** -0.5
    cosine, sine, gq, gk = cos_ref[...], sin_ref[...], gq_ref[...], gk_ref[...]
    mine = pl.ds(pl.multiple_of(c * BLOCK, BLOCK), BLOCK)
    earlier, own = pl.ds(CTX * BLOCK, BLOCK), pl.ds((CTX + 1) * BLOCK, BLOCK)

    loads[0].wait()

    def outputs_back(i):
        do_ref[:, tile(i)] = dot(dattn_ref[...], w_out[:, tile(i)], ((1,), (0,))).astype(BF16)

    each(outputs_back, 0, w_out.shape[1] // WIDE)

    def keys_back(m, h, carry):
        span = slice(m * rows, (m + 1) * rows)
        k, v = kv_ref[m, :, head_cols(h)], kv_ref[m, :, head_cols(kv + h)]
        for e in range(heads):
            cols = head_cols(h * heads + e)
            stack = slice(e * rows, (e + 1) * rows)
            q_low = rotated(qkv_ref[span, cols], gq, cosine, sine)[0]
            q_all[stack, :] = q_low
            p = softmax_parts(q_low, k, bias_ref[...])
            p_all[stack, :] = p.astype(BF16)
            do = do_ref[span, cols]
            do_all[stack, :] = do
            dp = dot(do, v, ((1,), (1,)))
            ds = (p * (dp - jnp.sum(dp * p, axis=-1, keepdims=True))).astype(BF16)
            ds_all[m * kv + h, stack, :] = ds
        grads[m, :, head_cols(kv + h)] = dot(p_all[...], do_all[...], ((0,), (0,))).astype(BF16)
        d_k = dot(ds_all[m * kv + h], q_all[...], ((0,), (0,))) * scale
        grads[m, :, head_cols(h)] = d_k.astype(BF16)
        return carry

    def queries_back(m, h, total):
        span = slice(m * rows, (m + 1) * rows)
        k = kv_ref[m, :, head_cols(h)]
        for e in range(heads):
            cols = head_cols(h * heads + e)
            ds = ds_all[m * kv + h, e * rows : (e + 1) * rows, :]
            dqr = (dot(ds, k, ((1,), (0,))) * scale).astype(BF16).astype(F32)
            u = qkv_ref[span, cols]
            scaling = lax.rsqrt(jnp.mean(u * u, axis=-1, keepdims=True) + EPS)
            dq, part = rotated_back(dqr, u * scaling, scaling, gq, cosine, sine)
            dqkv_ref[span, cols] = dq.astype(BF16)
            total = total + part
        return total

    copies = []
    for m in range(micro):
        lax.fori_loop(0, kv, functools.partial(keys_back, m), 0)
        for step in range(1, CTX):
            peer = lax.rem(c + step, CTX)
            part = grads.at[m, pl.ds(pl.multiple_of(peer * BLOCK, BLOCK), BLOCK)]
            copies.append(
                remote(
                    part, given.at[step - 1, m], send_sem.at[step, m], recv_sem.at[step, m],
                    ctx_peer(step),
                )
            )
        copies.append(
            remote(
                grads.at[m, earlier], given_side.at[m], send_sem.at[0, m], recv_sem.at[0, m],
                beside(),
            )
        )
        for copy in copies[-CTX:]:
            copy.start()
        if m == micro - 1:
            outputs(1)
    total = jnp.zeros((1, HEAD_SIZE), F32)
    for m in range(micro):
        total = lax.fori_loop(0, kv, functools.partial(queries_back, m), total)

    def tiles_out(buffer, left, right, out_ref, sems):
        def copy_out(i):
            slot = lax.rem(i, 2)
            return pltpu.make_async_copy(buffer.at[slot], out_ref.at[tile(i)], sems.at[i])

        def step(i):
            @pl.when(i >= 2)
            def _():
                copy_out(i - 2).wait()

            value = dot(left[:, tile(i)], right[...], ((0,), (0,)))
            buffer[lax.rem(i, 2)] = value.astype(BF16)
            copy_out(i).start()

        count = width // WIDE
        each(step, 0, count)
        return lambda: each(lambda i: copy_out(i).wait(), count - 2, count)

    end_out = tiles_out(tall_tile, dattn_ref, o_ref, grad_out_ref, tile_sem.at[0])
    loads[1].wait()

    def queries_in(i):
        part_sum[:, tile(i)] = dot(dqkv_ref[:, :q_cols], w_qkv[tile(i), :q_cols], ((1,), (1,)))

    each(queries_in, 0, width // WIDE)
    k_total = jnp.zeros((1, HEAD_SIZE), F32)
    for m in range(micro):
        for copy in copies[m * CTX : (m + 1) * CTX]:
            copy.wait_recv()
        for h in range(2 * kv):
            cols = slice(h * HEAD_SIZE, (h + 1) * HEAD_SIZE)
            at = slice(q_cols + h * HEAD_SIZE, q_cols + (h + 1) * HEAD_SIZE)
            prompt = grads[m, mine, cols].astype(F32)
            for step in range(CTX - 1):
                prompt = prompt + given[step, m, :, cols].astype(F32)
            cont = grads[m, own, cols].astype(F32) + given_side[m, :, cols].astype(F32)
            e = jnp.concatenate([prompt, cont], axis=0).astype(BF16)
            span = slice(m * rows, (m + 1) * rows)
            if h < kv:
                _, normed, scaling = rotated(qkv_ref[span, at], gk, cosine, sine)
                d, part = rotated_back(e.astype(F32), normed, scaling, gk, cosine, sine)
                k_total = k_total + part
                dqkv_ref[span, at] = d.astype(BF16)
            else:
                dqkv_ref[span, at] = e
    gains_ref[0:1, :] = total
    gains_ref[1:2, :] = k_total

    def keys_in(i):
        part_sum[:, tile(i)] += dot(dqkv_ref[:, q_cols:], w_qkv[tile(i), q_cols:], ((1,), (1,)))

    each(keys_in, 0, width // WIDE)
    for m in range(micro):
        away = pl.ds(pl.multiple_of(m * rows + tp * BLOCK, BLOCK), BLOCK)
        swap_give[m * BLOCK : (m + 1) * BLOCK, :] = part_sum[away, :].astype(BF16)
    swap = remote(swap_give, swap_take, swap_sem.at[0], swap_sem.at[1], {"tp": 1 - tp})
    swap.start()
    outputs(2)
    outputs(3)
    end_qkv = tiles_out(wide_tile, a_ref, dqkv_ref, grad_qkv_ref, tile_sem.at[1])
    swap.wait()
    for m in range(micro):
        kept = pl.ds(pl.multiple_of(m * rows + (1 - tp) * BLOCK, BLOCK), BLOCK)
        span = slice(m * BLOCK, (m + 1) * BLOCK)
        given_grad_ref[span, :] = part_sum[kept, :] + swap_take[span, :].astype(F32)
    for copy in copies:
        copy.wait_send()
    end_out()
    end_qkv()
    stay.wait()
    each(lambda s: output(s).wait(), 1, CHIPS)


def forward(tokens, gain_in, gain_moe, heads_in, select, w_qkv, w_out, moe_rows, kv):
    total, width = tokens.shape
    cols = w_qkv.shape[1]
    heads = cols // HEAD_SIZE // kv - 2
    q_cols, kv_cols = kv * heads * HEAD_SIZE, 2 * kv * HEAD_SIZE
    rows, keys = heads_in[-1].shape
    micro = total // rows
    vmem, any_space = (pl.BlockSpec(memory_space=space) for space in (pltpu.VMEM, pl.ANY))
    dma = pltpu.SemaphoreType.DMA
    return pl.pallas_call(
        functools.partial(forward_kernel, kv, heads),
        in_specs=[vmem] * 9 + [any_space] * 3,
        out_specs=[vmem] * 5 + [any_space] * 2,
        out_shape=[
            jax.ShapeDtypeStruct((total, width), BF16),
            jax.ShapeDtypeStruct((total, cols), F32),
            jax.ShapeDtypeStruct((micro, keys, kv_cols), BF16),
            jax.ShapeDtypeStruct((total, q_cols), BF16),
            jax.ShapeDtypeStruct((micro * BLOCK, width), F32),
            jax.ShapeDtypeStruct((select.shape[1], width), BF16),
            jax.ShapeDtypeStruct((EARLY,) + moe_rows.shape[1:], BF16),
        ],
        scratch_shapes=[
            pltpu.VMEM((width, cols), BF16),
            pltpu.VMEM((width, q_cols), BF16),
            pltpu.VMEM((micro, keys, kv_cols), BF16),
            pltpu.VMEM((total, width), F32),
            pltpu.VMEM((micro * BLOCK, width), BF16),
            pltpu.VMEM((micro * BLOCK, width), BF16),
            pltpu.VMEM((select.shape[1], width), BF16),
            dma((CTX, micro)), dma((CTX, micro)), dma((2,)), dma((2,)), dma,
            dma((CHIPS,)), dma((CHIPS,)),
        ],
        compiler_params=pltpu.CompilerParams(
            collective_id=2, has_side_effects=True, vmem_limit_bytes=56 * 1024 * 1024
        ),
        cost_estimate=pl.CostEstimate(flops=0, bytes_accessed=250_000_000, transcendentals=0),
        name="attention_forward",
    )(tokens, gain_in, gain_moe, *heads_in, select, w_qkv, w_out, moe_rows)


def backward(qkv, heads_in, kv_all, d_attn, o, a, w_out, w_qkv, eo, kv):
    heads = qkv.shape[1] // HEAD_SIZE // kv - 2
    bias = heads_in[-1]
    rows, keys = bias.shape
    micro, _, kv_cols = kv_all.shape
    width, cols = w_qkv.shape
    total, q_cols = qkv.shape[0], kv * heads * HEAD_SIZE
    vmem, any_space = (pl.BlockSpec(memory_space=space) for space in (pltpu.VMEM, pl.ANY))
    dma = pltpu.SemaphoreType.DMA
    return pl.pallas_call(
        functools.partial(backward_kernel, kv, heads),
        in_specs=[vmem] * 10 + [any_space] * 3,
        out_specs=[vmem] * 2 + [any_space] * 3,
        out_shape=[
            jax.ShapeDtypeStruct((micro * BLOCK, width), F32),
            jax.ShapeDtypeStruct((2, HEAD_SIZE), F32),
            jax.ShapeDtypeStruct((width, cols), BF16),
            jax.ShapeDtypeStruct((width, q_cols), BF16),
            jax.ShapeDtypeStruct(eo.shape, BF16),
        ],
        scratch_shapes=[
            pltpu.VMEM((width, q_cols), BF16),
            pltpu.VMEM((width, cols), BF16),
            pltpu.VMEM((total, q_cols), BF16),
            pltpu.VMEM((total, cols), BF16),
            pltpu.VMEM((total, width), F32),
            pltpu.VMEM((2, WIDE, cols), BF16),
            pltpu.VMEM((2, WIDE, q_cols), BF16),
            pltpu.VMEM((micro, keys, kv_cols), BF16),
            pltpu.VMEM((CTX - 1, micro, BLOCK, kv_cols), BF16),
            pltpu.VMEM((micro, BLOCK, kv_cols), BF16),
            pltpu.VMEM((heads * rows, keys), BF16),
            pltpu.VMEM((micro * kv, heads * rows, keys), BF16),
            pltpu.VMEM((heads * rows, HEAD_SIZE), BF16),
            pltpu.VMEM((heads * rows, HEAD_SIZE), BF16),
            pltpu.VMEM((micro * BLOCK, width), BF16),
            pltpu.VMEM((micro * BLOCK, width), BF16),
            dma((CTX, micro)), dma((CTX, micro)), dma((2,)), dma((2, width // WIDE)), dma((2,)),
            dma((CHIPS,)), dma((CHIPS,)),
        ],
        compiler_params=pltpu.CompilerParams(
            collective_id=3, has_side_effects=True, vmem_limit_bytes=56 * 1024 * 1024
        ),
        cost_estimate=pl.CostEstimate(flops=0, bytes_accessed=250_000_000, transcendentals=0),
        name="attention_backward",
    )(qkv, *heads_in, kv_all, d_attn, o, a, w_out, w_qkv, eo)


def normalize_back(rows, scaling, gain, upstream):
    normed = rows * scaling
    gain_grad = jnp.sum((upstream * normed).reshape(-1, rows.shape[-1]), axis=0)
    scaled = upstream * gain
    inner = jnp.mean(scaled * normed, axis=-1, keepdims=True)
    return scaling * (scaled - normed * inner), gain_grad


def swap_tp(value):
    return lax.ppermute(value, "tp", [(0, 1), (1, 0)])


def local(
    x_prompt, x_cont, cot_prompt, cot_cont, ids_prompt, ids_cont, gates_prompt, gates_cont,
    norm_gain, query_weight, key_matrix, value_matrix, out_weight, query_gain, key_gain, moe_gain,
    expert_gate, expert_up, expert_down,
):
    micro = x_prompt.shape[0]
    prompt_rows, cont_rows, width = x_prompt.shape[2], x_cont.shape[2], x_prompt.shape[3]
    block = cont_rows
    rows = 2 * block
    s = lax.axis_index("ctx")
    ctx = lax.axis_size("ctx")
    first = lax.axis_index("tp") == 0
    peers = lax.axis_size(ALL)
    q_cols, kv_cols = query_weight.shape[1], key_matrix.shape[1]
    kv = kv_cols // HEAD_SIZE
    qkv_cols = q_cols + 2 * kv_cols
    shard_rows = query_weight.shape[0]
    hidden = expert_gate.shape[2]
    slots = cont_rows * TOPK // peers

    def pad(v):
        return jnp.pad(v[:, 0], ((0, 0), (0, block - prompt_rows), (0, 0)))

    x_first, x_second = pad(x_prompt), x_cont[:, 0]
    own_tokens = jnp.where(first, x_second, x_first).astype(F32)
    own_cot = jnp.where(first, cot_cont[:, 0], pad(cot_prompt))
    ids_pad = jnp.pad(
        ids_prompt[:, 0], ((0, 0), (0, block - prompt_rows), (0, 0)), constant_values=-1
    )
    own_ids = jnp.where(first, ids_cont[:, 0], ids_pad)
    own_gates = jnp.where(first, gates_cont[:, 0], pad(gates_prompt))

    y, z, x = chip_at(jnp.arange(peers, dtype=jnp.int32), 1)
    near = (2 * y + x // 2) * ctx + 2 * z + x % 2
    order = jnp.pad(near, (0, HEAD_SIZE - peers), constant_values=-2)[None]

    def lanes(v):
        return jnp.pad(v, [(0, 0)] * (v.ndim - 1) + [(0, HEAD_SIZE - v.shape[-1])])

    extra = jnp.stack([lanes(v) for v in (norm_gain, moe_gain, query_gain, key_gain)])
    extra = jnp.pad(extra, ((0, shard_rows - extra.shape[0]), (0, 0)))
    own_experts = (expert_gate[0], expert_up[0], expert_down[0])
    w_qkv, w_out_extra, far_experts, routing = gather_weights(
        query_weight, key_matrix, value_matrix, out_weight, extra,
        own_ids.reshape(-1, TOPK), own_gates.reshape(-1, TOPK), order,
        own_cot.reshape(-1, width), peers * micro * slots, *own_experts,
    )
    select_near, mixing, spread = routing
    gains = w_out_extra[:, q_cols:].reshape(peers, shard_rows, HEAD_SIZE)[:, :4].astype(F32)
    gain_in, gain_moe = (gains[:, n, :shard_rows].reshape(-1) for n in (0, 1))
    head_rows = query_gain.shape[0]
    gain_query, gain_key = (gains[:, n, :head_rows].reshape(-1) for n in (2, 3))

    offsets = jnp.arange(rows, dtype=jnp.int32)
    is_prompt = offsets < block
    prompt_pos = s * prompt_rows + offsets
    cont_pos = s * cont_rows + offsets - block
    rot_place = jnp.where(is_prompt, prompt_pos, PROMPT + cont_pos % CL).astype(F32)
    steps_freq = jnp.arange(HEAD_SIZE // 2, dtype=F32) * (2.0 / HEAD_SIZE)
    angles = rot_place[:, None] * jnp.power(THETA, -steps_freq)[None, :]
    cosine, sine = jnp.cos(angles), jnp.sin(angles)
    cosine = jnp.concatenate([cosine, cosine], axis=1)
    sine = jnp.concatenate([-sine, sine], axis=1)
    keys = (ctx + 2) * block
    key_index = jnp.arange(keys, dtype=jnp.int32)[None, :]
    key_off = key_index % block
    key_prompt_pos = key_index // block * prompt_rows + key_off
    key_cont = (s - 1) * cont_rows + key_index - ctx * block
    is_cont = jnp.logical_not(is_prompt)[:, None]
    visible = jnp.where(
        key_index < ctx * block,
        jnp.logical_and(
            key_off < prompt_rows,
            jnp.logical_or(is_cont, key_prompt_pos <= prompt_pos[:, None]),
        ),
        jnp.logical_and(
            is_cont,
            jnp.logical_and(
                key_cont // CL == cont_pos[:, None] // CL, key_cont <= cont_pos[:, None]
            ),
        ),
    )
    bias = jnp.where(visible, 0.0, NEG).astype(F32)

    def arranged(own, other):
        return jnp.where(first, other, own), jnp.where(first, own, other)

    heads_in = (cosine, sine, gain_query[None], gain_key[None], bias)
    tokens = jnp.concatenate([x_first, x_second], axis=1).reshape(-1, width)
    slot_shape = (peers, micro * slots, width)
    spread = spread.reshape(slot_shape)
    a, qkv, kv_all, o, middle, send, d_eo_rows = forward(
        tokens, gain_in[None], gain_moe[None], heads_in, select_near, w_qkv, w_out_extra,
        spread, kv,
    )
    middle = middle.reshape(own_tokens.shape)
    b_scale = lax.rsqrt(jnp.mean(middle * middle, axis=-1, keepdims=True) + EPS)

    back, eo, wide_here, tall_here = moe(
        send.reshape(slot_shape), d_eo_rows, spread, own_experts, far_experts
    )
    d_b = dot(select_near, back.reshape(-1, width), ((1,), (0,))).reshape(middle.shape)
    middle_from, moe_total = normalize_back(middle, b_scale, gain_moe, d_b)
    d_h = own_cot.astype(F32) + middle_from
    d_h_low = d_h.astype(BF16)
    d_attn = jnp.concatenate(arranged(d_h_low, swap_tp(d_h_low)), axis=1).reshape(-1, width)

    input_grad, head_totals, grad_qkv, grad_out, eo_back = backward(
        qkv, heads_in, kv_all, d_attn, o, a, w_out_extra, w_qkv, eo, kv
    )
    moe_out = dot(mixing, eo_back.reshape(-1, width), ((1,), (0,)))
    moe_out = (moe_out[: micro * block] + moe_out[micro * block :]).reshape(middle.shape)
    y_own = (middle + moe_out).astype(BF16)
    scale_in = lax.rsqrt(jnp.mean(own_tokens * own_tokens, axis=-1, keepdims=True) + EPS)
    token_from, norm_total = normalize_back(
        own_tokens, scale_in, gain_in, input_grad.reshape(own_tokens.shape)
    )
    x_own = (d_h + token_from).astype(BF16)

    extra_grads = jnp.stack(
        [
            lanes(v.reshape(peers, -1))
            for v in (norm_total, moe_total, head_totals[0], head_totals[1])
        ],
        axis=1,
    )
    extra_grads = jnp.pad(extra_grads, ((0, 0), (0, shard_rows - extra_grads.shape[1]), (0, 0)))
    extra_grads = extra_grads.reshape(-1, HEAD_SIZE).astype(BF16)
    share, share_out, wide_there, tall_there, y_other, x_other = scatter_grads(
        grad_qkv, grad_out, extra_grads, wide_here, tall_here, y_own, x_own
    )
    out_first, out_second = arranged(y_own, y_other)
    grad_first, grad_second = arranged(x_own, x_other)
    grad_wide = jnp.where(native(), wide_here, wide_there).astype(F32)
    grad_down = jnp.where(native(), tall_here, tall_there).astype(F32)
    gain_share = share_out[:, q_cols:]
    return (
        out_first[:, None, :prompt_rows],
        out_second[:, None],
        grad_first[:, None, :prompt_rows],
        grad_second[:, None],
        gain_share[0, :shard_rows],
        share[:, :q_cols],
        share[:, q_cols : q_cols + kv_cols],
        share[:, q_cols + kv_cols : qkv_cols],
        share_out[:, :q_cols],
        gain_share[2, :head_rows],
        gain_share[3, :head_rows],
        gain_share[1, :shard_rows],
        grad_wide[None, :, :hidden],
        grad_wide[None, :, hidden:],
        grad_down[None],
    )


def solution(mesh):
    rows = P(None, "fsdp", "ctx", None)
    vector = P(("fsdp", "ctx"))
    matrix = P(("fsdp", "ctx"), "tp")
    wide = P(("fsdp", "ctx"), None, "tp")
    tall = P(("fsdp", "ctx"), "tp", None)
    in_specs = (rows,) * 8 + (vector,) + (matrix,) * 4 + (vector,) * 3 + (wide, wide, tall)
    out_specs = (rows,) * 4 + (vector,) + (matrix,) * 4 + (vector,) * 3 + (wide, wide, tall)
    return jax.shard_map(local, mesh=mesh, in_specs=in_specs, out_specs=out_specs, check_vma=False)
```

```python
import functools

import jax
import jax.numpy as jnp
from jax import lax
from jax.experimental import pallas as pl
from jax.experimental.pallas import tpu as pltpu
from jax.sharding import PartitionSpec as P

HEAD_SIZE = 128
TOPK = 8
PROMPT = 448
CL = 128
EPS = 1e-06
THETA = 1000000.0
NEG = -1e30
F32 = jnp.float32
BF16 = jnp.bfloat16
ALL = ("fsdp", "ctx")
MESH = pl.DeviceIdType.MESH
RING = 4
VMEM_LIMIT = 48 * 1024 * 1024


def dot(a, b, dims):
    return lax.dot_general(a, b, (dims, ((), ())), preferred_element_type=F32)


def remote(src, dst, send_sem, recv_sem, where):
    return pltpu.make_async_remote_copy(
        src_ref=src, dst_ref=dst, send_sem=send_sem, recv_sem=recv_sem, device_id=where,
        device_id_type=MESH,
    )


def place():
    f, c = lax.axis_index("fsdp"), lax.axis_index("ctx")
    return f // 2, f % 2, c // 2, c % 2


def device(y, core, z, x):
    return {"fsdp": y * 2 + core, "ctx": z * 2 + x}


def greet(partners):
    barrier = pltpu.get_barrier_semaphore()
    for partner in partners:
        pl.semaphore_signal(barrier, inc=1, device_id=partner, device_id_type=MESH)
    pl.semaphore_wait(barrier, len(partners))


def neighbours():
    y, core, z, x = place()
    up, down = (lambda v: lax.rem(v + 1, RING)), (lambda v: lax.rem(v + RING - 1, RING))
    return [
        device(y, core, z, 1 - x),
        device(y, 1 - core, z, x),
        device(up(y), core, z, x),
        device(down(y), core, z, x),
        device(y, core, up(z), x),
        device(y, core, down(z), x),
    ]


def other_tp():
    return {"tp": 1 - lax.axis_index("tp")}


def opposite():
    f = lax.axis_index("fsdp")
    return {"fsdp": f + 1 - 2 * (f % 2), "tp": 1 - lax.axis_index("tp")}


def native():
    return lax.axis_index("fsdp") % 2 == lax.axis_index("tp")


def swap_opposite(src, dst, send_sem, recv_sem):
    return pltpu.make_async_remote_copy(
        src_ref=src, dst_ref=dst, send_sem=send_sem, recv_sem=recv_sem, device_id=opposite(),
        device_id_type=MESH,
    )


def route(ids, gates, experts, size, select_ref, mix_ref):
    tokens, slots = ids.shape[0], mix_ref.shape[1]
    block, places = tokens // 2, size // 2
    chosen = jnp.zeros((tokens, experts.shape[1]), F32)
    weight = jnp.zeros((tokens, experts.shape[1]), F32)
    for k in range(ids.shape[1]):
        same = ids[:, k : k + 1] == experts
        chosen = chosen + jnp.where(same, 1.0, 0.0)
        weight = weight + jnp.where(same, gates[:, k : k + 1], 0.0)
    t = lax.broadcasted_iota(jnp.int32, (tokens, tokens), 0)
    u = lax.broadcasted_iota(jnp.int32, (tokens, tokens), 1)
    earlier = jnp.logical_and(u < t, (u >= block) == (t >= block))
    rank = dot(jnp.where(earlier, 1.0, 0.0).astype(BF16), chosen.astype(BF16), ((1,), (0,)))
    rank = jnp.where(chosen > 0.0, rank, -1.0).astype(BF16)
    e = lax.broadcasted_iota(jnp.int32, (experts.shape[1], slots), 0)
    j = lax.broadcasted_iota(jnp.int32, (experts.shape[1], slots), 1)
    spread = jnp.where(jnp.logical_and(j >= e * size, j < (e + 1) * size), 1.0, 0.0).astype(BF16)
    j = lax.broadcasted_iota(jnp.int32, (tokens, slots), 1)
    later = lax.broadcasted_iota(jnp.int32, (tokens, slots), 0) >= block
    place = (j & (places - 1)).astype(F32)
    mine = ((j & places) != 0) == later
    there = jnp.logical_and(dot(rank, spread, ((1,), (0,))) == place, mine)
    if select_ref is not None:
        select_ref[...] = jnp.where(there, 1.0, 0.0).astype(BF16)
    high = weight.astype(BF16)
    low = (weight - high.astype(F32)).astype(BF16)
    mix_ref[0:tokens, :] = jnp.where(there, dot(high, spread, ((1,), (0,))), 0.0).astype(BF16)
    mix_ref[tokens:, :] = jnp.where(there, dot(low, spread, ((1,), (0,))), 0.0).astype(BF16)


def gather_kernel(
    query_ref, key_ref, value_ref, out_ref, extra_ref, ids_ref, gates_ref, experts_ref, cot_ref,
    gate_ref, up_ref, down_ref,
    a_all, b_all, gate_all, up_all, down_all, near_ref, mix_ref, rows_ref,
    a_own, b_own, mix, rows, rows_sem, fill_sem, local_sem, send_sem, recv_sem, away_sem, home_sem, give_sem, take_sem,
):
    y, core, z, x = place()
    fills = []
    for own, refs in ((a_own, (query_ref, key_ref, value_ref)), (b_own, (out_ref, extra_ref))):
        at = 0
        for ref in refs:
            part = own.at[:, pl.ds(at, ref.shape[1])]
            fills.append(pltpu.make_async_copy(ref, part, fill_sem.at[len(fills)]))
            at += ref.shape[1]
    for copy in fills:
        copy.start()
    greet(neighbours() + [opposite()])
    for copy in fills:
        copy.wait()
    shards = ((gate_ref, gate_all), (up_ref, up_all), (down_ref, down_all))
    moved = [
        swap_opposite(p, q, give_sem.at[n], take_sem.at[n]) for n, (p, q) in enumerate(shards)
    ]
    refs, own = (a_all, b_all), (a_own, b_own)
    started = []
    count = [0, 0]

    def chunk(n, i, j):
        return refs[n].at[j, core, i] if n == 0 else refs[n].at[i, core, j]

    def to(n, first, second):
        return device(second, core, first, x) if n == 0 else device(first, core, second, x)

    def send(n, ref, where, slot):
        copy = pltpu.make_async_remote_copy(
            src_ref=ref, dst_ref=ref, send_sem=send_sem.at[n, slot], recv_sem=recv_sem.at[n, slot],
            device_id=where, device_id_type=MESH,
        )
        copy.start()
        started.append(copy)

    def arrived(n, ref, slot):
        pltpu.make_async_remote_copy(
            src_ref=ref, dst_ref=ref, send_sem=send_sem.at[n, slot], recv_sem=recv_sem.at[n, slot],
            device_id=device(y, core, z, x), device_id_type=MESH,
        ).wait_recv()

    homes = []

    def across(n, i, j):
        slot = count[n]
        count[n] += 1
        ref = chunk(n, i, j)
        copy = pltpu.make_async_remote_copy(
            src_ref=ref, dst_ref=ref, send_sem=away_sem.at[n, slot], recv_sem=home_sem.at[n, slot],
            device_id=device(y, 1 - core, z, x), device_id_type=MESH,
        )
        copy.start()
        homes.append(copy)

    def second(n, i, j, k):
        base = 5 + 4 * k
        send(n, chunk(n, i, j), to(n, me[n][0], up(j)), base)
        send(n, chunk(n, i, j), to(n, me[n][0], down(j)), base + 1)
        across(n, i, j)

    up, down = (lambda v: lax.rem(v + 1, RING)), (lambda v: lax.rem(v + RING - 1, RING))
    me = ((z, y), (y, z))
    locals_ = []
    for n in (0, 1):
        i, j = me[n]
        keep = pltpu.make_async_copy(own[n], chunk(n, i, j).at[x], local_sem.at[n])
        keep.start()
        locals_.append(keep)
        copy = pltpu.make_async_remote_copy(
            src_ref=own[n], dst_ref=chunk(n, i, j).at[x], send_sem=send_sem.at[n, 0],
            recv_sem=recv_sem.at[n, 0], device_id=device(y, core, z, 1 - x), device_id_type=MESH,
        )
        copy.start()
        started.append(copy)
    size = rows.shape[0] // (RING * RING * RING)
    ids, gates = ids_ref[...], gates_ref[...]
    route(ids, gates, experts_ref[0:1, :], size, None, mix)
    route(ids, gates, experts_ref[1:2, :], size, near_ref, mix_ref)
    for n in (0, 1):
        i, j = me[n]
        locals_[n].wait()
        arrived(n, chunk(n, i, j).at[1 - x], 0)
        send(n, chunk(n, i, j), to(n, up(i), j), 1)
        send(n, chunk(n, i, j), to(n, down(i), j), 2)
    for n in (0, 1):
        i, j = me[n]
        second(n, i, j, 0)

    @pl.when(jnp.logical_not(native()))
    def _():
        for copy in moved:
            copy.start()

    part, tokens = 256, cot_ref.shape[0]
    for at in range(0, rows.shape[0], part):
        lanes = slice(at, at + part)
        total = dot(mix[0:tokens, lanes], cot_ref[...], ((0,), (0,)))
        total = total + dot(mix[tokens:, lanes], cot_ref[...], ((0,), (0,)))
        rows[lanes, :] = total.astype(BF16)
    keep_rows = pltpu.make_async_copy(rows, rows_ref, rows_sem)
    keep_rows.start()
    for n in (0, 1):
        i, j = me[n]
        arrived(n, chunk(n, down(i), j), 1)
        send(n, chunk(n, down(i), j).at[0], to(n, up(i), j), 3)
        second(n, down(i), j, 1)
    for n in (0, 1):
        i, j = me[n]
        arrived(n, chunk(n, up(i), j), 2)
        send(n, chunk(n, up(i), j).at[1], to(n, down(i), j), 4)
        second(n, up(i), j, 2)
    for n in (0, 1):
        i, j = me[n]
        far = lax.rem(i + 2, RING)
        arrived(n, chunk(n, far, j).at[0], 3)
        arrived(n, chunk(n, far, j).at[1], 4)
        second(n, far, j, 3)
    for k in range(4):
        for n in (0, 1):
            i, j = me[n]
            it = (i, down(i), up(i), lax.rem(i + 2, RING))[k]
            base = 5 + 4 * k
            arrived(n, chunk(n, it, down(j)), base)
            send(n, chunk(n, it, down(j)).at[0], to(n, i, up(j)), base + 2)
            across(n, it, down(j))
            arrived(n, chunk(n, it, up(j)), base + 1)
            send(n, chunk(n, it, up(j)).at[1], to(n, i, down(j)), base + 3)
            across(n, it, up(j))
    for k in range(4):
        for n in (0, 1):
            i, j = me[n]
            it = (i, down(i), up(i), lax.rem(i + 2, RING))[k]
            base = 5 + 4 * k
            far = lax.rem(j + 2, RING)
            arrived(n, chunk(n, it, far).at[0], base + 2)
            arrived(n, chunk(n, it, far).at[1], base + 3)
            across(n, it, far)
    keep_rows.wait()
    for copy in homes:
        copy.wait()
    for copy in started:
        copy.wait_send()

    @pl.when(jnp.logical_not(native()))
    def _():
        for copy in moved:
            copy.wait()


def gather_weights(query, key, value, out, extra, ids, gates, experts, cot, slots, gate, up, down):
    rows = query.shape[0]
    cols = (query.shape[1] + key.shape[1] + value.shape[1], out.shape[1] + extra.shape[1])
    shape = (RING, 2, RING, 2, rows)
    vmem, any_space = (pl.BlockSpec(memory_space=space) for space in (pltpu.VMEM, pl.ANY))
    tokens, width = cot.shape
    routing = [jax.ShapeDtypeStruct((n * tokens, slots), BF16) for n in (1, 2)]
    a_all, b_all, *rest = pl.pallas_call(
        gather_kernel,
        in_specs=[any_space] * 5 + [vmem] * 4 + [any_space] * 3,
        out_specs=[any_space] * 5 + [vmem] * 2 + [any_space],
        out_shape=[jax.ShapeDtypeStruct(shape + (c,), query.dtype) for c in cols]
        + [jax.ShapeDtypeStruct(v.shape, v.dtype) for v in (gate, up, down)]
        + routing + [jax.ShapeDtypeStruct((slots, width), BF16)],
        scratch_shapes=[pltpu.VMEM((rows, c), query.dtype) for c in cols] + [
            pltpu.VMEM((2 * tokens, slots), BF16),
            pltpu.VMEM((slots, width), BF16),
            pltpu.SemaphoreType.DMA,
            pltpu.SemaphoreType.DMA((5,)),
            pltpu.SemaphoreType.DMA((2,)),
            pltpu.SemaphoreType.DMA((2, 21)),
            pltpu.SemaphoreType.DMA((2, 21)),
            pltpu.SemaphoreType.DMA((2, 16)),
            pltpu.SemaphoreType.DMA((2, 16)),
            pltpu.SemaphoreType.DMA((3,)),
            pltpu.SemaphoreType.DMA((3,)),
        ],
        compiler_params=pltpu.CompilerParams(
            collective_id=0, has_side_effects=True, vmem_limit_bytes=VMEM_LIMIT
        ),
        cost_estimate=pl.CostEstimate(flops=0, bytes_accessed=250_000_000, transcendentals=0),
        name="gather_weights",
    )(query, key, value, out, extra, ids, gates, experts, cot, gate, up, down)
    return a_all.reshape(-1, cols[0]), b_all.reshape(-1, cols[1]), rest[:3], rest[3:]


ORDER = (2, 1, 3, 0)
SLICE = 16


def up(v):
    return lax.rem(v + 1, RING)


def down(v):
    return lax.rem(v + RING - 1, RING)


def add_into(target, *terms):
    flat = [target.shape[0]] if len(target.shape) == 3 else []
    for lead in range(flat[0]) if flat else (None,):
        for start in range(0, target.shape[-2], SLICE):
            at = (pl.ds(start, SLICE), slice(None))
            at = at if lead is None else (lead,) + at
            total = terms[0][at].astype(F32)
            for term in terms[1:]:
                total = total + term[at].astype(F32)
            target[at] = total.astype(target.dtype)


def scatter_kernel(
    a_ref, b_ref, extra_ref, wide_ref, tall_ref, y_ref, x_ref,
    a_out, b_out, wide_out, tall_out, y_out, x_out, a_mine, b_mine, a_theirs, b_theirs, a_one, b_one, a_two, b_two,
    a_first, b_first, a_last, b_last, a_x, b_x, load_sem, send_sem, recv_sem,
    gains_here, gains_there,
    extra_load_sem, extra_send_sem, extra_recv_sem, give_sem, take_sem, gains_sem, token_sem,
):
    y, core, z, x = place()
    greet(neighbours() + [other_tp(), opposite()])
    moved = [
        swap_opposite(wide_ref, wide_out, give_sem.at[0], take_sem.at[0]),
        swap_opposite(tall_ref, tall_out, give_sem.at[1], take_sem.at[1]),
    ]

    tokens = [
        pltpu.make_async_remote_copy(
            src_ref=src, dst_ref=dst, send_sem=token_sem.at[n, 0], recv_sem=token_sem.at[n, 1],
            device_id=other_tp(), device_id_type=MESH,
        )
        for n, (src, dst) in enumerate(((y_ref, y_out), (x_ref, x_out)))
    ]
    for copy in tokens:
        copy.start()

    @pl.when(jnp.logical_not(native()))
    def _():
        for copy in moved:
            copy.start()

    grads, outs = (a_ref, b_ref), (a_out, b_out)
    mine, theirs = (a_mine, b_mine), (a_theirs, b_theirs)
    one, two = (a_one, b_one), (a_two, b_two)
    first, last, side = (a_first, b_first), (a_last, b_last), (a_x, b_x)
    me = ((z, y), (y, z))
    sent = []

    def chunk(n, i, j, c):
        return grads[n].at[j, c, i] if n == 0 else grads[n].at[i, c, j]

    def to(n, i, j):
        return device(j, core, i, x) if n == 0 else device(i, core, j, x)

    def copy_of(n, src, dst, slot, where):
        return pltpu.make_async_remote_copy(
            src_ref=src, dst_ref=dst, send_sem=send_sem.at[n, slot], recv_sem=recv_sem.at[n, slot],
            device_id=where, device_id_type=MESH,
        )

    def send(n, src, dst, slot, where):
        copy = copy_of(n, src, dst, slot, where)
        copy.start()
        sent.append(copy)

    def arrived(n, dst, slot):
        copy_of(n, dst, dst, slot, device(y, core, z, x)).wait_recv()

    cols = b_ref.shape[-1]

    def columns(ref, start, count):
        return ref.at[:, :, pl.ds(start, count)]

    def extra_copy(slot):
        ref = columns(theirs[1].at[slot], cols, extra_ref.shape[-1])
        far = extra_ref.at[lax.rem(y + slot // RING, RING), 1 - core, lax.rem(z + slot % RING, RING)]
        return pltpu.make_async_remote_copy(
            src_ref=far, dst_ref=ref, send_sem=extra_send_sem.at[slot],
            recv_sem=extra_recv_sem.at[slot], device_id=device(y, 1 - core, z, x),
            device_id_type=MESH,
        )

    def extra_load(slot):
        near = extra_ref.at[lax.rem(y + slot // RING, RING), core, lax.rem(z + slot % RING, RING)]
        return pltpu.make_async_copy(
            near, columns(mine[1].at[slot], cols, extra_ref.shape[-1]), extra_load_sem.at[slot]
        )

    def load(n, di, dj):
        i, j = me[n]
        slot = di * RING + dj
        target = mine[n].at[slot] if n == 0 else columns(mine[n].at[slot], 0, cols)
        return pltpu.make_async_copy(
            chunk(n, lax.rem(i + di, RING), lax.rem(j + dj, RING), core), target,
            load_sem.at[n, slot],
        )

    for dj in ORDER:
        for di in ORDER:
            for n in (0, 1):
                i, j = me[n]
                slot = di * RING + dj
                there = chunk(n, lax.rem(i + di, RING), lax.rem(j + dj, RING), 1 - core)
                target = theirs[n].at[slot] if n == 0 else columns(theirs[n].at[slot], 0, cols)
                send(n, there, target, slot, device(y, 1 - core, z, x))
                load(n, di, dj).start()
                if n == 1:
                    extra_copy(slot).start()
                    extra_load(slot).start()

    def ready(n, di, dj):
        slot = di * RING + dj
        load(n, di, dj).wait()
        if n == 0:
            arrived(n, theirs[n].at[slot], slot)
        else:
            arrived(n, columns(theirs[n].at[slot], 0, cols), slot)
            extra_load(slot).wait()
            extra_copy(slot).wait_recv()
        return slot

    for di in ORDER:
        for n in (0, 1):
            i, j = me[n]
            slot = ready(n, di, 2)
            add_into(mine[n].at[slot], mine[n].at[slot], theirs[n].at[slot])
            for half in (0, 1):
                send(
                    n, mine[n].at[slot, half], one[n].at[di, half], 16 + di * 2 + half,
                    to(n, i, up(j) if half == 0 else down(j)),
                )
    for di in ORDER:
        for n in (0, 1):
            i, j = me[n]
            for half, dj in ((0, 1), (1, 3)):
                slot = ready(n, di, dj)
                arrived(n, one[n].at[di, half], 16 + di * 2 + half)
                add_into(
                    mine[n].at[slot, half], mine[n].at[slot, half], theirs[n].at[slot, half],
                    one[n].at[di, half],
                )
                add_into(
                    mine[n].at[slot, 1 - half], mine[n].at[slot, 1 - half],
                    theirs[n].at[slot, 1 - half],
                )
                send(
                    n, mine[n].at[slot], two[n].at[di, half], 24 + di * 2 + half,
                    to(n, i, up(j) if half == 0 else down(j)),
                )
    for di in ORDER:
        for n in (0, 1):
            i, j = me[n]
            slot = ready(n, di, 0)
            for half in (0, 1):
                arrived(n, two[n].at[di, half], 24 + di * 2 + half)
            add_into(
                mine[n].at[slot], mine[n].at[slot], theirs[n].at[slot], two[n].at[di, 0],
                two[n].at[di, 1],
            )
            if di == 2:
                for half in (0, 1):
                    send(
                        n, mine[n].at[slot, half], first[n].at[half], 32 + half,
                        to(n, up(i) if half == 0 else down(i), j),
                    )
            elif di != 0:
                half = 0 if di == 1 else 1
                arrived(n, first[n].at[half], 32 + half)
                add_into(mine[n].at[slot, half], mine[n].at[slot, half], first[n].at[half])
                send(
                    n, mine[n].at[slot], last[n].at[half], 34 + half,
                    to(n, up(i) if half == 0 else down(i), j),
                )
    for n in (0, 1):
        for half in (0, 1):
            arrived(n, last[n].at[half], 34 + half)
        add_into(mine[n].at[0], mine[n].at[0], last[n].at[0], last[n].at[1])
        send(n, mine[n].at[0, 1 - x], side[n], 36, device(y, core, z, 1 - x))
    for n in (0, 1):
        arrived(n, side[n], 36)
        add_into(outs[n], mine[n].at[0, x], side[n])
    gains_here[...] = b_out[:, cols:]
    gains = pltpu.make_async_remote_copy(
        src_ref=gains_here, dst_ref=gains_there, send_sem=gains_sem.at[0],
        recv_sem=gains_sem.at[1], device_id=other_tp(), device_id_type=MESH,
    )
    gains.start()
    for copy in sent:
        copy.wait_send()
    for slot in range(RING * RING):
        extra_copy(slot).wait_send()
    gains.wait()
    for copy in tokens:
        copy.wait()
    b_out[:, cols:] = gains_here[...] + gains_there[...]

    @pl.when(jnp.logical_not(native()))
    def _():
        for copy in moved:
            copy.wait()


def scatter_grads(a, b, extra, wide, tall, y, x):
    peers = RING * RING * 4
    rows = a.shape[0] // peers
    shape = (RING, 2, RING, 2, rows)
    cols = (a.shape[1], b.shape[1] + extra.shape[1])
    buffers = []
    for lead in ((16, 2), (16, 2), (4, 2), (4, 2, 2), (2,), (2, 2), ()):
        buffers += [pltpu.VMEM(lead + (rows, c), a.dtype) for c in cols]
    any_space = pl.BlockSpec(memory_space=pl.ANY)
    return pl.pallas_call(
        scatter_kernel,
        in_specs=[any_space] * 7,
        out_specs=[pl.BlockSpec(memory_space=pltpu.VMEM)] * 2 + [any_space] * 4,
        out_shape=[jax.ShapeDtypeStruct((rows, c), F32) for c in cols]
        + [jax.ShapeDtypeStruct(v.shape, v.dtype) for v in (wide, tall, y, x)],
        scratch_shapes=buffers + [
            pltpu.SemaphoreType.DMA((2, 16)),
            pltpu.SemaphoreType.DMA((2, 37)),
            pltpu.SemaphoreType.DMA((2, 37)),
            pltpu.VMEM((rows, extra.shape[1]), F32),
            pltpu.VMEM((rows, extra.shape[1]), F32),
            pltpu.SemaphoreType.DMA((16,)),
            pltpu.SemaphoreType.DMA((16,)),
            pltpu.SemaphoreType.DMA((16,)),
            pltpu.SemaphoreType.DMA((2,)),
            pltpu.SemaphoreType.DMA((2,)),
            pltpu.SemaphoreType.DMA((2,)),
            pltpu.SemaphoreType.DMA((2, 2)),
        ],
        compiler_params=pltpu.CompilerParams(
            collective_id=1, has_side_effects=True, vmem_limit_bytes=44 * 1024 * 1024
        ),
        cost_estimate=pl.CostEstimate(flops=0, bytes_accessed=250_000_000, transcendentals=0),
        name="scatter_grads",
    )(*(v.reshape(shape + (v.shape[1],)) for v in (a, b, extra)), wide, tall, y, x)


CHIPS = RING * RING * RING
GROUP = 16
MIX = 11
AHEAD = 2
TILE = 256


def chip_at(slot, sign):
    f, c, t = lax.axis_index("fsdp"), lax.axis_index("ctx"), lax.axis_index("tp")
    k = lax.rem(slot * MIX, CHIPS) * sign
    turn = 0 if sign > 0 else RING
    far = [lax.div(k, RING * RING), lax.rem(lax.div(k, RING), RING), lax.rem(k, RING)]
    own = [lax.div(f, 2), lax.div(c, 2), t * 2 + lax.rem(c, 2)]
    return [lax.rem(o + d + turn, RING) for o, d in zip(own, far)]


def device_at(slot, sign):
    y, z, x = chip_at(slot, sign)
    core = lax.rem(lax.axis_index("fsdp"), 2)
    return {"fsdp": y * 2 + core, "ctx": z * 2 + lax.rem(x, 2), "tp": lax.div(x, 2)}


def chip_number(slot, sign):
    y, z, x = chip_at(slot, sign)
    return (y * 2 * RING + z * 2 + lax.rem(x, 2)) * 2 + lax.div(x, 2)


def signal_chips(barrier):
    f, c, t = lax.axis_index("fsdp"), lax.axis_index("ctx"), lax.axis_index("tp")
    y, z, x = lax.div(f, 2), lax.div(c, 2), t * 2 + lax.rem(c, 2)
    core = lax.rem(f, 2)
    line = [lax.rem(x + d, RING) for d in range(RING)]
    line = [(lax.rem(v, 2), lax.div(v, 2)) for v in line]

    def plane(i, carry):
        far_y = lax.rem(y + lax.div(i, RING), RING) * 2 + core
        far_z = lax.rem(z + lax.rem(i, RING), RING) * 2
        for d, (low, high) in enumerate(line):

            @pl.when(jnp.logical_or(i > 0, d > 0))
            def _(low=low, high=high):
                pl.semaphore_signal(
                    barrier, inc=1, device_id={"fsdp": far_y, "ctx": far_z + low, "tp": high},
                    device_id_type=MESH,
                )

        return carry

    lax.fori_loop(0, RING * RING, plane, 0)


def other_core():
    f = lax.axis_index("fsdp")
    return {"fsdp": f + 1 - 2 * (f % 2)}


def moe_kernel(
    send_ref, deo_ref, gate_ref, up_ref, down_ref, gate_far, up_far, down_far,
    back_ref, eo_ref, wide_ref, tall_ref,
    rows, deos, gu, down, z, dgu, wide, tall, give, take,
    go_sem, come_sem, load_sem, weight_sem, share_send, share_recv, part_send, part_recv,
    back_send, back_recv, eo_sem,
):
    size, hidden = send_ref.shape[1], down_ref.shape[0]
    count = GROUP * size
    groups = CHIPS // GROUP
    width = down_ref.shape[1]

    def each(body, low, high):
        def step(i, carry):
            body(i)
            return carry

        lax.fori_loop(low, high, step, 0)

    barrier = pltpu.get_barrier_semaphore()
    signal_chips(barrier)
    pl.semaphore_signal(barrier, inc=1, device_id=other_core(), device_id_type=MESH)
    pl.semaphore_wait(barrier, CHIPS)

    def slot_rows(s):
        return pl.ds(pl.multiple_of(s * size, size), size)

    def group_rows(g):
        return pl.ds(pl.multiple_of(g * count, count), count)

    def go(s):
        return remote(
            send_ref.at[s], rows.at[0, slot_rows(s)], go_sem.at[s], come_sem.at[s], device_at(s, 1)
        )

    def stay(s):
        return pltpu.make_async_copy(send_ref.at[s], rows.at[0, slot_rows(s)], come_sem.at[s])

    def load(s):
        return pltpu.make_async_copy(
            deo_ref.at[chip_number(s, -1)], deos.at[0, slot_rows(s)], load_sem.at[s]
        )

    def sent_rows(n, s):
        slot = lax.rem(lax.div(s, GROUP), 2)
        return give.at[n, slot, slot_rows(lax.rem(s, GROUP))]

    def back(s):
        return remote(
            sent_rows(0, s), back_ref.at[s], back_send.at[s], back_recv.at[s], device_at(s, -1)
        )

    def back_stay():
        return pltpu.make_async_copy(
            give.at[0, 0, pl.ds(0, size)], back_ref.at[0], back_recv.at[0]
        )

    def out(s):
        return pltpu.make_async_copy(
            sent_rows(1, s), eo_ref.at[s], eo_sem.at[s]
        )

    def share(n, g):
        ref = (rows, deos)[n]
        return remote(
            ref.at[0, group_rows(g)], ref.at[1, group_rows(g)], share_send.at[n, g],
            share_recv.at[n, g], other_core(),
        )

    def part(n, g):
        slot = lax.rem(g, 2)
        return remote(
            give.at[n, slot], take.at[n, slot], part_send.at[n, g], part_recv.at[n, g],
            other_core(),
        )

    places = (gu.at[:, pl.ds(0, hidden)], gu.at[:, pl.ds(hidden, hidden)], down)
    weights = [
        [pltpu.make_async_copy(src, dst, weight_sem.at[n]) for n, (src, dst) in enumerate(pairs)]
        for pairs in (
            zip((gate_ref, up_ref, down_ref), places), zip((gate_far, up_far, down_far), places)
        )
    ]

    def on_weights(act):
        for condition, copies in zip((native(), jnp.logical_not(native())), weights):

            @pl.when(condition)
            def _(copies=copies):
                for copy in copies:
                    act(copy)

    stay(0).start()
    each(lambda s: go(s).start(), 1, AHEAD * GROUP)
    each(lambda s: load(s).start(), 0, CHIPS)
    on_weights(lambda copy: copy.start())

    def tiles(body):
        each(lambda i: body(pl.ds(pl.multiple_of(i * TILE, TILE), TILE)), 0, width // TILE)

    def clear(at):
        wide[at, :] = jnp.zeros((TILE, 2 * hidden), F32)
        tall[:, at] = jnp.zeros((hidden, TILE), F32)

    tiles(clear)

    def through(side, g):
        at = group_rows(g)
        pre = dot(rows[side, at, :], gu[...], ((1,), (0,)))
        dz = dot(deos[side, at, :], down[...], ((1,), (1,)))
        gate, u = pre[:, :hidden], pre[:, hidden:]
        sig = 1.0 / (1.0 + jnp.exp(-gate))
        act = gate * sig
        z[side] = (act * u).astype(BF16)
        dgu[side, :, :hidden] = (dz * u * sig * (1.0 + gate * (1.0 - sig))).astype(BF16)
        dgu[side, :, hidden:] = (dz * act).astype(BF16)

    def to_rows(side):
        return dot(dgu[side], gu[...], ((1,), (1,)))

    def to_outputs(side):
        return dot(z[side], down[...], ((1,), (0,)))

    on_weights(lambda copy: copy.wait())

    def group(g):
        first, last, slot = g * GROUP, (g + 1) * GROUP, lax.rem(g, 2)

        @pl.when(g == 0)
        def _():
            stay(0).wait()

        each(lambda s: go(s).wait_recv(), lax.max(first, 1), last)
        each(lambda s: load(s).wait(), first, last)
        each(
            lambda s: go(s).start(), lax.min(first + AHEAD * GROUP, CHIPS),
            lax.min(last + AHEAD * GROUP, CHIPS),
        )
        for n in (0, 1):
            share(n, g).start()
        through(0, g)
        for n in (0, 1):
            share(n, g).wait_recv()
        through(1, g)

        @pl.when(g >= 2)
        def _():
            @pl.when(g == 2)
            def _():
                back_stay().wait()

            each(lambda s: back(s).wait_send(), lax.max(first - 2 * GROUP, 1), last - 2 * GROUP)
            each(lambda s: out(s).wait(), first - 2 * GROUP, last - 2 * GROUP)

        give[0, slot] = to_rows(1).astype(BF16)
        part(0, g).start()
        give[1, slot] = to_outputs(1).astype(BF16)
        part(1, g).start()
        own = to_rows(0)
        part(0, g).wait()
        give[0, slot] = (own + take[0, slot].astype(F32)).astype(BF16)

        @pl.when(g == 0)
        def _():
            back_stay().start()

        each(lambda s: back(s).start(), lax.max(first, 1), last)
        own = to_outputs(0)
        part(1, g).wait()
        give[1, slot] = (own + take[1, slot].astype(F32)).astype(BF16)
        each(lambda s: out(s).start(), first, last)
        at = group_rows(g)

        def weight_grads(cols):
            wide[cols, :] += dot(rows[0, at, cols], dgu[0], ((0,), (0,))) + dot(
                rows[1, at, cols], dgu[1], ((0,), (0,))
            )
            tall[:, cols] += dot(z[0], deos[0, at, cols], ((0,), (0,))) + dot(
                z[1], deos[1, at, cols], ((0,), (0,))
            )

        tiles(weight_grads)

    each(group, 0, groups)

    def store(at):
        wide_ref[at, :] = wide[at, :].astype(BF16)
        tall_ref[:, at] = tall[:, at].astype(BF16)

    tiles(store)
    for g in range(groups):
        for n in (0, 1):
            share(n, g).wait_send()
    each(lambda s: out(s).wait(), (groups - 2) * GROUP, CHIPS)
    each(lambda s: back(s).wait_send(), (groups - 2) * GROUP, CHIPS)
    each(lambda s: go(s).wait_send(), 1, CHIPS)
    each(lambda s: back(s).wait_recv(), 1, CHIPS)


def moe(send, d_eo, own, far):
    chips, size, width = send.shape
    hidden = own[2].shape[0]
    total, groups = chips * size, chips // GROUP
    count = GROUP * size
    vmem, any_space = (pl.BlockSpec(memory_space=space) for space in (pltpu.VMEM, pl.ANY))
    shapes = [send.shape, send.shape, (width, 2 * hidden), (hidden, width)]
    dma = pltpu.SemaphoreType.DMA
    return pl.pallas_call(
        moe_kernel,
        in_specs=[any_space] * 8,
        out_specs=[any_space] * 2 + [vmem] * 2,
        out_shape=[jax.ShapeDtypeStruct(shape, BF16) for shape in shapes],
        scratch_shapes=[
            pltpu.VMEM((2, total, width), BF16),
            pltpu.VMEM((2, total, width), BF16),
            pltpu.VMEM((width, 2 * hidden), BF16),
            pltpu.VMEM((hidden, width), BF16),
            pltpu.VMEM((2, count, hidden), BF16),
            pltpu.VMEM((2, count, 2 * hidden), BF16),
            pltpu.VMEM((width, 2 * hidden), F32),
            pltpu.VMEM((hidden, width), F32),
            pltpu.VMEM((2, 2, count, width), BF16),
            pltpu.VMEM((2, 2, count, width), BF16),
            dma((chips,)), dma((chips,)), dma((chips,)), dma((3,)),
            dma((2, groups)), dma((2, groups)), dma((2, groups)), dma((2, groups)),
            dma((chips,)), dma((chips,)), dma((chips,)),
        ],
        compiler_params=pltpu.CompilerParams(
            collective_id=4, has_side_effects=True, vmem_limit_bytes=56 * 1024 * 1024
        ),
        cost_estimate=pl.CostEstimate(flops=0, bytes_accessed=400_000_000, transcendentals=0),
        name="experts",
    )(send, d_eo, *own, *far)


BLOCK = 64
CTX = 8
WIDE = 256


def rotated(u, gain, cosine, sine):
    scaling = lax.rsqrt(jnp.mean(u * u, axis=-1, keepdims=True) + EPS)
    normed = u * scaling
    n = normed * gain
    rot = n * cosine + pltpu.roll(n, HEAD_SIZE // 2, 1) * sine
    return rot.astype(BF16), normed, scaling


def rotated_back(e, normed, scaling, gain, cosine, sine):
    back = e * cosine + pltpu.roll(e * sine, HEAD_SIZE // 2, 1)
    scaled = back * gain
    inner = jnp.mean(scaled * normed, axis=-1, keepdims=True)
    return scaling * (scaled - normed * inner), jnp.sum(back * normed, axis=0, keepdims=True)


def ctx_peer(step):
    return {"ctx": lax.rem(lax.axis_index("ctx") + step, CTX)}


def beside():
    c = lax.axis_index("ctx")
    return {"ctx": c + 1 - 2 * lax.rem(c, 2)}


def softmax_parts(q_low, k, bias):
    s = dot(q_low, k, ((1,), (1,))) * (HEAD_SIZE ** -0.5) + bias
    e = jnp.exp(s - jnp.max(s, axis=-1, keepdims=True))
    return e / jnp.sum(e, axis=-1, keepdims=True)


def share_kernel(kv, rows_ref, cos_ref, sin_ref, gk_ref, kv_ref, held, send_sem, recv_sem):
    c = lax.axis_index("ctx")
    greet([ctx_peer(step) for step in range(1, CTX)])
    micro, rows = held.shape[0], 2 * BLOCK
    cosine, sine, gk = cos_ref[...], sin_ref[...], gk_ref[...]
    mine = pl.ds(pl.multiple_of(c * BLOCK, BLOCK), BLOCK)
    earlier, own = pl.ds(CTX * BLOCK, BLOCK), pl.ds((CTX + 1) * BLOCK, BLOCK)
    copies = []
    for m in range(micro):
        span = slice(m * rows, (m + 1) * rows)
        for h in range(2 * kv):
            cols = slice(h * HEAD_SIZE, (h + 1) * HEAD_SIZE)
            u = rows_ref[span, cols]
            low = rotated(u, gk, cosine, sine)[0] if h < kv else u.astype(BF16)
            held[m, mine, cols] = low[:BLOCK]
            held[m, own, cols] = low[BLOCK:]
        for step in range(1, CTX):
            part = held.at[m, mine]
            copies.append(
                remote(part, part, send_sem.at[step, m], recv_sem.at[step, m], ctx_peer(step))
            )
        copies.append(
            remote(
                held.at[m, own], held.at[m, earlier], send_sem.at[0, m], recv_sem.at[0, m], beside()
            )
        )
        for copy in copies[-CTX:]:
            copy.start()
    for m in range(micro):
        for step in range(1, CTX):
            source = lax.rem(c + CTX - step, CTX)
            part = held.at[m, pl.ds(pl.multiple_of(source * BLOCK, BLOCK), BLOCK)]
            remote(
                part, part, send_sem.at[step, m], recv_sem.at[step, m], ctx_peer(step)
            ).wait_recv()
        copies[(m + 1) * CTX - 1].wait_recv()
        kv_ref[m] = held[m]
    for copy in copies:
        copy.wait_send()


def attention_kernel(heads, q_ref, cos_ref, sin_ref, gq_ref, bias_ref, k_ref, v_ref, o_ref):
    cosine, sine, gq = cos_ref[...], sin_ref[...], gq_ref[...]
    for e in range(heads):
        cols = slice(e * HEAD_SIZE, (e + 1) * HEAD_SIZE)
        q_low = rotated(q_ref[:, cols], gq, cosine, sine)[0]
        p = softmax_parts(q_low, k_ref[...], bias_ref[...]).astype(BF16)
        o_ref[:, cols] = dot(p, v_ref[...], ((1,), (0,))).astype(BF16)


def backward_kernel(
    kv, heads, qkv_ref, cos_ref, sin_ref, gq_ref, gk_ref, bias_ref, kv_ref, o_ref, a_ref,
    select_ref, middle_ref, cot_ref, gain_moe_ref, w_out_ref, w_qkv_ref, eo_ref, back_ref,
    given_grad_ref, gains_ref, d_h_ref, moe_ref, grad_qkv_ref, grad_out_ref, eo_back_ref,
    w_out, w_qkv, dattn_ref, back_tile, d_b, do_ref, dqkv_ref, part_sum, wide_tile, tall_tile, grads, given, given_side,
    p_all, ds_all, q_all, do_all, swap_give, swap_take,
    send_sem, recv_sem, load_sem, tile_sem, swap_sem, share_sem, back_sem, eo_send, eo_recv,
):
    c, tp = lax.axis_index("ctx"), lax.axis_index("tp")
    width = w_out.shape[0]

    def each(body, low, high):
        def step(i, carry):
            body(i)
            return carry

        lax.fori_loop(low, high, step, 0)

    def tile(i):
        return pl.ds(pl.multiple_of(i * WIDE, WIDE), WIDE)

    def back_load(i):
        slot = lax.rem(i, 2)
        return pltpu.make_async_copy(
            back_ref.at[:, tile(i)], back_tile.at[slot], back_sem.at[i]
        )

    back_load(0).start()
    barrier = pltpu.get_barrier_semaphore()
    signal_chips(barrier)
    loads = [
        pltpu.make_async_copy(w_out_ref.at[:, pl.ds(0, w_out.shape[1])], w_out, load_sem.at[0]),
        pltpu.make_async_copy(w_qkv_ref, w_qkv, load_sem.at[1]),
    ]
    for copy in loads:
        copy.start()
    pl.semaphore_wait(barrier, CHIPS - 1)

    def output(s):
        return remote(
            eo_ref.at[s], eo_back_ref.at[s], eo_send.at[s], eo_recv.at[s], device_at(s, -1)
        )

    def outputs(quarter):
        each(lambda s: output(s).start(), max(quarter * GROUP, 1), (quarter + 1) * GROUP)

    stay = pltpu.make_async_copy(eo_ref.at[0], eo_back_ref.at[0], eo_recv.at[0])
    stay.start()
    outputs(0)
    micro, rows = grads.shape[0], 2 * BLOCK
    q_cols = kv * heads * HEAD_SIZE
    scale = HEAD_SIZE ** -0.5
    cosine, sine, gq, gk = cos_ref[...], sin_ref[...], gq_ref[...], gk_ref[...]
    mine = pl.ds(pl.multiple_of(c * BLOCK, BLOCK), BLOCK)
    earlier, own = pl.ds(CTX * BLOCK, BLOCK), pl.ds((CTX + 1) * BLOCK, BLOCK)

    def combine(i):
        @pl.when(i + 1 < width // WIDE)
        def _():
            back_load(i + 1).start()

        back_load(i).wait()
        d_b[:, tile(i)] = dot(select_ref[...], back_tile[lax.rem(i, 2)], ((1,), (0,)))

    each(combine, 0, width // WIDE)
    moe_total = jnp.zeros((1, width), F32)
    shares = []
    for m in range(micro):
        span = slice(m * BLOCK, (m + 1) * BLOCK)
        u, g = middle_ref[span, :], d_b[span, :]
        scaling = lax.rsqrt(jnp.mean(u * u, axis=-1, keepdims=True) + EPS)
        normed = u * scaling
        moe_total = moe_total + jnp.sum(g * normed, axis=0, keepdims=True)
        scaled = g * gain_moe_ref[...]
        inner = jnp.mean(scaled * normed, axis=-1, keepdims=True)
        d_h = cot_ref[span, :].astype(F32) + scaling * (scaled - normed * inner)
        d_h_ref[span, :] = d_h
        place = pl.ds(pl.multiple_of(m * rows + (1 - tp) * BLOCK, BLOCK), BLOCK)
        dattn_ref[place, :] = d_h.astype(BF16)
        part = dattn_ref.at[place]
        shares.append(remote(part, part, share_sem.at[0, m], share_sem.at[1, m], {"tp": 1 - tp}))
        shares[-1].start()
    moe_ref[...] = moe_total
    for m in range(micro):
        place = pl.ds(pl.multiple_of(m * rows + tp * BLOCK, BLOCK), BLOCK)
        part = dattn_ref.at[place]
        remote(part, part, share_sem.at[0, m], share_sem.at[1, m], {"tp": 1 - tp}).wait_recv()
    outputs(1)
    loads[0].wait()

    def outputs_back(i):
        do_ref[:, tile(i)] = dot(dattn_ref[...], w_out[:, tile(i)], ((1,), (0,))).astype(BF16)

    each(outputs_back, 0, w_out.shape[1] // WIDE)

    def head_cols(h):
        return pl.ds(pl.multiple_of(h * HEAD_SIZE, HEAD_SIZE), HEAD_SIZE)

    def keys_back(m, h, carry):
        span = slice(m * rows, (m + 1) * rows)
        k, v = kv_ref[m, :, head_cols(h)], kv_ref[m, :, head_cols(kv + h)]
        for e in range(heads):
            cols = head_cols(h * heads + e)
            stack = slice(e * rows, (e + 1) * rows)
            q_low = rotated(qkv_ref[span, cols], gq, cosine, sine)[0]
            q_all[stack, :] = q_low
            p = softmax_parts(q_low, k, bias_ref[...])
            p_all[stack, :] = p.astype(BF16)
            do = do_ref[span, cols]
            do_all[stack, :] = do
            dp = dot(do, v, ((1,), (1,)))
            ds = (p * (dp - jnp.sum(dp * p, axis=-1, keepdims=True))).astype(BF16)
            ds_all[m * kv + h, stack, :] = ds
        grads[m, :, head_cols(kv + h)] = dot(p_all[...], do_all[...], ((0,), (0,))).astype(BF16)
        d_k = dot(ds_all[m * kv + h], q_all[...], ((0,), (0,))) * scale
        grads[m, :, head_cols(h)] = d_k.astype(BF16)
        return carry

    def queries_back(m, h, total):
        span = slice(m * rows, (m + 1) * rows)
        k = kv_ref[m, :, head_cols(h)]
        for e in range(heads):
            cols = head_cols(h * heads + e)
            ds = ds_all[m * kv + h, e * rows : (e + 1) * rows, :]
            dqr = (dot(ds, k, ((1,), (0,))) * scale).astype(BF16).astype(F32)
            u = qkv_ref[span, cols]
            scaling = lax.rsqrt(jnp.mean(u * u, axis=-1, keepdims=True) + EPS)
            dq, part = rotated_back(dqr, u * scaling, scaling, gq, cosine, sine)
            dqkv_ref[span, cols] = dq.astype(BF16)
            total = total + part
        return total

    copies = []
    for m in range(micro):
        lax.fori_loop(0, kv, functools.partial(keys_back, m), 0)
        for step in range(1, CTX):
            peer = lax.rem(c + step, CTX)
            part = grads.at[m, pl.ds(pl.multiple_of(peer * BLOCK, BLOCK), BLOCK)]
            copies.append(
                remote(
                    part, given.at[step - 1, m], send_sem.at[step, m], recv_sem.at[step, m],
                    ctx_peer(step),
                )
            )
        copies.append(
            remote(
                grads.at[m, earlier], given_side.at[m], send_sem.at[0, m], recv_sem.at[0, m],
                beside(),
            )
        )
        for copy in copies[-CTX:]:
            copy.start()
        if m == micro - 1:
            outputs(2)
    total = jnp.zeros((1, HEAD_SIZE), F32)
    for m in range(micro):
        total = lax.fori_loop(0, kv, functools.partial(queries_back, m), total)

    def tiles_out(buffer, left, right, out_ref, sems):
        def copy_out(i):
            slot = lax.rem(i, 2)
            return pltpu.make_async_copy(buffer.at[slot], out_ref.at[tile(i)], sems.at[i])

        def step(i):
            @pl.when(i >= 2)
            def _():
                copy_out(i - 2).wait()

            value = dot(left[:, tile(i)], right[...], ((0,), (0,)))
            buffer[lax.rem(i, 2)] = value.astype(BF16)
            copy_out(i).start()

        count = width // WIDE
        each(step, 0, count)
        return lambda: each(lambda i: copy_out(i).wait(), count - 2, count)

    end_out = tiles_out(tall_tile, dattn_ref, o_ref, grad_out_ref, tile_sem.at[0])
    loads[1].wait()

    def queries_in(i):
        part_sum[:, tile(i)] = dot(dqkv_ref[:, :q_cols], w_qkv[tile(i), :q_cols], ((1,), (1,)))

    each(queries_in, 0, width // WIDE)
    k_total = jnp.zeros((1, HEAD_SIZE), F32)
    for m in range(micro):
        for copy in copies[m * CTX : (m + 1) * CTX]:
            copy.wait_recv()
        for h in range(2 * kv):
            cols = slice(h * HEAD_SIZE, (h + 1) * HEAD_SIZE)
            at = slice(q_cols + h * HEAD_SIZE, q_cols + (h + 1) * HEAD_SIZE)
            prompt = grads[m, mine, cols].astype(F32)
            for step in range(CTX - 1):
                prompt = prompt + given[step, m, :, cols].astype(F32)
            cont = grads[m, own, cols].astype(F32) + given_side[m, :, cols].astype(F32)
            e = jnp.concatenate([prompt, cont], axis=0).astype(BF16)
            span = slice(m * rows, (m + 1) * rows)
            if h < kv:
                _, normed, scaling = rotated(qkv_ref[span, at], gk, cosine, sine)
                d, part = rotated_back(e.astype(F32), normed, scaling, gk, cosine, sine)
                k_total = k_total + part
                dqkv_ref[span, at] = d.astype(BF16)
            else:
                dqkv_ref[span, at] = e
    gains_ref[0:1, :] = total
    gains_ref[1:2, :] = k_total

    def keys_in(i):
        part_sum[:, tile(i)] += dot(dqkv_ref[:, q_cols:], w_qkv[tile(i), q_cols:], ((1,), (1,)))

    each(keys_in, 0, width // WIDE)
    for m in range(micro):
        away = pl.ds(pl.multiple_of(m * rows + tp * BLOCK, BLOCK), BLOCK)
        swap_give[m * BLOCK : (m + 1) * BLOCK, :] = part_sum[away, :].astype(BF16)
    swap = remote(swap_give, swap_take, swap_sem.at[0], swap_sem.at[1], {"tp": 1 - tp})
    swap.start()
    outputs(3)
    end_qkv = tiles_out(wide_tile, a_ref, dqkv_ref, grad_qkv_ref, tile_sem.at[1])
    swap.wait()
    for m in range(micro):
        kept = pl.ds(pl.multiple_of(m * rows + (1 - tp) * BLOCK, BLOCK), BLOCK)
        span = slice(m * BLOCK, (m + 1) * BLOCK)
        given_grad_ref[span, :] = part_sum[kept, :] + swap_take[span, :].astype(F32)
    for copy in copies + shares:
        copy.wait_send()
    end_out()
    end_qkv()
    stay.wait()
    each(lambda s: output(s).wait(), 1, CHIPS)


def share_keys(qkv, cosine, sine, gain_key, kv, keys, micro):
    rows, cols = qkv.shape[0], 2 * kv * HEAD_SIZE
    last = qkv.shape[1] // cols - 1

    def whole(shape):
        return pl.BlockSpec(shape, lambda i: (0,) * len(shape))

    return pl.pallas_call(
        functools.partial(share_kernel, kv),
        grid=(1,),
        in_specs=[pl.BlockSpec((rows, cols), lambda i: (0, last)), whole(cosine.shape)]
        + [whole(sine.shape), whole(gain_key.shape)],
        out_specs=whole((micro, keys, cols)),
        out_shape=jax.ShapeDtypeStruct((micro, keys, cols), BF16),
        scratch_shapes=[
            pltpu.VMEM((micro, keys, cols), BF16),
            pltpu.SemaphoreType.DMA((CTX, micro)),
            pltpu.SemaphoreType.DMA((CTX, micro)),
        ],
        compiler_params=pltpu.CompilerParams(
            collective_id=2, has_side_effects=True, vmem_limit_bytes=VMEM_LIMIT
        ),
        cost_estimate=pl.CostEstimate(flops=0, bytes_accessed=50_000_000, transcendentals=0),
        name="share_keys",
    )(qkv, cosine, sine, gain_key)


def attention(qkv, cosine, sine, gain_query, bias, kv_all, kv):
    micro, keys, cols = kv_all.shape
    rows = bias.shape[0]
    heads = qkv.shape[1] // HEAD_SIZE // kv - 2
    width = heads * HEAD_SIZE

    def whole(v):
        return pl.BlockSpec(v.shape, lambda m, g: (0,) * v.ndim)

    return pl.pallas_call(
        functools.partial(attention_kernel, heads),
        grid=(micro, kv),
        in_specs=[pl.BlockSpec((rows, width), lambda m, g: (m, g))]
        + [whole(v) for v in (cosine, sine, gain_query, bias)]
        + [
            pl.BlockSpec((None, keys, HEAD_SIZE), lambda m, g: (m, 0, g)),
            pl.BlockSpec((None, keys, HEAD_SIZE), lambda m, g: (m, 0, kv + g)),
        ],
        out_specs=pl.BlockSpec((rows, width), lambda m, g: (m, g)),
        out_shape=jax.ShapeDtypeStruct((micro * rows, kv * width), BF16),
        compiler_params=pltpu.CompilerParams(vmem_limit_bytes=VMEM_LIMIT),
        cost_estimate=pl.CostEstimate(flops=0, bytes_accessed=60_000_000, transcendentals=0),
        name="attention_forward",
    )(qkv, cosine, sine, gain_query, bias, kv_all, kv_all)


def backward(qkv, heads_in, kv_all, o, a, moe_in, w_out, w_qkv, eo, back, kv):
    heads = qkv.shape[1] // HEAD_SIZE // kv - 2
    bias = heads_in[-1]
    rows, keys = bias.shape
    micro, _, kv_cols = kv_all.shape
    width, cols = w_qkv.shape
    total, q_cols = qkv.shape[0], kv * heads * HEAD_SIZE
    vmem, any_space = (pl.BlockSpec(memory_space=space) for space in (pltpu.VMEM, pl.ANY))
    dma = pltpu.SemaphoreType.DMA
    return pl.pallas_call(
        functools.partial(backward_kernel, kv, heads),
        in_specs=[vmem] * 13 + [any_space] * 4,
        out_specs=[vmem] * 4 + [any_space] * 3,
        out_shape=[
            jax.ShapeDtypeStruct((micro * BLOCK, width), F32),
            jax.ShapeDtypeStruct((2, HEAD_SIZE), F32),
            jax.ShapeDtypeStruct((micro * BLOCK, width), F32),
            jax.ShapeDtypeStruct((1, width), F32),
            jax.ShapeDtypeStruct((width, cols), BF16),
            jax.ShapeDtypeStruct((width, q_cols), BF16),
            jax.ShapeDtypeStruct(eo.shape, BF16),
        ],
        scratch_shapes=[
            pltpu.VMEM((width, q_cols), BF16),
            pltpu.VMEM((width, cols), BF16),
            pltpu.VMEM((total, width), BF16),
            pltpu.VMEM((2, back.shape[0], WIDE), BF16),
            pltpu.VMEM((micro * BLOCK, width), F32),
            pltpu.VMEM((total, q_cols), BF16),
            pltpu.VMEM((total, cols), BF16),
            pltpu.VMEM((total, width), F32),
            pltpu.VMEM((2, WIDE, cols), BF16),
            pltpu.VMEM((2, WIDE, q_cols), BF16),
            pltpu.VMEM((micro, keys, kv_cols), BF16),
            pltpu.VMEM((CTX - 1, micro, BLOCK, kv_cols), BF16),
            pltpu.VMEM((micro, BLOCK, kv_cols), BF16),
            pltpu.VMEM((heads * rows, keys), BF16),
            pltpu.VMEM((micro * kv, heads * rows, keys), BF16),
            pltpu.VMEM((heads * rows, HEAD_SIZE), BF16),
            pltpu.VMEM((heads * rows, HEAD_SIZE), BF16),
            pltpu.VMEM((micro * BLOCK, width), BF16),
            pltpu.VMEM((micro * BLOCK, width), BF16),
            dma((CTX, micro)), dma((CTX, micro)), dma((2,)), dma((2, width // WIDE)), dma((2,)),
            dma((2, micro)), dma((width // WIDE,)),
            dma((CHIPS,)), dma((CHIPS,)),
        ],
        compiler_params=pltpu.CompilerParams(
            collective_id=3, has_side_effects=True, vmem_limit_bytes=60 * 1024 * 1024
        ),
        cost_estimate=pl.CostEstimate(flops=0, bytes_accessed=250_000_000, transcendentals=0),
        name="attention_backward",
    )(qkv, *heads_in, kv_all, o, a, *moe_in, w_out, w_qkv, eo, back)


def normalize(rows, gain):
    scaling = lax.rsqrt(jnp.mean(rows * rows, axis=-1, keepdims=True) + EPS)
    return rows * scaling * gain, scaling


def normalize_back(rows, scaling, gain, upstream):
    normed = rows * scaling
    gain_grad = jnp.sum((upstream * normed).reshape(-1, rows.shape[-1]), axis=0)
    scaled = upstream * gain
    inner = jnp.mean(scaled * normed, axis=-1, keepdims=True)
    return scaling * (scaled - normed * inner), gain_grad


def swap_tp(value):
    return lax.ppermute(value, "tp", [(0, 1), (1, 0)])


def local(
    x_prompt, x_cont, cot_prompt, cot_cont, ids_prompt, ids_cont, gates_prompt, gates_cont,
    norm_gain, query_weight, key_matrix, value_matrix, out_weight, query_gain, key_gain, moe_gain,
    expert_gate, expert_up, expert_down,
):
    micro = x_prompt.shape[0]
    prompt_rows, cont_rows, width = x_prompt.shape[2], x_cont.shape[2], x_prompt.shape[3]
    block = cont_rows
    rows = 2 * block
    s = lax.axis_index("ctx")
    ctx = lax.axis_size("ctx")
    first = lax.axis_index("tp") == 0
    peers = lax.axis_size(ALL)
    q_cols, kv_cols = query_weight.shape[1], key_matrix.shape[1]
    kv = kv_cols // HEAD_SIZE
    qkv_cols = q_cols + 2 * kv_cols
    shard_rows = query_weight.shape[0]
    hidden = expert_gate.shape[2]
    slots = cont_rows * TOPK // peers

    fsdp, tp = lax.axis_size("fsdp"), lax.axis_size("tp")
    chips = [(2 * y, c, t) for y in range(fsdp // 2) for c in range(ctx) for t in range(tp)]
    groups = [[((f + core) * ctx + c) * tp + t for f, c, t in chips] for core in range(2)]
    expert_of = jnp.array([(f + t) * ctx + c for f, c, t in chips], jnp.int32)

    def exchange(rows_of):
        return lax.all_to_all(
            rows_of, ("fsdp", "ctx", "tp"), split_axis=0, concat_axis=0, tiled=True,
            axis_index_groups=groups,
        )

    def pad(v):
        return jnp.pad(v[:, 0], ((0, 0), (0, block - prompt_rows), (0, 0)))

    x_first, x_second = pad(x_prompt), x_cont[:, 0]
    own_tokens = jnp.where(first, x_second, x_first).astype(F32)
    own_cot = jnp.where(first, cot_cont[:, 0], pad(cot_prompt))
    ids_pad = jnp.pad(
        ids_prompt[:, 0], ((0, 0), (0, block - prompt_rows), (0, 0)), constant_values=-1
    )
    own_ids = jnp.where(first, ids_cont[:, 0], ids_pad)
    own_gates = jnp.where(first, gates_cont[:, 0], pad(gates_prompt))

    y, z, x = chip_at(jnp.arange(peers, dtype=jnp.int32), 1)
    near = (2 * y + x // 2) * ctx + 2 * z + x % 2
    order = jnp.pad(jnp.stack([expert_of, near]), ((0, 0), (0, HEAD_SIZE - peers)), constant_values=-2)

    def lanes(v):
        return jnp.pad(v, [(0, 0)] * (v.ndim - 1) + [(0, HEAD_SIZE - v.shape[-1])])

    extra = jnp.stack([lanes(v) for v in (norm_gain, moe_gain, query_gain, key_gain)])
    extra = jnp.pad(extra, ((0, shard_rows - extra.shape[0]), (0, 0)))
    own_experts = (expert_gate[0], expert_up[0], expert_down[0])
    w_qkv, w_out_extra, far_experts, routing = gather_weights(
        query_weight, key_matrix, value_matrix, out_weight, extra,
        own_ids.reshape(-1, TOPK), own_gates.reshape(-1, TOPK), order,
        own_cot.reshape(-1, width), peers * micro * slots, *own_experts,
    )
    select_near, mixing, spread = routing
    w_out = w_out_extra[:, :q_cols]
    gains = w_out_extra[:, q_cols:].reshape(peers, shard_rows, HEAD_SIZE)[:, :4].astype(F32)
    gain_in, gain_moe = (gains[:, n, :shard_rows].reshape(-1) for n in (0, 1))
    head_rows = query_gain.shape[0]
    gain_query, gain_key = (gains[:, n, :head_rows].reshape(-1) for n in (2, 3))

    offsets = jnp.arange(rows, dtype=jnp.int32)
    is_prompt = offsets < block
    prompt_pos = s * prompt_rows + offsets
    cont_pos = s * cont_rows + offsets - block
    rot_place = jnp.where(is_prompt, prompt_pos, PROMPT + cont_pos % CL).astype(F32)
    steps_freq = jnp.arange(HEAD_SIZE // 2, dtype=F32) * (2.0 / HEAD_SIZE)
    angles = rot_place[:, None] * jnp.power(THETA, -steps_freq)[None, :]
    cosine, sine = jnp.cos(angles), jnp.sin(angles)
    cosine = jnp.concatenate([cosine, cosine], axis=1)
    sine = jnp.concatenate([-sine, sine], axis=1)
    keys = (ctx + 2) * block
    key_index = jnp.arange(keys, dtype=jnp.int32)[None, :]
    key_off = key_index % block
    key_prompt_pos = key_index // block * prompt_rows + key_off
    key_cont = (s - 1) * cont_rows + key_index - ctx * block
    is_cont = jnp.logical_not(is_prompt)[:, None]
    visible = jnp.where(
        key_index < ctx * block,
        jnp.logical_and(
            key_off < prompt_rows,
            jnp.logical_or(is_cont, key_prompt_pos <= prompt_pos[:, None]),
        ),
        jnp.logical_and(
            is_cont,
            jnp.logical_and(
                key_cont // CL == cont_pos[:, None] // CL, key_cont <= cont_pos[:, None]
            ),
        ),
    )
    bias = jnp.where(visible, 0.0, NEG).astype(F32)

    def arranged(own, other):
        return jnp.where(first, other, own), jnp.where(first, own, other)

    def sum_own(part):
        part = part.reshape(micro, rows, width)
        given = jnp.where(first, part[:, :block], part[:, block:]).astype(BF16)
        kept = jnp.where(first, part[:, block:], part[:, :block])
        return kept + swap_tp(given).astype(F32)

    tokens = jnp.concatenate([x_first, x_second], axis=1).astype(F32).reshape(-1, width)
    a = normalize(tokens, gain_in)[0].astype(BF16)
    qkv = dot(a, w_qkv, ((1,), (0,)))
    heads_in = (cosine, sine, gain_query[None], gain_key[None], bias)
    kv_all = share_keys(qkv, cosine, sine, gain_key[None], kv, keys, micro)

    spread, kv_all = lax.optimization_barrier((spread, kv_all))
    d_eo_rows = exchange(spread).reshape(peers, micro * slots, width)
    o = attention(qkv, cosine, sine, gain_query[None], bias, kv_all, kv)
    middle = own_tokens + sum_own(dot(o, w_out, ((1,), (1,))))
    b_normed, b_scale = normalize(middle, gain_moe)
    b_low = b_normed.astype(BF16)

    send = dot(select_near, b_low.reshape(-1, width), ((0,), (0,))).astype(BF16)
    back, eo, wide_here, tall_here = moe(
        send.reshape(d_eo_rows.shape), d_eo_rows, own_experts, far_experts
    )
    moe_in = (
        select_near, middle.reshape(-1, width), own_cot.reshape(-1, width), gain_moe[None]
    )
    input_grad, head_totals, d_h, moe_total, grad_qkv, grad_out, eo_back = backward(
        qkv, heads_in, kv_all, o, a, moe_in, w_out_extra, w_qkv, eo, back.reshape(-1, width), kv
    )
    d_h = d_h.reshape(middle.shape)
    moe_out = dot(mixing, eo_back.reshape(-1, width), ((1,), (0,)))
    moe_out = (moe_out[: micro * block] + moe_out[micro * block :]).reshape(middle.shape)
    y_own = (middle + moe_out).astype(BF16)
    scale_in = lax.rsqrt(jnp.mean(own_tokens * own_tokens, axis=-1, keepdims=True) + EPS)
    token_from, norm_total = normalize_back(
        own_tokens, scale_in, gain_in, input_grad.reshape(own_tokens.shape)
    )
    x_own = (d_h + token_from).astype(BF16)

    extra_grads = jnp.stack(
        [
            lanes(v.reshape(peers, -1))
            for v in (norm_total, moe_total, head_totals[0], head_totals[1])
        ],
        axis=1,
    )
    extra_grads = jnp.pad(extra_grads, ((0, 0), (0, shard_rows - extra_grads.shape[1]), (0, 0)))
    extra_grads = extra_grads.reshape(-1, HEAD_SIZE).astype(BF16)
    share, share_out, wide_there, tall_there, y_other, x_other = scatter_grads(
        grad_qkv, grad_out, extra_grads, wide_here, tall_here, y_own, x_own
    )
    out_first, out_second = arranged(y_own, y_other)
    grad_first, grad_second = arranged(x_own, x_other)
    grad_wide = jnp.where(native(), wide_here, wide_there).astype(F32)
    grad_down = jnp.where(native(), tall_here, tall_there).astype(F32)
    gain_share = share_out[:, q_cols:]
    return (
        out_first[:, None, :prompt_rows],
        out_second[:, None],
        grad_first[:, None, :prompt_rows],
        grad_second[:, None],
        gain_share[0, :shard_rows],
        share[:, :q_cols],
        share[:, q_cols : q_cols + kv_cols],
        share[:, q_cols + kv_cols : qkv_cols],
        share_out[:, :q_cols],
        gain_share[2, :head_rows],
        gain_share[3, :head_rows],
        gain_share[1, :shard_rows],
        grad_wide[None, :, :hidden],
        grad_wide[None, :, hidden:],
        grad_down[None],
    )


def solution(mesh):
    rows = P(None, "fsdp", "ctx", None)
    vector = P(("fsdp", "ctx"))
    matrix = P(("fsdp", "ctx"), "tp")
    wide = P(("fsdp", "ctx"), None, "tp")
    tall = P(("fsdp", "ctx"), "tp", None)
    in_specs = (rows,) * 8 + (vector,) + (matrix,) * 4 + (vector,) * 3 + (wide, wide, tall)
    out_specs = (rows,) * 4 + (vector,) + (matrix,) * 4 + (vector,) * 3 + (wide, wide, tall)
    return jax.shard_map(local, mesh=mesh, in_specs=in_specs, out_specs=out_specs, check_vma=False)
```

```python
import functools

import jax
import jax.numpy as jnp
from jax import lax
from jax.experimental import pallas as pl
from jax.experimental.pallas import tpu as pltpu
from jax.sharding import PartitionSpec as P

HEAD_SIZE = 128
TOPK = 8
PROMPT = 448
CL = 128
EPS = 1e-06
THETA = 1000000.0
NEG = -1e30
F32 = jnp.float32
BF16 = jnp.bfloat16
ALL = ("fsdp", "ctx")
MESH = pl.DeviceIdType.MESH
RING = 4
VMEM_LIMIT = 48 * 1024 * 1024


def dot(a, b, dims):
    return lax.dot_general(a, b, (dims, ((), ())), preferred_element_type=F32)


def remote(src, dst, send_sem, recv_sem, where):
    return pltpu.make_async_remote_copy(
        src_ref=src, dst_ref=dst, send_sem=send_sem, recv_sem=recv_sem, device_id=where,
        device_id_type=MESH,
    )


def place():
    f, c = lax.axis_index("fsdp"), lax.axis_index("ctx")
    return f // 2, f % 2, c // 2, c % 2


def device(y, core, z, x):
    return {"fsdp": y * 2 + core, "ctx": z * 2 + x}


def greet(partners):
    barrier = pltpu.get_barrier_semaphore()
    for partner in partners:
        pl.semaphore_signal(barrier, inc=1, device_id=partner, device_id_type=MESH)
    pl.semaphore_wait(barrier, len(partners))


def neighbours():
    y, core, z, x = place()
    up, down = (lambda v: lax.rem(v + 1, RING)), (lambda v: lax.rem(v + RING - 1, RING))
    return [
        device(y, core, z, 1 - x),
        device(y, 1 - core, z, x),
        device(up(y), core, z, x),
        device(down(y), core, z, x),
        device(y, core, up(z), x),
        device(y, core, down(z), x),
    ]


def other_tp():
    return {"tp": 1 - lax.axis_index("tp")}


def opposite():
    f = lax.axis_index("fsdp")
    return {"fsdp": f + 1 - 2 * (f % 2), "tp": 1 - lax.axis_index("tp")}


def native():
    return lax.axis_index("fsdp") % 2 == lax.axis_index("tp")


def swap_opposite(src, dst, send_sem, recv_sem):
    return pltpu.make_async_remote_copy(
        src_ref=src, dst_ref=dst, send_sem=send_sem, recv_sem=recv_sem, device_id=opposite(),
        device_id_type=MESH,
    )


def route(ids, gates, experts, size, select_ref, mix_ref):
    tokens, slots = ids.shape[0], mix_ref.shape[1]
    block, places = tokens // 2, size // 2
    chosen = jnp.zeros((tokens, experts.shape[1]), F32)
    weight = jnp.zeros((tokens, experts.shape[1]), F32)
    for k in range(ids.shape[1]):
        same = ids[:, k : k + 1] == experts
        chosen = chosen + jnp.where(same, 1.0, 0.0)
        weight = weight + jnp.where(same, gates[:, k : k + 1], 0.0)
    t = lax.broadcasted_iota(jnp.int32, (tokens, tokens), 0)
    u = lax.broadcasted_iota(jnp.int32, (tokens, tokens), 1)
    earlier = jnp.logical_and(u < t, (u >= block) == (t >= block))
    rank = dot(jnp.where(earlier, 1.0, 0.0).astype(BF16), chosen.astype(BF16), ((1,), (0,)))
    rank = jnp.where(chosen > 0.0, rank, -1.0).astype(BF16)
    e = lax.broadcasted_iota(jnp.int32, (experts.shape[1], slots), 0)
    j = lax.broadcasted_iota(jnp.int32, (experts.shape[1], slots), 1)
    spread = jnp.where(jnp.logical_and(j >= e * size, j < (e + 1) * size), 1.0, 0.0).astype(BF16)
    j = lax.broadcasted_iota(jnp.int32, (tokens, slots), 1)
    later = lax.broadcasted_iota(jnp.int32, (tokens, slots), 0) >= block
    place = (j & (places - 1)).astype(F32)
    mine = ((j & places) != 0) == later
    there = jnp.logical_and(dot(rank, spread, ((1,), (0,))) == place, mine)
    if select_ref is not None:
        select_ref[...] = jnp.where(there, 1.0, 0.0).astype(BF16)
    high = weight.astype(BF16)
    low = (weight - high.astype(F32)).astype(BF16)
    mix_ref[0:tokens, :] = jnp.where(there, dot(high, spread, ((1,), (0,))), 0.0).astype(BF16)
    mix_ref[tokens:, :] = jnp.where(there, dot(low, spread, ((1,), (0,))), 0.0).astype(BF16)


def gather_kernel(
    query_ref, key_ref, value_ref, out_ref, extra_ref, ids_ref, gates_ref, experts_ref, cot_ref,
    gate_ref, up_ref, down_ref,
    a_all, b_all, gate_all, up_all, down_all, near_ref, mix_ref, rows_ref,
    a_own, b_own, mix, rows, rows_sem, fill_sem, local_sem, send_sem, recv_sem, away_sem, home_sem, give_sem, take_sem,
):
    y, core, z, x = place()
    fills = []
    for own, refs in ((a_own, (query_ref, key_ref, value_ref)), (b_own, (out_ref, extra_ref))):
        at = 0
        for ref in refs:
            part = own.at[:, pl.ds(at, ref.shape[1])]
            fills.append(pltpu.make_async_copy(ref, part, fill_sem.at[len(fills)]))
            at += ref.shape[1]
    for copy in fills:
        copy.start()
    greet(neighbours() + [opposite()])
    for copy in fills:
        copy.wait()
    shards = ((gate_ref, gate_all), (up_ref, up_all), (down_ref, down_all))
    moved = [
        swap_opposite(p, q, give_sem.at[n], take_sem.at[n]) for n, (p, q) in enumerate(shards)
    ]
    refs, own = (a_all, b_all), (a_own, b_own)
    started = []
    count = [0, 0]

    def chunk(n, i, j):
        return refs[n].at[j, core, i] if n == 0 else refs[n].at[i, core, j]

    def to(n, first, second):
        return device(second, core, first, x) if n == 0 else device(first, core, second, x)

    def send(n, ref, where, slot):
        copy = pltpu.make_async_remote_copy(
            src_ref=ref, dst_ref=ref, send_sem=send_sem.at[n, slot], recv_sem=recv_sem.at[n, slot],
            device_id=where, device_id_type=MESH,
        )
        copy.start()
        started.append(copy)

    def arrived(n, ref, slot):
        pltpu.make_async_remote_copy(
            src_ref=ref, dst_ref=ref, send_sem=send_sem.at[n, slot], recv_sem=recv_sem.at[n, slot],
            device_id=device(y, core, z, x), device_id_type=MESH,
        ).wait_recv()

    homes = []

    def across(n, i, j):
        slot = count[n]
        count[n] += 1
        ref = chunk(n, i, j)
        copy = pltpu.make_async_remote_copy(
            src_ref=ref, dst_ref=ref, send_sem=away_sem.at[n, slot], recv_sem=home_sem.at[n, slot],
            device_id=device(y, 1 - core, z, x), device_id_type=MESH,
        )
        copy.start()
        homes.append(copy)

    def second(n, i, j, k):
        base = 5 + 4 * k
        send(n, chunk(n, i, j), to(n, me[n][0], up(j)), base)
        send(n, chunk(n, i, j), to(n, me[n][0], down(j)), base + 1)
        across(n, i, j)

    up, down = (lambda v: lax.rem(v + 1, RING)), (lambda v: lax.rem(v + RING - 1, RING))
    me = ((z, y), (y, z))
    locals_ = []
    for n in (0, 1):
        i, j = me[n]
        keep = pltpu.make_async_copy(own[n], chunk(n, i, j).at[x], local_sem.at[n])
        keep.start()
        locals_.append(keep)
        copy = pltpu.make_async_remote_copy(
            src_ref=own[n], dst_ref=chunk(n, i, j).at[x], send_sem=send_sem.at[n, 0],
            recv_sem=recv_sem.at[n, 0], device_id=device(y, core, z, 1 - x), device_id_type=MESH,
        )
        copy.start()
        started.append(copy)
    size = rows.shape[0] // (RING * RING * RING)
    ids, gates = ids_ref[...], gates_ref[...]
    route(ids, gates, experts_ref[0:1, :], size, None, mix)
    route(ids, gates, experts_ref[1:2, :], size, near_ref, mix_ref)
    for n in (0, 1):
        i, j = me[n]
        locals_[n].wait()
        arrived(n, chunk(n, i, j).at[1 - x], 0)
        send(n, chunk(n, i, j), to(n, up(i), j), 1)
        send(n, chunk(n, i, j), to(n, down(i), j), 2)
    for n in (0, 1):
        i, j = me[n]
        second(n, i, j, 0)

    @pl.when(jnp.logical_not(native()))
    def _():
        for copy in moved:
            copy.start()

    part, tokens = 256, cot_ref.shape[0]
    for at in range(0, rows.shape[0], part):
        lanes = slice(at, at + part)
        total = dot(mix[0:tokens, lanes], cot_ref[...], ((0,), (0,)))
        total = total + dot(mix[tokens:, lanes], cot_ref[...], ((0,), (0,)))
        rows[lanes, :] = total.astype(BF16)
    keep_rows = pltpu.make_async_copy(rows, rows_ref, rows_sem)
    keep_rows.start()
    for n in (0, 1):
        i, j = me[n]
        arrived(n, chunk(n, down(i), j), 1)
        send(n, chunk(n, down(i), j).at[0], to(n, up(i), j), 3)
        second(n, down(i), j, 1)
    for n in (0, 1):
        i, j = me[n]
        arrived(n, chunk(n, up(i), j), 2)
        send(n, chunk(n, up(i), j).at[1], to(n, down(i), j), 4)
        second(n, up(i), j, 2)
    for n in (0, 1):
        i, j = me[n]
        far = lax.rem(i + 2, RING)
        arrived(n, chunk(n, far, j).at[0], 3)
        arrived(n, chunk(n, far, j).at[1], 4)
        second(n, far, j, 3)
    for k in range(4):
        for n in (0, 1):
            i, j = me[n]
            it = (i, down(i), up(i), lax.rem(i + 2, RING))[k]
            base = 5 + 4 * k
            arrived(n, chunk(n, it, down(j)), base)
            send(n, chunk(n, it, down(j)).at[0], to(n, i, up(j)), base + 2)
            across(n, it, down(j))
            arrived(n, chunk(n, it, up(j)), base + 1)
            send(n, chunk(n, it, up(j)).at[1], to(n, i, down(j)), base + 3)
            across(n, it, up(j))
    for k in range(4):
        for n in (0, 1):
            i, j = me[n]
            it = (i, down(i), up(i), lax.rem(i + 2, RING))[k]
            base = 5 + 4 * k
            far = lax.rem(j + 2, RING)
            arrived(n, chunk(n, it, far).at[0], base + 2)
            arrived(n, chunk(n, it, far).at[1], base + 3)
            across(n, it, far)
    keep_rows.wait()
    for copy in homes:
        copy.wait()
    for copy in started:
        copy.wait_send()

    @pl.when(jnp.logical_not(native()))
    def _():
        for copy in moved:
            copy.wait()


def gather_weights(query, key, value, out, extra, ids, gates, experts, cot, slots, gate, up, down):
    rows = query.shape[0]
    cols = (query.shape[1] + key.shape[1] + value.shape[1], out.shape[1] + extra.shape[1])
    shape = (RING, 2, RING, 2, rows)
    vmem, any_space = (pl.BlockSpec(memory_space=space) for space in (pltpu.VMEM, pl.ANY))
    tokens, width = cot.shape
    routing = [jax.ShapeDtypeStruct((n * tokens, slots), BF16) for n in (1, 2)]
    a_all, b_all, *rest = pl.pallas_call(
        gather_kernel,
        in_specs=[any_space] * 5 + [vmem] * 4 + [any_space] * 3,
        out_specs=[any_space] * 5 + [vmem] * 2 + [any_space],
        out_shape=[jax.ShapeDtypeStruct(shape + (c,), query.dtype) for c in cols]
        + [jax.ShapeDtypeStruct(v.shape, v.dtype) for v in (gate, up, down)]
        + routing + [jax.ShapeDtypeStruct((slots, width), BF16)],
        scratch_shapes=[pltpu.VMEM((rows, c), query.dtype) for c in cols] + [
            pltpu.VMEM((2 * tokens, slots), BF16),
            pltpu.VMEM((slots, width), BF16),
            pltpu.SemaphoreType.DMA,
            pltpu.SemaphoreType.DMA((5,)),
            pltpu.SemaphoreType.DMA((2,)),
            pltpu.SemaphoreType.DMA((2, 21)),
            pltpu.SemaphoreType.DMA((2, 21)),
            pltpu.SemaphoreType.DMA((2, 16)),
            pltpu.SemaphoreType.DMA((2, 16)),
            pltpu.SemaphoreType.DMA((3,)),
            pltpu.SemaphoreType.DMA((3,)),
        ],
        compiler_params=pltpu.CompilerParams(
            collective_id=0, has_side_effects=True, vmem_limit_bytes=VMEM_LIMIT
        ),
        cost_estimate=pl.CostEstimate(flops=0, bytes_accessed=250_000_000, transcendentals=0),
        name="gather_weights",
    )(query, key, value, out, extra, ids, gates, experts, cot, gate, up, down)
    return a_all.reshape(-1, cols[0]), b_all.reshape(-1, cols[1]), rest[:3], rest[3:]


ORDER = (2, 1, 3, 0)
SLICE = 16


def up(v):
    return lax.rem(v + 1, RING)


def down(v):
    return lax.rem(v + RING - 1, RING)


def add_into(target, *terms):
    flat = [target.shape[0]] if len(target.shape) == 3 else []
    for lead in range(flat[0]) if flat else (None,):
        for start in range(0, target.shape[-2], SLICE):
            at = (pl.ds(start, SLICE), slice(None))
            at = at if lead is None else (lead,) + at
            total = terms[0][at].astype(F32)
            for term in terms[1:]:
                total = total + term[at].astype(F32)
            target[at] = total.astype(target.dtype)


def scatter_kernel(
    a_ref, b_ref, extra_ref, wide_ref, tall_ref, y_ref,
    a_out, b_out, wide_out, tall_out, y_out, a_mine, b_mine, a_theirs, b_theirs, a_one, b_one, a_two, b_two,
    a_first, b_first, a_last, b_last, a_x, b_x, load_sem, send_sem, recv_sem,
    gains_here, gains_there,
    extra_load_sem, extra_send_sem, extra_recv_sem, give_sem, take_sem, gains_sem, token_sem,
):
    y, core, z, x = place()
    greet(neighbours() + [other_tp(), opposite()])
    moved = [
        swap_opposite(wide_ref, wide_out, give_sem.at[0], take_sem.at[0]),
        swap_opposite(tall_ref, tall_out, give_sem.at[1], take_sem.at[1]),
    ]

    tokens = [
        pltpu.make_async_remote_copy(
            src_ref=src, dst_ref=dst, send_sem=token_sem.at[n, 0], recv_sem=token_sem.at[n, 1],
            device_id=other_tp(), device_id_type=MESH,
        )
        for n, (src, dst) in enumerate(((y_ref, y_out),))
    ]
    for copy in tokens:
        copy.start()

    @pl.when(jnp.logical_not(native()))
    def _():
        for copy in moved:
            copy.start()

    grads, outs = (a_ref, b_ref), (a_out, b_out)
    mine, theirs = (a_mine, b_mine), (a_theirs, b_theirs)
    one, two = (a_one, b_one), (a_two, b_two)
    first, last, side = (a_first, b_first), (a_last, b_last), (a_x, b_x)
    me = ((z, y), (y, z))
    sent = []

    def chunk(n, i, j, c):
        return grads[n].at[j, c, i] if n == 0 else grads[n].at[i, c, j]

    def to(n, i, j):
        return device(j, core, i, x) if n == 0 else device(i, core, j, x)

    def copy_of(n, src, dst, slot, where):
        return pltpu.make_async_remote_copy(
            src_ref=src, dst_ref=dst, send_sem=send_sem.at[n, slot], recv_sem=recv_sem.at[n, slot],
            device_id=where, device_id_type=MESH,
        )

    def send(n, src, dst, slot, where):
        copy = copy_of(n, src, dst, slot, where)
        copy.start()
        sent.append(copy)

    def arrived(n, dst, slot):
        copy_of(n, dst, dst, slot, device(y, core, z, x)).wait_recv()

    cols = b_ref.shape[-1]

    def columns(ref, start, count):
        return ref.at[:, :, pl.ds(start, count)]

    def extra_copy(slot):
        ref = columns(theirs[1].at[slot], cols, extra_ref.shape[-1])
        far = extra_ref.at[lax.rem(y + slot // RING, RING), 1 - core, lax.rem(z + slot % RING, RING)]
        return pltpu.make_async_remote_copy(
            src_ref=far, dst_ref=ref, send_sem=extra_send_sem.at[slot],
            recv_sem=extra_recv_sem.at[slot], device_id=device(y, 1 - core, z, x),
            device_id_type=MESH,
        )

    def extra_load(slot):
        near = extra_ref.at[lax.rem(y + slot // RING, RING), core, lax.rem(z + slot % RING, RING)]
        return pltpu.make_async_copy(
            near, columns(mine[1].at[slot], cols, extra_ref.shape[-1]), extra_load_sem.at[slot]
        )

    def load(n, di, dj):
        i, j = me[n]
        slot = di * RING + dj
        target = mine[n].at[slot] if n == 0 else columns(mine[n].at[slot], 0, cols)
        return pltpu.make_async_copy(
            chunk(n, lax.rem(i + di, RING), lax.rem(j + dj, RING), core), target,
            load_sem.at[n, slot],
        )

    for dj in ORDER:
        for di in ORDER:
            for n in (0, 1):
                i, j = me[n]
                slot = di * RING + dj
                there = chunk(n, lax.rem(i + di, RING), lax.rem(j + dj, RING), 1 - core)
                target = theirs[n].at[slot] if n == 0 else columns(theirs[n].at[slot], 0, cols)
                send(n, there, target, slot, device(y, 1 - core, z, x))
                load(n, di, dj).start()
                if n == 1:
                    extra_copy(slot).start()
                    extra_load(slot).start()

    def ready(n, di, dj):
        slot = di * RING + dj
        load(n, di, dj).wait()
        if n == 0:
            arrived(n, theirs[n].at[slot], slot)
        else:
            arrived(n, columns(theirs[n].at[slot], 0, cols), slot)
            extra_load(slot).wait()
            extra_copy(slot).wait_recv()
        return slot

    for di in ORDER:
        for n in (0, 1):
            i, j = me[n]
            slot = ready(n, di, 2)
            add_into(mine[n].at[slot], mine[n].at[slot], theirs[n].at[slot])
            for half in (0, 1):
                send(
                    n, mine[n].at[slot, half], one[n].at[di, half], 16 + di * 2 + half,
                    to(n, i, up(j) if half == 0 else down(j)),
                )
    for di in ORDER:
        for n in (0, 1):
            i, j = me[n]
            for half, dj in ((0, 1), (1, 3)):
                slot = ready(n, di, dj)
                arrived(n, one[n].at[di, half], 16 + di * 2 + half)
                add_into(
                    mine[n].at[slot, half], mine[n].at[slot, half], theirs[n].at[slot, half],
                    one[n].at[di, half],
                )
                add_into(
                    mine[n].at[slot, 1 - half], mine[n].at[slot, 1 - half],
                    theirs[n].at[slot, 1 - half],
                )
                send(
                    n, mine[n].at[slot], two[n].at[di, half], 24 + di * 2 + half,
                    to(n, i, up(j) if half == 0 else down(j)),
                )
    for di in ORDER:
        for n in (0, 1):
            i, j = me[n]
            slot = ready(n, di, 0)
            for half in (0, 1):
                arrived(n, two[n].at[di, half], 24 + di * 2 + half)
            add_into(
                mine[n].at[slot], mine[n].at[slot], theirs[n].at[slot], two[n].at[di, 0],
                two[n].at[di, 1],
            )
            if di == 2:
                for half in (0, 1):
                    send(
                        n, mine[n].at[slot, half], first[n].at[half], 32 + half,
                        to(n, up(i) if half == 0 else down(i), j),
                    )
            elif di != 0:
                half = 0 if di == 1 else 1
                arrived(n, first[n].at[half], 32 + half)
                add_into(mine[n].at[slot, half], mine[n].at[slot, half], first[n].at[half])
                send(
                    n, mine[n].at[slot], last[n].at[half], 34 + half,
                    to(n, up(i) if half == 0 else down(i), j),
                )
    for n in (0, 1):
        for half in (0, 1):
            arrived(n, last[n].at[half], 34 + half)
        add_into(mine[n].at[0], mine[n].at[0], last[n].at[0], last[n].at[1])
        send(n, mine[n].at[0, 1 - x], side[n], 36, device(y, core, z, 1 - x))
    for n in (0, 1):
        arrived(n, side[n], 36)
        add_into(outs[n], mine[n].at[0, x], side[n])
    gains_here[...] = b_out[:, cols:]
    gains = pltpu.make_async_remote_copy(
        src_ref=gains_here, dst_ref=gains_there, send_sem=gains_sem.at[0],
        recv_sem=gains_sem.at[1], device_id=other_tp(), device_id_type=MESH,
    )
    gains.start()
    for copy in sent:
        copy.wait_send()
    for slot in range(RING * RING):
        extra_copy(slot).wait_send()
    gains.wait()
    for copy in tokens:
        copy.wait()
    b_out[:, cols:] = gains_here[...] + gains_there[...]

    @pl.when(jnp.logical_not(native()))
    def _():
        for copy in moved:
            copy.wait()


def scatter_grads(a, b, extra, wide, tall, y):
    peers = RING * RING * 4
    rows = a.shape[0] // peers
    shape = (RING, 2, RING, 2, rows)
    cols = (a.shape[1], b.shape[1] + extra.shape[1])
    buffers = []
    for lead in ((16, 2), (16, 2), (4, 2), (4, 2, 2), (2,), (2, 2), ()):
        buffers += [pltpu.VMEM(lead + (rows, c), a.dtype) for c in cols]
    any_space = pl.BlockSpec(memory_space=pl.ANY)
    return pl.pallas_call(
        scatter_kernel,
        in_specs=[any_space] * 6,
        out_specs=[pl.BlockSpec(memory_space=pltpu.VMEM)] * 2 + [any_space] * 3,
        out_shape=[jax.ShapeDtypeStruct((rows, c), F32) for c in cols]
        + [jax.ShapeDtypeStruct(v.shape, v.dtype) for v in (wide, tall, y)],
        scratch_shapes=buffers + [
            pltpu.SemaphoreType.DMA((2, 16)),
            pltpu.SemaphoreType.DMA((2, 37)),
            pltpu.SemaphoreType.DMA((2, 37)),
            pltpu.VMEM((rows, extra.shape[1]), F32),
            pltpu.VMEM((rows, extra.shape[1]), F32),
            pltpu.SemaphoreType.DMA((16,)),
            pltpu.SemaphoreType.DMA((16,)),
            pltpu.SemaphoreType.DMA((16,)),
            pltpu.SemaphoreType.DMA((2,)),
            pltpu.SemaphoreType.DMA((2,)),
            pltpu.SemaphoreType.DMA((2,)),
            pltpu.SemaphoreType.DMA((2, 2)),
        ],
        compiler_params=pltpu.CompilerParams(
            collective_id=1, has_side_effects=True, vmem_limit_bytes=44 * 1024 * 1024
        ),
        cost_estimate=pl.CostEstimate(flops=0, bytes_accessed=250_000_000, transcendentals=0),
        name="scatter_grads",
    )(*(v.reshape(shape + (v.shape[1],)) for v in (a, b, extra)), wide, tall, y)


CHIPS = RING * RING * RING
GROUP = 16
MIX = 11
AHEAD = 2
TILE = 256


def chip_at(slot, sign):
    f, c, t = lax.axis_index("fsdp"), lax.axis_index("ctx"), lax.axis_index("tp")
    k = lax.rem(slot * MIX, CHIPS) * sign
    turn = 0 if sign > 0 else RING
    far = [lax.div(k, RING * RING), lax.rem(lax.div(k, RING), RING), lax.rem(k, RING)]
    own = [lax.div(f, 2), lax.div(c, 2), t * 2 + lax.rem(c, 2)]
    return [lax.rem(o + d + turn, RING) for o, d in zip(own, far)]


def device_at(slot, sign):
    y, z, x = chip_at(slot, sign)
    core = lax.rem(lax.axis_index("fsdp"), 2)
    return {"fsdp": y * 2 + core, "ctx": z * 2 + lax.rem(x, 2), "tp": lax.div(x, 2)}


def chip_number(slot, sign):
    y, z, x = chip_at(slot, sign)
    return (y * 2 * RING + z * 2 + lax.rem(x, 2)) * 2 + lax.div(x, 2)


def signal_chips(barrier):
    f, c, t = lax.axis_index("fsdp"), lax.axis_index("ctx"), lax.axis_index("tp")
    y, z, x = lax.div(f, 2), lax.div(c, 2), t * 2 + lax.rem(c, 2)
    core = lax.rem(f, 2)
    line = [lax.rem(x + d, RING) for d in range(RING)]
    line = [(lax.rem(v, 2), lax.div(v, 2)) for v in line]

    def plane(i, carry):
        far_y = lax.rem(y + lax.div(i, RING), RING) * 2 + core
        far_z = lax.rem(z + lax.rem(i, RING), RING) * 2
        for d, (low, high) in enumerate(line):

            @pl.when(jnp.logical_or(i > 0, d > 0))
            def _(low=low, high=high):
                pl.semaphore_signal(
                    barrier, inc=1, device_id={"fsdp": far_y, "ctx": far_z + low, "tp": high},
                    device_id_type=MESH,
                )

        return carry

    lax.fori_loop(0, RING * RING, plane, 0)


def other_core():
    f = lax.axis_index("fsdp")
    return {"fsdp": f + 1 - 2 * (f % 2)}


def moe_kernel(
    send_ref, deo_ref, gate_ref, up_ref, down_ref, gate_far, up_far, down_far,
    back_ref, eo_ref, wide_ref, tall_ref,
    rows, deos, gu, down, z, dgu, wide, tall, give, take,
    go_sem, come_sem, load_sem, weight_sem, share_send, share_recv, part_send, part_recv,
    back_send, back_recv, eo_sem,
):
    size, hidden = send_ref.shape[1], down_ref.shape[0]
    count = GROUP * size
    groups = CHIPS // GROUP
    width = down_ref.shape[1]

    def each(body, low, high):
        def step(i, carry):
            body(i)
            return carry

        lax.fori_loop(low, high, step, 0)

    barrier = pltpu.get_barrier_semaphore()
    signal_chips(barrier)
    pl.semaphore_signal(barrier, inc=1, device_id=other_core(), device_id_type=MESH)
    pl.semaphore_wait(barrier, CHIPS)

    def slot_rows(s):
        return pl.ds(pl.multiple_of(s * size, size), size)

    def group_rows(g):
        return pl.ds(pl.multiple_of(g * count, count), count)

    def go(s):
        return remote(
            send_ref.at[s], rows.at[0, slot_rows(s)], go_sem.at[s], come_sem.at[s], device_at(s, 1)
        )

    def stay(s):
        return pltpu.make_async_copy(send_ref.at[s], rows.at[0, slot_rows(s)], come_sem.at[s])

    def load(s):
        return pltpu.make_async_copy(
            deo_ref.at[chip_number(s, -1)], deos.at[0, slot_rows(s)], load_sem.at[s]
        )

    def sent_rows(n, s):
        slot = lax.rem(lax.div(s, GROUP), 2)
        return give.at[n, slot, slot_rows(lax.rem(s, GROUP))]

    def back(s):
        return remote(
            sent_rows(0, s), back_ref.at[s], back_send.at[s], back_recv.at[s], device_at(s, -1)
        )

    def back_stay():
        return pltpu.make_async_copy(
            give.at[0, 0, pl.ds(0, size)], back_ref.at[0], back_recv.at[0]
        )

    def out(s):
        return pltpu.make_async_copy(
            sent_rows(1, s), eo_ref.at[s], eo_sem.at[s]
        )

    def share(n, g):
        ref = (rows, deos)[n]
        return remote(
            ref.at[0, group_rows(g)], ref.at[1, group_rows(g)], share_send.at[n, g],
            share_recv.at[n, g], other_core(),
        )

    def part(n, g):
        slot = lax.rem(g, 2)
        return remote(
            give.at[n, slot], take.at[n, slot], part_send.at[n, g], part_recv.at[n, g],
            other_core(),
        )

    places = (gu.at[:, pl.ds(0, hidden)], gu.at[:, pl.ds(hidden, hidden)], down)
    weights = [
        [pltpu.make_async_copy(src, dst, weight_sem.at[n]) for n, (src, dst) in enumerate(pairs)]
        for pairs in (
            zip((gate_ref, up_ref, down_ref), places), zip((gate_far, up_far, down_far), places)
        )
    ]

    def on_weights(act):
        for condition, copies in zip((native(), jnp.logical_not(native())), weights):

            @pl.when(condition)
            def _(copies=copies):
                for copy in copies:
                    act(copy)

    stay(0).start()
    each(lambda s: go(s).start(), 1, AHEAD * GROUP)
    each(lambda s: load(s).start(), 0, CHIPS)
    on_weights(lambda copy: copy.start())

    def tiles(body):
        each(lambda i: body(pl.ds(pl.multiple_of(i * TILE, TILE), TILE)), 0, width // TILE)

    def clear(at):
        wide[at, :] = jnp.zeros((TILE, 2 * hidden), F32)
        tall[:, at] = jnp.zeros((hidden, TILE), F32)

    tiles(clear)

    def through(side, g):
        at = group_rows(g)
        pre = dot(rows[side, at, :], gu[...], ((1,), (0,)))
        dz = dot(deos[side, at, :], down[...], ((1,), (1,)))
        gate, u = pre[:, :hidden], pre[:, hidden:]
        sig = 1.0 / (1.0 + jnp.exp(-gate))
        act = gate * sig
        z[side] = (act * u).astype(BF16)
        dgu[side, :, :hidden] = (dz * u * sig * (1.0 + gate * (1.0 - sig))).astype(BF16)
        dgu[side, :, hidden:] = (dz * act).astype(BF16)

    def to_rows(side):
        return dot(dgu[side], gu[...], ((1,), (1,)))

    def to_outputs(side):
        return dot(z[side], down[...], ((1,), (0,)))

    on_weights(lambda copy: copy.wait())

    def group(g):
        first, last, slot = g * GROUP, (g + 1) * GROUP, lax.rem(g, 2)

        @pl.when(g == 0)
        def _():
            stay(0).wait()

        each(lambda s: go(s).wait_recv(), lax.max(first, 1), last)
        each(lambda s: load(s).wait(), first, last)
        each(
            lambda s: go(s).start(), lax.min(first + AHEAD * GROUP, CHIPS),
            lax.min(last + AHEAD * GROUP, CHIPS),
        )
        for n in (0, 1):
            share(n, g).start()
        through(0, g)
        for n in (0, 1):
            share(n, g).wait_recv()
        through(1, g)

        @pl.when(g >= 2)
        def _():
            @pl.when(g == 2)
            def _():
                back_stay().wait()

            each(lambda s: back(s).wait_send(), lax.max(first - 2 * GROUP, 1), last - 2 * GROUP)
            each(lambda s: out(s).wait(), first - 2 * GROUP, last - 2 * GROUP)

        give[0, slot] = to_rows(1).astype(BF16)
        part(0, g).start()
        give[1, slot] = to_outputs(1).astype(BF16)
        part(1, g).start()
        own = to_rows(0)
        part(0, g).wait()
        give[0, slot] = (own + take[0, slot].astype(F32)).astype(BF16)

        @pl.when(g == 0)
        def _():
            back_stay().start()

        each(lambda s: back(s).start(), lax.max(first, 1), last)
        own = to_outputs(0)
        part(1, g).wait()
        give[1, slot] = (own + take[1, slot].astype(F32)).astype(BF16)
        each(lambda s: out(s).start(), first, last)
        at = group_rows(g)

        def weight_grads(cols):
            wide[cols, :] += dot(rows[0, at, cols], dgu[0], ((0,), (0,))) + dot(
                rows[1, at, cols], dgu[1], ((0,), (0,))
            )
            tall[:, cols] += dot(z[0], deos[0, at, cols], ((0,), (0,))) + dot(
                z[1], deos[1, at, cols], ((0,), (0,))
            )

        tiles(weight_grads)

    each(group, 0, groups)

    def store(at):
        wide_ref[at, :] = wide[at, :].astype(BF16)
        tall_ref[:, at] = tall[:, at].astype(BF16)

    tiles(store)
    for g in range(groups):
        for n in (0, 1):
            share(n, g).wait_send()
    each(lambda s: out(s).wait(), (groups - 2) * GROUP, CHIPS)
    each(lambda s: back(s).wait_send(), (groups - 2) * GROUP, CHIPS)
    each(lambda s: go(s).wait_send(), 1, CHIPS)
    each(lambda s: back(s).wait_recv(), 1, CHIPS)


def moe(send, d_eo, own, far):
    chips, size, width = send.shape
    hidden = own[2].shape[0]
    total, groups = chips * size, chips // GROUP
    count = GROUP * size
    vmem, any_space = (pl.BlockSpec(memory_space=space) for space in (pltpu.VMEM, pl.ANY))
    shapes = [send.shape, send.shape, (width, 2 * hidden), (hidden, width)]
    dma = pltpu.SemaphoreType.DMA
    return pl.pallas_call(
        moe_kernel,
        in_specs=[any_space] * 8,
        out_specs=[any_space] * 2 + [vmem] * 2,
        out_shape=[jax.ShapeDtypeStruct(shape, BF16) for shape in shapes],
        scratch_shapes=[
            pltpu.VMEM((2, total, width), BF16),
            pltpu.VMEM((2, total, width), BF16),
            pltpu.VMEM((width, 2 * hidden), BF16),
            pltpu.VMEM((hidden, width), BF16),
            pltpu.VMEM((2, count, hidden), BF16),
            pltpu.VMEM((2, count, 2 * hidden), BF16),
            pltpu.VMEM((width, 2 * hidden), F32),
            pltpu.VMEM((hidden, width), F32),
            pltpu.VMEM((2, 2, count, width), BF16),
            pltpu.VMEM((2, 2, count, width), BF16),
            dma((chips,)), dma((chips,)), dma((chips,)), dma((3,)),
            dma((2, groups)), dma((2, groups)), dma((2, groups)), dma((2, groups)),
            dma((chips,)), dma((chips,)), dma((chips,)),
        ],
        compiler_params=pltpu.CompilerParams(
            collective_id=4, has_side_effects=True, vmem_limit_bytes=56 * 1024 * 1024
        ),
        cost_estimate=pl.CostEstimate(flops=0, bytes_accessed=400_000_000, transcendentals=0),
        name="experts",
    )(send, d_eo, *own, *far)


BLOCK = 64
CTX = 8
WIDE = 256


def rotated(u, gain, cosine, sine):
    scaling = lax.rsqrt(jnp.mean(u * u, axis=-1, keepdims=True) + EPS)
    normed = u * scaling
    n = normed * gain
    rot = n * cosine + pltpu.roll(n, HEAD_SIZE // 2, 1) * sine
    return rot.astype(BF16), normed, scaling


def rotated_back(e, normed, scaling, gain, cosine, sine):
    back = e * cosine + pltpu.roll(e * sine, HEAD_SIZE // 2, 1)
    scaled = back * gain
    inner = jnp.mean(scaled * normed, axis=-1, keepdims=True)
    return scaling * (scaled - normed * inner), jnp.sum(back * normed, axis=0, keepdims=True)


def ctx_peer(step):
    return {"ctx": lax.rem(lax.axis_index("ctx") + step, CTX)}


def beside():
    c = lax.axis_index("ctx")
    return {"ctx": c + 1 - 2 * lax.rem(c, 2)}


def softmax_parts(q_low, k, bias):
    s = dot(q_low, k, ((1,), (1,))) * (HEAD_SIZE ** -0.5) + bias
    e = jnp.exp(s - jnp.max(s, axis=-1, keepdims=True))
    return e / jnp.sum(e, axis=-1, keepdims=True)


def share_kernel(kv, rows_ref, cos_ref, sin_ref, gk_ref, kv_ref, held, send_sem, recv_sem):
    c = lax.axis_index("ctx")
    greet([ctx_peer(step) for step in range(1, CTX)])
    micro, rows = held.shape[0], 2 * BLOCK
    cosine, sine, gk = cos_ref[...], sin_ref[...], gk_ref[...]
    mine = pl.ds(pl.multiple_of(c * BLOCK, BLOCK), BLOCK)
    earlier, own = pl.ds(CTX * BLOCK, BLOCK), pl.ds((CTX + 1) * BLOCK, BLOCK)
    copies = []
    for m in range(micro):
        span = slice(m * rows, (m + 1) * rows)
        for h in range(2 * kv):
            cols = slice(h * HEAD_SIZE, (h + 1) * HEAD_SIZE)
            u = rows_ref[span, cols]
            low = rotated(u, gk, cosine, sine)[0] if h < kv else u.astype(BF16)
            held[m, mine, cols] = low[:BLOCK]
            held[m, own, cols] = low[BLOCK:]
        for step in range(1, CTX):
            part = held.at[m, mine]
            copies.append(
                remote(part, part, send_sem.at[step, m], recv_sem.at[step, m], ctx_peer(step))
            )
        copies.append(
            remote(
                held.at[m, own], held.at[m, earlier], send_sem.at[0, m], recv_sem.at[0, m], beside()
            )
        )
        for copy in copies[-CTX:]:
            copy.start()
    for m in range(micro):
        for step in range(1, CTX):
            source = lax.rem(c + CTX - step, CTX)
            part = held.at[m, pl.ds(pl.multiple_of(source * BLOCK, BLOCK), BLOCK)]
            remote(
                part, part, send_sem.at[step, m], recv_sem.at[step, m], ctx_peer(step)
            ).wait_recv()
        copies[(m + 1) * CTX - 1].wait_recv()
        kv_ref[m] = held[m]
    for copy in copies:
        copy.wait_send()


def attention_kernel(heads, q_ref, cos_ref, sin_ref, gq_ref, bias_ref, k_ref, v_ref, o_ref):
    cosine, sine, gq = cos_ref[...], sin_ref[...], gq_ref[...]
    for e in range(heads):
        cols = slice(e * HEAD_SIZE, (e + 1) * HEAD_SIZE)
        q_low = rotated(q_ref[:, cols], gq, cosine, sine)[0]
        p = softmax_parts(q_low, k_ref[...], bias_ref[...]).astype(BF16)
        o_ref[:, cols] = dot(p, v_ref[...], ((1,), (0,))).astype(BF16)


def backward_kernel(
    kv, heads, qkv_ref, cos_ref, sin_ref, gq_ref, gk_ref, bias_ref, kv_ref, o_ref, a_ref,
    select_ref, middle_ref, cot_ref, gain_moe_ref, tokens_ref, gain_in_ref, w_out_ref, w_qkv_ref, eo_ref, back_ref,
    x_ref, gains_ref, norm_ref, moe_ref, x_other_ref, grad_qkv_ref, grad_out_ref, eo_back_ref,
    w_out, w_qkv, dattn_ref, back_tile, d_b, d_h_ref, do_ref, dqkv_ref, part_sum, wide_tile, tall_tile, grads, given, given_side,
    p_all, ds_all, q_all, do_all, swap_give, swap_take,
    send_sem, recv_sem, load_sem, tile_sem, swap_sem, share_sem, back_sem, x_sem, eo_send, eo_recv,
):
    c, tp = lax.axis_index("ctx"), lax.axis_index("tp")
    width = w_out.shape[0]

    def each(body, low, high):
        def step(i, carry):
            body(i)
            return carry

        lax.fori_loop(low, high, step, 0)

    def tile(i):
        return pl.ds(pl.multiple_of(i * WIDE, WIDE), WIDE)

    def back_load(i):
        slot = lax.rem(i, 2)
        return pltpu.make_async_copy(
            back_ref.at[:, tile(i)], back_tile.at[slot], back_sem.at[i]
        )

    back_load(0).start()
    barrier = pltpu.get_barrier_semaphore()
    signal_chips(barrier)
    loads = [
        pltpu.make_async_copy(w_out_ref.at[:, pl.ds(0, w_out.shape[1])], w_out, load_sem.at[0]),
        pltpu.make_async_copy(w_qkv_ref, w_qkv, load_sem.at[1]),
    ]
    for copy in loads:
        copy.start()
    pl.semaphore_wait(barrier, CHIPS - 1)

    def output(s):
        return remote(
            eo_ref.at[s], eo_back_ref.at[s], eo_send.at[s], eo_recv.at[s], device_at(s, -1)
        )

    def outputs(quarter):
        each(lambda s: output(s).start(), max(quarter * GROUP, 1), (quarter + 1) * GROUP)

    stay = pltpu.make_async_copy(eo_ref.at[0], eo_back_ref.at[0], eo_recv.at[0])
    stay.start()
    outputs(0)
    micro, rows = grads.shape[0], 2 * BLOCK
    q_cols = kv * heads * HEAD_SIZE
    scale = HEAD_SIZE ** -0.5
    cosine, sine, gq, gk = cos_ref[...], sin_ref[...], gq_ref[...], gk_ref[...]
    mine = pl.ds(pl.multiple_of(c * BLOCK, BLOCK), BLOCK)
    earlier, own = pl.ds(CTX * BLOCK, BLOCK), pl.ds((CTX + 1) * BLOCK, BLOCK)

    def combine(i):
        @pl.when(i + 1 < width // WIDE)
        def _():
            back_load(i + 1).start()

        back_load(i).wait()
        d_b[:, tile(i)] = dot(select_ref[...], back_tile[lax.rem(i, 2)], ((1,), (0,)))

    each(combine, 0, width // WIDE)
    moe_total = jnp.zeros((1, width), F32)
    shares = []
    for m in range(micro):
        span = slice(m * BLOCK, (m + 1) * BLOCK)
        u, g = middle_ref[span, :], d_b[span, :]
        scaling = lax.rsqrt(jnp.mean(u * u, axis=-1, keepdims=True) + EPS)
        normed = u * scaling
        moe_total = moe_total + jnp.sum(g * normed, axis=0, keepdims=True)
        scaled = g * gain_moe_ref[...]
        inner = jnp.mean(scaled * normed, axis=-1, keepdims=True)
        d_h = cot_ref[span, :].astype(F32) + scaling * (scaled - normed * inner)
        d_h_ref[span, :] = d_h
        place = pl.ds(pl.multiple_of(m * rows + (1 - tp) * BLOCK, BLOCK), BLOCK)
        dattn_ref[place, :] = d_h.astype(BF16)
        part = dattn_ref.at[place]
        shares.append(remote(part, part, share_sem.at[0, m], share_sem.at[1, m], {"tp": 1 - tp}))
        shares[-1].start()
    moe_ref[...] = moe_total
    for m in range(micro):
        place = pl.ds(pl.multiple_of(m * rows + tp * BLOCK, BLOCK), BLOCK)
        part = dattn_ref.at[place]
        remote(part, part, share_sem.at[0, m], share_sem.at[1, m], {"tp": 1 - tp}).wait_recv()
    outputs(1)
    loads[0].wait()

    def outputs_back(i):
        do_ref[:, tile(i)] = dot(dattn_ref[...], w_out[:, tile(i)], ((1,), (0,))).astype(BF16)

    each(outputs_back, 0, w_out.shape[1] // WIDE)

    def head_cols(h):
        return pl.ds(pl.multiple_of(h * HEAD_SIZE, HEAD_SIZE), HEAD_SIZE)

    def keys_back(m, h, carry):
        span = slice(m * rows, (m + 1) * rows)
        k, v = kv_ref[m, :, head_cols(h)], kv_ref[m, :, head_cols(kv + h)]
        for e in range(heads):
            cols = head_cols(h * heads + e)
            stack = slice(e * rows, (e + 1) * rows)
            q_low = rotated(qkv_ref[span, cols], gq, cosine, sine)[0]
            q_all[stack, :] = q_low
            p = softmax_parts(q_low, k, bias_ref[...])
            p_all[stack, :] = p.astype(BF16)
            do = do_ref[span, cols]
            do_all[stack, :] = do
            dp = dot(do, v, ((1,), (1,)))
            ds = (p * (dp - jnp.sum(dp * p, axis=-1, keepdims=True))).astype(BF16)
            ds_all[m * kv + h, stack, :] = ds
        grads[m, :, head_cols(kv + h)] = dot(p_all[...], do_all[...], ((0,), (0,))).astype(BF16)
        d_k = dot(ds_all[m * kv + h], q_all[...], ((0,), (0,))) * scale
        grads[m, :, head_cols(h)] = d_k.astype(BF16)
        return carry

    def queries_back(m, h, total):
        span = slice(m * rows, (m + 1) * rows)
        k = kv_ref[m, :, head_cols(h)]
        for e in range(heads):
            cols = head_cols(h * heads + e)
            ds = ds_all[m * kv + h, e * rows : (e + 1) * rows, :]
            dqr = (dot(ds, k, ((1,), (0,))) * scale).astype(BF16).astype(F32)
            u = qkv_ref[span, cols]
            scaling = lax.rsqrt(jnp.mean(u * u, axis=-1, keepdims=True) + EPS)
            dq, part = rotated_back(dqr, u * scaling, scaling, gq, cosine, sine)
            dqkv_ref[span, cols] = dq.astype(BF16)
            total = total + part
        return total

    copies = []
    for m in range(micro):
        lax.fori_loop(0, kv, functools.partial(keys_back, m), 0)
        for step in range(1, CTX):
            peer = lax.rem(c + step, CTX)
            part = grads.at[m, pl.ds(pl.multiple_of(peer * BLOCK, BLOCK), BLOCK)]
            copies.append(
                remote(
                    part, given.at[step - 1, m], send_sem.at[step, m], recv_sem.at[step, m],
                    ctx_peer(step),
                )
            )
        copies.append(
            remote(
                grads.at[m, earlier], given_side.at[m], send_sem.at[0, m], recv_sem.at[0, m],
                beside(),
            )
        )
        for copy in copies[-CTX:]:
            copy.start()
        if m == micro - 1:
            outputs(2)
    total = jnp.zeros((1, HEAD_SIZE), F32)
    for m in range(micro):
        total = lax.fori_loop(0, kv, functools.partial(queries_back, m), total)

    def tiles_out(buffer, left, right, out_ref, sems):
        def copy_out(i):
            slot = lax.rem(i, 2)
            return pltpu.make_async_copy(buffer.at[slot], out_ref.at[tile(i)], sems.at[i])

        def step(i):
            @pl.when(i >= 2)
            def _():
                copy_out(i - 2).wait()

            value = dot(left[:, tile(i)], right[...], ((0,), (0,)))
            buffer[lax.rem(i, 2)] = value.astype(BF16)
            copy_out(i).start()

        count = width // WIDE
        each(step, 0, count)
        return lambda: each(lambda i: copy_out(i).wait(), count - 2, count)

    end_out = tiles_out(tall_tile, dattn_ref, o_ref, grad_out_ref, tile_sem.at[0])
    loads[1].wait()

    def queries_in(i):
        part_sum[:, tile(i)] = dot(dqkv_ref[:, :q_cols], w_qkv[tile(i), :q_cols], ((1,), (1,)))

    each(queries_in, 0, width // WIDE)
    k_total = jnp.zeros((1, HEAD_SIZE), F32)
    for m in range(micro):
        for copy in copies[m * CTX : (m + 1) * CTX]:
            copy.wait_recv()
        for h in range(2 * kv):
            cols = slice(h * HEAD_SIZE, (h + 1) * HEAD_SIZE)
            at = slice(q_cols + h * HEAD_SIZE, q_cols + (h + 1) * HEAD_SIZE)
            prompt = grads[m, mine, cols].astype(F32)
            for step in range(CTX - 1):
                prompt = prompt + given[step, m, :, cols].astype(F32)
            cont = grads[m, own, cols].astype(F32) + given_side[m, :, cols].astype(F32)
            e = jnp.concatenate([prompt, cont], axis=0).astype(BF16)
            span = slice(m * rows, (m + 1) * rows)
            if h < kv:
                _, normed, scaling = rotated(qkv_ref[span, at], gk, cosine, sine)
                d, part = rotated_back(e.astype(F32), normed, scaling, gk, cosine, sine)
                k_total = k_total + part
                dqkv_ref[span, at] = d.astype(BF16)
            else:
                dqkv_ref[span, at] = e
    gains_ref[0:1, :] = total
    gains_ref[1:2, :] = k_total

    def keys_in(i):
        part_sum[:, tile(i)] += dot(dqkv_ref[:, q_cols:], w_qkv[tile(i), q_cols:], ((1,), (1,)))

    each(keys_in, 0, width // WIDE)
    for m in range(micro):
        away = pl.ds(pl.multiple_of(m * rows + tp * BLOCK, BLOCK), BLOCK)
        swap_give[m * BLOCK : (m + 1) * BLOCK, :] = part_sum[away, :].astype(BF16)
    swap = remote(swap_give, swap_take, swap_sem.at[0], swap_sem.at[1], {"tp": 1 - tp})
    swap.start()
    outputs(3)
    end_qkv = tiles_out(wide_tile, a_ref, dqkv_ref, grad_qkv_ref, tile_sem.at[1])
    swap.wait()
    norm_total = jnp.zeros((1, width), F32)
    for m in range(micro):
        kept = pl.ds(pl.multiple_of(m * rows + (1 - tp) * BLOCK, BLOCK), BLOCK)
        span = slice(m * BLOCK, (m + 1) * BLOCK)
        g = part_sum[kept, :] + swap_take[span, :].astype(F32)
        u = tokens_ref[span, :].astype(F32)
        scaling = lax.rsqrt(jnp.mean(u * u, axis=-1, keepdims=True) + EPS)
        normed = u * scaling
        norm_total = norm_total + jnp.sum(g * normed, axis=0, keepdims=True)
        scaled = g * gain_in_ref[...]
        inner = jnp.mean(scaled * normed, axis=-1, keepdims=True)
        x_ref[span, :] = (d_h_ref[span, :] + scaling * (scaled - normed * inner)).astype(BF16)
        swap_give[span, :] = x_ref[span, :]
    norm_ref[...] = norm_total
    x_swap = remote(swap_give, x_other_ref, x_sem.at[0], x_sem.at[1], {"tp": 1 - tp})
    x_swap.start()
    for copy in copies + shares:
        copy.wait_send()
    x_swap.wait()
    end_out()
    end_qkv()
    stay.wait()
    each(lambda s: output(s).wait(), 1, CHIPS)


def share_keys(qkv, cosine, sine, gain_key, kv, keys, micro):
    rows, cols = qkv.shape[0], 2 * kv * HEAD_SIZE
    last = qkv.shape[1] // cols - 1

    def whole(shape):
        return pl.BlockSpec(shape, lambda i: (0,) * len(shape))

    return pl.pallas_call(
        functools.partial(share_kernel, kv),
        grid=(1,),
        in_specs=[pl.BlockSpec((rows, cols), lambda i: (0, last)), whole(cosine.shape)]
        + [whole(sine.shape), whole(gain_key.shape)],
        out_specs=whole((micro, keys, cols)),
        out_shape=jax.ShapeDtypeStruct((micro, keys, cols), BF16),
        scratch_shapes=[
            pltpu.VMEM((micro, keys, cols), BF16),
            pltpu.SemaphoreType.DMA((CTX, micro)),
            pltpu.SemaphoreType.DMA((CTX, micro)),
        ],
        compiler_params=pltpu.CompilerParams(
            collective_id=2, has_side_effects=True, vmem_limit_bytes=VMEM_LIMIT
        ),
        cost_estimate=pl.CostEstimate(flops=0, bytes_accessed=50_000_000, transcendentals=0),
        name="share_keys",
    )(qkv, cosine, sine, gain_key)


def attention(qkv, cosine, sine, gain_query, bias, kv_all, kv):
    micro, keys, cols = kv_all.shape
    rows = bias.shape[0]
    heads = qkv.shape[1] // HEAD_SIZE // kv - 2
    width = heads * HEAD_SIZE

    def whole(v):
        return pl.BlockSpec(v.shape, lambda m, g: (0,) * v.ndim)

    return pl.pallas_call(
        functools.partial(attention_kernel, heads),
        grid=(micro, kv),
        in_specs=[pl.BlockSpec((rows, width), lambda m, g: (m, g))]
        + [whole(v) for v in (cosine, sine, gain_query, bias)]
        + [
            pl.BlockSpec((None, keys, HEAD_SIZE), lambda m, g: (m, 0, g)),
            pl.BlockSpec((None, keys, HEAD_SIZE), lambda m, g: (m, 0, kv + g)),
        ],
        out_specs=pl.BlockSpec((rows, width), lambda m, g: (m, g)),
        out_shape=jax.ShapeDtypeStruct((micro * rows, kv * width), BF16),
        compiler_params=pltpu.CompilerParams(vmem_limit_bytes=VMEM_LIMIT),
        cost_estimate=pl.CostEstimate(flops=0, bytes_accessed=60_000_000, transcendentals=0),
        name="attention_forward",
    )(qkv, cosine, sine, gain_query, bias, kv_all, kv_all)


def backward(qkv, heads_in, kv_all, o, a, moe_in, w_out, w_qkv, eo, back, kv):
    heads = qkv.shape[1] // HEAD_SIZE // kv - 2
    bias = heads_in[-1]
    rows, keys = bias.shape
    micro, _, kv_cols = kv_all.shape
    width, cols = w_qkv.shape
    total, q_cols = qkv.shape[0], kv * heads * HEAD_SIZE
    vmem, any_space = (pl.BlockSpec(memory_space=space) for space in (pltpu.VMEM, pl.ANY))
    dma = pltpu.SemaphoreType.DMA
    return pl.pallas_call(
        functools.partial(backward_kernel, kv, heads),
        in_specs=[vmem] * 15 + [any_space] * 4,
        out_specs=[vmem] * 4 + [any_space] * 4,
        out_shape=[
            jax.ShapeDtypeStruct((micro * BLOCK, width), BF16),
            jax.ShapeDtypeStruct((2, HEAD_SIZE), F32),
            jax.ShapeDtypeStruct((1, width), F32),
            jax.ShapeDtypeStruct((1, width), F32),
            jax.ShapeDtypeStruct((micro * BLOCK, width), BF16),
            jax.ShapeDtypeStruct((width, cols), BF16),
            jax.ShapeDtypeStruct((width, q_cols), BF16),
            jax.ShapeDtypeStruct(eo.shape, BF16),
        ],
        scratch_shapes=[
            pltpu.VMEM((width, q_cols), BF16),
            pltpu.VMEM((width, cols), BF16),
            pltpu.VMEM((total, width), BF16),
            pltpu.VMEM((2, back.shape[0], WIDE), BF16),
            pltpu.VMEM((micro * BLOCK, width), F32),
            pltpu.VMEM((micro * BLOCK, width), F32),
            pltpu.VMEM((total, q_cols), BF16),
            pltpu.VMEM((total, cols), BF16),
            pltpu.VMEM((total, width), F32),
            pltpu.VMEM((2, WIDE, cols), BF16),
            pltpu.VMEM((2, WIDE, q_cols), BF16),
            pltpu.VMEM((micro, keys, kv_cols), BF16),
            pltpu.VMEM((CTX - 1, micro, BLOCK, kv_cols), BF16),
            pltpu.VMEM((micro, BLOCK, kv_cols), BF16),
            pltpu.VMEM((heads * rows, keys), BF16),
            pltpu.VMEM((micro * kv, heads * rows, keys), BF16),
            pltpu.VMEM((heads * rows, HEAD_SIZE), BF16),
            pltpu.VMEM((heads * rows, HEAD_SIZE), BF16),
            pltpu.VMEM((micro * BLOCK, width), BF16),
            pltpu.VMEM((micro * BLOCK, width), BF16),
            dma((CTX, micro)), dma((CTX, micro)), dma((2,)), dma((2, width // WIDE)), dma((2,)),
            dma((2, micro)), dma((width // WIDE,)), dma((2,)),
            dma((CHIPS,)), dma((CHIPS,)),
        ],
        compiler_params=pltpu.CompilerParams(
            collective_id=3, has_side_effects=True, vmem_limit_bytes=60 * 1024 * 1024
        ),
        cost_estimate=pl.CostEstimate(flops=0, bytes_accessed=250_000_000, transcendentals=0),
        name="attention_backward",
    )(qkv, *heads_in, kv_all, o, a, *moe_in, w_out, w_qkv, eo, back)


def normalize(rows, gain):
    scaling = lax.rsqrt(jnp.mean(rows * rows, axis=-1, keepdims=True) + EPS)
    return rows * scaling * gain, scaling


def normalize_back(rows, scaling, gain, upstream):
    normed = rows * scaling
    gain_grad = jnp.sum((upstream * normed).reshape(-1, rows.shape[-1]), axis=0)
    scaled = upstream * gain
    inner = jnp.mean(scaled * normed, axis=-1, keepdims=True)
    return scaling * (scaled - normed * inner), gain_grad


def swap_tp(value):
    return lax.ppermute(value, "tp", [(0, 1), (1, 0)])


def local(
    x_prompt, x_cont, cot_prompt, cot_cont, ids_prompt, ids_cont, gates_prompt, gates_cont,
    norm_gain, query_weight, key_matrix, value_matrix, out_weight, query_gain, key_gain, moe_gain,
    expert_gate, expert_up, expert_down,
):
    micro = x_prompt.shape[0]
    prompt_rows, cont_rows, width = x_prompt.shape[2], x_cont.shape[2], x_prompt.shape[3]
    block = cont_rows
    rows = 2 * block
    s = lax.axis_index("ctx")
    ctx = lax.axis_size("ctx")
    first = lax.axis_index("tp") == 0
    peers = lax.axis_size(ALL)
    q_cols, kv_cols = query_weight.shape[1], key_matrix.shape[1]
    kv = kv_cols // HEAD_SIZE
    qkv_cols = q_cols + 2 * kv_cols
    shard_rows = query_weight.shape[0]
    hidden = expert_gate.shape[2]
    slots = cont_rows * TOPK // peers

    fsdp, tp = lax.axis_size("fsdp"), lax.axis_size("tp")
    chips = [(2 * y, c, t) for y in range(fsdp // 2) for c in range(ctx) for t in range(tp)]
    groups = [[((f + core) * ctx + c) * tp + t for f, c, t in chips] for core in range(2)]
    expert_of = jnp.array([(f + t) * ctx + c for f, c, t in chips], jnp.int32)

    def exchange(rows_of):
        return lax.all_to_all(
            rows_of, ("fsdp", "ctx", "tp"), split_axis=0, concat_axis=0, tiled=True,
            axis_index_groups=groups,
        )

    def pad(v):
        return jnp.pad(v[:, 0], ((0, 0), (0, block - prompt_rows), (0, 0)))

    x_first, x_second = pad(x_prompt), x_cont[:, 0]
    own_tokens = jnp.where(first, x_second, x_first).astype(F32)
    own_cot = jnp.where(first, cot_cont[:, 0], pad(cot_prompt))
    ids_pad = jnp.pad(
        ids_prompt[:, 0], ((0, 0), (0, block - prompt_rows), (0, 0)), constant_values=-1
    )
    own_ids = jnp.where(first, ids_cont[:, 0], ids_pad)
    own_gates = jnp.where(first, gates_cont[:, 0], pad(gates_prompt))

    y, z, x = chip_at(jnp.arange(peers, dtype=jnp.int32), 1)
    near = (2 * y + x // 2) * ctx + 2 * z + x % 2
    order = jnp.pad(jnp.stack([expert_of, near]), ((0, 0), (0, HEAD_SIZE - peers)), constant_values=-2)

    def lanes(v):
        return jnp.pad(v, [(0, 0)] * (v.ndim - 1) + [(0, HEAD_SIZE - v.shape[-1])])

    extra = jnp.stack([lanes(v) for v in (norm_gain, moe_gain, query_gain, key_gain)])
    extra = jnp.pad(extra, ((0, shard_rows - extra.shape[0]), (0, 0)))
    own_experts = (expert_gate[0], expert_up[0], expert_down[0])
    w_qkv, w_out_extra, far_experts, routing = gather_weights(
        query_weight, key_matrix, value_matrix, out_weight, extra,
        own_ids.reshape(-1, TOPK), own_gates.reshape(-1, TOPK), order,
        own_cot.reshape(-1, width), peers * micro * slots, *own_experts,
    )
    select_near, mixing, spread = routing
    w_out = w_out_extra[:, :q_cols]
    gains = w_out_extra[:, q_cols:].reshape(peers, shard_rows, HEAD_SIZE)[:, :4].astype(F32)
    gain_in, gain_moe = (gains[:, n, :shard_rows].reshape(-1) for n in (0, 1))
    head_rows = query_gain.shape[0]
    gain_query, gain_key = (gains[:, n, :head_rows].reshape(-1) for n in (2, 3))

    offsets = jnp.arange(rows, dtype=jnp.int32)
    is_prompt = offsets < block
    prompt_pos = s * prompt_rows + offsets
    cont_pos = s * cont_rows + offsets - block
    rot_place = jnp.where(is_prompt, prompt_pos, PROMPT + cont_pos % CL).astype(F32)
    steps_freq = jnp.arange(HEAD_SIZE // 2, dtype=F32) * (2.0 / HEAD_SIZE)
    angles = rot_place[:, None] * jnp.power(THETA, -steps_freq)[None, :]
    cosine, sine = jnp.cos(angles), jnp.sin(angles)
    cosine = jnp.concatenate([cosine, cosine], axis=1)
    sine = jnp.concatenate([-sine, sine], axis=1)
    keys = (ctx + 2) * block
    key_index = jnp.arange(keys, dtype=jnp.int32)[None, :]
    key_off = key_index % block
    key_prompt_pos = key_index // block * prompt_rows + key_off
    key_cont = (s - 1) * cont_rows + key_index - ctx * block
    is_cont = jnp.logical_not(is_prompt)[:, None]
    visible = jnp.where(
        key_index < ctx * block,
        jnp.logical_and(
            key_off < prompt_rows,
            jnp.logical_or(is_cont, key_prompt_pos <= prompt_pos[:, None]),
        ),
        jnp.logical_and(
            is_cont,
            jnp.logical_and(
                key_cont // CL == cont_pos[:, None] // CL, key_cont <= cont_pos[:, None]
            ),
        ),
    )
    bias = jnp.where(visible, 0.0, NEG).astype(F32)

    def arranged(own, other):
        return jnp.where(first, other, own), jnp.where(first, own, other)

    def sum_own(part):
        part = part.reshape(micro, rows, width)
        given = jnp.where(first, part[:, :block], part[:, block:]).astype(BF16)
        kept = jnp.where(first, part[:, block:], part[:, :block])
        return kept + swap_tp(given).astype(F32)

    tokens = jnp.concatenate([x_first, x_second], axis=1).astype(F32).reshape(-1, width)
    a = normalize(tokens, gain_in)[0].astype(BF16)
    qkv = dot(a, w_qkv, ((1,), (0,)))
    heads_in = (cosine, sine, gain_query[None], gain_key[None], bias)
    kv_all = share_keys(qkv, cosine, sine, gain_key[None], kv, keys, micro)

    spread, kv_all = lax.optimization_barrier((spread, kv_all))
    d_eo_rows = exchange(spread).reshape(peers, micro * slots, width)
    o = attention(qkv, cosine, sine, gain_query[None], bias, kv_all, kv)
    middle = own_tokens + sum_own(dot(o, w_out, ((1,), (1,))))
    b_normed, b_scale = normalize(middle, gain_moe)
    b_low = b_normed.astype(BF16)

    send = dot(select_near, b_low.reshape(-1, width), ((0,), (0,))).astype(BF16)
    back, eo, wide_here, tall_here = moe(
        send.reshape(d_eo_rows.shape), d_eo_rows, own_experts, far_experts
    )
    moe_in = (
        select_near, middle.reshape(-1, width), own_cot.reshape(-1, width), gain_moe[None],
        own_tokens.astype(BF16).reshape(-1, width), gain_in[None],
    )
    x_own, head_totals, norm_total, moe_total, x_other, grad_qkv, grad_out, eo_back = backward(
        qkv, heads_in, kv_all, o, a, moe_in, w_out_extra, w_qkv, eo, back.reshape(-1, width), kv
    )
    x_own, x_other = x_own.reshape(middle.shape), x_other.reshape(middle.shape)
    moe_out = dot(mixing, eo_back.reshape(-1, width), ((1,), (0,)))
    moe_out = (moe_out[: micro * block] + moe_out[micro * block :]).reshape(middle.shape)
    y_own = (middle + moe_out).astype(BF16)
    extra_grads = jnp.stack(
        [
            lanes(v.reshape(peers, -1))
            for v in (norm_total, moe_total, head_totals[0], head_totals[1])
        ],
        axis=1,
    )
    extra_grads = jnp.pad(extra_grads, ((0, 0), (0, shard_rows - extra_grads.shape[1]), (0, 0)))
    extra_grads = extra_grads.reshape(-1, HEAD_SIZE).astype(BF16)
    share, share_out, wide_there, tall_there, y_other = scatter_grads(
        grad_qkv, grad_out, extra_grads, wide_here, tall_here, y_own
    )
    out_first, out_second = arranged(y_own, y_other)
    grad_first, grad_second = arranged(x_own, x_other)
    grad_wide = jnp.where(native(), wide_here, wide_there).astype(F32)
    grad_down = jnp.where(native(), tall_here, tall_there).astype(F32)
    gain_share = share_out[:, q_cols:]
    return (
        out_first[:, None, :prompt_rows],
        out_second[:, None],
        grad_first[:, None, :prompt_rows],
        grad_second[:, None],
        gain_share[0, :shard_rows],
        share[:, :q_cols],
        share[:, q_cols : q_cols + kv_cols],
        share[:, q_cols + kv_cols : qkv_cols],
        share_out[:, :q_cols],
        gain_share[2, :head_rows],
        gain_share[3, :head_rows],
        gain_share[1, :shard_rows],
        grad_wide[None, :, :hidden],
        grad_wide[None, :, hidden:],
        grad_down[None],
    )


def solution(mesh):
    rows = P(None, "fsdp", "ctx", None)
    vector = P(("fsdp", "ctx"))
    matrix = P(("fsdp", "ctx"), "tp")
    wide = P(("fsdp", "ctx"), None, "tp")
    tall = P(("fsdp", "ctx"), "tp", None)
    in_specs = (rows,) * 8 + (vector,) + (matrix,) * 4 + (vector,) * 3 + (wide, wide, tall)
    out_specs = (rows,) * 4 + (vector,) + (matrix,) * 4 + (vector,) * 3 + (wide, wide, tall)
    return jax.shard_map(local, mesh=mesh, in_specs=in_specs, out_specs=out_specs, check_vma=False)
```
